32 devices in a mesh: blk: 4 (over z), expert: 8 (over y, x, core).
Axes of the slice: x: 2, y: 2, z: 4, core: 2. Of those that a mesh axis runs over, the one named last changes fastest.
Arguments:
- tokens: bfloat16 [16, 2048, 768], P('expert', 'blk'), may hold values from -6 to 6
- doc_ids: int32 [16, 2048], P('expert'), may hold values from 0 to 28, as said below
- routes: int32 [4, 16, 512, 1], P('blk', 'expert'), may hold values from 0 to 7; in each aligned block of 1024 rows (0 to 1023, 1024 to 2047, ..., all dimensions but the last counted through in order) at most 256 rows name the same one
- ln1_gain: float32 [768], replicated, may hold values from 0.5 to 1.5
- ln1_bias: float32 [768], replicated, may hold values from -1 to 1
- qkv_weight: bfloat16 [768, 2304], P('expert'), may hold values from -0.21875 to 0.21875
- qv_bias: float32 [2, 768], replicated, may hold values from -1 to 1
- out_weight: bfloat16 [768, 768], P('expert'), may hold values from -1.5 to 1.5
- out_bias: float32 [768], replicated, may hold values from -1 to 1
- ln2_gain: float32 [768], replicated, may hold values from 0.5 to 1.5
- ln2_bias: float32 [768], replicated, may hold values from -1 to 1
- centroids: bfloat16 [8, 768], replicated, may hold values from -0.15625 to 0.15625
- up_weight: bfloat16 [8, 768, 3072], P('expert'), may hold values from -0.21875 to 0.21875
- up_bias: float32 [8, 3072], P('expert'), may hold values from -0.6 to 0.6
- down_weight: bfloat16 [8, 3072, 768], P('expert'), may hold values from -0.21875 to 0.21875
- down_bias: float32 [8, 768], P('expert'), may hold values from -0.6 to 0.6
- cotangent: bfloat16 [16, 2048, 768], P('expert', 'blk'), may hold values from -6 to 6
Outputs:
- layer_out: float32 [16, 2048, 768], P('expert', 'blk')
- token_grad: float32 [16, 2048, 768], P('expert', 'blk')
- ln1_gain_grad: float32 [768], P('expert')
- ln1_bias_grad: float32 [768], P('expert')
- qkv_grad: float32 [768, 2304], P('expert')
- qv_bias_grad: float32 [2, 768], P(None, 'expert')
- out_weight_grad: float32 [768, 768], P('expert')
- out_bias_grad: float32 [768], P('expert')
- ln2_gain_grad: float32 [768], P('expert')
- ln2_bias_grad: float32 [768], P('expert')
- centroid_grad: float32 [8, 768], P(None, 'expert')
- up_grad: float32 [8, 768, 3072], P('expert', 'blk')
- up_bias_grad: float32 [8, 3072], P('expert', 'blk')
- down_grad: float32 [8, 3072, 768], P('expert', 'blk')
- down_bias_grad: float32 [8, 768], P('expert', 'blk')
The draws below stay inside these ranges and needn't reach their ends.
Inputs may be any that keep to these rules, and one draw needn't show every extreme that they name: `doc_ids`: within a row the numbers start at 0, never fall and rise by at most one from a position to the next; equal numbers mark one document. In each group of 2 rows (rows g * 2 up to g * 2 + 1), half of the rows hold one document of 2048 tokens, and each other row holds documents of 64 to 256 tokens, one of exactly 256; the last document of a row may be cut shorter by the row's end. In every draw some row reaches the largest number. `routes`: among the tokens of one device (aligned blocks of 1024 consecutive entries in the array's order) at most 256 name one expert; in every draw some device names some expert exactly 256 times.
All inputs are finite; a program needn't handle non-finite values.
Results may differ from the reference program's by a relative error of at most 0.018.
Values may be sent and summed in bfloat16 or wider, within the bound.
A program may use at most 320 MiB of HBM per device.

```python
import math
import jax
import jax.numpy as jnp
import numpy as np
from jax import lax

D = 768
HEADS = 12
HEAD_DIM = 64
FF = 3072
SEQ = 2048
SHORT = 256
ROWS = 2
EXPERTS = 8
SPAN = 512
ROWS_ALL = 16
CAP = 256
N_BLK = 4
N_EXPERT = 8


def draw_doc_ids(key, part):
    key = jax.random.fold_in(key, 11)
    length_key, place_key, order_key, dense_key = jax.random.split(key, 4)
    most_docs = SEQ // (SHORT // 4)
    groups = ROWS_ALL // ROWS
    scores = jax.random.randint(order_key, (groups, ROWS), 0, 1 << 20) * ROWS + jnp.arange(ROWS, dtype=jnp.int32)[None, :]
    ranking = jnp.argsort(jnp.argsort(scores, axis=1), axis=1)
    single = (ranking < ROWS // 2).reshape(ROWS_ALL)
    dense_group = jax.random.randint(dense_key, (), 0, groups)
    dense_row = ((ranking == ROWS // 2) & (jnp.arange(groups, dtype=jnp.int32)[:, None] == dense_group)).reshape(ROWS_ALL)
    lengths = jax.random.randint(length_key, (ROWS_ALL, most_docs), SHORT // 4, SHORT + 1)
    chosen = jax.random.randint(place_key, (ROWS_ALL, 1), 0, SEQ // SHORT)
    columns = jnp.arange(most_docs, dtype=jnp.int32)[None, :]
    lengths = jnp.where(dense_row[:, None], SHORT // 4, lengths)
    lengths = jnp.where(columns == chosen, SHORT, lengths)
    bounds = jnp.cumsum(lengths, axis=1)
    places = jnp.arange(SEQ, dtype=jnp.int32)
    numbers = jnp.sum((bounds[:, None, :] <= places[None, :, None]).astype(jnp.int32), axis=2)
    return jnp.where(single[:, None], 0, numbers).astype(jnp.int32)


def levels(stream_key, dims, pieces, least, high):
    def one(dim, parts):
        draws = jax.random.uniform(jax.random.fold_in(jax.random.fold_in(stream_key, 6), dim), (parts,), jnp.float32, least / len(pieces), high / len(pieces))
        return jnp.repeat(jnp.exp(draws), dims[dim] // parts).reshape((-1,) + (1,) * (len(dims) - dim - 1))

    level = one(*pieces[0])
    for cut in pieces[1:]:
        level = level * one(*cut)
    return level


def deal_out(stream_key, own, number, rows, number_of, top, most, skew):
    order = jax.random.permutation(stream_key, number_of)
    crowded, usual = portions_of(number_of, rows * top, most, skew, True), portions_of(number_of, rows * top, most, skew, False)
    places = jnp.arange(number_of)

    def named(sizes, turn):
        used = int((sizes > 0).sum())
        fixed = max(1, used // 4)
        moved = fixed + (places - fixed + turn * (used - fixed)) % max(1, number_of - fixed)
        return jnp.zeros((number_of,), jnp.int32).at[order[jnp.where(places < fixed, places, moved)]].set(jnp.asarray(sizes, jnp.int32))

    sizes = jnp.where(number % 4 == 0, named(crowded, number // 4), named(usual, number - number // 4 - 1))
    mixed = jax.random.permutation(jax.random.fold_in(own, 3), number_of)
    source_of, taker = mixed[0:number_of // 2 * 2:2], mixed[1:number_of // 2 * 2:2]
    margin = jnp.minimum(sizes[source_of] - 1, most - sizes[taker]) // 2
    margin = jnp.where((source_of == order[0]) | (taker == order[0]) | (sizes[taker] == 0), 0, jnp.maximum(margin, 0))
    moved = jax.random.randint(jax.random.fold_in(own, 4), (number_of // 2,), 0, 1 << 20) % (margin + 1)
    sizes = sizes.at[source_of].add(-moved).at[taker].add(moved)
    labels = jnp.searchsorted(jnp.cumsum(sizes), jnp.arange(rows * top), side="right").astype(jnp.int32)
    table = labels.reshape(top, rows).T
    table = table[jax.random.permutation(jax.random.fold_in(own, 1), rows)]
    turn = jax.random.randint(jax.random.fold_in(own, 2), (rows, 1), 0, top)
    return jnp.take_along_axis(table, (jnp.arange(top)[None, :] + turn) % top, axis=1)


def portions_of(number_of, total, limit, lean, full):
    weights = [(1 << 20) // math.isqrt(standing ** lean) + 1 for standing in range(1, number_of + 1)]
    largest = limit if full else min(limit, max(-(-total // number_of), total * weights[0] // sum(weights)))
    least = 1 if total - largest >= number_of - 1 else 0
    given, spare = [largest] + [least] * (number_of - 1), total - largest - least * (number_of - 1)
    while spare > 0:
        movable = [i for i in range(1, number_of) if given[i] < largest] or [i for i in range(1, number_of) if given[i] < limit]
        pool, budget = sum([weights[i] for i in movable]), spare
        for i in movable:
            addition = min(limit - given[i], max(1, budget * weights[i] // pool), spare)
            given[i] = given[i] + addition
            spare = spare - addition
    return np.array(given)


def bell_draw(rng, shape, scale, bound, shards=(), kind=jnp.bfloat16):
    array = scale * jax.random.normal(rng, shape, jnp.float32)
    if shards:
        array = array * levels(rng, shape, shards, -0.22, 0.18)
    return jnp.clip(array, -bound, bound).astype(kind)


def setup_inputs(seed: int = 0) -> dict:
    key_list = jax.random.split(jax.random.key(seed), 18)
    tokens = bell_draw(key_list[0], (ROWS_ALL, SEQ, D), 1.0, 6.0, ((0, 8), (1, 4)))
    doc_ids = draw_doc_ids(jax.random.fold_in(key_list[17], 71), 0)
    routes_keys = jax.random.split(jax.random.fold_in(key_list[2], 1), N_BLK * ROWS_ALL * SPAN // (ROWS * SPAN))
    routes_turns = jax.random.permutation(jax.random.fold_in(key_list[2], 3), N_BLK * ROWS_ALL * SPAN // (ROWS * SPAN))
    routes = jax.vmap(lambda own, number: deal_out(jax.random.fold_in(key_list[2], 2), own, number, ROWS * SPAN, EXPERTS, 1, CAP, 1))(routes_keys, routes_turns).reshape((N_BLK, ROWS_ALL, SPAN, 1))
    ln1_gain = jnp.clip(1.0 + 0.1 * jax.random.normal(key_list[3], (D,), jnp.float32), 0.5, 1.5)
    ln1_bias = bell_draw(key_list[4], (D,), 0.2, 1.0, (), jnp.float32)
    qkv_weight = bell_draw(key_list[5], (D, 3 * D), D ** -0.5, 0.21875, ((0, 8),))
    qv_bias = bell_draw(key_list[6], (2, D), 0.2, 1.0, (), jnp.float32)
    out_weight = bell_draw(key_list[7], (D, D), 16 ** -0.5, 1.5, ((0, 8),))
    out_bias = bell_draw(key_list[8], (D,), 0.2, 1.0, (), jnp.float32)
    ln2_gain = jnp.clip(1.0 + 0.1 * jax.random.normal(key_list[9], (D,), jnp.float32), 0.5, 1.5)
    ln2_bias = bell_draw(key_list[10], (D,), 0.2, 1.0, (), jnp.float32)
    centroids = bell_draw(key_list[11], (EXPERTS, D), (2 * D) ** -0.5, 0.15625)
    up_weight = bell_draw(key_list[12], (EXPERTS, D, FF), D ** -0.5, 0.21875, ((0, 8),))
    up_bias = bell_draw(key_list[13], (EXPERTS, FF), 0.1, 0.6, ((0, 8),), jnp.float32)
    down_weight = bell_draw(key_list[14], (EXPERTS, FF, D), (FF // 4) ** -0.5, 0.21875, ((0, 8),))
    down_bias = bell_draw(key_list[15], (EXPERTS, D), 0.1, 0.6, ((0, 8),), jnp.float32)
    cotangent = bell_draw(key_list[16], (ROWS_ALL, SEQ, D), 1.0, 6.0, ((0, 8), (1, 4)))
    return dict(tokens=tokens, doc_ids=doc_ids, routes=routes, ln1_gain=ln1_gain, ln1_bias=ln1_bias, qkv_weight=qkv_weight, qv_bias=qv_bias, out_weight=out_weight, out_bias=out_bias, ln2_gain=ln2_gain, ln2_bias=ln2_bias, centroids=centroids, up_weight=up_weight, up_bias=up_bias, down_weight=down_weight, down_bias=down_bias, cotangent=cotangent)


NEGATIVE = -1e+30
EPSILON = 1e-05

@jax.custom_vjp
def low(v):
    return lax.optimization_barrier(v.astype(jnp.bfloat16)).astype(jnp.float32)

@jax.custom_vjp
def low_back(v):
    return v

def low_keep(v):
    return (low(v), None)

def low_pass(kept, grad):
    return (grad,)

def back_keep(v):
    return (v, None)

def back_low(kept, grad):
    return (low(grad),)
low.defvjp(low_keep, low_pass)
low_back.defvjp(back_keep, back_low)

def layer_norm(values, scales, shifts):
    average = lax.optimization_barrier(jnp.mean(values, axis=-1, keepdims=True))
    centred = values - average
    variance = lax.optimization_barrier(jnp.mean(centred * centred, axis=-1, keepdims=True))
    return centred * lax.rsqrt(variance + EPSILON) * scales + shifts

def reference(tokens, doc_ids, routes, ln1_gain, ln1_bias, qkv_weight, qv_bias, out_weight, out_bias, ln2_gain, ln2_bias, centroids, up_weight, up_bias, down_weight, down_bias, cotangent):
    highest = lax.Precision.HIGHEST
    score_scale = HEAD_DIM ** (-0.5)
    total_rows = ROWS_ALL * SEQ
    route_grid = routes[..., 0]
    device_routes = route_grid.reshape(N_BLK, N_EXPERT, ROWS * SPAN)
    onehot = (device_routes[..., None] == jnp.arange(EXPERTS, dtype=jnp.int32)).astype(jnp.int32)
    ranking = jnp.cumsum(onehot, axis=2) - 1
    slot_of = lax.optimization_barrier(jnp.sum(ranking * onehot, axis=3))
    block_no = jnp.arange(N_BLK, dtype=jnp.int32)[:, None, None, None]
    group_no = jnp.arange(N_EXPERT, dtype=jnp.int32)[None, :, None, None]
    row_no = jnp.arange(ROWS, dtype=jnp.int32)[None, None, :, None]
    cell_no = jnp.arange(SPAN, dtype=jnp.int32)[None, None, None, :]
    token_no = ((group_no * ROWS + row_no) * SEQ + block_no * SPAN + cell_no).reshape(N_BLK, N_EXPERT, ROWS * SPAN)
    column_no = (block_no[..., 0] * N_EXPERT + group_no[..., 0]) * CAP + slot_of
    width_all = N_BLK * N_EXPERT * CAP
    slot_table = jnp.full((EXPERTS, width_all), total_rows, jnp.int32).at[device_routes.reshape(-1), column_no.reshape(-1)].set(token_no.reshape(-1))
    slot_place = jnp.zeros((total_rows,), jnp.int32).at[token_no.reshape(-1)].set((device_routes * width_all + column_no).reshape(-1))
    expert_of = route_grid.transpose(1, 0, 2).reshape(total_rows)

    def forward(tokens_in, gain_one, shift_one, qkv_in, qv_in, out_in, out_shift, gain_two, shift_two, centroid_in, up_in, up_shift, down_in, down_shift):

        def attend_row(packed):
            row_tokens, row_ids = packed
            normed = low(layer_norm(row_tokens, gain_one, shift_one))
            bias_row = jnp.concatenate([qv_in[0], jnp.zeros((D,), jnp.float32), qv_in[1]])
            projected = low_back(low(jnp.dot(normed, qkv_in, precision=highest) + bias_row))
            query_all = projected[:, :D].reshape(SEQ, HEADS, HEAD_DIM)
            key_rows = projected[:, D:2 * D].reshape(SEQ, HEADS, HEAD_DIM)
            value_rows = projected[:, 2 * D:].reshape(SEQ, HEADS, HEAD_DIM)
            key_pos = jnp.arange(SEQ, dtype=jnp.int32)
            block_len = min(512, SEQ)

            def attend_block(offset):
                query_part = lax.dynamic_slice_in_dim(query_all, offset, block_len, 0)
                raw_scores = low_back(jnp.einsum('qhd,khd->hqk', query_part, key_rows, precision=highest) * score_scale)
                query_ids = lax.dynamic_slice_in_dim(row_ids, offset, block_len, 0)
                query_pos = offset + jnp.arange(block_len, dtype=jnp.int32)
                visible = (query_ids[:, None] == row_ids[None, :]) & (key_pos[None, :] <= query_pos[:, None])
                masked = jnp.where(visible[None], raw_scores, NEGATIVE)
                top_score = lax.optimization_barrier(jnp.max(masked, axis=-1, keepdims=True))
                log_total = top_score + jnp.log(lax.optimization_barrier(jnp.sum(jnp.exp(masked - top_score), axis=-1, keepdims=True)))
                weights = low(jnp.exp(masked - log_total))
                return jnp.einsum('hqk,khd->qhd', weights, value_rows, precision=highest)
            offsets = jnp.arange(SEQ // block_len, dtype=jnp.int32) * block_len
            attended = lax.map(jax.checkpoint(attend_block), offsets).reshape(SEQ, D)
            attended = low_back(low(attended))
            return row_tokens + low_back(jnp.dot(attended, out_in, precision=highest)) + out_shift
        middle = lax.map(jax.checkpoint(attend_row), (tokens_in, doc_ids))
        flat_middle = middle.reshape(total_rows, D)
        normed_two = layer_norm(flat_middle, gain_two, shift_two)
        expert_in = low_back(low(normed_two))
        padded = jnp.concatenate([expert_in, jnp.zeros((1, D), jnp.float32)])

        def expert_apply(packed):
            index_row, weight_first, shift_first, weight_second, shift_second = packed
            rows_in = padded[index_row]
            hidden = low_back(jnp.dot(rows_in, weight_first, precision=highest) + shift_first)
            active = low(jax.nn.gelu(hidden, approximate=False))
            return low_back(low(jnp.dot(active, weight_second, precision=highest) + shift_second))
        produced = lax.map(jax.checkpoint(expert_apply), (slot_table, up_in, up_shift, down_in, down_shift))
        expert_rows = produced.reshape(-1, D)[slot_place]
        centroid_rows = centroid_in[expert_of]
        gate_value = jax.nn.sigmoid(lax.optimization_barrier(jnp.sum(normed_two * centroid_rows, axis=1)))
        return (flat_middle + gate_value[:, None] * expert_rows).reshape(ROWS_ALL, SEQ, D)
    result, pullback = jax.vjp(forward, tokens.astype(jnp.float32), ln1_gain, ln1_bias, qkv_weight.astype(jnp.float32), qv_bias, out_weight.astype(jnp.float32), out_bias, ln2_gain, ln2_bias, centroids.astype(jnp.float32), up_weight.astype(jnp.float32), up_bias, down_weight.astype(jnp.float32), down_bias)
    gradients = pullback(cotangent.astype(jnp.float32))
    return (result, gradients[0], gradients[1], gradients[2], gradients[3], gradients[4], gradients[5], gradients[6], gradients[7], gradients[8], gradients[9], gradients[10], gradients[11], gradients[12], gradients[13])
```

```python
import functools

import jax
import jax.numpy as jnp
from jax import lax
from jax.experimental import pallas as pl
from jax.experimental.pallas import tpu as pltpu
from jax.sharding import PartitionSpec as P

HEADS = 12
SHORT = 256
NEGATIVE = -1e30
EPSILON = 1e-05
BF = jnp.bfloat16
F32 = jnp.float32


def dot_nn(a, b):
    return lax.dot_general(a, b, (((1,), (0,)), ((), ())), preferred_element_type=F32)


def dot_nt(a, b):
    return lax.dot_general(a, b, (((1,), (1,)), ((), ())), preferred_element_type=F32)


def norm_parts(values):
    average = jnp.mean(values, axis=-1, keepdims=True)
    centred = values - average
    variance = jnp.mean(centred * centred, axis=-1, keepdims=True)
    scale = lax.rsqrt(variance + EPSILON)
    return centred * scale, scale


def layer_norm(values, gain, bias):
    return norm_parts(values)[0] * gain + bias


def norm_back(upstream, normal, scale, gain):
    t = upstream * gain
    inner = (
        t
        - jnp.mean(t, axis=-1, keepdims=True)
        - normal * jnp.mean(t * normal, axis=-1, keepdims=True)
    )
    return inner * scale, jnp.sum(upstream * normal, axis=0), jnp.sum(upstream, axis=0)


def split_heads(qkv):
    size = qkv.shape[1] // 3
    scale = size ** (-0.5)
    return (
        (qkv[:, :size].astype(F32) * scale).astype(BF),
        qkv[:, size : 2 * size],
        qkv[:, 2 * size :],
    )


def causal(rows, columns, shift):
    row = lax.broadcasted_iota(jnp.int32, (rows, columns), 0)
    column = lax.broadcasted_iota(jnp.int32, (rows, columns), 1)
    return row <= column + shift


def long_forward(x_ref, w_ref, b_ref, qkv_ref, wide_ref, low_ref, total_ref, *, block):
    qkv = (dot_nn(x_ref[...], w_ref[0]) + b_ref[0]).astype(BF)
    qkv_ref[0] = qkv
    query, key, value = split_heads(qkv)
    value_t = value.T
    visible = causal(block, block, 0)
    for i in range(x_ref.shape[0] // block):
        lo, hi = i * block, (i + 1) * block
        own = query[lo:hi]
        near = jnp.where(visible, dot_nt(key[lo:hi], own), NEGATIVE)
        top = jnp.max(near, axis=0, keepdims=True)
        if i:
            far = dot_nt(key[:lo], own)
            top = jnp.maximum(top, jnp.max(far, axis=0, keepdims=True))
        near = jnp.exp(near - top)
        total = jnp.sum(near, axis=0, keepdims=True)
        out = dot_nn(value_t[:, lo:hi], near.astype(BF))
        if i:
            far = jnp.exp(far - top)
            total = total + jnp.sum(far, axis=0, keepdims=True)
            out = out + dot_nn(value_t[:, :lo], far.astype(BF))
        out = out / total
        wide_ref[:, lo:hi] = out
        low_ref[i] = out.astype(BF)
        total_ref[0, :, lo:hi] = top + jnp.log(total)


def long_backward(
    qkv_ref, grad_ref, wide_ref, total_ref, out_ref, key_acc, value_acc, *, block
):
    query, key, value = split_heads(qkv_ref[0])
    size = query.shape[1]
    scale = size ** (-0.5)
    key_t = key.T
    visible = causal(block, block, 0)
    count = query.shape[0] // block
    key_acc[...] = jnp.zeros_like(key_acc)
    value_acc[...] = jnp.zeros_like(value_acc)
    for i in range(count):
        lo, hi = i * block, (i + 1) * block
        own = query[lo:hi]
        grad_t = grad_ref[i]
        grad = grad_t.T
        delta = jnp.sum(grad_t.astype(F32) * wide_ref[:, lo:hi], axis=0, keepdims=True)
        total = total_ref[0, :, lo:hi]
        query_grad = None
        for start, stop in ((lo, hi), (0, lo)):
            if start == stop:
                continue
            weights = jnp.exp(dot_nt(key[start:stop], own) - total)
            if start == lo:
                weights = jnp.where(visible, weights, 0.0)
            scores = weights * (dot_nt(value[start:stop], grad) - delta)
            scores_low = scores.astype(BF)
            value_acc[start:stop] += dot_nn(weights.astype(BF), grad)
            key_acc[start:stop] += dot_nn(scores_low, own)
            part = dot_nn(key_t[:, start:stop], scores_low)
            query_grad = part if query_grad is None else query_grad + part
        out_ref[i, 0] = (query_grad * scale).astype(BF)
    key_grad = key_acc[...].T.astype(BF)
    value_grad = value_acc[...].T.astype(BF)
    for i in range(count):
        out_ref[i, 1] = key_grad[:, i * block : (i + 1) * block]
        out_ref[i, 2] = value_grad[:, i * block : (i + 1) * block]


def short_visible(key_ids, query_ids, i, block, halo):
    lo = i * block
    same = key_ids[lo : lo + halo + block] == query_ids[:, lo : lo + block]
    return same & causal(halo + block, block, halo)


def short_forward(
    x_ref, w_ref, b_ref, key_ids, query_ids, qkv_ref, wide_ref, low_ref, total_ref, *, block
):
    qkv = (dot_nn(x_ref[...], w_ref[0]) + b_ref[0]).astype(BF)
    qkv_ref[0] = qkv
    query, key, value = split_heads(qkv)
    value_t = value.T
    span = query_ids.shape[1]
    halo = x_ref.shape[0] - span
    for i in range(span // block):
        lo, hi = i * block, (i + 1) * block
        visible = short_visible(key_ids[...], query_ids[...], i, block, halo)
        scores = dot_nt(key[lo : hi + halo], query[lo + halo : hi + halo])
        scores = jnp.where(visible, scores, NEGATIVE)
        top = jnp.max(scores, axis=0, keepdims=True)
        scores = jnp.exp(scores - top)
        total = jnp.sum(scores, axis=0, keepdims=True)
        out = dot_nn(value_t[:, lo : hi + halo], scores.astype(BF)) / total
        wide_ref[:, lo:hi] = out
        low_ref[:, lo:hi] = out.astype(BF)
        total_ref[0, :, lo:hi] = top + jnp.log(total)


def short_backward(
    qkv_ref,
    grad_ref,
    wide_ref,
    total_ref,
    key_ids,
    query_ids,
    query_out,
    own_out,
    halo_out,
    key_acc,
    value_acc,
    *,
    block,
):
    query, key, value = split_heads(qkv_ref[0])
    scale = query.shape[1] ** (-0.5)
    key_t = key.T
    span = query_ids.shape[1]
    halo = query.shape[0] - span
    key_acc[...] = jnp.zeros_like(key_acc)
    value_acc[...] = jnp.zeros_like(value_acc)
    for i in range(span // block):
        lo, hi = i * block, (i + 1) * block
        visible = short_visible(key_ids[...], query_ids[...], i, block, halo)
        own = query[lo + halo : hi + halo]
        grad_t = grad_ref[:, lo:hi]
        grad = grad_t.T
        delta = jnp.sum(grad_t.astype(F32) * wide_ref[:, lo:hi], axis=0, keepdims=True)
        scores = dot_nt(key[lo : hi + halo], own)
        weights = jnp.exp(jnp.where(visible, scores, NEGATIVE) - total_ref[0, :, lo:hi])
        scores = weights * (dot_nt(value[lo : hi + halo], grad) - delta)
        scores_low = scores.astype(BF)
        value_acc[lo : hi + halo] += dot_nn(weights.astype(BF), grad)
        key_acc[lo : hi + halo] += dot_nn(scores_low, own)
        part = dot_nn(key_t[:, lo : hi + halo], scores_low)
        query_out[:, lo:hi] = (part * scale).astype(BF)
    for n, acc in enumerate((key_acc, value_acc)):
        whole = acc[...].T
        halo_out[n] = whole[:, :halo].astype(BF)
        own_out[n] = whole[:, halo:]


def whole_spec(shape):
    return pl.BlockSpec(shape, lambda *_: (0,) * len(shape))


def call(kernel, grid, ins, in_specs, outs, out_specs, scratch, flops, bytes_accessed, vmem=56 << 20):
    return pl.pallas_call(
        kernel,
        grid=grid,
        in_specs=in_specs,
        out_specs=out_specs,
        out_shape=outs,
        scratch_shapes=scratch,
        compiler_params=pltpu.CompilerParams(vmem_limit_bytes=vmem),
        cost_estimate=pl.CostEstimate(
            flops=int(flops), bytes_accessed=int(bytes_accessed), transcendentals=0
        ),
    )(*ins)


def gelu_parts(hidden):
    cdf = 0.5 * (1.0 + lax.erf(hidden * 0.7071067811865476))
    density = jnp.exp(-0.5 * hidden * hidden) * 0.3989422804014327
    return hidden * cdf, cdf + hidden * density


def expert_kernel(
    x_ref,
    cot_ref,
    up_ref,
    down_ref,
    up_shift_ref,
    down_shift_ref,
    centroid_ref,
    out_ref,
    grad_ref,
    up_out,
    down_out,
    up_shift_out,
    down_shift_out,
    gate_ref,
    low_ref,
    xt_ref,
    gt_ref,
    out_acc,
    grad_acc,
    *,
    chunk,
):
    step = pl.program_id(0)
    rows = x_ref.shape[0]

    @pl.when(step == 0)
    def _():
        for lo in range(0, rows, chunk):
            x = x_ref[lo : lo + chunk]
            logit = jnp.sum(x.astype(F32) * centroid_ref[...], axis=1, keepdims=True)
            gate = 1.0 / (1.0 + jnp.exp(-logit))
            gate_ref[lo : lo + chunk] = gate
            low = (cot_ref[lo : lo + chunk].astype(F32) * gate).astype(BF)
            low_ref[lo : lo + chunk] = low
            xt_ref[:, lo : lo + chunk] = x.T
            gt_ref[:, lo : lo + chunk] = low.T
            part = jnp.sum(low.astype(F32), axis=0, keepdims=True)
            if lo:
                down_shift_out[...] += part
            else:
                down_shift_out[...] = part
        out_acc[...] = jnp.zeros_like(out_acc)
        grad_acc[...] = jnp.zeros_like(grad_acc)

    up_total = None
    for lo in range(0, rows, chunk):
        x = x_ref[lo : lo + chunk]
        low = low_ref[lo : lo + chunk]
        hidden = dot_nn(x, up_ref[...]) + up_shift_ref[...]
        active, slope = gelu_parts(hidden)
        active = active.astype(BF)
        grad_hidden = dot_nt(low, down_ref[...]) * slope
        grad_low = grad_hidden.astype(BF)
        out_acc[lo : lo + chunk] += dot_nn(active, down_ref[...])
        grad_acc[lo : lo + chunk] += dot_nt(grad_low, up_ref[...])
        up_part = dot_nn(xt_ref[:, lo : lo + chunk], grad_low)
        down_part = dot_nn(gt_ref[:, lo : lo + chunk], active)
        shift_part = jnp.sum(grad_low.astype(F32), axis=0, keepdims=True)
        if up_total is None:
            up_total, down_total, shift_total = up_part, down_part, shift_part
        else:
            up_total, down_total, shift_total = (
                up_total + up_part,
                down_total + down_part,
                shift_total + shift_part,
            )
    up_out[...] = up_total.astype(BF)
    down_out[0] = down_total.astype(BF)
    up_shift_out[...] = shift_total

    @pl.when(step == pl.num_programs(0) - 1)
    def _():
        for lo in range(0, rows, chunk):
            gate = gate_ref[lo : lo + chunk]
            out = (out_acc[lo : lo + chunk] + down_shift_ref[...]).astype(BF)
            out_ref[lo : lo + chunk] = out
            inner = jnp.sum(
                cot_ref[lo : lo + chunk].astype(F32) * out.astype(F32), axis=1, keepdims=True
            )
            logit_grad = inner * gate * (1.0 - gate)
            grad_ref[lo : lo + chunk] = (
                grad_acc[lo : lo + chunk] + logit_grad * centroid_ref[...]
            ).astype(BF)


def run_expert(x, cot, up_weight, down_weight, up_shift, down_shift, centroid, slices):
    rows, width = x.shape
    hidden = up_weight.shape[1]
    block = hidden // 8
    per = hidden // slices // block
    chunk = min(512, rows)
    steps = hidden // block
    return call(
        functools.partial(expert_kernel, chunk=chunk),
        (steps,),
        (x, cot, up_weight, down_weight, up_shift, down_shift, centroid),
        [
            whole_spec((rows, width)),
            whole_spec((rows, width)),
            pl.BlockSpec((width, block), lambda f: (0, f)),
            pl.BlockSpec((block, width), lambda f: (f, 0)),
            pl.BlockSpec((1, block), lambda f: (0, f)),
            whole_spec((1, width)),
            whole_spec((1, width)),
        ],
        (
            jax.ShapeDtypeStruct((rows, width), BF),
            jax.ShapeDtypeStruct((rows, width), BF),
            jax.ShapeDtypeStruct((width, hidden), BF),
            jax.ShapeDtypeStruct((slices, width, hidden // slices), BF),
            jax.ShapeDtypeStruct((1, hidden), F32),
            jax.ShapeDtypeStruct((1, width), F32),
        ),
        (
            whole_spec((rows, width)),
            whole_spec((rows, width)),
            pl.BlockSpec((width, block), lambda f: (0, f)),
            pl.BlockSpec((1, width, block), lambda f: (f // per, 0, f % per)),
            pl.BlockSpec((1, block), lambda f: (0, f)),
            whole_spec((1, width)),
        ),
        [
            pltpu.VMEM((rows, 1), F32),
            pltpu.VMEM((rows, width), BF),
            pltpu.VMEM((width, rows), BF),
            pltpu.VMEM((width, rows), BF),
            pltpu.VMEM((rows, width), F32),
            pltpu.VMEM((rows, width), F32),
        ],
        12 * rows * width * hidden,
        8 * width * hidden + 8 * rows * width,
    )


def halving_scatter(parts, axis, count):
    me = lax.axis_index(axis)
    bit = 1
    held = parts
    while bit < count:
        pairs = [(i, i ^ bit) for i in range(count)]
        half = held.reshape((held.shape[0] // 2, 2) + held.shape[1:])
        mine = (me // bit) % 2
        keep = lax.dynamic_index_in_dim(half, mine, 1, keepdims=False)
        send = lax.dynamic_index_in_dim(half, 1 - mine, 1, keepdims=False)
        came = lax.ppermute(send, axis, pairs)
        held = keep.astype(F32) + came.astype(F32)
        bit *= 2
        if bit < count:
            held = held.astype(BF)
    return held[0]


def on_device(
    tokens,
    doc_ids,
    routes,
    ln1_gain,
    ln1_bias,
    qkv_weight,
    qv_bias,
    out_weight,
    out_bias,
    ln2_gain,
    ln2_bias,
    centroids,
    up_weight,
    up_bias,
    down_weight,
    down_bias,
    cotangent,
):
    rows, span, width = tokens.shape
    heads = HEADS
    size = width // heads
    blocks = lax.axis_size("blk")
    own = lax.axis_index("blk")
    count = rows * span
    length = blocks * span
    halo = min(SHORT, span)
    share = -(-heads // blocks)
    pad_heads = share * blocks - heads

    gathered = lax.all_gather(
        jnp.concatenate([qkv_weight, out_weight], axis=1), "expert", axis=0, tiled=True
    )
    full_qkv = gathered[:, : 3 * width]
    full_out = gathered[:, 3 * width :]
    head_weight = (
        full_qkv.reshape(width, 3, heads, size).transpose(2, 0, 1, 3).reshape(heads, width, 3 * size)
    )
    shift_row = jnp.stack([qv_bias[0], jnp.zeros((width,), F32), qv_bias[1]])
    head_shift = (
        shift_row.reshape(3, heads, size).transpose(1, 0, 2).reshape(heads, 1, 3 * size)
    )
    long_weight = lax.dynamic_slice_in_dim(
        jnp.pad(head_weight, ((0, pad_heads), (0, 0), (0, 0))), own * share, share, 0
    )
    long_shift = lax.dynamic_slice_in_dim(
        jnp.pad(head_shift, ((0, pad_heads), (0, 0), (0, 0))), own * share, share, 0
    )

    long_at = (doc_ids[0, -1] != 0).astype(jnp.int32)

    def pick(pair, at):
        return lax.dynamic_index_in_dim(pair, at, 0, keepdims=False)

    def in_order(long_part, short_part, axis):
        first = jnp.where(long_at == 0, long_part, short_part)
        second = jnp.where(long_at == 0, short_part, long_part)
        return jnp.concatenate([first, second], axis=axis)

    long_tokens = pick(tokens, long_at)
    short_tokens = pick(tokens, 1 - long_at)
    all_tokens = lax.all_gather(long_tokens, "blk", axis=0, tiled=True)
    halo_tokens = lax.ppermute(
        short_tokens[span - halo :], "blk", [(i, i + 1) for i in range(blocks - 1)]
    )
    short_ids = jnp.concatenate(
        [jnp.full((halo,), -1, jnp.int32), pick(doc_ids, 1 - long_at)]
    )
    short_ids = lax.dynamic_slice_in_dim(short_ids, own * span, halo + span, 0)
    key_ids = short_ids[:, None]
    query_ids = short_ids[None, halo:]

    def low_norm(part):
        return layer_norm(part.astype(F32), ln1_gain, ln1_bias).astype(BF)

    long_normed = low_norm(all_tokens)
    short_normed = low_norm(jnp.concatenate([halo_tokens, short_tokens], axis=0))

    long_qkv, long_wide, long_low, long_total = call(
        functools.partial(long_forward, block=span),
        (share,),
        (long_normed, long_weight, long_shift),
        [
            whole_spec((length, width)),
            pl.BlockSpec((1, width, 3 * size), lambda h: (h, 0, 0)),
            pl.BlockSpec((1, 1, 3 * size), lambda h: (h, 0, 0)),
        ],
        (
            jax.ShapeDtypeStruct((share, length, 3 * size), BF),
            jax.ShapeDtypeStruct((share * size, length), F32),
            jax.ShapeDtypeStruct((blocks, share * size, span), BF),
            jax.ShapeDtypeStruct((share, 1, length), F32),
        ),
        (
            pl.BlockSpec((1, length, 3 * size), lambda h: (h, 0, 0)),
            pl.BlockSpec((size, length), lambda h: (h, 0)),
            pl.BlockSpec((blocks, size, span), lambda h: (0, h, 0)),
            pl.BlockSpec((1, 1, length), lambda h: (h, 0, 0)),
        ),
        [],
        2 * share * length * (width * 3 * size + length * 256),
        6 * length * width,
    )
    long_attended = lax.all_to_all(long_low, "blk", 0, 0, tiled=True).reshape(-1, span)[:width]
    short_qkv, short_wide, short_low, short_total = call(
        functools.partial(short_forward, block=halo),
        (heads,),
        (short_normed, head_weight, head_shift, key_ids, query_ids),
        [
            whole_spec((halo + span, width)),
            pl.BlockSpec((1, width, 3 * size), lambda h: (h, 0, 0)),
            pl.BlockSpec((1, 1, 3 * size), lambda h: (h, 0, 0)),
            whole_spec((halo + span, 1)),
            whole_spec((1, span)),
        ],
        (
            jax.ShapeDtypeStruct((heads, halo + span, 3 * size), BF),
            jax.ShapeDtypeStruct((width, span), F32),
            jax.ShapeDtypeStruct((width, span), BF),
            jax.ShapeDtypeStruct((heads, 1, span), F32),
        ),
        (
            pl.BlockSpec((1, halo + span, 3 * size), lambda h: (h, 0, 0)),
            pl.BlockSpec((size, span), lambda h: (h, 0)),
            pl.BlockSpec((size, span), lambda h: (h, 0)),
            pl.BlockSpec((1, 1, span), lambda h: (h, 0, 0)),
        ),
        [],
        2 * heads * (halo + span) * (width * 3 * size + 2 * halo * 256),
        8 * span * width,
    )
    attended_t = in_order(long_attended, short_low, 1)

    expert_count = centroids.shape[0]
    capacity = 2 * count // expert_count
    slots = expert_count * capacity
    route_flat = routes.reshape(count)
    onehot = route_flat[:, None] == jnp.arange(expert_count, dtype=jnp.int32)[None, :]
    ranking = jnp.cumsum(onehot.astype(jnp.int32), axis=0) - 1
    slot_of = route_flat * capacity + jnp.sum(jnp.where(onehot, ranking, 0), axis=1)
    slot_line = jnp.arange(slots, dtype=jnp.int32)
    to_slots = (slot_line[:, None] == slot_of[None, :]).astype(BF)
    from_slots = (slot_of[:, None] == slot_line[None, :]).astype(BF)

    def exchange(flat):
        sent = flat.reshape(expert_count, capacity, width)
        return lax.all_to_all(sent, "expert", 0, 0, tiled=True).reshape(slots, width)

    grad_low = cotangent.reshape(count, width)
    received_cot = exchange(dot_nn(to_slots, grad_low).astype(BF))

    token_rows = tokens.astype(F32).reshape(count, width)
    middle = (
        token_rows
        + lax.dot_general(
            attended_t, full_out, (((0,), (0,)), ((), ())), preferred_element_type=F32
        )
        + out_bias
    )
    normal_two, scale_two = norm_parts(middle)
    normed_two = normal_two * ln2_gain + ln2_bias
    received = exchange(dot_nn(to_slots, normed_two.astype(BF)).astype(BF))
    centroid_rows = jnp.dot(onehot.astype(BF), centroids, preferred_element_type=F32)
    gate = jax.nn.sigmoid(jnp.sum(normed_two * centroid_rows, axis=1))

    own_centroid = lax.dynamic_index_in_dim(
        centroids.astype(F32), lax.axis_index("expert"), 0, keepdims=True
    )
    produced, slot_grad, up_term, down_term, up_shift_term, down_shift_term = run_expert(
        received,
        received_cot,
        up_weight[0],
        down_weight[0],
        up_bias,
        down_bias,
        own_centroid,
        blocks,
    )
    back_grad = exchange(slot_grad)
    back_out = exchange(produced)
    up_sum = halving_scatter(up_term.reshape(blocks, width // blocks, -1), "blk", blocks)
    down_sum = halving_scatter(down_term, "blk", blocks).T

    grad_normed_two = dot_nn(from_slots, back_grad)
    inner_two, ln2_gain_term, ln2_bias_term = norm_back(
        grad_normed_two, normal_two, scale_two, ln2_gain
    )
    grad_out = grad_low.astype(F32)
    grad_middle = grad_out + inner_two
    out_shift_term = jnp.sum(grad_middle, axis=0)
    grad_middle_low = grad_middle.astype(BF)
    grad_attended_t = lax.dot_general(
        full_out, grad_middle_low, (((1,), (1,)), ((), ())), preferred_element_type=F32
    ).astype(BF)
    grad_pair = grad_attended_t.reshape(width, rows, span)
    long_grad = lax.dynamic_index_in_dim(grad_pair, long_at, 1, keepdims=False)
    short_grad = lax.dynamic_index_in_dim(grad_pair, 1 - long_at, 1, keepdims=False)
    long_grad = jnp.pad(long_grad, ((0, pad_heads * size), (0, 0)))
    long_grad = lax.all_to_all(
        long_grad.reshape(blocks, share * size, span), "blk", 0, 0, tiled=True
    )
    out_term = lax.dot_general(
        attended_t, grad_middle_low, (((1,), (0,)), ((), ())), preferred_element_type=F32
    )

    long_back = call(
        functools.partial(long_backward, block=span),
        (share,),
        (long_qkv, long_grad, long_wide, long_total),
        [
            pl.BlockSpec((1, length, 3 * size), lambda h: (h, 0, 0)),
            pl.BlockSpec((blocks, size, span), lambda h: (0, h, 0)),
            pl.BlockSpec((size, length), lambda h: (h, 0)),
            pl.BlockSpec((1, 1, length), lambda h: (h, 0, 0)),
        ],
        jax.ShapeDtypeStruct((blocks, 3, share * size, span), BF),
        pl.BlockSpec((blocks, 3, size, span), lambda h: (0, 0, h, 0)),
        [pltpu.VMEM((length, size), F32), pltpu.VMEM((length, size), F32)],
        5 * share * length * length * 256,
        8 * length * width,
    )
    long_back = lax.all_to_all(long_back, "blk", 0, 0, tiled=True)
    long_back = long_back.transpose(1, 0, 2, 3).reshape(3, -1, span)[:, :width]
    query_back, own_back, halo_back = call(
        functools.partial(short_backward, block=halo),
        (heads,),
        (short_qkv, short_grad, short_wide, short_total, key_ids, query_ids),
        [
            pl.BlockSpec((1, halo + span, 3 * size), lambda h: (h, 0, 0)),
            pl.BlockSpec((size, span), lambda h: (h, 0)),
            pl.BlockSpec((size, span), lambda h: (h, 0)),
            pl.BlockSpec((1, 1, span), lambda h: (h, 0, 0)),
            whole_spec((halo + span, 1)),
            whole_spec((1, span)),
        ],
        (
            jax.ShapeDtypeStruct((width, span), BF),
            jax.ShapeDtypeStruct((2, width, span), F32),
            jax.ShapeDtypeStruct((2, width, halo), BF),
        ),
        (
            pl.BlockSpec((size, span), lambda h: (h, 0)),
            pl.BlockSpec((2, size, span), lambda h: (0, h, 0)),
            pl.BlockSpec((2, size, halo), lambda h: (0, h, 0)),
        ),
        [pltpu.VMEM((halo + span, size), F32), pltpu.VMEM((halo + span, size), F32)],
        5 * heads * span * 2 * 2 * halo * 256,
        16 * span * width,
    )
    halo_back = lax.ppermute(halo_back, "blk", [(i + 1, i) for i in range(blocks - 1)])
    own_back = own_back + jnp.pad(halo_back.astype(F32), ((0, 0), (0, 0), (span - halo, 0)))
    short_back = jnp.concatenate([query_back[None], own_back.astype(BF)], axis=0)
    back_t = in_order(
        long_back.reshape(3 * width, span), short_back.reshape(3 * width, span), 1
    )

    normal_one, scale_one = norm_parts(token_rows)
    normed_low = (normal_one * ln1_gain + ln1_bias).astype(BF)
    qkv_term = lax.dot_general(
        normed_low, back_t, (((0,), (1,)), ((), ())), preferred_element_type=F32
    )
    qv_sums = jnp.sum(back_t.astype(F32), axis=1)
    grad_normed_one = lax.dot_general(
        back_t, full_qkv, (((0,), (1,)), ((), ())), preferred_element_type=F32
    )
    inner_one, ln1_gain_term, ln1_bias_term = norm_back(
        grad_normed_one, normal_one, scale_one, ln1_gain
    )
    grad_tokens = grad_middle + inner_one

    expert_rows = dot_nn(from_slots, back_out)
    result = middle + gate[:, None] * expert_rows
    grad_logit = jnp.sum(grad_out * expert_rows, axis=1) * gate * (1.0 - gate)
    centroid_term = jnp.einsum(
        "te,td->de",
        onehot.astype(F32) * grad_logit[:, None],
        normed_two,
        precision=lax.Precision.HIGHEST,
    )

    small = jnp.stack(
        [
            qv_sums[:width],
            qv_sums[2 * width :],
            out_shift_term,
            ln1_gain_term,
            ln1_bias_term,
            ln2_gain_term,
            ln2_bias_term,
        ],
        axis=1,
    )
    n_small = small.shape[1]
    packed = jnp.concatenate([qkv_term, out_term, small, centroid_term], axis=1).astype(BF)
    packed = lax.psum_scatter(packed, "expert", scatter_dimension=0, tiled=True)
    packed = lax.psum(packed, "blk").astype(F32)
    qkv_sum = packed[:, : 3 * width]
    out_sum = packed[:, 3 * width : 4 * width]
    small_sum = packed[:, 4 * width : 4 * width + n_small]
    centroid_sum = packed[:, 4 * width + n_small :].T
    shift_sum = lax.psum_scatter(
        jnp.concatenate(
            [up_shift_term.reshape(blocks, -1), down_shift_term.reshape(blocks, -1)], axis=1
        ).astype(BF),
        "blk",
        scatter_dimension=0,
        tiled=True,
    ).astype(F32)
    up_shift_sum = shift_sum[:, : up_bias.shape[1] // blocks]
    down_shift_sum = shift_sum[:, up_bias.shape[1] // blocks :]
    return (
        result.reshape(rows, span, width),
        grad_tokens.reshape(rows, span, width),
        small_sum[:, 3],
        small_sum[:, 4],
        qkv_sum,
        small_sum[:, :2].T,
        out_sum,
        small_sum[:, 2],
        small_sum[:, 5],
        small_sum[:, 6],
        centroid_sum,
        up_sum[None],
        up_shift_sum,
        down_sum[None],
        down_shift_sum,
    )


def solution(mesh):
    return jax.shard_map(
        on_device,
        mesh=mesh,
        in_specs=(
            P("expert", "blk", None),
            P("expert", None),
            P("blk", "expert", None, None),
            P(),
            P(),
            P("expert", None),
            P(),
            P("expert", None),
            P(),
            P(),
            P(),
            P(),
            P("expert", None, None),
            P("expert", None),
            P("expert", None, None),
            P("expert", None),
            P("expert", "blk", None),
        ),
        out_specs=(
            P("expert", "blk", None),
            P("expert", "blk", None),
            P("expert"),
            P("expert"),
            P("expert", None),
            P(None, "expert"),
            P("expert", None),
            P("expert"),
            P("expert"),
            P("expert"),
            P(None, "expert"),
            P("expert", "blk", None),
            P("expert", "blk"),
            P("expert", "blk", None),
            P("expert", "blk"),
        ),
        check_vma=False,
    )
```

```python
import functools

import jax
import jax.numpy as jnp
from jax import lax
from jax.experimental import pallas as pl
from jax.experimental.pallas import tpu as pltpu
from jax.sharding import PartitionSpec as P

HEADS = 12
SHORT = 256
NEGATIVE = -1e30
EPSILON = 1e-05
BF = jnp.bfloat16
F32 = jnp.float32


def dot_nn(a, b):
    return lax.dot_general(a, b, (((1,), (0,)), ((), ())), preferred_element_type=F32)


def dot_nt(a, b):
    return lax.dot_general(a, b, (((1,), (1,)), ((), ())), preferred_element_type=F32)


def norm_parts(values):
    average = jnp.mean(values, axis=-1, keepdims=True)
    centred = values - average
    variance = jnp.mean(centred * centred, axis=-1, keepdims=True)
    scale = lax.rsqrt(variance + EPSILON)
    return centred * scale, scale


def layer_norm(values, gain, bias):
    return norm_parts(values)[0] * gain + bias


def norm_back(upstream, normal, scale, gain):
    t = upstream * gain
    inner = (
        t
        - jnp.mean(t, axis=-1, keepdims=True)
        - normal * jnp.mean(t * normal, axis=-1, keepdims=True)
    )
    return inner * scale, jnp.sum(upstream * normal, axis=0), jnp.sum(upstream, axis=0)


def causal(rows, columns, shift):
    row = lax.broadcasted_iota(jnp.int32, (rows, columns), 0)
    column = lax.broadcasted_iota(jnp.int32, (rows, columns), 1)
    return row <= column + shift


def norm_low(values, gain, bias):
    return layer_norm(values.astype(F32), gain, bias).astype(BF)


def project(x_ref, gain_ref, bias_ref, weights, shifts, stores, size, chunk):
    rows = x_ref.shape[0]
    for lo in range(0, rows, chunk):
        low = norm_low(x_ref[lo : lo + chunk], gain_ref[...], bias_ref[...])
        for kind, (weight, shift) in enumerate(zip(weights, shifts)):
            part = dot_nn(low, weight[...])
            if shift is not None:
                part = part + shift[...]
            part = part.astype(BF)
            for head in range(part.shape[1] // size):
                stores[kind, head, lo : lo + chunk] = part[:, head * size : (head + 1) * size]


def scaled(query):
    return (query.astype(F32) * query.shape[-1] ** (-0.5)).astype(BF)


def long_forward(
    x_ref,
    gain_ref,
    bias_ref,
    query_weight,
    key_weight,
    value_weight,
    query_shift,
    value_shift,
    qkv_ref,
    wide_ref,
    low_ref,
    total_ref,
    *,
    block,
):
    head = pl.program_id(0)
    size = qkv_ref.shape[3]

    @pl.when(head == 0)
    def _():
        project(
            x_ref,
            gain_ref,
            bias_ref,
            (query_weight, key_weight, value_weight),
            (query_shift, None, value_shift),
            qkv_ref,
            size,
            block,
        )

    query, key, value = scaled(qkv_ref[0, head]), qkv_ref[1, head], qkv_ref[2, head]
    value_t = value.T
    visible = causal(block, block, 0)
    for i in range(x_ref.shape[0] // block):
        lo, hi = i * block, (i + 1) * block
        own = query[lo:hi]
        near = jnp.where(visible, dot_nt(key[lo:hi], own), NEGATIVE)
        top = jnp.max(near, axis=0, keepdims=True)
        if i:
            far = dot_nt(key[:lo], own)
            top = jnp.maximum(top, jnp.max(far, axis=0, keepdims=True))
        near = jnp.exp(near - top)
        total = jnp.sum(near, axis=0, keepdims=True)
        out = dot_nn(value_t[:, lo:hi], near.astype(BF))
        if i:
            far = jnp.exp(far - top)
            total = total + jnp.sum(far, axis=0, keepdims=True)
            out = out + dot_nn(value_t[:, :lo], far.astype(BF))
        out = out / total
        wide_ref[:, lo:hi] = out
        low_ref[i] = out.astype(BF)
        total_ref[0, :, lo:hi] = top + jnp.log(total)


def long_backward(
    qkv_ref, grad_ref, wide_ref, total_ref, out_ref, key_acc, value_acc, *, block
):
    query, key, value = scaled(qkv_ref[0, 0]), qkv_ref[1, 0], qkv_ref[2, 0]
    scale = query.shape[1] ** (-0.5)
    key_t = key.T
    visible = causal(block, block, 0)
    count = query.shape[0] // block
    key_acc[...] = jnp.zeros_like(key_acc)
    value_acc[...] = jnp.zeros_like(value_acc)
    for i in range(count):
        lo, hi = i * block, (i + 1) * block
        own = query[lo:hi]
        grad_t = grad_ref[i]
        grad = grad_t.T
        delta = jnp.sum(grad_t.astype(F32) * wide_ref[:, lo:hi], axis=0, keepdims=True)
        total = total_ref[0, :, lo:hi]
        query_grad = None
        for start, stop in ((lo, hi), (0, lo)):
            if start == stop:
                continue
            weights = jnp.exp(dot_nt(key[start:stop], own) - total)
            if start == lo:
                weights = jnp.where(visible, weights, 0.0)
            scores = weights * (dot_nt(value[start:stop], grad) - delta)
            scores_low = scores.astype(BF)
            value_acc[start:stop] += dot_nn(weights.astype(BF), grad)
            key_acc[start:stop] += dot_nn(scores_low, own)
            part = dot_nn(key_t[:, start:stop], scores_low)
            query_grad = part if query_grad is None else query_grad + part
        out_ref[i, 0] = (query_grad * scale).astype(BF)
    key_grad = key_acc[...].T.astype(BF)
    value_grad = value_acc[...].T.astype(BF)
    for i in range(count):
        out_ref[i, 1] = key_grad[:, i * block : (i + 1) * block]
        out_ref[i, 2] = value_grad[:, i * block : (i + 1) * block]


def short_visible(key_ids, query_ids, i, block, halo):
    lo = i * block
    same = key_ids[lo : lo + halo + block] == query_ids[:, lo : lo + block]
    return same & causal(halo + block, block, halo)


def short_forward(
    x_ref,
    gain_ref,
    bias_ref,
    weight_ref,
    shift_ref,
    key_ids,
    query_ids,
    qkv_ref,
    wide_ref,
    low_ref,
    total_ref,
    *,
    block,
):
    head = pl.program_id(0)
    width = x_ref.shape[1]

    @pl.when(head == 0)
    def _():
        kinds = [slice(n * width, (n + 1) * width) for n in range(3)]
        project(
            x_ref,
            gain_ref,
            bias_ref,
            [weight_ref.at[:, kind] for kind in kinds],
            (shift_ref.at[0:1], None, shift_ref.at[1:2]),
            qkv_ref,
            qkv_ref.shape[3],
            block,
        )

    query, key, value = scaled(qkv_ref[0, head]), qkv_ref[1, head], qkv_ref[2, head]
    value_t = value.T
    span = query_ids.shape[1]
    halo = x_ref.shape[0] - span
    for i in range(span // block):
        lo, hi = i * block, (i + 1) * block
        visible = short_visible(key_ids[...], query_ids[...], i, block, halo)
        scores = dot_nt(key[lo : hi + halo], query[lo + halo : hi + halo])
        scores = jnp.where(visible, scores, NEGATIVE)
        top = jnp.max(scores, axis=0, keepdims=True)
        scores = jnp.exp(scores - top)
        total = jnp.sum(scores, axis=0, keepdims=True)
        out = dot_nn(value_t[:, lo : hi + halo], scores.astype(BF)) / total
        wide_ref[:, lo:hi] = out
        low_ref[:, lo:hi] = out.astype(BF)
        total_ref[0, :, lo:hi] = top + jnp.log(total)


def short_backward(
    qkv_ref,
    grad_ref,
    wide_ref,
    total_ref,
    key_ids,
    query_ids,
    query_out,
    own_out,
    halo_out,
    key_acc,
    value_acc,
    *,
    block,
):
    query, key, value = scaled(qkv_ref[0, 0]), qkv_ref[1, 0], qkv_ref[2, 0]
    scale = query.shape[1] ** (-0.5)
    key_t = key.T
    span = query_ids.shape[1]
    halo = query.shape[0] - span
    key_acc[...] = jnp.zeros_like(key_acc)
    value_acc[...] = jnp.zeros_like(value_acc)
    for i in range(span // block):
        lo, hi = i * block, (i + 1) * block
        visible = short_visible(key_ids[...], query_ids[...], i, block, halo)
        own = query[lo + halo : hi + halo]
        grad_t = grad_ref[:, lo:hi]
        grad = grad_t.T
        delta = jnp.sum(grad_t.astype(F32) * wide_ref[:, lo:hi], axis=0, keepdims=True)
        scores = dot_nt(key[lo : hi + halo], own)
        weights = jnp.exp(jnp.where(visible, scores, NEGATIVE) - total_ref[0, :, lo:hi])
        scores = weights * (dot_nt(value[lo : hi + halo], grad) - delta)
        scores_low = scores.astype(BF)
        value_acc[lo : hi + halo] += dot_nn(weights.astype(BF), grad)
        key_acc[lo : hi + halo] += dot_nn(scores_low, own)
        part = dot_nn(key_t[:, lo : hi + halo], scores_low)
        query_out[:, lo:hi] = (part * scale).astype(BF)
    for n, acc in enumerate((key_acc, value_acc)):
        whole = acc[...].T
        halo_out[n] = whole[:, :halo].astype(BF)
        own_out[n] = whole[:, halo:]


def whole_spec(shape):
    return pl.BlockSpec(shape, lambda *_: (0,) * len(shape))


def call(kernel, grid, ins, in_specs, outs, out_specs, scratch, flops, bytes_accessed, vmem=56 << 20):
    return pl.pallas_call(
        kernel,
        grid=grid,
        in_specs=in_specs,
        out_specs=out_specs,
        out_shape=outs,
        scratch_shapes=scratch,
        compiler_params=pltpu.CompilerParams(vmem_limit_bytes=vmem),
        cost_estimate=pl.CostEstimate(
            flops=int(flops), bytes_accessed=int(bytes_accessed), transcendentals=0
        ),
    )(*ins)


MESH = pl.DeviceIdType.MESH


def gather_kernel(
    experts,
    blocks,
    qkv_ref,
    out_ref,
    row_ref,
    edge_ref,
    full_qkv,
    full_out,
    all_rows,
    halo_ref,
    shard_send,
    shard_recv,
    row_send,
    row_recv,
    edge_sem,
    local_sem,
):
    me, z = lax.axis_index("expert"), lax.axis_index("blk")
    mate = me + 1 - 2 * lax.rem(me, 2)
    peers = [lax.rem(me + 2 * d, experts) for d in range(1, experts // 2)]
    barrier = pltpu.get_barrier_semaphore()
    for peer in [mate] + peers:
        pl.semaphore_signal(barrier, inc=1, device_id={"expert": peer}, device_id_type=MESH)
    for d in range(1, blocks):
        pl.semaphore_signal(
            barrier, inc=1, device_id={"blk": lax.rem(z + d, blocks)}, device_id_type=MESH
        )
    pl.semaphore_wait(barrier, len(peers) + blocks)

    arrays = ((qkv_ref, full_qkv), (out_ref, full_out))

    def shard(n, source, slot, turn, target):
        return pltpu.make_async_remote_copy(
            src_ref=source,
            dst_ref=arrays[n][1].at[slot],
            send_sem=shard_send.at[n, turn],
            recv_sem=shard_recv.at[n, slot],
            device_id={"expert": target},
            device_id_type=MESH,
        )

    def row(source, slot, turn, target):
        return pltpu.make_async_remote_copy(
            src_ref=source,
            dst_ref=all_rows.at[slot],
            send_sem=row_send.at[turn],
            recv_sem=row_recv.at[slot],
            device_id={"blk": target},
            device_id_type=MESH,
        )

    to_right, to_left = z + 1 < blocks, z > 0
    right, left = lax.rem(z + 1, blocks), lax.rem(z + blocks - 1, blocks)
    edge = pltpu.make_async_remote_copy(
        src_ref=edge_ref,
        dst_ref=halo_ref,
        send_sem=edge_sem.at[0],
        recv_sem=edge_sem.at[1],
        device_id={"blk": right},
        device_id_type=MESH,
    )
    no_edge = pltpu.make_async_copy(edge_ref, halo_ref, edge_sem.at[1])

    @pl.when(to_right)
    def _():
        row(row_ref, z, 0, right).start()
        edge.start()

    @pl.when(to_left)
    def _():
        row(row_ref, z, 1, left).start()

    @pl.when(jnp.logical_not(to_left))
    def _():
        no_edge.start()

    sent = []
    for n in range(2):
        for turn, peer in enumerate(peers):
            sent.append(shard(n, arrays[n][0], me, turn, peer))
        sent.append(shard(n, arrays[n][0], me, len(peers), mate))
    for copy in sent:
        copy.start()
    local = [
        pltpu.make_async_copy(qkv_ref, full_qkv.at[me], local_sem.at[0]),
        pltpu.make_async_copy(out_ref, full_out.at[me], local_sem.at[1]),
        pltpu.make_async_copy(row_ref, all_rows.at[z], local_sem.at[2]),
    ]
    for copy in local:
        copy.start()

    def hand_on(k):
        @pl.when(z - k >= 0)
        def _():
            slot = jnp.maximum(z - k, 0)
            row(all_rows.at[slot], slot, 2 * k, right).wait_recv()

            @pl.when(to_right)
            def _():
                row(all_rows.at[slot], slot, 2 * k, right).start()

        @pl.when(z + k < blocks)
        def _():
            slot = jnp.minimum(z + k, blocks - 1)
            row(all_rows.at[slot], slot, 2 * k + 1, left).wait_recv()

            @pl.when(to_left)
            def _():
                row(all_rows.at[slot], slot, 2 * k + 1, left).start()

    hand_on(1)
    for turn, peer in enumerate(peers):
        for n in range(2):
            copy = shard(n, arrays[n][1].at[peer], peer, len(peers) + 1 + turn, mate)
            copy.wait_recv()
            copy.start()
            sent.append(copy)
    for k in range(2, blocks):
        hand_on(k)
    for turn in range(experts // 2):
        slot = lax.rem(mate + 2 * turn, experts)
        for n in range(2):
            shard(n, arrays[n][1].at[slot], slot, 0, mate).wait_recv()
    for copy in sent:
        copy.wait_send()
    for copy in local:
        copy.wait()

    @pl.when(to_right)
    def _():
        row(row_ref, z, 0, right).wait_send()
        edge.wait_send()

    @pl.when(to_left)
    def _():
        row(row_ref, z, 1, left).wait_send()
        edge.wait_recv()

    @pl.when(jnp.logical_not(to_left))
    def _():
        no_edge.wait()

    for k in range(1, blocks):
        @pl.when((z - k >= 0) & to_right)
        def _(k=k):
            slot = jnp.maximum(z - k, 0)
            row(all_rows.at[slot], slot, 2 * k, right).wait_send()

        @pl.when((z + k < blocks) & to_left)
        def _(k=k):
            slot = jnp.minimum(z + k, blocks - 1)
            row(all_rows.at[slot], slot, 2 * k + 1, left).wait_send()


def gather(qkv_weight, out_weight, row, edge, experts, blocks):
    any_spec = pl.BlockSpec(memory_space=pl.ANY)
    return pl.pallas_call(
        functools.partial(gather_kernel, experts, blocks),
        in_specs=[any_spec] * 4,
        out_specs=(any_spec,) * 4,
        out_shape=(
            jax.ShapeDtypeStruct((experts,) + qkv_weight.shape, BF),
            jax.ShapeDtypeStruct((experts,) + out_weight.shape, BF),
            jax.ShapeDtypeStruct((blocks,) + row.shape, BF),
            jax.ShapeDtypeStruct(edge.shape, BF),
        ),
        scratch_shapes=[
            pltpu.SemaphoreType.DMA((2, experts)),
            pltpu.SemaphoreType.DMA((2, experts)),
            pltpu.SemaphoreType.DMA((2 * blocks,)),
            pltpu.SemaphoreType.DMA((blocks,)),
            pltpu.SemaphoreType.DMA((2,)),
            pltpu.SemaphoreType.DMA((3,)),
        ],
        compiler_params=pltpu.CompilerParams(collective_id=0, has_side_effects=True),
    )(qkv_weight, out_weight, row, edge)


def gelu_parts(hidden):
    cdf = 0.5 * (1.0 + lax.erf(hidden * 0.7071067811865476))
    density = jnp.exp(-0.5 * hidden * hidden) * 0.3989422804014327
    return hidden * cdf, cdf + hidden * density


def expert_kernel(
    experts,
    blocks,
    steps,
    chunk,
    x_hbm,
    cot_hbm,
    *refs,
):
    ups, refs = refs[:blocks], refs[blocks:]
    downs, refs = refs[:blocks], refs[blocks:]
    up_shifts, refs = refs[:blocks], refs[blocks:]
    (
        down_shift_ref,
        centroid_ref,
        back_grad,
        back_out,
        up_sum,
        down_sum,
        up_shift_out,
        down_shift_out,
        x_buf,
        low_buf,
        xt_ref,
        gt_ref,
        out_acc,
        grad_acc,
        gate_ref,
        x_send,
        x_recv,
        back_send,
        back_recv,
        local_sem,
        *refs,
    ) = refs
    rounds = (blocks - 1).bit_length()
    up_held, down_held = refs[: rounds + 1], refs[rounds + 1 : 2 * rounds + 2]
    part_send, part_recv = refs[2 * rounds + 2 :]
    step = pl.program_id(0)
    me, z = lax.axis_index("expert"), lax.axis_index("blk")
    capacity, width = x_buf.shape[1:]
    rows = experts * capacity
    lanes = 128

    def x_copy(d):
        target = lax.rem(me + d, experts)
        return pltpu.make_async_remote_copy(
            src_ref=x_hbm.at[target],
            dst_ref=x_buf.at[me],
            send_sem=x_send.at[d],
            recv_sem=x_recv.at[d],
            device_id={"expert": target},
            device_id_type=MESH,
        )

    def back_copy(n, d):
        target = lax.rem(me + d, experts)
        return pltpu.make_async_remote_copy(
            src_ref=(low_buf, x_buf)[n].at[target],
            dst_ref=(back_grad, back_out)[n].at[me],
            send_sem=back_send.at[n, d],
            recv_sem=back_recv.at[n, d],
            device_id={"expert": target},
            device_id_type=MESH,
        )

    def back_local(n):
        return pltpu.make_async_copy(
            (low_buf, x_buf)[n].at[me], (back_grad, back_out)[n].at[me], local_sem.at[n]
        )

    def part_copies(r, p):
        bit = 1 << r
        mine = lax.rem(z // bit, 2)
        partner = z + bit - 2 * bit * mine
        copies = []
        for k in range((blocks >> r) // 2):
            for n, held in enumerate((up_held, down_held)):
                copies.append(
                    pltpu.make_async_remote_copy(
                        src_ref=held[r].at[p, 2 * k + 1 - mine],
                        dst_ref=held[r + 1].at[p, k],
                        send_sem=part_send.at[r, n, p, k],
                        recv_sem=part_recv.at[r, n, p, k],
                        device_id={"blk": partner},
                        device_id_type=MESH,
                    )
                )
        return copies

    def add_parts(r, p):
        mine = lax.rem(z // (1 << r), 2)
        for copy in part_copies(r, p):
            copy.wait_recv()
        for k in range((blocks >> r) // 2):
            up = up_held[r][p, 2 * k + mine].astype(F32) + up_held[r + 1][p, k].astype(F32)
            down = down_held[r][p, 2 * k + mine].astype(F32) + down_held[r + 1][p, k].astype(F32)
            if r + 1 < rounds:
                up_held[r + 1][p, k] = up.astype(BF)
                down_held[r + 1][p, k] = down.astype(BF)
            else:
                for j in range(blocks):
                    at = j * steps * lanes + p * lanes
                    up_sum[:, at : at + lanes] = up[:, j * lanes : (j + 1) * lanes]
                down_sum[p * lanes : (p + 1) * lanes, :] = down.T
        if r + 1 < rounds:
            for copy in part_copies(r + 1, p):
                copy.start()

    cot_copy = pltpu.make_async_copy(cot_hbm, low_buf, local_sem.at[2])
    own_copy = pltpu.make_async_copy(x_hbm.at[me], x_buf.at[me], local_sem.at[3])
    x_flat, low_flat = x_buf.reshape(rows, width), low_buf.reshape(rows, width)

    @pl.when(step == 0)
    def _():
        barrier = pltpu.get_barrier_semaphore()
        for d in range(1, experts):
            pl.semaphore_signal(
                barrier, inc=1, device_id={"expert": lax.rem(me + d, experts)}, device_id_type=MESH
            )
        for r in range(rounds):
            bit = 1 << r
            partner = z + bit - 2 * bit * lax.rem(z // bit, 2)
            pl.semaphore_signal(barrier, inc=1, device_id={"blk": partner}, device_id_type=MESH)
        cot_copy.start()
        own_copy.start()
        pl.semaphore_wait(barrier, experts - 1 + rounds)
        for d in range(1, experts):
            x_copy(d).start()
        out_acc[...] = jnp.zeros_like(out_acc)
        grad_acc[...] = jnp.zeros_like(grad_acc)
        cot_copy.wait()
        own_copy.wait()
        for d in range(1, experts):
            x_copy(d).wait_recv()
        for lo in range(0, rows, chunk):
            x = x_flat[lo : lo + chunk]
            logit = jnp.sum(x.astype(F32) * centroid_ref[...], axis=1, keepdims=True)
            gate = 1.0 / (1.0 + jnp.exp(-logit))
            gate_ref[lo : lo + chunk] = gate
            low = (low_flat[lo : lo + chunk].astype(F32) * gate).astype(BF)
            low_flat[lo : lo + chunk] = low
            xt_ref[:, lo : lo + chunk] = x.T
            gt_ref[:, lo : lo + chunk] = low.T
            part = jnp.sum(low.astype(F32), axis=0, keepdims=True)
            if lo:
                down_shift_out[...] += part
            else:
                down_shift_out[...] = part

    up = jnp.concatenate([ref[...] for ref in ups], axis=1)
    down = jnp.concatenate([ref[...] for ref in downs], axis=0)
    up_shift = jnp.concatenate([ref[...] for ref in up_shifts], axis=1)
    totals = None
    for lo in range(0, rows, chunk):
        x = x_flat[lo : lo + chunk]
        low = low_flat[lo : lo + chunk]
        hidden = dot_nn(x, up) + up_shift
        active, slope = gelu_parts(hidden)
        active = active.astype(BF)
        grad_low = (dot_nt(low, down) * slope).astype(BF)
        out_acc[lo : lo + chunk] += dot_nn(active, down)
        grad_acc[lo : lo + chunk] += dot_nt(grad_low, up)
        parts = (
            dot_nn(xt_ref[:, lo : lo + chunk], grad_low),
            dot_nn(gt_ref[:, lo : lo + chunk], active),
            jnp.sum(grad_low.astype(F32), axis=0, keepdims=True),
        )
        totals = parts if totals is None else tuple(a + b for a, b in zip(totals, parts))
    up_total, down_total, shift_total = totals
    up_total = up_total.astype(BF)
    depth = width // blocks
    for j in range(blocks):
        up_held[0][step, j] = up_total[j * depth : (j + 1) * depth]
        down_held[0][step, j] = down_total[:, j * lanes : (j + 1) * lanes].astype(BF)
        up_shift_out[j] = shift_total[:, j * lanes : (j + 1) * lanes]
    for copy in part_copies(0, step):
        copy.start()

    tasks = sorted(
        ((r, p) for p in range(steps) for r in range(rounds)), key=lambda task: (sum(task), task[0])
    )
    early = [[] for _ in range(steps)]
    for turn, task in enumerate(tasks):
        at = 2 * (task[1] + 1) + 2 * task[0]
        if at < steps - 1:
            early[at].append(task)
    for at in range(steps):
        if early[at]:

            @pl.when(step == at)
            def _(at=at):
                for r, p in early[at]:
                    add_parts(r, p)

    @pl.when(step == steps - 1)
    def _():
        for d in range(1, experts):
            x_copy(d).wait_send()
        for lo in range(0, rows, chunk):
            gate = gate_ref[lo : lo + chunk]
            out = (out_acc[lo : lo + chunk] + down_shift_ref[...]).astype(BF)
            inner = jnp.sum(
                low_flat[lo : lo + chunk].astype(F32) * out.astype(F32), axis=1, keepdims=True
            )
            x_flat[lo : lo + chunk] = out
            low_flat[lo : lo + chunk] = (
                grad_acc[lo : lo + chunk] + inner * (1.0 - gate) * centroid_ref[...]
            ).astype(BF)
        back_local(0).start()
        for d in range(1, experts):
            back_copy(0, d).start()
        back_local(1).start()
        left = [task for task in tasks if all(task not in done for done in early)]
        half = len(left) // 2
        for r, p in left[:half]:
            add_parts(r, p)
        for d in range(1, experts):
            back_copy(0, d).wait_send()
            back_copy(1, d).start()
        for r, p in left[half:]:
            add_parts(r, p)
        for n in range(2):
            back_local(n).wait()
            for d in range(1, experts):
                back_copy(n, d).wait_recv()
        for d in range(1, experts):
            back_copy(1, d).wait_send()
        for p in range(steps):
            for r in range(rounds):
                for copy in part_copies(r, p):
                    copy.wait_send()


def run_expert(x, cot, up_weight, down_weight, up_shift, down_shift, centroid, blocks):
    experts, capacity, width = x.shape
    rows = experts * capacity
    hidden = up_weight.shape[1]
    lanes = 128
    steps = hidden // blocks // lanes
    rounds = (blocks - 1).bit_length()
    chunk = min(512, rows)
    depth = width // blocks
    any_spec = pl.BlockSpec(memory_space=pl.ANY)

    def once(shape):
        return pl.BlockSpec(shape, lambda f: (0,) * len(shape), pipeline_mode=pl.Buffered(1))

    return pl.pallas_call(
        functools.partial(expert_kernel, experts, blocks, steps, chunk),
        grid=(steps,),
        in_specs=[any_spec] * 2
        + [pl.BlockSpec((width, lanes), lambda f, j=j: (0, j * steps + f)) for j in range(blocks)]
        + [pl.BlockSpec((lanes, width), lambda f, j=j: (j * steps + f, 0)) for j in range(blocks)]
        + [pl.BlockSpec((1, lanes), lambda f, j=j: (0, j * steps + f)) for j in range(blocks)]
        + [once((1, width))] * 2,
        out_specs=(
            any_spec,
            any_spec,
            once((depth, hidden)),
            once((hidden // blocks, width)),
            pl.BlockSpec((blocks, 1, lanes), lambda f: (0, 0, f)),
            once((1, width)),
        ),
        out_shape=(
            jax.ShapeDtypeStruct(x.shape, BF),
            jax.ShapeDtypeStruct(x.shape, BF),
            jax.ShapeDtypeStruct((depth, hidden), F32),
            jax.ShapeDtypeStruct((hidden // blocks, width), F32),
            jax.ShapeDtypeStruct((blocks, 1, hidden // blocks), F32),
            jax.ShapeDtypeStruct((1, width), F32),
        ),
        scratch_shapes=[
            pltpu.VMEM(x.shape, BF),
            pltpu.VMEM(x.shape, BF),
            pltpu.VMEM((width, rows), BF),
            pltpu.VMEM((width, rows), BF),
            pltpu.VMEM((rows, width), F32),
            pltpu.VMEM((rows, width), F32),
            pltpu.VMEM((rows, 1), F32),
            pltpu.SemaphoreType.DMA((experts,)),
            pltpu.SemaphoreType.DMA((experts,)),
            pltpu.SemaphoreType.DMA((2, experts)),
            pltpu.SemaphoreType.DMA((2, experts)),
            pltpu.SemaphoreType.DMA((4,)),
        ]
        + [pltpu.VMEM((steps, blocks >> r, depth, blocks * lanes), BF) for r in range(rounds + 1)]
        + [pltpu.VMEM((steps, blocks >> r, width, lanes), BF) for r in range(rounds + 1)]
        + [
            pltpu.SemaphoreType.DMA((rounds, 2, steps, blocks // 2)),
            pltpu.SemaphoreType.DMA((rounds, 2, steps, blocks // 2)),
        ],
        compiler_params=pltpu.CompilerParams(
            collective_id=1, has_side_effects=True, vmem_limit_bytes=62 << 20
        ),
        cost_estimate=pl.CostEstimate(
            flops=12 * rows * width * hidden, bytes_accessed=40 << 20, transcendentals=0
        ),
    )(
        x,
        cot,
        *([up_weight] * blocks),
        *([down_weight] * blocks),
        *([up_shift] * blocks),
        down_shift,
        centroid,
    )


def on_device(
    tokens,
    doc_ids,
    routes,
    ln1_gain,
    ln1_bias,
    qkv_weight,
    qv_bias,
    out_weight,
    out_bias,
    ln2_gain,
    ln2_bias,
    centroids,
    up_weight,
    up_bias,
    down_weight,
    down_bias,
    cotangent,
):
    rows, span, width = tokens.shape
    heads = HEADS
    size = width // heads
    blocks = lax.axis_size("blk")
    own = lax.axis_index("blk")
    count = rows * span
    length = blocks * span
    halo = min(SHORT, span)
    share = -(-heads // blocks)
    pad_heads = share * blocks - heads

    long_at = (doc_ids[0, -1] != 0).astype(jnp.int32)

    def pick(pair, at):
        return lax.dynamic_index_in_dim(pair, at, 0, keepdims=False)

    def in_order(long_part, short_part, axis):
        first = jnp.where(long_at == 0, long_part, short_part)
        second = jnp.where(long_at == 0, short_part, long_part)
        return jnp.concatenate([first, second], axis=axis)

    long_tokens = pick(tokens, long_at)
    short_tokens = pick(tokens, 1 - long_at)
    full_qkv, full_out, all_tokens, halo_tokens = gather(
        qkv_weight,
        out_weight,
        long_tokens,
        short_tokens[span - halo :],
        lax.axis_size("expert"),
        blocks,
    )
    full_qkv = full_qkv.reshape(width, 3 * width)
    full_out = full_out.reshape(width, width)
    all_tokens = all_tokens.reshape(length, width)
    ln1_rows = (ln1_gain[None], ln1_bias[None])

    def own_heads(matrix):
        padded = jnp.pad(matrix, ((0, 0), (0, pad_heads * size)))
        return lax.dynamic_slice_in_dim(padded, own * share * size, share * size, 1)

    long_weights = [own_heads(full_qkv[:, n * width : (n + 1) * width]) for n in range(3)]
    long_shifts = [own_heads(qv_bias[n][None]) for n in range(2)]
    short_ids = jnp.concatenate(
        [jnp.full((halo,), -1, jnp.int32), pick(doc_ids, 1 - long_at)]
    )
    short_ids = lax.dynamic_slice_in_dim(short_ids, own * span, halo + span, 0)
    key_ids = short_ids[:, None]
    query_ids = short_ids[None, halo:]

    part = share * size
    long_qkv, long_wide, long_low, long_total = call(
        functools.partial(long_forward, block=span),
        (share,),
        (all_tokens, *ln1_rows, *long_weights, *long_shifts),
        [whole_spec((length, width))]
        + [whole_spec((1, width))] * 2
        + [whole_spec((width, part))] * 3
        + [whole_spec((1, part))] * 2,
        (
            jax.ShapeDtypeStruct((3, share, length, size), BF),
            jax.ShapeDtypeStruct((share * size, length), F32),
            jax.ShapeDtypeStruct((blocks, share * size, span), BF),
            jax.ShapeDtypeStruct((share, 1, length), F32),
        ),
        (
            whole_spec((3, share, length, size)),
            pl.BlockSpec((size, length), lambda h: (h, 0)),
            pl.BlockSpec((blocks, size, span), lambda h: (0, h, 0)),
            pl.BlockSpec((1, 1, length), lambda h: (h, 0, 0)),
        ),
        [],
        2 * share * length * (width * 3 * size + length * 256),
        6 * length * width,
    )
    long_attended = lax.all_to_all(long_low, "blk", 0, 0, tiled=True).reshape(-1, span)[:width]
    short_qkv, short_wide, short_low, short_total = call(
        functools.partial(short_forward, block=halo),
        (heads,),
        (
            jnp.concatenate([halo_tokens, short_tokens], axis=0),
            *ln1_rows,
            full_qkv,
            qv_bias,
            key_ids,
            query_ids,
        ),
        [
            whole_spec((halo + span, width)),
            whole_spec((1, width)),
            whole_spec((1, width)),
            whole_spec((width, 3 * width)),
            whole_spec((2, width)),
            whole_spec((halo + span, 1)),
            whole_spec((1, span)),
        ],
        (
            jax.ShapeDtypeStruct((3, heads, halo + span, size), BF),
            jax.ShapeDtypeStruct((width, span), F32),
            jax.ShapeDtypeStruct((width, span), BF),
            jax.ShapeDtypeStruct((heads, 1, span), F32),
        ),
        (
            whole_spec((3, heads, halo + span, size)),
            pl.BlockSpec((size, span), lambda h: (h, 0)),
            pl.BlockSpec((size, span), lambda h: (h, 0)),
            pl.BlockSpec((1, 1, span), lambda h: (h, 0, 0)),
        ),
        [],
        2 * heads * (halo + span) * (width * 3 * size + 2 * halo * 256),
        8 * span * width,
    )
    attended_t = in_order(long_attended, short_low, 1)

    expert_count = centroids.shape[0]
    capacity = 2 * count // expert_count
    slots = expert_count * capacity
    route_flat = routes.reshape(count)
    onehot = route_flat[:, None] == jnp.arange(expert_count, dtype=jnp.int32)[None, :]
    ranking = jnp.cumsum(onehot.astype(jnp.int32), axis=0) - 1
    slot_of = route_flat * capacity + jnp.sum(jnp.where(onehot, ranking, 0), axis=1)
    slot_line = jnp.arange(slots, dtype=jnp.int32)
    to_slots = (slot_line[:, None] == slot_of[None, :]).astype(BF)
    from_slots = (slot_of[:, None] == slot_line[None, :]).astype(BF)

    def to_experts(flat):
        return dot_nn(to_slots, flat).astype(BF).reshape(expert_count, capacity, width)

    grad_low = cotangent.reshape(count, width)
    received_cot = lax.all_to_all(to_experts(grad_low), "expert", 0, 0, tiled=True)

    token_rows = tokens.astype(F32).reshape(count, width)
    middle = (
        token_rows
        + lax.dot_general(
            attended_t, full_out, (((0,), (0,)), ((), ())), preferred_element_type=F32
        )
        + out_bias
    )
    normal_two, scale_two = norm_parts(middle)
    normed_two = normal_two * ln2_gain + ln2_bias
    outgoing = to_experts(normed_two.astype(BF))
    centroid_rows = jnp.dot(onehot.astype(BF), centroids, preferred_element_type=F32)
    gate = jax.nn.sigmoid(jnp.sum(normed_two * centroid_rows, axis=1))

    own_centroid = lax.dynamic_index_in_dim(
        centroids.astype(F32), lax.axis_index("expert"), 0, keepdims=True
    )
    back_grad, back_out, up_sum, down_sum, up_shift_term, down_shift_term = run_expert(
        outgoing,
        received_cot,
        up_weight[0],
        down_weight[0],
        up_bias,
        down_bias,
        own_centroid,
        blocks,
    )
    back_grad = back_grad.reshape(slots, width)
    back_out = back_out.reshape(slots, width)

    grad_normed_two = dot_nn(from_slots, back_grad)
    inner_two, ln2_gain_term, ln2_bias_term = norm_back(
        grad_normed_two, normal_two, scale_two, ln2_gain
    )
    grad_out = grad_low.astype(F32)
    grad_middle = grad_out + inner_two
    out_shift_term = jnp.sum(grad_middle, axis=0)
    grad_middle_low = grad_middle.astype(BF)
    grad_attended_t = lax.dot_general(
        full_out, grad_middle_low, (((1,), (1,)), ((), ())), preferred_element_type=F32
    ).astype(BF)
    grad_pair = grad_attended_t.reshape(width, rows, span)
    long_grad = lax.dynamic_index_in_dim(grad_pair, long_at, 1, keepdims=False)
    short_grad = lax.dynamic_index_in_dim(grad_pair, 1 - long_at, 1, keepdims=False)
    long_grad = jnp.pad(long_grad, ((0, pad_heads * size), (0, 0)))
    long_grad = lax.all_to_all(
        long_grad.reshape(blocks, share * size, span), "blk", 0, 0, tiled=True
    )
    out_term = lax.dot_general(
        attended_t, grad_middle_low, (((1,), (0,)), ((), ())), preferred_element_type=F32
    )

    long_back = call(
        functools.partial(long_backward, block=span),
        (share,),
        (long_qkv, long_grad, long_wide, long_total),
        [
            pl.BlockSpec((3, 1, length, size), lambda h: (0, h, 0, 0)),
            pl.BlockSpec((blocks, size, span), lambda h: (0, h, 0)),
            pl.BlockSpec((size, length), lambda h: (h, 0)),
            pl.BlockSpec((1, 1, length), lambda h: (h, 0, 0)),
        ],
        jax.ShapeDtypeStruct((blocks, 3, share * size, span), BF),
        pl.BlockSpec((blocks, 3, size, span), lambda h: (0, 0, h, 0)),
        [pltpu.VMEM((length, size), F32), pltpu.VMEM((length, size), F32)],
        5 * share * length * length * 256,
        8 * length * width,
    )
    long_back = lax.all_to_all(long_back, "blk", 0, 0, tiled=True)
    long_back = long_back.transpose(1, 0, 2, 3).reshape(3, -1, span)[:, :width]
    query_back, own_back, halo_back = call(
        functools.partial(short_backward, block=halo),
        (heads,),
        (short_qkv, short_grad, short_wide, short_total, key_ids, query_ids),
        [
            pl.BlockSpec((3, 1, halo + span, size), lambda h: (0, h, 0, 0)),
            pl.BlockSpec((size, span), lambda h: (h, 0)),
            pl.BlockSpec((size, span), lambda h: (h, 0)),
            pl.BlockSpec((1, 1, span), lambda h: (h, 0, 0)),
            whole_spec((halo + span, 1)),
            whole_spec((1, span)),
        ],
        (
            jax.ShapeDtypeStruct((width, span), BF),
            jax.ShapeDtypeStruct((2, width, span), F32),
            jax.ShapeDtypeStruct((2, width, halo), BF),
        ),
        (
            pl.BlockSpec((size, span), lambda h: (h, 0)),
            pl.BlockSpec((2, size, span), lambda h: (0, h, 0)),
            pl.BlockSpec((2, size, halo), lambda h: (0, h, 0)),
        ),
        [pltpu.VMEM((halo + span, size), F32), pltpu.VMEM((halo + span, size), F32)],
        5 * heads * span * 2 * 2 * halo * 256,
        16 * span * width,
    )
    halo_back = lax.ppermute(halo_back, "blk", [(i + 1, i) for i in range(blocks - 1)])
    own_back = own_back + jnp.pad(halo_back.astype(F32), ((0, 0), (0, 0), (span - halo, 0)))
    short_back = jnp.concatenate([query_back[None], own_back.astype(BF)], axis=0)
    back_t = in_order(
        long_back.reshape(3 * width, span), short_back.reshape(3 * width, span), 1
    )

    normal_one, scale_one = norm_parts(token_rows)
    normed_low = (normal_one * ln1_gain + ln1_bias).astype(BF)
    qkv_term = lax.dot_general(
        normed_low, back_t, (((0,), (1,)), ((), ())), preferred_element_type=F32
    )
    qv_sums = jnp.sum(back_t.astype(F32), axis=1)
    grad_normed_one = lax.dot_general(
        back_t, full_qkv, (((0,), (1,)), ((), ())), preferred_element_type=F32
    )
    inner_one, ln1_gain_term, ln1_bias_term = norm_back(
        grad_normed_one, normal_one, scale_one, ln1_gain
    )
    grad_tokens = grad_middle + inner_one

    expert_rows = dot_nn(from_slots, back_out)
    result = middle + gate[:, None] * expert_rows
    grad_logit = jnp.sum(grad_out * expert_rows, axis=1) * gate * (1.0 - gate)
    centroid_term = jnp.einsum(
        "te,td->de",
        onehot.astype(F32) * grad_logit[:, None],
        normed_two,
        precision=lax.Precision.HIGHEST,
    )

    small = jnp.stack(
        [
            qv_sums[:width],
            qv_sums[2 * width :],
            out_shift_term,
            ln1_gain_term,
            ln1_bias_term,
            ln2_gain_term,
            ln2_bias_term,
        ],
        axis=1,
    )
    n_small = small.shape[1]
    packed = jnp.concatenate([qkv_term, out_term, small, centroid_term], axis=1).astype(BF)
    packed = lax.psum_scatter(packed, "expert", scatter_dimension=0, tiled=True)
    packed = lax.psum(packed, "blk").astype(F32)
    qkv_sum = packed[:, : 3 * width]
    out_sum = packed[:, 3 * width : 4 * width]
    small_sum = packed[:, 4 * width : 4 * width + n_small]
    centroid_sum = packed[:, 4 * width + n_small :].T
    shift_sum = lax.psum_scatter(
        jnp.concatenate(
            [up_shift_term.reshape(blocks, -1), down_shift_term.reshape(blocks, -1)], axis=1
        ).astype(BF),
        "blk",
        scatter_dimension=0,
        tiled=True,
    ).astype(F32)
    up_shift_sum = shift_sum[:, : up_bias.shape[1] // blocks]
    down_shift_sum = shift_sum[:, up_bias.shape[1] // blocks :]
    return (
        result.reshape(rows, span, width),
        grad_tokens.reshape(rows, span, width),
        small_sum[:, 3],
        small_sum[:, 4],
        qkv_sum,
        small_sum[:, :2].T,
        out_sum,
        small_sum[:, 2],
        small_sum[:, 5],
        small_sum[:, 6],
        centroid_sum,
        up_sum[None],
        up_shift_sum,
        down_sum[None],
        down_shift_sum,
    )


def solution(mesh):
    return jax.shard_map(
        on_device,
        mesh=mesh,
        in_specs=(
            P("expert", "blk", None),
            P("expert", None),
            P("blk", "expert", None, None),
            P(),
            P(),
            P("expert", None),
            P(),
            P("expert", None),
            P(),
            P(),
            P(),
            P(),
            P("expert", None, None),
            P("expert", None),
            P("expert", None, None),
            P("expert", None),
            P("expert", "blk", None),
        ),
        out_specs=(
            P("expert", "blk", None),
            P("expert", "blk", None),
            P("expert"),
            P("expert"),
            P("expert", None),
            P(None, "expert"),
            P("expert", None),
            P("expert"),
            P("expert"),
            P("expert"),
            P(None, "expert"),
            P("expert", "blk", None),
            P("expert", "blk"),
            P("expert", "blk", None),
            P("expert", "blk"),
        ),
        check_vma=False,
    )
```

```python
import functools

import jax
import jax.numpy as jnp
from jax import lax
from jax.experimental import pallas as pl
from jax.experimental.pallas import tpu as pltpu
from jax.sharding import PartitionSpec as P

HEADS = 12
SHORT = 256
NEGATIVE = -1e30
EPSILON = 1e-05
BF = jnp.bfloat16
F32 = jnp.float32


def dot_nn(a, b):
    return lax.dot_general(a, b, (((1,), (0,)), ((), ())), preferred_element_type=F32)


def dot_nt(a, b):
    return lax.dot_general(a, b, (((1,), (1,)), ((), ())), preferred_element_type=F32)


def norm_parts(values):
    average = jnp.mean(values, axis=-1, keepdims=True)
    centred = values - average
    variance = jnp.mean(centred * centred, axis=-1, keepdims=True)
    scale = lax.rsqrt(variance + EPSILON)
    return centred * scale, scale


def layer_norm(values, gain, bias):
    return norm_parts(values)[0] * gain + bias


def norm_back(upstream, normal, scale, gain):
    t = upstream * gain
    inner = (
        t
        - jnp.mean(t, axis=-1, keepdims=True)
        - normal * jnp.mean(t * normal, axis=-1, keepdims=True)
    )
    return inner * scale, jnp.sum(upstream * normal, axis=0), jnp.sum(upstream, axis=0)


def causal(rows, columns, shift):
    row = lax.broadcasted_iota(jnp.int32, (rows, columns), 0)
    column = lax.broadcasted_iota(jnp.int32, (rows, columns), 1)
    return row <= column + shift


def norm_low(values, gain, bias):
    return layer_norm(values.astype(F32), gain, bias).astype(BF)


def scaled(query):
    return (query.astype(F32) * query.shape[-1] ** (-0.5)).astype(BF)


def long_backward(
    qkv_ref, grad_ref, wide_ref, total_ref, out_ref, key_acc, value_acc, *, block
):
    query, key, value = scaled(qkv_ref[0, 0]), qkv_ref[1, 0], qkv_ref[2, 0]
    scale = query.shape[1] ** (-0.5)
    key_t = key.T
    visible = causal(block, block, 0)
    count = query.shape[0] // block
    key_acc[...] = jnp.zeros_like(key_acc)
    value_acc[...] = jnp.zeros_like(value_acc)
    for i in range(count):
        lo, hi = i * block, (i + 1) * block
        own = query[lo:hi]
        grad_t = grad_ref[i]
        grad = grad_t.T
        delta = jnp.sum(grad_t.astype(F32) * wide_ref[:, lo:hi], axis=0, keepdims=True)
        total = total_ref[0, :, lo:hi]
        query_grad = None
        for start, stop in ((lo, hi), (0, lo)):
            if start == stop:
                continue
            weights = jnp.exp(dot_nt(key[start:stop], own) - total)
            if start == lo:
                weights = jnp.where(visible, weights, 0.0)
            scores = weights * (dot_nt(value[start:stop], grad) - delta)
            scores_low = scores.astype(BF)
            value_acc[start:stop] += dot_nn(weights.astype(BF), grad)
            key_acc[start:stop] += dot_nn(scores_low, own)
            part = dot_nn(key_t[:, start:stop], scores_low)
            query_grad = part if query_grad is None else query_grad + part
        out_ref[i, 0] = (query_grad * scale).astype(BF)
    key_grad = key_acc[...].T.astype(BF)
    value_grad = value_acc[...].T.astype(BF)
    for i in range(count):
        out_ref[i, 1] = key_grad[:, i * block : (i + 1) * block]
        out_ref[i, 2] = value_grad[:, i * block : (i + 1) * block]


def short_visible(key_ids, query_ids, i, block, halo):
    lo = i * block
    same = key_ids[lo : lo + halo + block] == query_ids[:, lo : lo + block]
    return same & causal(halo + block, block, halo)


def short_backward(
    qkv_ref,
    grad_ref,
    wide_ref,
    total_ref,
    key_ids,
    query_ids,
    query_out,
    own_out,
    halo_out,
    key_acc,
    value_acc,
    *,
    block,
):
    query, key, value = scaled(qkv_ref[0, 0]), qkv_ref[1, 0], qkv_ref[2, 0]
    scale = query.shape[1] ** (-0.5)
    key_t = key.T
    span = query_ids.shape[1]
    halo = query.shape[0] - span
    key_acc[...] = jnp.zeros_like(key_acc)
    value_acc[...] = jnp.zeros_like(value_acc)
    for i in range(span // block):
        lo, hi = i * block, (i + 1) * block
        visible = short_visible(key_ids[...], query_ids[...], i, block, halo)
        own = query[lo + halo : hi + halo]
        grad_t = grad_ref[:, lo:hi]
        grad = grad_t.T
        delta = jnp.sum(grad_t.astype(F32) * wide_ref[:, lo:hi], axis=0, keepdims=True)
        scores = dot_nt(key[lo : hi + halo], own)
        weights = jnp.exp(jnp.where(visible, scores, NEGATIVE) - total_ref[0, :, lo:hi])
        scores = weights * (dot_nt(value[lo : hi + halo], grad) - delta)
        scores_low = scores.astype(BF)
        value_acc[lo : hi + halo] += dot_nn(weights.astype(BF), grad)
        key_acc[lo : hi + halo] += dot_nn(scores_low, own)
        part = dot_nn(key_t[:, lo : hi + halo], scores_low)
        query_out[:, lo:hi] = (part * scale).astype(BF)
    for n, acc in enumerate((key_acc, value_acc)):
        whole = acc[...].T
        halo_out[n] = whole[:, :halo].astype(BF)
        own_out[n] = whole[:, halo:]


def whole_spec(shape):
    return pl.BlockSpec(shape, lambda *_: (0,) * len(shape))


def call(kernel, grid, ins, in_specs, outs, out_specs, scratch, flops, bytes_accessed, vmem=56 << 20):
    return pl.pallas_call(
        kernel,
        grid=grid,
        in_specs=in_specs,
        out_specs=out_specs,
        out_shape=outs,
        scratch_shapes=scratch,
        compiler_params=pltpu.CompilerParams(vmem_limit_bytes=vmem),
        cost_estimate=pl.CostEstimate(
            flops=int(flops), bytes_accessed=int(bytes_accessed), transcendentals=0
        ),
    )(*ins)


MESH = pl.DeviceIdType.MESH


def remote(source, target, send_sem, recv_sem, device):
    return pltpu.make_async_remote_copy(
        src_ref=source,
        dst_ref=target,
        send_sem=send_sem,
        recv_sem=recv_sem,
        device_id=device,
        device_id_type=MESH,
    )


def greet(experts, blocks):
    me, z = lax.axis_index("expert"), lax.axis_index("blk")
    barrier = pltpu.get_barrier_semaphore()
    for d in range(1, experts):
        pl.semaphore_signal(
            barrier, inc=1, device_id={"expert": lax.rem(me + d, experts)}, device_id_type=MESH
        )
    for d in range(1, blocks):
        pl.semaphore_signal(
            barrier, inc=1, device_id={"blk": lax.rem(z + d, blocks)}, device_id_type=MESH
        )
    pl.semaphore_wait(barrier, experts + blocks - 2)


def front_kernel(
    experts,
    blocks,
    heads,
    gathers,
    block,
    short_block,
    qkv_ref,
    out_ref,
    row_ref,
    short_ref,
    cot_ref,
    gain_ref,
    bias_ref,
    shift_ref,
    key_ids,
    query_ids,
    *refs,
):
    if gathers:
        (full_qkv, full_out), refs = refs[:2], refs[2:]
    else:
        full_qkv = qkv_ref
    (
        received_cot,
        attended,
        long_qkv,
        long_wide,
        long_total,
        short_qkv,
        short_wide,
        short_low,
        short_total,
        weights,
        rows_buf,
        short_buf,
        long_store,
        short_store,
        low_stage,
        shard_send,
        shard_recv,
        row_send,
        row_recv,
        edge_sem,
        local_sem,
        cot_send,
        cot_recv,
        low_send,
        low_recv,
    ) = refs
    me, z = lax.axis_index("expert"), lax.axis_index("blk")
    step = pl.program_id(0)
    mate = me + 1 - 2 * lax.rem(me, 2)
    peers = [lax.rem(me + 2 * d, experts) for d in range(1, experts // 2)]
    share, size = long_store.shape[1], long_store.shape[3]
    length = blocks * block
    span = block
    halo = short_buf.shape[0] - span
    shard_rows = qkv_ref.shape[1]

    def qkv_part(slot):
        return full_qkv.at[:, pl.ds(pl.multiple_of(slot * shard_rows, shard_rows), shard_rows)]

    def shard(n, own, slot, turn, target):
        part = (qkv_part(slot), full_out.at[slot])[n]
        source = (qkv_ref, out_ref)[n] if own else part
        return remote(
            source, part, shard_send.at[n, turn], shard_recv.at[n, slot], {"expert": target}
        )

    def row(slot, turn, target):
        return remote(
            rows_buf.at[slot],
            rows_buf.at[slot],
            row_send.at[turn],
            row_recv.at[slot],
            {"blk": target},
        )

    def own_row(turn, target):
        return remote(
            row_ref, rows_buf.at[z], row_send.at[turn], row_recv.at[z], {"blk": target}
        )

    to_right, to_left = z + 1 < blocks, z > 0
    right, left = lax.rem(z + 1, blocks), lax.rem(z + blocks - 1, blocks)
    last_rows = short_ref.at[pl.ds(span - halo, halo)]
    halo_rows = short_buf.at[pl.ds(0, halo)]
    edge = remote(last_rows, halo_rows, edge_sem.at[0], edge_sem.at[1], {"blk": right})
    no_edge = pltpu.make_async_copy(last_rows, halo_rows, edge_sem.at[1])
    local = [
        pltpu.make_async_copy(row_ref, rows_buf.at[z], local_sem.at[0]),
        pltpu.make_async_copy(short_ref, short_buf.at[pl.ds(halo, span)], local_sem.at[1]),
    ]
    own_cot = pltpu.make_async_copy(cot_ref.at[me], received_cot.at[me], local_sem.at[2])
    load_weights = pltpu.make_async_copy(full_qkv, weights, local_sem.at[3])
    own_shards = []
    sent = []
    handed = []
    if gathers:
        own_shards = [
            pltpu.make_async_copy(qkv_ref, qkv_part(me), local_sem.at[4]),
            pltpu.make_async_copy(out_ref, full_out.at[me], local_sem.at[5]),
        ]
        for n in range(2):
            for turn, peer in enumerate(peers):
                sent.append(shard(n, True, me, turn, peer))
            sent.append(shard(n, True, me, len(peers), mate))
            for turn, peer in enumerate(peers):
                handed.append(shard(n, False, peer, len(peers) + 1 + turn, mate))

    def cot_copy(d):
        target = lax.rem(me + d, experts)
        return remote(
            cot_ref.at[target],
            received_cot.at[me],
            cot_send.at[d],
            cot_recv.at[d],
            {"expert": target},
        )

    def low_copy(head, d):
        target = lax.rem(z + d, blocks)
        return remote(
            low_stage.at[target, head],
            attended.at[z, head],
            low_send.at[head, d],
            low_recv.at[head, d],
            {"blk": target},
        )

    def low_local(head):
        return pltpu.make_async_copy(
            low_stage.at[z, head], attended.at[z, head], low_send.at[head, 0]
        )

    def hand_on(k):
        @pl.when(z - k >= 0)
        def _():
            slot = jnp.maximum(z - k, 0)
            row(slot, 2 * k, right).wait_recv()

            @pl.when(to_right)
            def _():
                row(slot, 2 * k, right).start()

        @pl.when(z + k < blocks)
        def _():
            slot = jnp.minimum(z + k, blocks - 1)
            row(slot, 2 * k + 1, left).wait_recv()

            @pl.when(to_left)
            def _():
                row(slot, 2 * k + 1, left).start()

    def project(source, lo, count, groups, store):
        low = norm_low(source, gain_ref[...], bias_ref[...])
        for n, group in enumerate(groups):
            part = (dot_nn(low, weights[group]) + shift_ref[group]).astype(BF)
            for kind in range(3):
                for head in range(share):
                    at = (kind * share + head) * size
                    if n * share + head < store.shape[1]:
                        store[kind, n * share + head, lo : lo + count] = part[:, at : at + size]

    @pl.when(step == 0)
    def _():
        for copy in local + own_shards:
            copy.start()
        greet(experts, blocks)

        @pl.when(to_right)
        def _():
            own_row(0, right).start()
            edge.start()

        @pl.when(to_left)
        def _():
            own_row(1, left).start()

        @pl.when(jnp.logical_not(to_left))
        def _():
            no_edge.start()

        for copy in sent:
            copy.start()
        hand_on(1)
        for copy in handed:
            copy.wait_recv()
            copy.start()
        if gathers:
            for turn in range(experts // 2):
                for n in range(2):
                    shard(n, False, lax.rem(mate + 2 * turn, experts), 0, mate).wait_recv()
        for copy in own_shards:
            copy.wait()
        load_weights.start()
        own_cot.start()
        for d in range(1, experts):
            cot_copy(d).start()

        @pl.when(to_left)
        def _():
            edge.wait_recv()

        @pl.when(jnp.logical_not(to_left))
        def _():
            no_edge.wait()

        for copy in local:
            copy.wait()
        load_weights.wait()
        for lo in range(0, halo + span, short_block):
            project(short_buf[lo : lo + short_block], lo, short_block, range(blocks), short_store)

    for k in range(2, blocks):

        @pl.when(step == (k - 1) * heads // (blocks - 1))
        def _(k=k):
            hand_on(k)

    @pl.when(step < heads)
    def _():
        query, key, value = (short_store[kind, step] for kind in range(3))
        for kind, part in enumerate((query, key, value)):
            short_qkv[kind, 0] = part
        query = scaled(query)
        value_t = value.T
        for i in range(span // short_block):
            lo, hi = i * short_block, (i + 1) * short_block
            visible = short_visible(key_ids[...], query_ids[...], i, short_block, halo)
            scores = dot_nt(key[lo : hi + halo], query[lo + halo : hi + halo])
            scores = jnp.where(visible, scores, NEGATIVE)
            top = jnp.max(scores, axis=0, keepdims=True)
            scores = jnp.exp(scores - top)
            total = jnp.sum(scores, axis=0, keepdims=True)
            out = dot_nn(value_t[:, lo : hi + halo], scores.astype(BF)) / total
            short_wide[:, lo:hi] = out
            short_low[:, lo:hi] = out.astype(BF)
            short_total[0, :, lo:hi] = top + jnp.log(total)

    @pl.when(step == heads)
    def _():
        for slot in range(blocks):
            project(rows_buf[slot], slot * block, block, [z], long_store)

    @pl.when(step >= heads)
    def _():
        head = step - heads
        query, key, value = (long_store[kind, head] for kind in range(3))
        for kind, part in enumerate((query, key, value)):
            long_qkv[kind, 0] = part
        query = scaled(query)
        value_t = value.T
        visible = causal(block, block, 0)
        for i in range(blocks):
            lo, hi = i * block, (i + 1) * block
            own = query[lo:hi]
            near = jnp.where(visible, dot_nt(key[lo:hi], own), NEGATIVE)
            top = jnp.max(near, axis=0, keepdims=True)
            if i:
                far = dot_nt(key[:lo], own)
                top = jnp.maximum(top, jnp.max(far, axis=0, keepdims=True))
            near = jnp.exp(near - top)
            total = jnp.sum(near, axis=0, keepdims=True)
            out = dot_nn(value_t[:, lo:hi], near.astype(BF))
            if i:
                far = jnp.exp(far - top)
                total = total + jnp.sum(far, axis=0, keepdims=True)
                out = out + dot_nn(value_t[:, :lo], far.astype(BF))
            out = out / total
            long_wide[:, lo:hi] = out
            low_stage[i, head] = out.astype(BF)
            long_total[0, :, lo:hi] = top + jnp.log(total)
        low_local(head).start()
        for d in range(1, blocks):
            low_copy(head, d).start()

    @pl.when(step == heads + share - 1)
    def _():
        for head in range(share):
            low_local(head).wait()
            for d in range(1, blocks):
                low_copy(head, d).wait()
        own_cot.wait()
        for d in range(1, experts):
            cot_copy(d).wait()
        for copy in sent + handed:
            copy.wait_send()

        @pl.when(to_right)
        def _():
            own_row(0, right).wait_send()
            edge.wait_send()

        @pl.when(to_left)
        def _():
            own_row(1, left).wait_send()

        for k in range(1, blocks):

            @pl.when((z - k >= 0) & to_right)
            def _(k=k):
                row(jnp.maximum(z - k, 0), 2 * k, right).wait_send()

            @pl.when((z + k < blocks) & to_left)
            def _(k=k):
                row(jnp.minimum(z + k, blocks - 1), 2 * k + 1, left).wait_send()


def run_front(
    qkv_shard, out_shard, row, short_row, cot, gain, bias, shifts, key_ids, query_ids, experts, blocks
):
    span, width = row.shape
    size = width // HEADS
    halo = key_ids.shape[0] - span
    part = qkv_shard.shape[2]
    share = part // size // 3
    length = blocks * span
    gathers = qkv_shard.shape[1] % 16 == 0
    if not gathers:
        qkv_shard = lax.all_gather(qkv_shard, "expert", axis=1, tiled=True)
        full_out = lax.all_gather(out_shard, "expert", axis=0, tiled=True)
    any_spec = pl.BlockSpec(memory_space=pl.ANY)
    dma = pltpu.SemaphoreType.DMA

    def whole(shape):
        return pl.BlockSpec(shape, lambda f: (0,) * len(shape), pipeline_mode=pl.Buffered(1))

    def short_head(*shape):
        return pl.BlockSpec(
            shape, lambda f: (0,) * (len(shape) - 3) + (jnp.minimum(f, HEADS - 1), 0, 0)
        )

    def long_head(*shape):
        return pl.BlockSpec(
            shape, lambda f: (0,) * (len(shape) - 3) + (jnp.maximum(f - HEADS, 0), 0, 0)
        )

    def flat_short(*shape):
        return pl.BlockSpec(shape, lambda f: (jnp.minimum(f, HEADS - 1), 0))

    gathered_shapes = (
        jax.ShapeDtypeStruct((blocks, width, part), BF),
        jax.ShapeDtypeStruct((experts,) + out_shard.shape, BF),
    )
    results = pl.pallas_call(
        functools.partial(
            front_kernel, experts, blocks, HEADS, gathers, span, min(SHORT, span)
        ),
        grid=(HEADS + share,),
        in_specs=[any_spec] * 5
        + [
            whole((1, width)),
            whole((1, width)),
            whole((blocks, 1, part)),
            whole((halo + span, 1)),
            whole((1, span)),
        ],
        out_specs=((any_spec,) * 2 if gathers else ())
        + (
            any_spec,
            any_spec,
            long_head(3, 1, length, size),
            pl.BlockSpec((size, length), lambda f: (jnp.maximum(f - HEADS, 0), 0)),
            long_head(1, 1, length),
            short_head(3, 1, halo + span, size),
            flat_short(size, span),
            flat_short(size, span),
            short_head(1, 1, span),
        ),
        out_shape=(gathered_shapes if gathers else ())
        + (
            jax.ShapeDtypeStruct(cot.shape, BF),
            jax.ShapeDtypeStruct((blocks, share, size, span), BF),
            jax.ShapeDtypeStruct((3, share, length, size), BF),
            jax.ShapeDtypeStruct((share * size, length), F32),
            jax.ShapeDtypeStruct((share, 1, length), F32),
            jax.ShapeDtypeStruct((3, HEADS, halo + span, size), BF),
            jax.ShapeDtypeStruct((width, span), F32),
            jax.ShapeDtypeStruct((width, span), BF),
            jax.ShapeDtypeStruct((HEADS, 1, span), F32),
        ),
        scratch_shapes=[
            pltpu.VMEM((blocks, width, part), BF),
            pltpu.VMEM((blocks, span, width), BF),
            pltpu.VMEM((halo + span, width), BF),
            pltpu.VMEM((3, share, length, size), BF),
            pltpu.VMEM((3, HEADS, halo + span, size), BF),
            pltpu.VMEM((blocks, share, size, span), BF),
            dma((2, experts)),
            dma((2, experts)),
            dma((2 * blocks,)),
            dma((blocks,)),
            dma((2,)),
            dma((6,)),
            dma((experts,)),
            dma((experts,)),
            dma((share, blocks)),
            dma((share, blocks)),
        ],
        compiler_params=pltpu.CompilerParams(
            collective_id=0, has_side_effects=True, vmem_limit_bytes=56 << 20
        ),
    )(qkv_shard, out_shard, row, short_row, cot, gain, bias, shifts, key_ids, query_ids)
    if gathers:
        return results[0], results[1].reshape(-1, out_shard.shape[1]), results[2:]
    return qkv_shard, full_out, results


def gelu_parts(hidden):
    cdf = 0.5 * (1.0 + lax.erf(hidden * 0.7071067811865476))
    density = jnp.exp(-0.5 * hidden * hidden) * 0.3989422804014327
    return hidden * cdf, cdf + hidden * density


def expert_kernel(
    experts,
    blocks,
    steps,
    chunk,
    x_hbm,
    cot_hbm,
    *refs,
):
    ups, refs = refs[:blocks], refs[blocks:]
    downs, refs = refs[:blocks], refs[blocks:]
    up_shifts, refs = refs[:blocks], refs[blocks:]
    (
        down_shift_ref,
        centroid_ref,
        back_grad,
        back_out,
        up_sum,
        down_sum,
        up_shift_out,
        down_shift_out,
        x_buf,
        low_buf,
        xt_ref,
        gt_ref,
        out_acc,
        grad_acc,
        gate_ref,
        x_send,
        x_recv,
        back_send,
        back_recv,
        local_sem,
        *refs,
    ) = refs
    rounds = (blocks - 1).bit_length()
    up_held, down_held = refs[: rounds + 1], refs[rounds + 1 : 2 * rounds + 2]
    part_send, part_recv = refs[2 * rounds + 2 :]
    step = pl.program_id(0)
    me, z = lax.axis_index("expert"), lax.axis_index("blk")
    capacity, width = x_buf.shape[1:]
    rows = experts * capacity
    lanes = 128

    def x_copy(d):
        target = lax.rem(me + d, experts)
        return pltpu.make_async_remote_copy(
            src_ref=x_hbm.at[target],
            dst_ref=x_buf.at[me],
            send_sem=x_send.at[d],
            recv_sem=x_recv.at[d],
            device_id={"expert": target},
            device_id_type=MESH,
        )

    def back_copy(n, d):
        target = lax.rem(me + d, experts)
        return pltpu.make_async_remote_copy(
            src_ref=(low_buf, x_buf)[n].at[target],
            dst_ref=(back_grad, back_out)[n].at[me],
            send_sem=back_send.at[n, d],
            recv_sem=back_recv.at[n, d],
            device_id={"expert": target},
            device_id_type=MESH,
        )

    def back_local(n):
        return pltpu.make_async_copy(
            (low_buf, x_buf)[n].at[me], (back_grad, back_out)[n].at[me], local_sem.at[n]
        )

    def part_copies(r, p):
        bit = 1 << r
        mine = lax.rem(z // bit, 2)
        partner = z + bit - 2 * bit * mine
        copies = []
        for k in range((blocks >> r) // 2):
            for n, held in enumerate((up_held, down_held)):
                copies.append(
                    pltpu.make_async_remote_copy(
                        src_ref=held[r].at[p, 2 * k + 1 - mine],
                        dst_ref=held[r + 1].at[p, k],
                        send_sem=part_send.at[r, n, p, k],
                        recv_sem=part_recv.at[r, n, p, k],
                        device_id={"blk": partner},
                        device_id_type=MESH,
                    )
                )
        return copies

    def add_parts(r, p):
        mine = lax.rem(z // (1 << r), 2)
        for copy in part_copies(r, p):
            copy.wait_recv()
        for k in range((blocks >> r) // 2):
            up = up_held[r][p, 2 * k + mine].astype(F32) + up_held[r + 1][p, k].astype(F32)
            down = down_held[r][p, 2 * k + mine].astype(F32) + down_held[r + 1][p, k].astype(F32)
            if r + 1 < rounds:
                up_held[r + 1][p, k] = up.astype(BF)
                down_held[r + 1][p, k] = down.astype(BF)
            else:
                for j in range(blocks):
                    at = j * steps * lanes + p * lanes
                    up_sum[:, at : at + lanes] = up[:, j * lanes : (j + 1) * lanes]
                down_sum[p * lanes : (p + 1) * lanes, :] = down.T
        if r + 1 < rounds:
            for copy in part_copies(r + 1, p):
                copy.start()

    cot_copy = pltpu.make_async_copy(cot_hbm, low_buf, local_sem.at[2])
    own_copy = pltpu.make_async_copy(x_hbm.at[me], x_buf.at[me], local_sem.at[3])
    x_flat, low_flat = x_buf.reshape(rows, width), low_buf.reshape(rows, width)

    @pl.when(step == 0)
    def _():
        barrier = pltpu.get_barrier_semaphore()
        for d in range(1, experts):
            pl.semaphore_signal(
                barrier, inc=1, device_id={"expert": lax.rem(me + d, experts)}, device_id_type=MESH
            )
        for r in range(rounds):
            bit = 1 << r
            partner = z + bit - 2 * bit * lax.rem(z // bit, 2)
            pl.semaphore_signal(barrier, inc=1, device_id={"blk": partner}, device_id_type=MESH)
        cot_copy.start()
        own_copy.start()
        pl.semaphore_wait(barrier, experts - 1 + rounds)
        for d in range(1, experts):
            x_copy(d).start()
        out_acc[...] = jnp.zeros_like(out_acc)
        grad_acc[...] = jnp.zeros_like(grad_acc)
        cot_copy.wait()
        own_copy.wait()
        for d in range(1, experts):
            x_copy(d).wait_recv()
        for lo in range(0, rows, chunk):
            x = x_flat[lo : lo + chunk]
            logit = jnp.sum(x.astype(F32) * centroid_ref[...], axis=1, keepdims=True)
            gate = 1.0 / (1.0 + jnp.exp(-logit))
            gate_ref[lo : lo + chunk] = gate
            low = (low_flat[lo : lo + chunk].astype(F32) * gate).astype(BF)
            low_flat[lo : lo + chunk] = low
            xt_ref[:, lo : lo + chunk] = x.T
            gt_ref[:, lo : lo + chunk] = low.T
            part = jnp.sum(low.astype(F32), axis=0, keepdims=True)
            if lo:
                down_shift_out[...] += part
            else:
                down_shift_out[...] = part

    up = jnp.concatenate([ref[...] for ref in ups], axis=1)
    down = jnp.concatenate([ref[...] for ref in downs], axis=0)
    up_shift = jnp.concatenate([ref[...] for ref in up_shifts], axis=1)
    totals = None
    for lo in range(0, rows, chunk):
        x = x_flat[lo : lo + chunk]
        low = low_flat[lo : lo + chunk]
        hidden = dot_nn(x, up) + up_shift
        active, slope = gelu_parts(hidden)
        active = active.astype(BF)
        grad_low = (dot_nt(low, down) * slope).astype(BF)
        out_acc[lo : lo + chunk] += dot_nn(active, down)
        grad_acc[lo : lo + chunk] += dot_nt(grad_low, up)
        parts = (
            dot_nn(xt_ref[:, lo : lo + chunk], grad_low),
            dot_nn(gt_ref[:, lo : lo + chunk], active),
            jnp.sum(grad_low.astype(F32), axis=0, keepdims=True),
        )
        totals = parts if totals is None else tuple(a + b for a, b in zip(totals, parts))
    up_total, down_total, shift_total = totals
    up_total = up_total.astype(BF)
    depth = width // blocks
    for j in range(blocks):
        up_held[0][step, j] = up_total[j * depth : (j + 1) * depth]
        down_held[0][step, j] = down_total[:, j * lanes : (j + 1) * lanes].astype(BF)
        up_shift_out[j] = shift_total[:, j * lanes : (j + 1) * lanes]
    for copy in part_copies(0, step):
        copy.start()

    tasks = sorted(
        ((r, p) for p in range(steps) for r in range(rounds)), key=lambda task: (sum(task), task[0])
    )
    early = [[] for _ in range(steps)]
    for turn, task in enumerate(tasks):
        at = 2 * (task[1] + 1) + 2 * task[0]
        if at < steps - 1:
            early[at].append(task)
    for at in range(steps):
        if early[at]:

            @pl.when(step == at)
            def _(at=at):
                for r, p in early[at]:
                    add_parts(r, p)

    @pl.when(step == steps - 1)
    def _():
        for d in range(1, experts):
            x_copy(d).wait_send()
        for lo in range(0, rows, chunk):
            gate = gate_ref[lo : lo + chunk]
            out = (out_acc[lo : lo + chunk] + down_shift_ref[...]).astype(BF)
            inner = jnp.sum(
                low_flat[lo : lo + chunk].astype(F32) * out.astype(F32), axis=1, keepdims=True
            )
            x_flat[lo : lo + chunk] = out
            low_flat[lo : lo + chunk] = (
                grad_acc[lo : lo + chunk] + inner * (1.0 - gate) * centroid_ref[...]
            ).astype(BF)
        back_local(0).start()
        for d in range(1, experts):
            back_copy(0, d).start()
        back_local(1).start()
        left = [task for task in tasks if all(task not in done for done in early)]
        half = len(left) // 2
        for r, p in left[:half]:
            add_parts(r, p)
        for d in range(1, experts):
            back_copy(0, d).wait_send()
            back_copy(1, d).start()
        for r, p in left[half:]:
            add_parts(r, p)
        for n in range(2):
            back_local(n).wait()
            for d in range(1, experts):
                back_copy(n, d).wait_recv()
        for d in range(1, experts):
            back_copy(1, d).wait_send()
        for p in range(steps):
            for r in range(rounds):
                for copy in part_copies(r, p):
                    copy.wait_send()


def run_expert(x, cot, up_weight, down_weight, up_shift, down_shift, centroid, blocks):
    experts, capacity, width = x.shape
    rows = experts * capacity
    hidden = up_weight.shape[1]
    lanes = 128
    steps = hidden // blocks // lanes
    rounds = (blocks - 1).bit_length()
    chunk = min(512, rows)
    depth = width // blocks
    any_spec = pl.BlockSpec(memory_space=pl.ANY)

    def once(shape):
        return pl.BlockSpec(shape, lambda f: (0,) * len(shape), pipeline_mode=pl.Buffered(1))

    return pl.pallas_call(
        functools.partial(expert_kernel, experts, blocks, steps, chunk),
        grid=(steps,),
        in_specs=[any_spec] * 2
        + [pl.BlockSpec((width, lanes), lambda f, j=j: (0, j * steps + f)) for j in range(blocks)]
        + [pl.BlockSpec((lanes, width), lambda f, j=j: (j * steps + f, 0)) for j in range(blocks)]
        + [pl.BlockSpec((1, lanes), lambda f, j=j: (0, j * steps + f)) for j in range(blocks)]
        + [once((1, width))] * 2,
        out_specs=(
            any_spec,
            any_spec,
            once((depth, hidden)),
            once((hidden // blocks, width)),
            pl.BlockSpec((blocks, 1, lanes), lambda f: (0, 0, f)),
            once((1, width)),
        ),
        out_shape=(
            jax.ShapeDtypeStruct(x.shape, BF),
            jax.ShapeDtypeStruct(x.shape, BF),
            jax.ShapeDtypeStruct((depth, hidden), F32),
            jax.ShapeDtypeStruct((hidden // blocks, width), F32),
            jax.ShapeDtypeStruct((blocks, 1, hidden // blocks), F32),
            jax.ShapeDtypeStruct((1, width), F32),
        ),
        scratch_shapes=[
            pltpu.VMEM(x.shape, BF),
            pltpu.VMEM(x.shape, BF),
            pltpu.VMEM((width, rows), BF),
            pltpu.VMEM((width, rows), BF),
            pltpu.VMEM((rows, width), F32),
            pltpu.VMEM((rows, width), F32),
            pltpu.VMEM((rows, 1), F32),
            pltpu.SemaphoreType.DMA((experts,)),
            pltpu.SemaphoreType.DMA((experts,)),
            pltpu.SemaphoreType.DMA((2, experts)),
            pltpu.SemaphoreType.DMA((2, experts)),
            pltpu.SemaphoreType.DMA((4,)),
        ]
        + [pltpu.VMEM((steps, blocks >> r, depth, blocks * lanes), BF) for r in range(rounds + 1)]
        + [pltpu.VMEM((steps, blocks >> r, width, lanes), BF) for r in range(rounds + 1)]
        + [
            pltpu.SemaphoreType.DMA((rounds, 2, steps, blocks // 2)),
            pltpu.SemaphoreType.DMA((rounds, 2, steps, blocks // 2)),
        ],
        compiler_params=pltpu.CompilerParams(
            collective_id=1, has_side_effects=True, vmem_limit_bytes=62 << 20
        ),
        cost_estimate=pl.CostEstimate(
            flops=12 * rows * width * hidden, bytes_accessed=40 << 20, transcendentals=0
        ),
    )(
        x,
        cot,
        *([up_weight] * blocks),
        *([down_weight] * blocks),
        *([up_shift] * blocks),
        down_shift,
        centroid,
    )


def reduce_kernel(experts, blocks, parts, *refs):
    arrays = 1 + max(piece[0] for part in parts for piece in part)
    ins, refs = refs[:arrays], refs[arrays:]
    outs, refs = refs[:arrays], refs[arrays:]
    number = len(parts)
    from_mate, refs = refs[:number], refs[number:]
    pair_sum, refs = refs[:number], refs[number:]
    from_chips, refs = refs[:number], refs[number:]
    group_sum, refs = refs[:number], refs[number:]
    from_line, refs = refs[:number], refs[number:]
    whole, refs = refs[:number], refs[number:]
    mate_send, mate_recv, chip_send, chip_recv, line_send, line_recv, back_send, back_recv = refs
    rounds = (blocks - 1).bit_length()
    chips = experts // 2
    me, z = lax.axis_index("expert"), lax.axis_index("blk")
    core = lax.rem(me, 2)
    chip = me // 2
    mate = me + 1 - 2 * core

    def line_partner(r):
        bit = 1 << r
        return z + bit - 2 * bit * lax.rem(z // bit, 2)

    barrier = pltpu.get_barrier_semaphore()
    pl.semaphore_signal(barrier, inc=1, device_id={"expert": mate}, device_id_type=MESH)
    for d in range(1, chips):
        peer = lax.rem(me + 2 * d, experts)
        pl.semaphore_signal(barrier, inc=1, device_id={"expert": peer}, device_id_type=MESH)
    for r in range(rounds):
        pl.semaphore_signal(
            barrier, inc=1, device_id={"blk": line_partner(r)}, device_id_type=MESH
        )
    pl.semaphore_wait(barrier, chips + rounds)

    def send(source, target, send_sem, recv_sem, device):
        return pltpu.make_async_remote_copy(
            src_ref=source,
            dst_ref=target,
            send_sem=send_sem,
            recv_sem=recv_sem,
            device_id=device,
            device_id_type=MESH,
        )

    def mate_copies(p):
        at = 0
        copies = []
        for n, (array, first, columns) in enumerate(parts[p]):
            copies.append(
                send(
                    ins[array].at[:, 1 - core, :, pl.ds(first, columns)],
                    from_mate[p].at[:, :, pl.ds(at, columns)],
                    mate_send.at[p, n],
                    mate_recv.at[p, n],
                    {"expert": mate},
                )
            )
            at += columns
        return copies

    def chip_copies(p):
        copies = []
        for d in range(1, chips):
            there = lax.rem(chip + d, chips)
            copies.append(
                send(
                    pair_sum[p].at[there],
                    from_chips[p].at[d - 1],
                    chip_send.at[p, d],
                    chip_recv.at[p, d],
                    {"expert": 2 * there + core},
                )
            )
        return copies

    def segment(p, r):
        groups = whole[p].shape[0]
        start = 0
        for n in range(r):
            start = start + lax.rem(z // (1 << n), 2) * (groups >> (n + 1))
        return start, groups >> r

    def line_copy(p, r):
        start, groups = segment(p, r)
        half = groups // 2
        mine = lax.rem(z // (1 << r), 2)
        return send(
            group_sum[p].at[pl.ds(start + (1 - mine) * half, half)],
            from_line[p].at[r, pl.ds(0, half)],
            line_send.at[p, r],
            line_recv.at[p, r],
            {"blk": line_partner(r)},
        )

    def back_copy(p, r):
        start, groups = segment(p, r + 1)
        return send(
            whole[p].at[pl.ds(start, groups)],
            whole[p].at[pl.ds(start, groups)],
            back_send.at[p, r],
            back_recv.at[p, r],
            {"blk": line_partner(r)},
        )

    def back_arrival(p, r):
        start, groups = segment(p, r)
        mine = lax.rem(z // (1 << r), 2)
        start = start + (1 - mine) * (groups // 2)
        return send(
            whole[p].at[pl.ds(start, groups // 2)],
            whole[p].at[pl.ds(start, groups // 2)],
            back_send.at[p, r],
            back_recv.at[p, r],
            {"blk": line_partner(r)},
        )

    def run(p, stage):
        if stage == 0:
            for copy in mate_copies(p):
                copy.start()
        elif stage == 1:
            for copy in mate_copies(p):
                copy.wait_recv()
            for k in range(chips):
                at = 0
                for array, first, columns in parts[p]:
                    own = ins[array][k, core, :, first : first + columns]
                    came = from_mate[p][k, :, at : at + columns]
                    pair_sum[p][k, :, at : at + columns] = (
                        own.astype(F32) + came.astype(F32)
                    ).astype(BF)
                    at += columns
            for copy in chip_copies(p):
                copy.start()
        elif stage == 2:
            for copy in chip_copies(p):
                copy.wait_recv()
            total = pair_sum[p][chip].astype(F32)
            for d in range(1, chips):
                total = total + from_chips[p][d - 1].astype(F32)
            low = total.astype(BF)
            used = low.shape[1] // 128
            for g in range(group_sum[p].shape[0]):
                if g < used:
                    group_sum[p][g] = low[:, g * 128 : (g + 1) * 128]
                else:
                    group_sum[p][g] = jnp.zeros(group_sum[p].shape[1:], BF)
            line_copy(p, 0).start()
        elif stage < 2 + rounds:
            add_line(p, stage - 3)
            line_copy(p, stage - 2).start()
        elif stage == 2 + rounds:
            r = rounds - 1
            add_line(p, r)
            start, groups = segment(p, rounds)
            whole[p][pl.ds(start, groups)] = group_sum[p][pl.ds(start, groups)]
            back_copy(p, r).start()
        else:
            r = rounds - 1 - (stage - 3 - rounds)
            back_arrival(p, r).wait_recv()
            if r:
                back_copy(p, r - 1).start()
            else:
                at = 0
                for array, first, columns in parts[p]:
                    for c in range(0, columns, 128):
                        outs[array][:, first + c : first + c + 128] = whole[p][
                            (at + c) // 128
                        ].astype(F32)
                    at += columns

    def add_line(p, r):
        line_copy(p, r).wait_recv()
        start, groups = segment(p, r + 1)
        held = group_sum[p][pl.ds(start, groups)].astype(F32)
        group_sum[p][pl.ds(start, groups)] = (
            held + from_line[p][r, pl.ds(0, groups)].astype(F32)
        ).astype(BF)

    stages = 3 + 2 * rounds
    for turn in range(number + stages - 1):
        for p in range(number):
            if 0 <= turn - p < stages:
                run(p, turn - p)
    for p in range(number):
        for copy in mate_copies(p) + chip_copies(p):
            copy.wait_send()
        for r in range(rounds):
            line_copy(p, r).wait_send()
            back_copy(p, r).wait_send()


def reduce_all(arrays, parts, experts, blocks):
    rows = arrays[0].shape[0] // experts
    chips = experts // 2
    rounds = (blocks - 1).bit_length()
    number = len(parts)
    widths = [sum(piece[2] for piece in part) for part in parts]
    groups = [-(-width // 128 // blocks) * blocks for width in widths]
    dma = pltpu.SemaphoreType.DMA
    return pl.pallas_call(
        functools.partial(reduce_kernel, experts, blocks, parts),
        in_specs=[pl.BlockSpec(memory_space=pltpu.VMEM)] * len(arrays),
        out_specs=tuple(pl.BlockSpec(memory_space=pltpu.VMEM) for _ in arrays),
        out_shape=tuple(jax.ShapeDtypeStruct((rows, a.shape[1]), F32) for a in arrays),
        scratch_shapes=[pltpu.VMEM((chips, rows, w), BF) for w in widths]
        + [pltpu.VMEM((chips, rows, w), BF) for w in widths]
        + [pltpu.VMEM((chips - 1, rows, w), BF) for w in widths]
        + [pltpu.VMEM((g, rows, 128), BF) for g in groups]
        + [pltpu.VMEM((rounds, g // 2, rows, 128), BF) for g in groups]
        + [pltpu.VMEM((g, rows, 128), BF) for g in groups]
        + [dma((number, 3)), dma((number, 3)), dma((number, chips)), dma((number, chips))]
        + [dma((number, rounds))] * 4,
        compiler_params=pltpu.CompilerParams(
            collective_id=2, has_side_effects=True, vmem_limit_bytes=40 << 20
        ),
    )(*[a.reshape(chips, 2, rows, a.shape[1]) for a in arrays])


def on_device(
    tokens,
    doc_ids,
    routes,
    ln1_gain,
    ln1_bias,
    qkv_weight,
    qv_bias,
    out_weight,
    out_bias,
    ln2_gain,
    ln2_bias,
    centroids,
    up_weight,
    up_bias,
    down_weight,
    down_bias,
    cotangent,
):
    rows, span, width = tokens.shape
    heads = HEADS
    size = width // heads
    blocks = lax.axis_size("blk")
    own = lax.axis_index("blk")
    count = rows * span
    length = blocks * span
    halo = min(SHORT, span)
    share = -(-heads // blocks)
    pad_heads = share * blocks - heads

    expert_count = centroids.shape[0]

    long_at = (doc_ids[0, -1] != 0).astype(jnp.int32)

    def ordered(pair):
        first = lax.dynamic_index_in_dim(pair, long_at, 0, keepdims=False)
        second = lax.dynamic_index_in_dim(pair, 1 - long_at, 0, keepdims=False)
        return jnp.stack([first, second])

    long_tokens = lax.dynamic_index_in_dim(tokens, long_at, 0, keepdims=False)
    short_tokens = lax.dynamic_index_in_dim(tokens, 1 - long_at, 0, keepdims=False)
    token_rows = jnp.concatenate([long_tokens, short_tokens]).astype(F32)

    capacity = 2 * count // expert_count
    slots = expert_count * capacity
    route_flat = routes.reshape(count)
    onehot = route_flat[:, None] == jnp.arange(expert_count, dtype=jnp.int32)[None, :]
    ranking = jnp.cumsum(onehot.astype(jnp.int32), axis=0) - 1
    slot_of = route_flat * capacity + jnp.sum(jnp.where(onehot, ranking, 0), axis=1)
    slot_line = jnp.arange(slots, dtype=jnp.int32)

    def to_experts(flat, slot_of):
        to_slots = (slot_line[:, None] == slot_of[None, :]).astype(BF)
        return dot_nn(to_slots, flat).astype(BF).reshape(expert_count, capacity, width)

    sent_cot = to_experts(cotangent.reshape(count, width), slot_of)
    slot_of = ordered(slot_of.reshape(rows, span)).reshape(count)
    route_flat = ordered(routes.reshape(rows, span)).reshape(count)
    onehot = route_flat[:, None] == jnp.arange(expert_count, dtype=jnp.int32)[None, :]
    from_slots = (slot_of[:, None] == slot_line[None, :]).astype(BF)
    grad_low = ordered(cotangent).reshape(count, width)

    def grouped(matrix):
        lead = matrix.shape[0]
        split = matrix.reshape(lead, 3, heads, size)
        split = jnp.pad(split, ((0, 0), (0, 0), (0, pad_heads), (0, 0)))
        split = split.reshape(lead, 3, blocks, share, size).transpose(2, 0, 1, 3, 4)
        return split.reshape(blocks, lead, 3 * share * size)

    def ungrouped(matrix):
        lead = matrix.shape[0]
        split = matrix.reshape(lead, blocks, 3, share, size).transpose(0, 2, 1, 3, 4)
        return split.reshape(lead, 3, blocks * share, size)[:, :, :heads].reshape(lead, 3, width)

    short_ids = jnp.concatenate(
        [
            jnp.full((halo,), -1, jnp.int32),
            lax.dynamic_index_in_dim(doc_ids, 1 - long_at, 0, keepdims=False),
        ]
    )
    short_ids = lax.dynamic_slice_in_dim(short_ids, own * span, halo + span, 0)
    key_ids = short_ids[:, None]
    query_ids = short_ids[None, halo:]
    shifts = jnp.concatenate([qv_bias[0], jnp.zeros((width,), F32), qv_bias[1]])
    full_qkv, full_out, rest = run_front(
        grouped(qkv_weight),
        out_weight,
        long_tokens,
        short_tokens,
        sent_cot,
        ln1_gain[None],
        ln1_bias[None],
        grouped(shifts[None]),
        key_ids,
        query_ids,
        expert_count,
        blocks,
    )
    (
        received_cot,
        long_attended,
        long_qkv,
        long_wide,
        long_total,
        short_qkv,
        short_wide,
        short_low,
        short_total,
    ) = rest
    long_attended = long_attended.reshape(-1, span)[:width]
    attended_t = jnp.concatenate([long_attended, short_low], axis=1)

    middle = (
        token_rows
        + lax.dot_general(
            attended_t, full_out, (((0,), (0,)), ((), ())), preferred_element_type=F32
        )
        + out_bias
    )
    normal_two, scale_two = norm_parts(middle)
    normed_two = normal_two * ln2_gain + ln2_bias
    outgoing = to_experts(normed_two.astype(BF), slot_of)
    centroid_rows = jnp.dot(onehot.astype(BF), centroids, preferred_element_type=F32)
    gate = jax.nn.sigmoid(jnp.sum(normed_two * centroid_rows, axis=1))

    own_centroid = lax.dynamic_index_in_dim(
        centroids.astype(F32), lax.axis_index("expert"), 0, keepdims=True
    )
    back_grad, back_out, up_sum, down_sum, up_shift_term, down_shift_term = run_expert(
        outgoing,
        received_cot,
        up_weight[0],
        down_weight[0],
        up_bias,
        down_bias,
        own_centroid,
        blocks,
    )
    back_grad = back_grad.reshape(slots, width)
    back_out = back_out.reshape(slots, width)

    grad_normed_two = dot_nn(from_slots, back_grad)
    inner_two, ln2_gain_term, ln2_bias_term = norm_back(
        grad_normed_two, normal_two, scale_two, ln2_gain
    )
    grad_out = grad_low.astype(F32)
    grad_middle = grad_out + inner_two
    out_shift_term = jnp.sum(grad_middle, axis=0)
    grad_middle_low = grad_middle.astype(BF)
    grad_attended_t = lax.dot_general(
        full_out, grad_middle_low, (((1,), (1,)), ((), ())), preferred_element_type=F32
    ).astype(BF)
    grad_pair = grad_attended_t.reshape(width, rows, span)
    long_grad, short_grad = grad_pair[:, 0], grad_pair[:, 1]
    long_grad = jnp.pad(long_grad, ((0, pad_heads * size), (0, 0)))
    long_grad = lax.all_to_all(
        long_grad.reshape(blocks, share * size, span), "blk", 0, 0, tiled=True
    )
    out_term = lax.dot_general(
        attended_t, grad_middle_low, (((1,), (0,)), ((), ())), preferred_element_type=F32
    )

    long_back = call(
        functools.partial(long_backward, block=span),
        (share,),
        (long_qkv, long_grad, long_wide, long_total),
        [
            pl.BlockSpec((3, 1, length, size), lambda h: (0, h, 0, 0)),
            pl.BlockSpec((blocks, size, span), lambda h: (0, h, 0)),
            pl.BlockSpec((size, length), lambda h: (h, 0)),
            pl.BlockSpec((1, 1, length), lambda h: (h, 0, 0)),
        ],
        jax.ShapeDtypeStruct((blocks, 3, share * size, span), BF),
        pl.BlockSpec((blocks, 3, size, span), lambda h: (0, 0, h, 0)),
        [pltpu.VMEM((length, size), F32), pltpu.VMEM((length, size), F32)],
        5 * share * length * length * 256,
        8 * length * width,
    )
    long_back = lax.all_to_all(long_back, "blk", 0, 0, tiled=True)
    query_back, own_back, halo_back = call(
        functools.partial(short_backward, block=halo),
        (heads,),
        (short_qkv, short_grad, short_wide, short_total, key_ids, query_ids),
        [
            pl.BlockSpec((3, 1, halo + span, size), lambda h: (0, h, 0, 0)),
            pl.BlockSpec((size, span), lambda h: (h, 0)),
            pl.BlockSpec((size, span), lambda h: (h, 0)),
            pl.BlockSpec((1, 1, span), lambda h: (h, 0, 0)),
            whole_spec((halo + span, 1)),
            whole_spec((1, span)),
        ],
        (
            jax.ShapeDtypeStruct((width, span), BF),
            jax.ShapeDtypeStruct((2, width, span), F32),
            jax.ShapeDtypeStruct((2, width, halo), BF),
        ),
        (
            pl.BlockSpec((size, span), lambda h: (h, 0)),
            pl.BlockSpec((2, size, span), lambda h: (0, h, 0)),
            pl.BlockSpec((2, size, halo), lambda h: (0, h, 0)),
        ),
        [pltpu.VMEM((halo + span, size), F32), pltpu.VMEM((halo + span, size), F32)],
        5 * heads * span * 2 * 2 * halo * 256,
        16 * span * width,
    )
    halo_back = lax.ppermute(halo_back, "blk", [(i + 1, i) for i in range(blocks - 1)])
    own_back = own_back + jnp.pad(halo_back.astype(F32), ((0, 0), (0, 0), (span - halo, 0)))
    short_back = jnp.concatenate([query_back[None], own_back.astype(BF)], axis=0)
    short_back = jnp.pad(
        short_back.reshape(3, heads, size, span), ((0, 0), (0, pad_heads), (0, 0), (0, 0))
    )
    short_back = short_back.reshape(3, blocks, share, size, span).transpose(1, 0, 2, 3, 4)
    back_t = jnp.concatenate(
        [long_back.reshape(-1, span), short_back.reshape(-1, span)], axis=1
    )

    normal_one, scale_one = norm_parts(token_rows)
    normed_low = (normal_one * ln1_gain + ln1_bias).astype(BF)
    qkv_term = lax.dot_general(
        normed_low, back_t, (((0,), (1,)), ((), ())), preferred_element_type=F32
    )
    qv_sums = ungrouped(jnp.sum(back_t.astype(F32), axis=1)[None])[0]
    grad_normed_one = lax.dot_general(
        back_t.reshape(blocks, -1, count),
        full_qkv,
        (((0, 1), (0, 2)), ((), ())),
        preferred_element_type=F32,
    )
    inner_one, ln1_gain_term, ln1_bias_term = norm_back(
        grad_normed_one, normal_one, scale_one, ln1_gain
    )
    grad_tokens = grad_middle + inner_one

    expert_rows = dot_nn(from_slots, back_out)
    result = middle + gate[:, None] * expert_rows
    grad_logit = jnp.sum(grad_out * expert_rows, axis=1) * gate * (1.0 - gate)
    centroid_term = jnp.einsum(
        "te,td->de",
        onehot.astype(F32) * grad_logit[:, None],
        normed_two,
        precision=lax.Precision.HIGHEST,
    )

    small = jnp.stack(
        [
            qv_sums[0],
            qv_sums[2],
            out_shift_term,
            ln1_gain_term,
            ln1_bias_term,
            ln2_gain_term,
            ln2_bias_term,
        ],
        axis=1,
    )
    n_small = small.shape[1]
    small = jnp.concatenate([small, centroid_term], axis=1)
    small = jnp.pad(small, ((0, 0), (0, 128 - small.shape[1])))
    columns = qkv_term.shape[1]
    half = -(-columns // 256) * 128
    qkv_sum, out_sum, small_sum = reduce_all(
        (qkv_term.astype(BF), out_term.astype(BF), small.astype(BF)),
        (
            ((1, 0, width), (2, 0, 128)),
            ((0, 0, half),),
            ((0, half, columns - half),),
        ),
        expert_count,
        blocks,
    )
    centroid_sum = small_sum[:, n_small : n_small + expert_count].T
    shift_sum = lax.psum_scatter(
        jnp.concatenate(
            [up_shift_term.reshape(blocks, -1), down_shift_term.reshape(blocks, -1)], axis=1
        ).astype(BF),
        "blk",
        scatter_dimension=0,
        tiled=True,
    ).astype(F32)
    up_shift_sum = shift_sum[:, : up_bias.shape[1] // blocks]
    down_shift_sum = shift_sum[:, up_bias.shape[1] // blocks :]
    return (
        ordered(result.reshape(rows, span, width)),
        ordered(grad_tokens.reshape(rows, span, width)),
        small_sum[:, 3],
        small_sum[:, 4],
        ungrouped(qkv_sum).reshape(-1, 3 * width),
        small_sum[:, :2].T,
        out_sum,
        small_sum[:, 2],
        small_sum[:, 5],
        small_sum[:, 6],
        centroid_sum,
        up_sum[None],
        up_shift_sum,
        down_sum[None],
        down_shift_sum,
    )


def solution(mesh):
    return jax.shard_map(
        on_device,
        mesh=mesh,
        in_specs=(
            P("expert", "blk", None),
            P("expert", None),
            P("blk", "expert", None, None),
            P(),
            P(),
            P("expert", None),
            P(),
            P("expert", None),
            P(),
            P(),
            P(),
            P(),
            P("expert", None, None),
            P("expert", None),
            P("expert", None, None),
            P("expert", None),
            P("expert", "blk", None),
        ),
        out_specs=(
            P("expert", "blk", None),
            P("expert", "blk", None),
            P("expert"),
            P("expert"),
            P("expert", None),
            P(None, "expert"),
            P("expert", None),
            P("expert"),
            P("expert"),
            P("expert"),
            P(None, "expert"),
            P("expert", "blk", None),
            P("expert", "blk"),
            P("expert", "blk", None),
            P("expert", "blk"),
        ),
        check_vma=False,
    )
```

```python
import functools

import jax
import jax.numpy as jnp
from jax import lax
from jax.experimental import pallas as pl
from jax.experimental.pallas import tpu as pltpu
from jax.sharding import PartitionSpec as P

HEADS = 12
SHORT = 256
NEGATIVE = -1e30
EPSILON = 1e-05
BF = jnp.bfloat16
F32 = jnp.float32


def dot_nn(a, b):
    return lax.dot_general(a, b, (((1,), (0,)), ((), ())), preferred_element_type=F32)


def dot_nt(a, b):
    return lax.dot_general(a, b, (((1,), (1,)), ((), ())), preferred_element_type=F32)


def norm_parts(values):
    average = jnp.mean(values, axis=-1, keepdims=True)
    centred = values - average
    variance = jnp.mean(centred * centred, axis=-1, keepdims=True)
    scale = lax.rsqrt(variance + EPSILON)
    return centred * scale, scale


def layer_norm(values, gain, bias):
    return norm_parts(values)[0] * gain + bias


def norm_back(upstream, normal, scale, gain):
    t = upstream * gain
    inner = (
        t
        - jnp.mean(t, axis=-1, keepdims=True)
        - normal * jnp.mean(t * normal, axis=-1, keepdims=True)
    )
    return inner * scale, jnp.sum(upstream * normal, axis=0), jnp.sum(upstream, axis=0)


def causal(rows, columns, shift):
    row = lax.broadcasted_iota(jnp.int32, (rows, columns), 0)
    column = lax.broadcasted_iota(jnp.int32, (rows, columns), 1)
    return row <= column + shift


def norm_low(values, gain, bias):
    return layer_norm(values.astype(F32), gain, bias).astype(BF)


def scaled(query):
    return (query.astype(F32) * query.shape[-1] ** (-0.5)).astype(BF)


def short_visible(key_ids, query_ids, i, block, halo):
    lo = i * block
    same = key_ids[lo : lo + halo + block] == query_ids[:, lo : lo + block]
    return same & causal(halo + block, block, halo)


MESH = pl.DeviceIdType.MESH


def remote(source, target, send_sem, recv_sem, device):
    return pltpu.make_async_remote_copy(
        src_ref=source,
        dst_ref=target,
        send_sem=send_sem,
        recv_sem=recv_sem,
        device_id=device,
        device_id_type=MESH,
    )


def greet(experts, blocks):
    me, z = lax.axis_index("expert"), lax.axis_index("blk")
    barrier = pltpu.get_barrier_semaphore()
    for d in range(1, experts):
        pl.semaphore_signal(
            barrier, inc=1, device_id={"expert": lax.rem(me + d, experts)}, device_id_type=MESH
        )
    for d in range(1, blocks):
        pl.semaphore_signal(
            barrier, inc=1, device_id={"blk": lax.rem(z + d, blocks)}, device_id_type=MESH
        )
    pl.semaphore_wait(barrier, experts + blocks - 2)


def front_kernel(
    experts,
    blocks,
    heads,
    gathers,
    block,
    short_block,
    qkv_ref,
    out_ref,
    row_ref,
    short_ref,
    cot_ref,
    gain_ref,
    bias_ref,
    shift_ref,
    key_ids,
    query_ids,
    *refs,
):
    if gathers:
        (full_qkv, full_out), refs = refs[:2], refs[2:]
    else:
        full_qkv = qkv_ref
    (
        received_cot,
        attended,
        long_qkv,
        long_wide,
        long_total,
        short_qkv,
        short_wide,
        short_low,
        short_total,
        weights,
        rows_buf,
        short_buf,
        long_store,
        short_store,
        low_stage,
        shard_send,
        shard_recv,
        row_send,
        row_recv,
        edge_sem,
        local_sem,
        cot_send,
        cot_recv,
        low_send,
        low_recv,
    ) = refs
    me, z = lax.axis_index("expert"), lax.axis_index("blk")
    step = pl.program_id(0)
    mate = me + 1 - 2 * lax.rem(me, 2)
    peers = [lax.rem(me + 2 * d, experts) for d in range(1, experts // 2)]
    share, size = long_store.shape[1], long_store.shape[3]
    length = blocks * block
    span = block
    halo = short_buf.shape[0] - span
    shard_rows = qkv_ref.shape[1]

    def qkv_part(slot):
        return full_qkv.at[:, pl.ds(pl.multiple_of(slot * shard_rows, shard_rows), shard_rows)]

    def shard(n, own, slot, turn, target):
        part = (qkv_part(slot), full_out.at[slot])[n]
        source = (qkv_ref, out_ref)[n] if own else part
        return remote(
            source, part, shard_send.at[n, turn], shard_recv.at[n, slot], {"expert": target}
        )

    def row(slot, turn, target):
        return remote(
            rows_buf.at[slot],
            rows_buf.at[slot],
            row_send.at[turn],
            row_recv.at[slot],
            {"blk": target},
        )

    def own_row(turn, target):
        return remote(
            row_ref, rows_buf.at[z], row_send.at[turn], row_recv.at[z], {"blk": target}
        )

    to_right, to_left = z + 1 < blocks, z > 0
    right, left = lax.rem(z + 1, blocks), lax.rem(z + blocks - 1, blocks)
    last_rows = short_ref.at[pl.ds(span - halo, halo)]
    halo_rows = short_buf.at[pl.ds(0, halo)]
    edge = remote(last_rows, halo_rows, edge_sem.at[0], edge_sem.at[1], {"blk": right})
    no_edge = pltpu.make_async_copy(last_rows, halo_rows, edge_sem.at[1])
    local = [
        pltpu.make_async_copy(row_ref, rows_buf.at[z], local_sem.at[0]),
        pltpu.make_async_copy(short_ref, short_buf.at[pl.ds(halo, span)], local_sem.at[1]),
    ]
    own_cot = pltpu.make_async_copy(cot_ref.at[me], received_cot.at[me], local_sem.at[2])
    load_weights = pltpu.make_async_copy(full_qkv, weights, local_sem.at[3])
    own_shards = []
    sent = []
    handed = []
    if gathers:
        own_shards = [
            pltpu.make_async_copy(qkv_ref, qkv_part(me), local_sem.at[4]),
            pltpu.make_async_copy(out_ref, full_out.at[me], local_sem.at[5]),
        ]
        for n in range(2):
            for turn, peer in enumerate(peers):
                sent.append(shard(n, True, me, turn, peer))
            sent.append(shard(n, True, me, len(peers), mate))
            for turn, peer in enumerate(peers):
                handed.append(shard(n, False, peer, len(peers) + 1 + turn, mate))

    def cot_copy(d):
        target = lax.rem(me + d, experts)
        return remote(
            cot_ref.at[target],
            received_cot.at[me],
            cot_send.at[d],
            cot_recv.at[d],
            {"expert": target},
        )

    def low_copy(head, d):
        target = lax.rem(z + d, blocks)
        return remote(
            low_stage.at[target, head],
            attended.at[z, head],
            low_send.at[head, d],
            low_recv.at[head, d],
            {"blk": target},
        )

    def low_local(head):
        return pltpu.make_async_copy(
            low_stage.at[z, head], attended.at[z, head], low_send.at[head, 0]
        )

    def hand_on(k):
        @pl.when(z - k >= 0)
        def _():
            slot = jnp.maximum(z - k, 0)
            row(slot, 2 * k, right).wait_recv()

            @pl.when(to_right)
            def _():
                row(slot, 2 * k, right).start()

        @pl.when(z + k < blocks)
        def _():
            slot = jnp.minimum(z + k, blocks - 1)
            row(slot, 2 * k + 1, left).wait_recv()

            @pl.when(to_left)
            def _():
                row(slot, 2 * k + 1, left).start()

    def project(source, lo, count, groups, store):
        low = norm_low(source, gain_ref[...], bias_ref[...])
        for n, group in enumerate(groups):
            part = (dot_nn(low, weights[group]) + shift_ref[group]).astype(BF)
            for kind in range(3):
                for head in range(share):
                    at = (kind * share + head) * size
                    if n * share + head < store.shape[1]:
                        store[kind, n * share + head, lo : lo + count] = part[:, at : at + size]

    @pl.when(step == 0)
    def _():
        for copy in local + own_shards:
            copy.start()
        greet(experts, blocks)

        @pl.when(to_right)
        def _():
            own_row(0, right).start()
            edge.start()

        @pl.when(to_left)
        def _():
            own_row(1, left).start()

        @pl.when(jnp.logical_not(to_left))
        def _():
            no_edge.start()

        for copy in sent:
            copy.start()
        hand_on(1)
        for copy in handed:
            copy.wait_recv()
            copy.start()
        if gathers:
            for turn in range(experts // 2):
                for n in range(2):
                    shard(n, False, lax.rem(mate + 2 * turn, experts), 0, mate).wait_recv()
        for copy in own_shards:
            copy.wait()
        load_weights.start()
        own_cot.start()
        for d in range(1, experts):
            cot_copy(d).start()

        @pl.when(to_left)
        def _():
            edge.wait_recv()

        @pl.when(jnp.logical_not(to_left))
        def _():
            no_edge.wait()

        for copy in local:
            copy.wait()
        load_weights.wait()
        for lo in range(0, halo + span, short_block):
            project(short_buf[lo : lo + short_block], lo, short_block, range(blocks), short_store)

    for k in range(2, blocks):

        @pl.when(step == (k - 1) * heads // (blocks - 1))
        def _(k=k):
            hand_on(k)

    @pl.when(step < heads)
    def _():
        query, key, value = (short_store[kind, step] for kind in range(3))
        for kind, part in enumerate((query, key, value)):
            short_qkv[kind, 0] = part
        query = scaled(query)
        value_t = value.T
        for i in range(span // short_block):
            lo, hi = i * short_block, (i + 1) * short_block
            visible = short_visible(key_ids[...], query_ids[...], i, short_block, halo)
            scores = dot_nt(key[lo : hi + halo], query[lo + halo : hi + halo])
            scores = jnp.where(visible, scores, NEGATIVE)
            top = jnp.max(scores, axis=0, keepdims=True)
            scores = jnp.exp(scores - top)
            total = jnp.sum(scores, axis=0, keepdims=True)
            out = dot_nn(value_t[:, lo : hi + halo], scores.astype(BF)) / total
            short_wide[:, lo:hi] = out
            short_low[:, lo:hi] = out.astype(BF)
            short_total[0, :, lo:hi] = top + jnp.log(total)

    @pl.when(step == heads)
    def _():
        for slot in range(blocks):
            project(rows_buf[slot], slot * block, block, [z], long_store)

    @pl.when(step >= heads)
    def _():
        head = step - heads
        query, key, value = (long_store[kind, head] for kind in range(3))
        for kind, part in enumerate((query, key, value)):
            long_qkv[kind, 0] = part
        query = scaled(query)
        value_t = value.T
        visible = causal(block, block, 0)
        for i in range(blocks):
            lo, hi = i * block, (i + 1) * block
            own = query[lo:hi]
            near = jnp.where(visible, dot_nt(key[lo:hi], own), NEGATIVE)
            top = jnp.max(near, axis=0, keepdims=True)
            if i:
                far = dot_nt(key[:lo], own)
                top = jnp.maximum(top, jnp.max(far, axis=0, keepdims=True))
            near = jnp.exp(near - top)
            total = jnp.sum(near, axis=0, keepdims=True)
            out = dot_nn(value_t[:, lo:hi], near.astype(BF))
            if i:
                far = jnp.exp(far - top)
                total = total + jnp.sum(far, axis=0, keepdims=True)
                out = out + dot_nn(value_t[:, :lo], far.astype(BF))
            out = out / total
            long_wide[:, lo:hi] = out
            low_stage[i, head] = out.astype(BF)
            long_total[0, :, lo:hi] = top + jnp.log(total)
        low_local(head).start()
        for d in range(1, blocks):
            low_copy(head, d).start()

    @pl.when(step == heads + share - 1)
    def _():
        for head in range(share):
            low_local(head).wait()
            for d in range(1, blocks):
                low_copy(head, d).wait()
        own_cot.wait()
        for d in range(1, experts):
            cot_copy(d).wait()
        for copy in sent + handed:
            copy.wait_send()

        @pl.when(to_right)
        def _():
            own_row(0, right).wait_send()
            edge.wait_send()

        @pl.when(to_left)
        def _():
            own_row(1, left).wait_send()

        for k in range(1, blocks):

            @pl.when((z - k >= 0) & to_right)
            def _(k=k):
                row(jnp.maximum(z - k, 0), 2 * k, right).wait_send()

            @pl.when((z + k < blocks) & to_left)
            def _(k=k):
                row(jnp.minimum(z + k, blocks - 1), 2 * k + 1, left).wait_send()


def run_front(
    qkv_shard, out_shard, row, short_row, cot, gain, bias, shifts, key_ids, query_ids, experts, blocks
):
    span, width = row.shape
    size = width // HEADS
    halo = key_ids.shape[0] - span
    part = qkv_shard.shape[2]
    share = part // size // 3
    length = blocks * span
    gathers = qkv_shard.shape[1] % 16 == 0
    if not gathers:
        qkv_shard = lax.all_gather(qkv_shard, "expert", axis=1, tiled=True)
        full_out = lax.all_gather(out_shard, "expert", axis=0, tiled=True)
    any_spec = pl.BlockSpec(memory_space=pl.ANY)
    dma = pltpu.SemaphoreType.DMA

    def whole(shape):
        return pl.BlockSpec(shape, lambda f: (0,) * len(shape), pipeline_mode=pl.Buffered(1))

    def short_head(*shape):
        return pl.BlockSpec(
            shape, lambda f: (0,) * (len(shape) - 3) + (jnp.minimum(f, HEADS - 1), 0, 0)
        )

    def long_head(*shape):
        return pl.BlockSpec(
            shape, lambda f: (0,) * (len(shape) - 3) + (jnp.maximum(f - HEADS, 0), 0, 0)
        )

    def flat_short(*shape):
        return pl.BlockSpec(shape, lambda f: (jnp.minimum(f, HEADS - 1), 0))

    gathered_shapes = (
        jax.ShapeDtypeStruct((blocks, width, part), BF),
        jax.ShapeDtypeStruct((experts,) + out_shard.shape, BF),
    )
    results = pl.pallas_call(
        functools.partial(
            front_kernel, experts, blocks, HEADS, gathers, span, min(SHORT, span)
        ),
        grid=(HEADS + share,),
        in_specs=[any_spec] * 5
        + [
            whole((1, width)),
            whole((1, width)),
            whole((blocks, 1, part)),
            whole((halo + span, 1)),
            whole((1, span)),
        ],
        out_specs=((any_spec,) * 2 if gathers else ())
        + (
            any_spec,
            any_spec,
            long_head(3, 1, length, size),
            pl.BlockSpec((size, length), lambda f: (jnp.maximum(f - HEADS, 0), 0)),
            long_head(1, 1, length),
            short_head(3, 1, halo + span, size),
            flat_short(size, span),
            flat_short(size, span),
            short_head(1, 1, span),
        ),
        out_shape=(gathered_shapes if gathers else ())
        + (
            jax.ShapeDtypeStruct(cot.shape, BF),
            jax.ShapeDtypeStruct((blocks, share, size, span), BF),
            jax.ShapeDtypeStruct((3, share, length, size), BF),
            jax.ShapeDtypeStruct((share * size, length), F32),
            jax.ShapeDtypeStruct((share, 1, length), F32),
            jax.ShapeDtypeStruct((3, HEADS, halo + span, size), BF),
            jax.ShapeDtypeStruct((width, span), F32),
            jax.ShapeDtypeStruct((width, span), BF),
            jax.ShapeDtypeStruct((HEADS, 1, span), F32),
        ),
        scratch_shapes=[
            pltpu.VMEM((blocks, width, part), BF),
            pltpu.VMEM((blocks, span, width), BF),
            pltpu.VMEM((halo + span, width), BF),
            pltpu.VMEM((3, share, length, size), BF),
            pltpu.VMEM((3, HEADS, halo + span, size), BF),
            pltpu.VMEM((blocks, share, size, span), BF),
            dma((2, experts)),
            dma((2, experts)),
            dma((2 * blocks,)),
            dma((blocks,)),
            dma((2,)),
            dma((6,)),
            dma((experts,)),
            dma((experts,)),
            dma((share, blocks)),
            dma((share, blocks)),
        ],
        compiler_params=pltpu.CompilerParams(
            collective_id=0, has_side_effects=True, vmem_limit_bytes=56 << 20
        ),
    )(qkv_shard, out_shard, row, short_row, cot, gain, bias, shifts, key_ids, query_ids)
    if gathers:
        return results[0], results[1].reshape(-1, out_shard.shape[1]), results[2:]
    return qkv_shard, full_out, results


def line_sums(z, blocks, up_held, down_held, part_send, part_recv, up_sum, down_sum):
    rounds = len(up_held) - 1
    lanes = down_held[0].shape[3]

    def part_copies(r, p):
        bit = 1 << r
        mine = lax.rem(z // bit, 2)
        partner = z + bit - 2 * bit * mine
        copies = []
        for k in range((blocks >> r) // 2):
            for n, held in enumerate((up_held, down_held)):
                copies.append(
                    remote(
                        held[r].at[p, 2 * k + 1 - mine],
                        held[r + 1].at[p, k],
                        part_send.at[r, n, p, k],
                        part_recv.at[r, n, p, k],
                        {"blk": partner},
                    )
                )
        return copies

    def add_parts(r, p):
        mine = lax.rem(z // (1 << r), 2)
        for copy in part_copies(r, p):
            copy.wait_recv()
        for k in range((blocks >> r) // 2):
            up = up_held[r][p, 2 * k + mine].astype(F32) + up_held[r + 1][p, k].astype(F32)
            down = down_held[r][p, 2 * k + mine].astype(F32) + down_held[r + 1][p, k].astype(F32)
            if r + 1 < rounds:
                up_held[r + 1][p, k] = up.astype(BF)
                down_held[r + 1][p, k] = down.astype(BF)
            else:
                up_sum[p] = up
                down_sum[p * lanes : (p + 1) * lanes, :] = down.T
        if r + 1 < rounds:
            for copy in part_copies(r + 1, p):
                copy.start()

    return part_copies, add_parts


def sum_scratch(parts, blocks, depth, width, first):
    rounds = (blocks - 1).bit_length()
    lanes = 128
    dma = pltpu.SemaphoreType.DMA
    return (
        [
            pltpu.VMEM((parts, blocks >> r, depth, blocks * lanes), BF)
            for r in range(first, rounds + 1)
        ]
        + [pltpu.VMEM((parts, blocks >> r, width, lanes), BF) for r in range(first, rounds + 1)]
        + [dma((rounds, 2, parts, blocks // 2)), dma((rounds, 2, parts, blocks // 2))]
    )


def gelu_parts(hidden):
    cdf = 0.5 * (1.0 + lax.erf(hidden * 0.7071067811865476))
    density = jnp.exp(-0.5 * hidden * hidden) * 0.3989422804014327
    return hidden * cdf, cdf + hidden * density


def expert_kernel(
    experts,
    blocks,
    steps,
    rest,
    chunk,
    x_hbm,
    cot_hbm,
    *refs,
):
    ups, refs = refs[:blocks], refs[blocks:]
    downs, refs = refs[:blocks], refs[blocks:]
    up_shifts, refs = refs[:blocks], refs[blocks:]
    (
        down_shift_ref,
        centroid_ref,
        back_grad,
        produced,
        up_sum,
        down_sum,
        up_rest,
        down_rest,
        up_shift_out,
        down_shift_out,
        x_buf,
        low_buf,
        xt_ref,
        gt_ref,
        out_acc,
        grad_acc,
        gate_ref,
        x_send,
        x_recv,
        back_send,
        back_recv,
        local_sem,
        *refs,
    ) = refs
    rounds = (blocks - 1).bit_length()
    up_held, down_held = refs[: rounds + 1], refs[rounds + 1 : 2 * rounds + 2]
    part_send, part_recv = refs[2 * rounds + 2 :]
    step = pl.program_id(0)
    me, z = lax.axis_index("expert"), lax.axis_index("blk")
    capacity, width = x_buf.shape[1:]
    rows = experts * capacity
    lanes = 128

    def x_copy(d):
        target = lax.rem(me + d, experts)
        return pltpu.make_async_remote_copy(
            src_ref=x_hbm.at[target],
            dst_ref=x_buf.at[me],
            send_sem=x_send.at[d],
            recv_sem=x_recv.at[d],
            device_id={"expert": target},
            device_id_type=MESH,
        )

    def back_copy(d):
        target = lax.rem(me + d, experts)
        return remote(
            low_buf.at[target],
            back_grad.at[me],
            back_send.at[d],
            back_recv.at[d],
            {"expert": target},
        )

    back_local = pltpu.make_async_copy(low_buf.at[me], back_grad.at[me], local_sem.at[0])
    out_copy = pltpu.make_async_copy(x_buf, produced, local_sem.at[1])

    part_copies, add_parts = line_sums(
        z, blocks, up_held, down_held, part_send, part_recv, up_sum, down_sum
    )
    cot_copy = pltpu.make_async_copy(cot_hbm, low_buf, local_sem.at[2])
    own_copy = pltpu.make_async_copy(x_hbm.at[me], x_buf.at[me], local_sem.at[3])
    x_flat, low_flat = x_buf.reshape(rows, width), low_buf.reshape(rows, width)

    @pl.when(step == 0)
    def _():
        barrier = pltpu.get_barrier_semaphore()
        for d in range(1, experts):
            pl.semaphore_signal(
                barrier, inc=1, device_id={"expert": lax.rem(me + d, experts)}, device_id_type=MESH
            )
        for r in range(rounds):
            bit = 1 << r
            partner = z + bit - 2 * bit * lax.rem(z // bit, 2)
            pl.semaphore_signal(barrier, inc=1, device_id={"blk": partner}, device_id_type=MESH)
        cot_copy.start()
        own_copy.start()
        pl.semaphore_wait(barrier, experts - 1 + rounds)
        for d in range(1, experts):
            x_copy(d).start()
        out_acc[...] = jnp.zeros_like(out_acc)
        grad_acc[...] = jnp.zeros_like(grad_acc)
        cot_copy.wait()
        own_copy.wait()
        for d in range(1, experts):
            x_copy(d).wait_recv()
        for lo in range(0, rows, chunk):
            x = x_flat[lo : lo + chunk]
            logit = jnp.sum(x.astype(F32) * centroid_ref[...], axis=1, keepdims=True)
            gate = 1.0 / (1.0 + jnp.exp(-logit))
            gate_ref[lo : lo + chunk] = gate
            low = (low_flat[lo : lo + chunk].astype(F32) * gate).astype(BF)
            low_flat[lo : lo + chunk] = low
            xt_ref[:, lo : lo + chunk] = x.T
            gt_ref[:, lo : lo + chunk] = low.T
            part = jnp.sum(low.astype(F32), axis=0, keepdims=True)
            if lo:
                down_shift_out[...] += part
            else:
                down_shift_out[...] = part

    up = jnp.concatenate([ref[...] for ref in ups], axis=1)
    down = jnp.concatenate([ref[...] for ref in downs], axis=0)
    up_shift = jnp.concatenate([ref[...] for ref in up_shifts], axis=1)
    totals = None
    for lo in range(0, rows, chunk):
        x = x_flat[lo : lo + chunk]
        low = low_flat[lo : lo + chunk]
        hidden = dot_nn(x, up) + up_shift
        active, slope = gelu_parts(hidden)
        active = active.astype(BF)
        grad_low = (dot_nt(low, down) * slope).astype(BF)
        out_acc[lo : lo + chunk] += dot_nn(active, down)
        grad_acc[lo : lo + chunk] += dot_nt(grad_low, up)
        parts = (
            dot_nn(xt_ref[:, lo : lo + chunk], grad_low),
            dot_nn(gt_ref[:, lo : lo + chunk], active),
            jnp.sum(grad_low.astype(F32), axis=0, keepdims=True),
        )
        totals = parts if totals is None else tuple(a + b for a, b in zip(totals, parts))
    up_total, down_total, shift_total = totals
    up_total = up_total.astype(BF)
    depth = width // blocks
    keep = steps - rest
    for j in range(blocks):
        up_shift_out[j] = shift_total[:, j * lanes : (j + 1) * lanes]

    def store(up_target, down_target):
        for j in range(blocks):
            up_target[j] = up_total[j * depth : (j + 1) * depth]
            down_target[j] = down_total[:, j * lanes : (j + 1) * lanes].astype(BF)

    @pl.when(step < keep)
    def _():
        store(up_held[0].at[step], down_held[0].at[step])
        for copy in part_copies(0, step):
            copy.start()

    @pl.when(step >= keep)
    def _():
        store(up_rest.at[0], down_rest.at[0])

    tasks = sorted(
        ((r, p) for p in range(keep) for r in range(rounds)), key=lambda task: (sum(task), task[0])
    )
    early = [[] for _ in range(steps)]
    for turn, task in enumerate(tasks):
        at = 2 * (task[1] + 1) + 2 * task[0]
        if at < steps - 1:
            early[at].append(task)
    for at in range(steps):
        if early[at]:

            @pl.when(step == at)
            def _(at=at):
                for r, p in early[at]:
                    add_parts(r, p)

    @pl.when(step == steps - 1)
    def _():
        for d in range(1, experts):
            x_copy(d).wait_send()
        for lo in range(0, rows, chunk):
            gate = gate_ref[lo : lo + chunk]
            out = (out_acc[lo : lo + chunk] + down_shift_ref[...]).astype(BF)
            inner = jnp.sum(
                low_flat[lo : lo + chunk].astype(F32) * out.astype(F32), axis=1, keepdims=True
            )
            x_flat[lo : lo + chunk] = out
            low_flat[lo : lo + chunk] = (
                grad_acc[lo : lo + chunk] + inner * (1.0 - gate) * centroid_ref[...]
            ).astype(BF)
        back_local.start()
        for d in range(1, experts):
            back_copy(d).start()
        out_copy.start()
        for r, p in tasks:
            if all((r, p) not in done for done in early):
                add_parts(r, p)
        back_local.wait()
        out_copy.wait()
        for d in range(1, experts):
            back_copy(d).wait()
        for p in range(keep):
            for r in range(rounds):
                for copy in part_copies(r, p):
                    copy.wait_send()


def run_expert(x, cot, up_weight, down_weight, up_shift, down_shift, centroid, blocks):
    experts, capacity, width = x.shape
    rows = experts * capacity
    hidden = up_weight.shape[1]
    lanes = 128
    steps = hidden // blocks // lanes
    rounds = (blocks - 1).bit_length()
    chunk = min(512, rows)
    depth = width // blocks
    rest = steps // 3
    keep = steps - rest
    any_spec = pl.BlockSpec(memory_space=pl.ANY)

    def once(shape):
        return pl.BlockSpec(shape, lambda f: (0,) * len(shape), pipeline_mode=pl.Buffered(1))

    return pl.pallas_call(
        functools.partial(expert_kernel, experts, blocks, steps, rest, chunk),
        grid=(steps,),
        in_specs=[any_spec] * 2
        + [pl.BlockSpec((width, lanes), lambda f, j=j: (0, j * steps + f)) for j in range(blocks)]
        + [pl.BlockSpec((lanes, width), lambda f, j=j: (j * steps + f, 0)) for j in range(blocks)]
        + [pl.BlockSpec((1, lanes), lambda f, j=j: (0, j * steps + f)) for j in range(blocks)]
        + [once((1, width))] * 2,
        out_specs=(
            any_spec,
            any_spec,
            once((keep, depth, blocks * lanes)),
            once((keep * lanes, width)),
            pl.BlockSpec(
                (1, blocks, depth, blocks * lanes), lambda f: (jnp.maximum(f - keep, 0), 0, 0, 0)
            ),
            pl.BlockSpec(
                (1, blocks, width, lanes), lambda f: (jnp.maximum(f - keep, 0), 0, 0, 0)
            ),
            pl.BlockSpec((blocks, 1, lanes), lambda f: (0, 0, f)),
            once((1, width)),
        ),
        out_shape=(
            jax.ShapeDtypeStruct(x.shape, BF),
            jax.ShapeDtypeStruct(x.shape, BF),
            jax.ShapeDtypeStruct((keep, depth, blocks * lanes), F32),
            jax.ShapeDtypeStruct((keep * lanes, width), F32),
            jax.ShapeDtypeStruct((rest, blocks, depth, blocks * lanes), BF),
            jax.ShapeDtypeStruct((rest, blocks, width, lanes), BF),
            jax.ShapeDtypeStruct((blocks, 1, hidden // blocks), F32),
            jax.ShapeDtypeStruct((1, width), F32),
        ),
        scratch_shapes=[
            pltpu.VMEM(x.shape, BF),
            pltpu.VMEM(x.shape, BF),
            pltpu.VMEM((width, rows), BF),
            pltpu.VMEM((width, rows), BF),
            pltpu.VMEM((rows, width), F32),
            pltpu.VMEM((rows, width), F32),
            pltpu.VMEM((rows, 1), F32),
            pltpu.SemaphoreType.DMA((experts,)),
            pltpu.SemaphoreType.DMA((experts,)),
            pltpu.SemaphoreType.DMA((experts,)),
            pltpu.SemaphoreType.DMA((experts,)),
            pltpu.SemaphoreType.DMA((4,)),
        ]
        + sum_scratch(keep, blocks, depth, width, 0),
        compiler_params=pltpu.CompilerParams(
            collective_id=1, has_side_effects=True, vmem_limit_bytes=62 << 20
        ),
        cost_estimate=pl.CostEstimate(
            flops=12 * rows * width * hidden, bytes_accessed=40 << 20, transcendentals=0
        ),
    )(
        x,
        cot,
        *([up_weight] * blocks),
        *([down_weight] * blocks),
        *([up_shift] * blocks),
        down_shift,
        centroid,
    )


def long_back_head(query, key, value, grad_ref, wide_ref, total_ref, out_ref, head, key_acc, value_acc):
    scale = query.shape[1] ** (-0.5)
    query = scaled(query)
    key_t = key.T
    count, _, _, block = grad_ref.shape
    visible = causal(block, block, 0)
    key_acc[...] = jnp.zeros_like(key_acc)
    value_acc[...] = jnp.zeros_like(value_acc)
    for i in range(count):
        lo, hi = i * block, (i + 1) * block
        own = query[lo:hi]
        grad_t = grad_ref[i, head]
        grad = grad_t.T
        delta = jnp.sum(grad_t.astype(F32) * wide_ref[:, lo:hi], axis=0, keepdims=True)
        total = total_ref[0, :, lo:hi]
        query_grad = None
        for start, stop in ((lo, hi), (0, lo)):
            if start == stop:
                continue
            weights = jnp.exp(dot_nt(key[start:stop], own) - total)
            if start == lo:
                weights = jnp.where(visible, weights, 0.0)
            scores = weights * (dot_nt(value[start:stop], grad) - delta)
            scores_low = scores.astype(BF)
            value_acc[start:stop] += dot_nn(weights.astype(BF), grad)
            key_acc[start:stop] += dot_nn(scores_low, own)
            part = dot_nn(key_t[:, start:stop], scores_low)
            query_grad = part if query_grad is None else query_grad + part
        out_ref[i, 0, head] = (query_grad * scale).astype(BF)
    key_grad = key_acc[...].T.astype(BF)
    value_grad = value_acc[...].T.astype(BF)
    for i in range(count):
        out_ref[i, 1, head] = key_grad[:, i * block : (i + 1) * block]
        out_ref[i, 2, head] = value_grad[:, i * block : (i + 1) * block]


def short_back_head(
    query, key, value, grad_t, wide_ref, total_ref, key_ids, query_ids, key_acc, value_acc, query_out, block
):
    scale = query.shape[1] ** (-0.5)
    query = scaled(query)
    key_t = key.T
    extent, span = query.shape[0], query_ids.shape[1]
    halo = extent - span
    key_acc[0:extent] = jnp.zeros((extent, key_acc.shape[1]), F32)
    value_acc[0:extent] = jnp.zeros((extent, key_acc.shape[1]), F32)
    for i in range(span // block):
        lo, hi = i * block, (i + 1) * block
        visible = short_visible(key_ids[...], query_ids[...], i, block, halo)
        own = query[lo + halo : hi + halo]
        part_t = grad_t[:, lo:hi]
        grad = part_t.T
        delta = jnp.sum(part_t.astype(F32) * wide_ref[:, lo:hi], axis=0, keepdims=True)
        scores = dot_nt(key[lo : hi + halo], own)
        weights = jnp.exp(jnp.where(visible, scores, NEGATIVE) - total_ref[0, :, lo:hi])
        scores = weights * (dot_nt(value[lo : hi + halo], grad) - delta)
        scores_low = scores.astype(BF)
        value_acc[lo : hi + halo] += dot_nn(weights.astype(BF), grad)
        key_acc[lo : hi + halo] += dot_nn(scores_low, own)
        part = dot_nn(key_t[:, lo : hi + halo], scores_low)
        query_out[:, lo:hi] = (part * scale).astype(BF)
    return key_acc[0:extent].T, value_acc[0:extent].T


def tail_kernel(
    experts,
    blocks,
    heads,
    lead,
    rest,
    back_grad,
    slot_ref,
    normal_ref,
    scale_ref,
    cot_ref,
    gain_ref,
    attended_ref,
    out_weight,
    long_qkv,
    long_wide,
    long_total,
    short_qkv,
    short_wide,
    short_total,
    key_ids,
    query_ids,
    produced,
    up_rest,
    down_rest,
    shift_ref,
    back_out,
    long_back,
    halo_in,
    grad_middle,
    out_term,
    sums_ref,
    query_out,
    own_out,
    up_sum,
    down_sum,
    shift_sum,
    grad_low,
    long_stage,
    short_grad,
    long_grad,
    back_stage,
    halo_stage,
    shift_in,
    key_acc,
    value_acc,
    out_send,
    out_recv,
    grad_send,
    grad_recv,
    back_send,
    back_recv,
    halo_send,
    halo_recv,
    shift_send,
    shift_recv,
    local_sem,
    *refs,
):
    rounds = (blocks - 1).bit_length()
    up_held = (up_rest,) + refs[:rounds]
    down_held = (down_rest,) + refs[rounds : 2 * rounds]
    part_send, part_recv = refs[2 * rounds :]
    step = pl.program_id(0)
    me, z = lax.axis_index("expert"), lax.axis_index("blk")
    share, size, span = long_stage.shape[1:]
    width = out_weight.shape[0]
    count = slot_ref.shape[0]
    halo = halo_stage.shape[3]
    chunk = min(256, span)
    part_copies, add_parts = line_sums(
        z, blocks, up_held, down_held, part_send, part_recv, up_sum, down_sum
    )
    line = [lax.rem(z + d, blocks) for d in range(blocks)]

    def out_copy(d):
        target = lax.rem(me + d, experts)
        return remote(
            produced.at[target], back_out.at[me], out_send.at[d], out_recv.at[d], {"expert": target}
        )

    def grad_copy(d):
        return remote(
            long_stage.at[line[d]], long_grad.at[z], grad_send.at[d], grad_recv.at[d], {"blk": line[d]}
        )

    def back_copy(head, d):
        return remote(
            back_stage.at[line[d], :, head],
            long_back.at[z, :, head],
            back_send.at[head, d],
            back_recv.at[head, d],
            {"blk": line[d]},
        )

    def back_local(head):
        return pltpu.make_async_copy(
            back_stage.at[z, :, head], long_back.at[z, :, head], back_send.at[head, 0]
        )

    def shift_copy(d):
        return remote(
            shift_ref.at[line[d]], shift_in.at[d], shift_send.at[d], shift_recv.at[d], {"blk": line[d]}
        )

    def halo_copy(n):
        part = pl.ds(0, lead) if n == 0 else pl.ds(lead, heads - lead)
        left = lax.rem(z + blocks - 1, blocks)
        return remote(
            halo_stage.at[:, part], halo_in.at[:, part], halo_send.at[n], halo_recv.at[n], {"blk": left}
        )

    def halo_local(n):
        part = pl.ds(0, lead) if n == 0 else pl.ds(lead, heads - lead)
        return pltpu.make_async_copy(halo_stage.at[:, part], halo_in.at[:, part], halo_recv.at[n])

    own_out_copy = pltpu.make_async_copy(produced.at[me], back_out.at[me], local_sem.at[0])

    def send_halo(n):
        @pl.when(z > 0)
        def _():
            halo_copy(n).start()

        @pl.when(z == blocks - 1)
        def _():
            halo_local(n).start()

    @pl.when(step == 0)
    def _():
        greet(experts, blocks)
        for copy in part_copies(0, 0):
            copy.start()
        for d in range(1, blocks):
            shift_copy(d).start()
        own_out_copy.start()
        for d in range(1, experts):
            out_copy(d).start()
        spare = blocks * share - heads
        flat_stage = long_stage.reshape(blocks * share, size, span)
        if spare:
            flat_stage[heads:] = jnp.zeros((spare, size, span), BF)
        slot_line = lax.broadcasted_iota(jnp.int32, (chunk, back_grad.shape[0]), 1)
        sums = None
        for lo in range(0, count, chunk):
            hi = lo + chunk
            chosen = (slot_ref[lo:hi] == slot_line).astype(F32).astype(BF)
            upstream = dot_nn(chosen, back_grad[...])
            normal = normal_ref[lo:hi]
            inner, gain_part, bias_part = norm_back(upstream, normal, scale_ref[lo:hi], gain_ref[...])
            middle = cot_ref[lo:hi].astype(F32) + inner
            grad_middle[lo:hi] = middle
            low = middle.astype(BF)
            grad_low[lo:hi] = low
            part = (gain_part, bias_part, jnp.sum(middle, axis=0))
            sums = part if sums is None else tuple(a + b for a, b in zip(sums, part))
            grad_t = dot_nt(out_weight[...], low).astype(BF).reshape(heads, size, chunk)
            if lo < span:
                flat_stage[:heads, :, lo:hi] = grad_t
            else:
                short_grad[:, :, lo - span : hi - span] = grad_t
            if hi == span:
                for d in range(1, blocks):
                    grad_copy(d).start()
        sums_ref[...] = jnp.zeros_like(sums_ref)
        for n, part in enumerate(sums):
            sums_ref[n] = part
        out_term[...] = dot_nn(attended_ref[...], grad_low[...]).astype(BF)

    first_long = lead + 1
    is_long = (step >= first_long) & (step < first_long + share)

    @pl.when((step > 0) & jnp.logical_not(is_long))
    def _():
        head = step - 1 - jnp.where(step >= first_long, share, 0)
        query, key, value = (short_qkv[kind, 0] for kind in range(3))
        grads = short_back_head(
            query,
            key,
            value,
            short_grad[head],
            short_wide,
            short_total,
            key_ids,
            query_ids,
            key_acc,
            value_acc,
            query_out,
            min(SHORT, span),
        )
        for n, grad in enumerate(grads):
            halo_stage[n, head] = grad[:, :halo].astype(BF)
            own_out[n] = grad[:, halo:]

    @pl.when(step == lead)
    def _():
        send_halo(0)

    @pl.when(step == first_long)
    def _():
        for d in range(1, blocks):
            grad_copy(d).wait_recv()
        long_grad[z] = long_stage[z]
        add_parts(0, 0)
        for p in range(1, rest):
            for copy in part_copies(0, p):
                copy.start()

    @pl.when(is_long)
    def _():
        head = step - first_long
        query, key, value = (long_qkv[kind, 0] for kind in range(3))
        long_back_head(
            query, key, value, long_grad, long_wide, long_total, back_stage, head, key_acc, value_acc
        )
        back_local(head).start()
        for d in range(1, blocks):
            back_copy(head, d).start()

    tasks = sorted(
        ((r, p) for p in range(rest) for r in range(rounds)), key=lambda task: (sum(task), task[0])
    )[1:]

    @pl.when(step == first_long + share)
    def _():
        for r, p in tasks[:-1]:
            add_parts(r, p)

    @pl.when(step == heads + share)
    def _():
        send_halo(1)
        if tasks:
            add_parts(*tasks[-1])
        for d in range(1, blocks):
            shift_copy(d).wait()
        total = shift_ref[z]
        for d in range(1, blocks):
            total = total + shift_in[d]
        shift_sum[...] = total
        own_out_copy.wait()
        for d in range(1, experts):
            out_copy(d).wait()
        for d in range(1, blocks):
            grad_copy(d).wait_send()
        for head in range(share):
            back_local(head).wait()
            for d in range(1, blocks):
                back_copy(head, d).wait()
        for p in range(rest):
            for r in range(rounds):
                for copy in part_copies(r, p):
                    copy.wait_send()
        for n in range(2):

            @pl.when(z > 0)
            def _(n=n):
                halo_copy(n).wait_send()

            @pl.when(z < blocks - 1)
            def _(n=n):
                halo_copy(n).wait_recv()

            @pl.when(z == blocks - 1)
            def _(n=n):
                halo_local(n).wait()


def run_tail(
    back_grad,
    slot_of,
    normal,
    scale,
    cot,
    gain,
    attended_t,
    out_weight,
    long_parts,
    short_parts,
    key_ids,
    query_ids,
    produced,
    up_rest,
    down_rest,
    shifts,
    blocks,
):
    experts = produced.shape[0]
    slots, width = back_grad.shape
    count = slot_of.shape[0]
    long_qkv, long_wide, long_total = long_parts
    short_qkv, short_wide, short_total = short_parts
    _, share, length, size = long_qkv.shape
    extent, span = short_qkv.shape[2], query_ids.shape[1]
    halo = extent - span
    heads = HEADS
    lead = heads // 2
    rest, _, depth, _ = up_rest.shape
    any_spec = pl.BlockSpec(memory_space=pl.ANY)
    dma = pltpu.SemaphoreType.DMA

    def whole(shape):
        return pl.BlockSpec(shape, lambda f: (0,) * len(shape), pipeline_mode=pl.Buffered(1))

    def short_at(f):
        return jnp.where(f <= lead, jnp.maximum(f - 1, 0), jnp.maximum(f - 1 - share, lead - 1))

    def long_at(f):
        return jnp.clip(f - 1 - lead, 0, share - 1)

    return pl.pallas_call(
        functools.partial(tail_kernel, experts, blocks, heads, lead, rest),
        grid=(1 + heads + share,),
        in_specs=[
            whole(back_grad.shape),
            whole(slot_of.shape),
            whole(normal.shape),
            whole(scale.shape),
            whole(cot.shape),
            whole(gain.shape),
            whole(attended_t.shape),
            whole(out_weight.shape),
            pl.BlockSpec((3, 1, length, size), lambda f: (0, long_at(f), 0, 0)),
            pl.BlockSpec((size, length), lambda f: (long_at(f), 0)),
            pl.BlockSpec((1, 1, length), lambda f: (long_at(f), 0, 0)),
            pl.BlockSpec((3, 1, extent, size), lambda f: (0, short_at(f), 0, 0)),
            pl.BlockSpec((size, span), lambda f: (short_at(f), 0)),
            pl.BlockSpec((1, 1, span), lambda f: (short_at(f), 0, 0)),
            whole(key_ids.shape),
            whole(query_ids.shape),
            any_spec,
            whole(up_rest.shape),
            whole(down_rest.shape),
            whole(shifts.shape),
        ],
        out_specs=(
            any_spec,
            any_spec,
            any_spec,
            whole((count, width)),
            whole((width, width)),
            whole((8, width)),
            pl.BlockSpec((size, span), lambda f: (short_at(f), 0)),
            pl.BlockSpec((2, size, span), lambda f: (0, short_at(f), 0)),
            whole((rest, depth, up_rest.shape[3])),
            whole((rest * 128, width)),
            whole(shifts.shape[1:]),
        ),
        out_shape=(
            jax.ShapeDtypeStruct(produced.shape, BF),
            jax.ShapeDtypeStruct((blocks, 3, share, size, span), BF),
            jax.ShapeDtypeStruct((2, heads, size, halo), BF),
            jax.ShapeDtypeStruct((count, width), F32),
            jax.ShapeDtypeStruct((width, width), BF),
            jax.ShapeDtypeStruct((8, width), F32),
            jax.ShapeDtypeStruct((width, span), BF),
            jax.ShapeDtypeStruct((2, width, span), F32),
            jax.ShapeDtypeStruct((rest, depth, up_rest.shape[3]), F32),
            jax.ShapeDtypeStruct((rest * 128, width), F32),
            jax.ShapeDtypeStruct(shifts.shape[1:], F32),
        ),
        scratch_shapes=[
            pltpu.VMEM((count, width), BF),
            pltpu.VMEM((blocks, share, size, span), BF),
            pltpu.VMEM((heads, size, span), BF),
            pltpu.VMEM((blocks, share, size, span), BF),
            pltpu.VMEM((blocks, 3, share, size, span), BF),
            pltpu.VMEM((2, heads, size, halo), BF),
            pltpu.VMEM(shifts.shape, F32),
            pltpu.VMEM((length, size), F32),
            pltpu.VMEM((length, size), F32),
            dma((experts,)),
            dma((experts,)),
            dma((blocks,)),
            dma((blocks,)),
            dma((share, blocks)),
            dma((share, blocks)),
            dma((2,)),
            dma((2,)),
            dma((blocks,)),
            dma((blocks,)),
            dma((1,)),
        ]
        + sum_scratch(rest, blocks, depth, width, 1),
        compiler_params=pltpu.CompilerParams(
            collective_id=3, has_side_effects=True, vmem_limit_bytes=60 << 20
        ),
    )(
        back_grad,
        slot_of,
        normal,
        scale,
        cot,
        gain,
        attended_t,
        out_weight,
        *long_parts,
        *short_parts,
        key_ids,
        query_ids,
        produced,
        up_rest,
        down_rest,
        shifts,
    )


def reduce_kernel(experts, blocks, parts, *refs):
    arrays = 1 + max(piece[0] for part in parts for piece in part)
    ins, refs = refs[:arrays], refs[arrays:]
    outs, refs = refs[:arrays], refs[arrays:]
    number = len(parts)
    from_mate, refs = refs[:number], refs[number:]
    pair_sum, refs = refs[:number], refs[number:]
    from_chips, refs = refs[:number], refs[number:]
    group_sum, refs = refs[:number], refs[number:]
    from_line, refs = refs[:number], refs[number:]
    whole, refs = refs[:number], refs[number:]
    mate_send, mate_recv, chip_send, chip_recv, line_send, line_recv, back_send, back_recv = refs
    rounds = (blocks - 1).bit_length()
    chips = experts // 2
    me, z = lax.axis_index("expert"), lax.axis_index("blk")
    core = lax.rem(me, 2)
    chip = me // 2
    mate = me + 1 - 2 * core

    def line_partner(r):
        bit = 1 << r
        return z + bit - 2 * bit * lax.rem(z // bit, 2)

    barrier = pltpu.get_barrier_semaphore()
    pl.semaphore_signal(barrier, inc=1, device_id={"expert": mate}, device_id_type=MESH)
    for d in range(1, chips):
        peer = lax.rem(me + 2 * d, experts)
        pl.semaphore_signal(barrier, inc=1, device_id={"expert": peer}, device_id_type=MESH)
    for r in range(rounds):
        pl.semaphore_signal(
            barrier, inc=1, device_id={"blk": line_partner(r)}, device_id_type=MESH
        )
    pl.semaphore_wait(barrier, chips + rounds)

    def send(source, target, send_sem, recv_sem, device):
        return pltpu.make_async_remote_copy(
            src_ref=source,
            dst_ref=target,
            send_sem=send_sem,
            recv_sem=recv_sem,
            device_id=device,
            device_id_type=MESH,
        )

    def mate_copies(p):
        at = 0
        copies = []
        for n, (array, first, columns) in enumerate(parts[p]):
            copies.append(
                send(
                    ins[array].at[:, 1 - core, :, pl.ds(first, columns)],
                    from_mate[p].at[:, :, pl.ds(at, columns)],
                    mate_send.at[p, n],
                    mate_recv.at[p, n],
                    {"expert": mate},
                )
            )
            at += columns
        return copies

    def chip_copies(p):
        copies = []
        for d in range(1, chips):
            there = lax.rem(chip + d, chips)
            copies.append(
                send(
                    pair_sum[p].at[there],
                    from_chips[p].at[d - 1],
                    chip_send.at[p, d],
                    chip_recv.at[p, d],
                    {"expert": 2 * there + core},
                )
            )
        return copies

    def segment(p, r):
        groups = whole[p].shape[0]
        start = 0
        for n in range(r):
            start = start + lax.rem(z // (1 << n), 2) * (groups >> (n + 1))
        return start, groups >> r

    def line_copy(p, r):
        start, groups = segment(p, r)
        half = groups // 2
        mine = lax.rem(z // (1 << r), 2)
        return send(
            group_sum[p].at[pl.ds(start + (1 - mine) * half, half)],
            from_line[p].at[r, pl.ds(0, half)],
            line_send.at[p, r],
            line_recv.at[p, r],
            {"blk": line_partner(r)},
        )

    def back_copy(p, r):
        start, groups = segment(p, r + 1)
        return send(
            whole[p].at[pl.ds(start, groups)],
            whole[p].at[pl.ds(start, groups)],
            back_send.at[p, r],
            back_recv.at[p, r],
            {"blk": line_partner(r)},
        )

    def back_arrival(p, r):
        start, groups = segment(p, r)
        mine = lax.rem(z // (1 << r), 2)
        start = start + (1 - mine) * (groups // 2)
        return send(
            whole[p].at[pl.ds(start, groups // 2)],
            whole[p].at[pl.ds(start, groups // 2)],
            back_send.at[p, r],
            back_recv.at[p, r],
            {"blk": line_partner(r)},
        )

    def run(p, stage):
        if stage == 0:
            for copy in mate_copies(p):
                copy.start()
        elif stage == 1:
            for copy in mate_copies(p):
                copy.wait_recv()
            for k in range(chips):
                at = 0
                for array, first, columns in parts[p]:
                    own = ins[array][k, core, :, first : first + columns]
                    came = from_mate[p][k, :, at : at + columns]
                    pair_sum[p][k, :, at : at + columns] = (
                        own.astype(F32) + came.astype(F32)
                    ).astype(BF)
                    at += columns
            for copy in chip_copies(p):
                copy.start()
        elif stage == 2:
            for copy in chip_copies(p):
                copy.wait_recv()
            total = pair_sum[p][chip].astype(F32)
            for d in range(1, chips):
                total = total + from_chips[p][d - 1].astype(F32)
            low = total.astype(BF)
            used = low.shape[1] // 128
            for g in range(group_sum[p].shape[0]):
                if g < used:
                    group_sum[p][g] = low[:, g * 128 : (g + 1) * 128]
                else:
                    group_sum[p][g] = jnp.zeros(group_sum[p].shape[1:], BF)
            line_copy(p, 0).start()
        elif stage < 2 + rounds:
            add_line(p, stage - 3)
            line_copy(p, stage - 2).start()
        elif stage == 2 + rounds:
            r = rounds - 1
            add_line(p, r)
            start, groups = segment(p, rounds)
            whole[p][pl.ds(start, groups)] = group_sum[p][pl.ds(start, groups)]
            back_copy(p, r).start()
        else:
            r = rounds - 1 - (stage - 3 - rounds)
            back_arrival(p, r).wait_recv()
            if r:
                back_copy(p, r - 1).start()
            else:
                at = 0
                for array, first, columns in parts[p]:
                    for c in range(0, columns, 128):
                        outs[array][:, first + c : first + c + 128] = whole[p][
                            (at + c) // 128
                        ].astype(F32)
                    at += columns

    def add_line(p, r):
        line_copy(p, r).wait_recv()
        start, groups = segment(p, r + 1)
        held = group_sum[p][pl.ds(start, groups)].astype(F32)
        group_sum[p][pl.ds(start, groups)] = (
            held + from_line[p][r, pl.ds(0, groups)].astype(F32)
        ).astype(BF)

    stages = 3 + 2 * rounds
    for turn in range(number + stages - 1):
        for p in range(number):
            if 0 <= turn - p < stages:
                run(p, turn - p)
    for p in range(number):
        for copy in mate_copies(p) + chip_copies(p):
            copy.wait_send()
        for r in range(rounds):
            line_copy(p, r).wait_send()
            back_copy(p, r).wait_send()


def reduce_all(arrays, parts, experts, blocks):
    rows = arrays[0].shape[0] // experts
    chips = experts // 2
    rounds = (blocks - 1).bit_length()
    number = len(parts)
    widths = [sum(piece[2] for piece in part) for part in parts]
    groups = [-(-width // 128 // blocks) * blocks for width in widths]
    dma = pltpu.SemaphoreType.DMA
    return pl.pallas_call(
        functools.partial(reduce_kernel, experts, blocks, parts),
        in_specs=[pl.BlockSpec(memory_space=pltpu.VMEM)] * len(arrays),
        out_specs=tuple(pl.BlockSpec(memory_space=pltpu.VMEM) for _ in arrays),
        out_shape=tuple(jax.ShapeDtypeStruct((rows, a.shape[1]), F32) for a in arrays),
        scratch_shapes=[pltpu.VMEM((chips, rows, w), BF) for w in widths]
        + [pltpu.VMEM((chips, rows, w), BF) for w in widths]
        + [pltpu.VMEM((chips - 1, rows, w), BF) for w in widths]
        + [pltpu.VMEM((g, rows, 128), BF) for g in groups]
        + [pltpu.VMEM((rounds, g // 2, rows, 128), BF) for g in groups]
        + [pltpu.VMEM((g, rows, 128), BF) for g in groups]
        + [dma((number, 3)), dma((number, 3)), dma((number, chips)), dma((number, chips))]
        + [dma((number, rounds))] * 4,
        compiler_params=pltpu.CompilerParams(
            collective_id=2, has_side_effects=True, vmem_limit_bytes=40 << 20
        ),
    )(*[a.reshape(chips, 2, rows, a.shape[1]) for a in arrays])


def on_device(
    tokens,
    doc_ids,
    routes,
    ln1_gain,
    ln1_bias,
    qkv_weight,
    qv_bias,
    out_weight,
    out_bias,
    ln2_gain,
    ln2_bias,
    centroids,
    up_weight,
    up_bias,
    down_weight,
    down_bias,
    cotangent,
):
    rows, span, width = tokens.shape
    heads = HEADS
    size = width // heads
    blocks = lax.axis_size("blk")
    own = lax.axis_index("blk")
    count = rows * span
    length = blocks * span
    halo = min(SHORT, span)
    share = -(-heads // blocks)
    pad_heads = share * blocks - heads

    expert_count = centroids.shape[0]

    long_at = (doc_ids[0, -1] != 0).astype(jnp.int32)

    def ordered(pair):
        first = lax.dynamic_index_in_dim(pair, long_at, 0, keepdims=False)
        second = lax.dynamic_index_in_dim(pair, 1 - long_at, 0, keepdims=False)
        return jnp.stack([first, second])

    long_tokens = lax.dynamic_index_in_dim(tokens, long_at, 0, keepdims=False)
    short_tokens = lax.dynamic_index_in_dim(tokens, 1 - long_at, 0, keepdims=False)
    token_rows = jnp.concatenate([long_tokens, short_tokens]).astype(F32)

    capacity = 2 * count // expert_count
    slots = expert_count * capacity
    route_flat = routes.reshape(count)
    onehot = route_flat[:, None] == jnp.arange(expert_count, dtype=jnp.int32)[None, :]
    ranking = jnp.cumsum(onehot.astype(jnp.int32), axis=0) - 1
    slot_of = route_flat * capacity + jnp.sum(jnp.where(onehot, ranking, 0), axis=1)
    slot_line = jnp.arange(slots, dtype=jnp.int32)

    def to_experts(flat, slot_of):
        to_slots = (slot_line[:, None] == slot_of[None, :]).astype(BF)
        return dot_nn(to_slots, flat).astype(BF).reshape(expert_count, capacity, width)

    sent_cot = to_experts(cotangent.reshape(count, width), slot_of)
    slot_of = ordered(slot_of.reshape(rows, span)).reshape(count)
    route_flat = ordered(routes.reshape(rows, span)).reshape(count)
    onehot = route_flat[:, None] == jnp.arange(expert_count, dtype=jnp.int32)[None, :]
    from_slots = (slot_of[:, None] == slot_line[None, :]).astype(BF)
    grad_low = ordered(cotangent).reshape(count, width)

    def grouped(matrix):
        lead = matrix.shape[0]
        split = matrix.reshape(lead, 3, heads, size)
        split = jnp.pad(split, ((0, 0), (0, 0), (0, pad_heads), (0, 0)))
        split = split.reshape(lead, 3, blocks, share, size).transpose(2, 0, 1, 3, 4)
        return split.reshape(blocks, lead, 3 * share * size)

    def ungrouped(matrix):
        lead = matrix.shape[0]
        split = matrix.reshape(lead, blocks, 3, share, size).transpose(0, 2, 1, 3, 4)
        return split.reshape(lead, 3, blocks * share, size)[:, :, :heads].reshape(lead, 3, width)

    short_ids = jnp.concatenate(
        [
            jnp.full((halo,), -1, jnp.int32),
            lax.dynamic_index_in_dim(doc_ids, 1 - long_at, 0, keepdims=False),
        ]
    )
    short_ids = lax.dynamic_slice_in_dim(short_ids, own * span, halo + span, 0)
    key_ids = short_ids[:, None]
    query_ids = short_ids[None, halo:]
    shifts = jnp.concatenate([qv_bias[0], jnp.zeros((width,), F32), qv_bias[1]])
    full_qkv, full_out, rest = run_front(
        grouped(qkv_weight),
        out_weight,
        long_tokens,
        short_tokens,
        sent_cot,
        ln1_gain[None],
        ln1_bias[None],
        grouped(shifts[None]),
        key_ids,
        query_ids,
        expert_count,
        blocks,
    )
    (
        received_cot,
        long_attended,
        long_qkv,
        long_wide,
        long_total,
        short_qkv,
        short_wide,
        short_low,
        short_total,
    ) = rest
    long_attended = long_attended.reshape(-1, span)[:width]
    attended_t = jnp.concatenate([long_attended, short_low], axis=1)

    middle = (
        token_rows
        + lax.dot_general(
            attended_t, full_out, (((0,), (0,)), ((), ())), preferred_element_type=F32
        )
        + out_bias
    )
    normal_two, scale_two = norm_parts(middle)
    normed_two = normal_two * ln2_gain + ln2_bias
    outgoing = to_experts(normed_two.astype(BF), slot_of)
    centroid_rows = jnp.dot(onehot.astype(BF), centroids, preferred_element_type=F32)
    gate = jax.nn.sigmoid(jnp.sum(normed_two * centroid_rows, axis=1))

    own_centroid = lax.dynamic_index_in_dim(
        centroids.astype(F32), lax.axis_index("expert"), 0, keepdims=True
    )
    back_grad, produced, up_first, down_first, up_rest, down_rest, up_shift, down_shift = run_expert(
        outgoing,
        received_cot,
        up_weight[0],
        down_weight[0],
        up_bias,
        down_bias,
        own_centroid,
        blocks,
    )
    shift_parts = jnp.concatenate([up_shift, down_shift.reshape(blocks, 1, -1)], axis=2)
    shift_parts = jnp.pad(shift_parts, ((0, 0), (0, 0), (0, -shift_parts.shape[2] % 128)))
    (
        back_out,
        long_back,
        halo_back,
        grad_middle,
        out_term,
        tail_sums,
        query_back,
        own_back,
        up_last,
        down_last,
        shift_sum,
    ) = run_tail(
        back_grad.reshape(slots, width),
        slot_of[:, None],
        normal_two,
        scale_two,
        grad_low,
        ln2_gain[None],
        attended_t,
        full_out,
        (long_qkv, long_wide, long_total),
        (short_qkv, short_wide, short_total),
        key_ids,
        query_ids,
        produced,
        up_rest,
        down_rest,
        shift_parts,
        blocks,
    )
    back_out = back_out.reshape(slots, width)
    ln2_gain_term, ln2_bias_term, out_shift_term = tail_sums[0], tail_sums[1], tail_sums[2]
    grad_out = grad_low.astype(F32)
    up_sum = jnp.concatenate([up_first, up_last], axis=0)
    up_sum = up_sum.reshape(-1, up_sum.shape[1], blocks, 128).transpose(1, 2, 0, 3)
    up_sum = up_sum.reshape(up_sum.shape[0], -1)
    down_sum = jnp.concatenate([down_first, down_last], axis=0)
    halo_back = jnp.where(own < blocks - 1, halo_back.reshape(2, width, halo).astype(F32), 0.0)
    own_back = own_back + jnp.pad(halo_back, ((0, 0), (0, 0), (span - halo, 0)))
    short_back = jnp.concatenate([query_back[None], own_back.astype(BF)], axis=0)
    short_back = jnp.pad(
        short_back.reshape(3, heads, size, span), ((0, 0), (0, pad_heads), (0, 0), (0, 0))
    )
    short_back = short_back.reshape(3, blocks, share, size, span).transpose(1, 0, 2, 3, 4)
    back_t = jnp.concatenate(
        [long_back.reshape(-1, span), short_back.reshape(-1, span)], axis=1
    )

    normal_one, scale_one = norm_parts(token_rows)
    normed_low = (normal_one * ln1_gain + ln1_bias).astype(BF)
    qkv_term = lax.dot_general(
        normed_low, back_t, (((0,), (1,)), ((), ())), preferred_element_type=F32
    )
    qv_sums = ungrouped(jnp.sum(back_t.astype(F32), axis=1)[None])[0]
    grad_normed_one = lax.dot_general(
        back_t.reshape(blocks, -1, count),
        full_qkv,
        (((0, 1), (0, 2)), ((), ())),
        preferred_element_type=F32,
    )
    inner_one, ln1_gain_term, ln1_bias_term = norm_back(
        grad_normed_one, normal_one, scale_one, ln1_gain
    )
    grad_tokens = grad_middle + inner_one

    expert_rows = dot_nn(from_slots, back_out)
    result = middle + gate[:, None] * expert_rows
    grad_logit = jnp.sum(grad_out * expert_rows, axis=1) * gate * (1.0 - gate)
    centroid_term = jnp.einsum(
        "te,td->de",
        onehot.astype(F32) * grad_logit[:, None],
        normed_two,
        precision=lax.Precision.HIGHEST,
    )

    small = jnp.stack(
        [
            qv_sums[0],
            qv_sums[2],
            out_shift_term,
            ln1_gain_term,
            ln1_bias_term,
            ln2_gain_term,
            ln2_bias_term,
        ],
        axis=1,
    )
    n_small = small.shape[1]
    small = jnp.concatenate([small, centroid_term], axis=1)
    small = jnp.pad(small, ((0, 0), (0, 128 - small.shape[1])))
    columns = qkv_term.shape[1]
    half = -(-columns // 256) * 128
    qkv_sum, out_sum, small_sum = reduce_all(
        (qkv_term.astype(BF), out_term, small.astype(BF)),
        (
            ((1, 0, width), (2, 0, 128)),
            ((0, 0, half),),
            ((0, half, columns - half),),
        ),
        expert_count,
        blocks,
    )
    centroid_sum = small_sum[:, n_small : n_small + expert_count].T
    shift_cut = up_bias.shape[1] // blocks
    up_shift_sum = shift_sum[:, :shift_cut]
    down_shift_sum = shift_sum[:, shift_cut : shift_cut + width // blocks]
    return (
        ordered(result.reshape(rows, span, width)),
        ordered(grad_tokens.reshape(rows, span, width)),
        small_sum[:, 3],
        small_sum[:, 4],
        ungrouped(qkv_sum).reshape(-1, 3 * width),
        small_sum[:, :2].T,
        out_sum,
        small_sum[:, 2],
        small_sum[:, 5],
        small_sum[:, 6],
        centroid_sum,
        up_sum[None],
        up_shift_sum,
        down_sum[None],
        down_shift_sum,
    )


def solution(mesh):
    return jax.shard_map(
        on_device,
        mesh=mesh,
        in_specs=(
            P("expert", "blk", None),
            P("expert", None),
            P("blk", "expert", None, None),
            P(),
            P(),
            P("expert", None),
            P(),
            P("expert", None),
            P(),
            P(),
            P(),
            P(),
            P("expert", None, None),
            P("expert", None),
            P("expert", None, None),
            P("expert", None),
            P("expert", "blk", None),
        ),
        out_specs=(
            P("expert", "blk", None),
            P("expert", "blk", None),
            P("expert"),
            P("expert"),
            P("expert", None),
            P(None, "expert"),
            P("expert", None),
            P("expert"),
            P("expert"),
            P("expert"),
            P(None, "expert"),
            P("expert", "blk", None),
            P("expert", "blk"),
            P("expert", "blk", None),
            P("expert", "blk"),
        ),
        check_vma=False,
    )
```

```python
import functools

import jax
import jax.numpy as jnp
from jax import lax
from jax.experimental import pallas as pl
from jax.experimental.pallas import tpu as pltpu
from jax.sharding import PartitionSpec as P

HEADS = 12
SHORT = 256
NEGATIVE = -1e30
EPSILON = 1e-05
BF = jnp.bfloat16
F32 = jnp.float32


def dot_nn(a, b):
    return lax.dot_general(a, b, (((1,), (0,)), ((), ())), preferred_element_type=F32)


def dot_nt(a, b):
    return lax.dot_general(a, b, (((1,), (1,)), ((), ())), preferred_element_type=F32)


def norm_parts(values):
    average = jnp.mean(values, axis=-1, keepdims=True)
    centred = values - average
    variance = jnp.mean(centred * centred, axis=-1, keepdims=True)
    scale = lax.rsqrt(variance + EPSILON)
    return centred * scale, scale


def layer_norm(values, gain, bias):
    return norm_parts(values)[0] * gain + bias


def norm_back(upstream, normal, scale, gain):
    t = upstream * gain
    inner = (
        t
        - jnp.mean(t, axis=-1, keepdims=True)
        - normal * jnp.mean(t * normal, axis=-1, keepdims=True)
    )
    return inner * scale, jnp.sum(upstream * normal, axis=0), jnp.sum(upstream, axis=0)


def causal(rows, columns, shift):
    row = lax.broadcasted_iota(jnp.int32, (rows, columns), 0)
    column = lax.broadcasted_iota(jnp.int32, (rows, columns), 1)
    return row <= column + shift


def norm_low(values, gain, bias):
    return layer_norm(values.astype(F32), gain, bias).astype(BF)


def scaled(query):
    return (query.astype(F32) * query.shape[-1] ** (-0.5)).astype(BF)


def short_visible(key_ids, query_ids, i, block, halo):
    lo = i * block
    same = key_ids[lo : lo + halo + block] == query_ids[:, lo : lo + block]
    return same & causal(halo + block, block, halo)


MESH = pl.DeviceIdType.MESH


def remote(source, target, send_sem, recv_sem, device):
    return pltpu.make_async_remote_copy(
        src_ref=source,
        dst_ref=target,
        send_sem=send_sem,
        recv_sem=recv_sem,
        device_id=device,
        device_id_type=MESH,
    )


def across(place, mask, count):
    bit = 1
    while bit < count:
        place_bit, mask_bit = lax.rem(place // bit, 2), lax.rem(mask // bit, 2)
        place = place + bit * mask_bit * (1 - 2 * place_bit)
        bit *= 2
    return place


def greet(experts, blocks):
    me, z = lax.axis_index("expert"), lax.axis_index("blk")
    barrier = pltpu.get_barrier_semaphore()
    for d in range(1, experts):
        pl.semaphore_signal(
            barrier, inc=1, device_id={"expert": lax.rem(me + d, experts)}, device_id_type=MESH
        )
    for d in range(1, blocks):
        pl.semaphore_signal(
            barrier, inc=1, device_id={"blk": lax.rem(z + d, blocks)}, device_id_type=MESH
        )
    pl.semaphore_wait(barrier, experts + blocks - 2)


def front_kernel(
    experts,
    blocks,
    heads,
    gathers,
    block,
    short_block,
    qkv_ref,
    out_ref,
    row_ref,
    short_ref,
    cot_ref,
    route_ref,
    vectors,
    shift_ref,
    key_ids,
    query_ids,
    *refs,
):
    if gathers:
        (full_qkv, full_out), refs = refs[:2], refs[2:]
    else:
        full_qkv = qkv_ref
    (
        received_cot,
        slot_out,
        attended,
        long_qkv,
        long_wide,
        long_total,
        short_qkv,
        short_wide,
        short_low,
        short_total,
        weights,
        rows_buf,
        short_buf,
        long_store,
        short_store,
        low_stage,
        cot_stage,
        shard_send,
        shard_recv,
        row_send,
        row_recv,
        edge_sem,
        local_sem,
        cot_send,
        cot_recv,
        low_send,
        low_recv,
    ) = refs
    me, z = lax.axis_index("expert"), lax.axis_index("blk")
    step = pl.program_id(0)
    mate = me + 1 - 2 * lax.rem(me, 2)
    peers = [lax.rem(me + 2 * d, experts) for d in range(1, experts // 2)]
    share, size = long_store.shape[1], long_store.shape[3]
    length = blocks * block
    span = block
    halo = short_buf.shape[0] - span
    shard_rows = qkv_ref.shape[1]

    def qkv_part(slot):
        return full_qkv.at[:, pl.ds(pl.multiple_of(slot * shard_rows, shard_rows), shard_rows)]

    def shard(n, own, slot, turn, target):
        part = (qkv_part(slot), full_out.at[slot])[n]
        source = (qkv_ref, out_ref)[n] if own else part
        return remote(
            source, part, shard_send.at[n, turn], shard_recv.at[n, slot], {"expert": target}
        )

    def row(slot, turn, target):
        return remote(
            rows_buf.at[slot],
            rows_buf.at[slot],
            row_send.at[turn],
            row_recv.at[slot],
            {"blk": target},
        )

    def own_row(turn, target):
        return remote(
            row_ref, rows_buf.at[z], row_send.at[turn], row_recv.at[z], {"blk": target}
        )

    to_right, to_left = z + 1 < blocks, z > 0
    right, left = lax.rem(z + 1, blocks), lax.rem(z + blocks - 1, blocks)
    last_rows = short_ref.at[pl.ds(span - halo, halo)]
    halo_rows = short_buf.at[pl.ds(0, halo)]
    edge = remote(last_rows, halo_rows, edge_sem.at[0], edge_sem.at[1], {"blk": right})
    no_edge = pltpu.make_async_copy(last_rows, halo_rows, edge_sem.at[1])
    local = [
        pltpu.make_async_copy(row_ref, rows_buf.at[z], local_sem.at[0]),
        pltpu.make_async_copy(short_ref, short_buf.at[pl.ds(halo, span)], local_sem.at[1]),
    ]
    own_cot = pltpu.make_async_copy(cot_stage.at[me], received_cot.at[me], local_sem.at[2])
    load_weights = pltpu.make_async_copy(full_qkv, weights, local_sem.at[3])
    own_shards = []
    sent = []
    handed = []
    if gathers:
        own_shards = [
            pltpu.make_async_copy(qkv_ref, qkv_part(me), local_sem.at[4]),
            pltpu.make_async_copy(out_ref, full_out.at[me], local_sem.at[5]),
        ]
        for n in range(2):
            for turn, peer in enumerate(peers):
                sent.append(shard(n, True, me, turn, peer))
            sent.append(shard(n, True, me, len(peers), mate))
            for turn, peer in enumerate(peers):
                handed.append(shard(n, False, peer, len(peers) + 1 + turn, mate))

    def cot_copy(d):
        target = lax.rem(me + d, experts)
        return remote(
            cot_stage.at[target],
            received_cot.at[me],
            cot_send.at[d],
            cot_recv.at[d],
            {"expert": target},
        )

    def low_copy(head, d):
        target = lax.rem(z + d, blocks)
        return remote(
            low_stage.at[target, head],
            attended.at[z, head],
            low_send.at[head, d],
            low_recv.at[head, d],
            {"blk": target},
        )

    def low_local(head):
        return pltpu.make_async_copy(
            low_stage.at[z, head], attended.at[z, head], low_send.at[head, 0]
        )

    def hand_on(k):
        @pl.when(z - k >= 0)
        def _():
            slot = jnp.maximum(z - k, 0)
            row(slot, 2 * k, right).wait_recv()

            @pl.when(to_right)
            def _():
                row(slot, 2 * k, right).start()

        @pl.when(z + k < blocks)
        def _():
            slot = jnp.minimum(z + k, blocks - 1)
            row(slot, 2 * k + 1, left).wait_recv()

            @pl.when(to_left)
            def _():
                row(slot, 2 * k + 1, left).start()

    def project(source, rows, groups, store):
        low = norm_low(source, vectors[0:1], vectors[1:2])
        for n, group in enumerate(groups):
            part = (dot_nn(low, weights[group]) + shift_ref[group]).astype(BF)
            for kind in range(3):
                for head in range(share):
                    at = (kind * share + head) * size
                    if n * share + head < store.shape[1]:
                        store[kind, n * share + head, rows] = part[:, at : at + size]

    def sort_cot():
        capacity, width = cot_stage.shape[1:]
        count = cot_ref.shape[0]
        lines = -(-experts // 8) * 8
        expert_line = lax.broadcasted_iota(jnp.int32, (lines, count), 0)
        named = (route_ref[...] == expert_line).astype(F32)
        upto = lax.broadcasted_iota(jnp.int32, (count, count), 0) <= lax.broadcasted_iota(
            jnp.int32, (count, count), 1
        )
        ranks = dot_nn(named.astype(BF), upto.astype(F32).astype(BF))
        slots = named * (ranks - 1.0 + (expert_line * capacity).astype(F32))
        slots = jnp.sum(slots, axis=0, keepdims=True).astype(jnp.int32)
        slot_out[...] = slots
        flat = cot_stage.reshape(experts * capacity, width)
        block_rows = min(512, experts * capacity)

        @pl.loop(0, experts * capacity // block_rows)
        def _(turn):
            first = pl.multiple_of(turn * block_rows, block_rows)
            line = lax.broadcasted_iota(jnp.int32, (block_rows, count), 0) + first
            chosen = (line == slots).astype(F32).astype(BF)
            flat[pl.ds(first, block_rows)] = dot_nn(chosen, cot_ref[...]).astype(BF)

    @pl.when(step == 0)
    def _():
        for copy in local + own_shards:
            copy.start()
        greet(experts, blocks)

        @pl.when(to_right)
        def _():
            own_row(0, right).start()
            edge.start()

        @pl.when(to_left)
        def _():
            own_row(1, left).start()

        @pl.when(jnp.logical_not(to_left))
        def _():
            no_edge.start()

        for copy in sent:
            copy.start()
        sort_cot()
        hand_on(1)
        for copy in handed:
            copy.wait_recv()
            copy.start()
        if gathers:
            for turn in range(experts // 2):
                for n in range(2):
                    shard(n, False, lax.rem(mate + 2 * turn, experts), 0, mate).wait_recv()
        for copy in own_shards:
            copy.wait()
        load_weights.start()
        own_cot.start()
        for d in range(1, experts):
            cot_copy(d).start()

        @pl.when(to_left)
        def _():
            edge.wait_recv()

        @pl.when(jnp.logical_not(to_left))
        def _():
            no_edge.wait()

        for copy in local:
            copy.wait()
        load_weights.wait()

        @pl.loop(0, (halo + span) // short_block)
        def _(turn):
            rows = pl.ds(pl.multiple_of(turn * short_block, short_block), short_block)
            project(short_buf[rows], rows, range(blocks), short_store)

    for k in range(2, blocks):

        @pl.when(step == (k - 1) * heads // (blocks - 1))
        def _(k=k):
            hand_on(k)

    @pl.when(step < heads)
    def _():
        query, key, value = (short_store[kind, step] for kind in range(3))
        for kind, part in enumerate((query, key, value)):
            short_qkv[kind, 0] = part
        query = scaled(query)
        value_t = value.T
        for i in range(span // short_block):
            lo, hi = i * short_block, (i + 1) * short_block
            visible = short_visible(key_ids[...], query_ids[...], i, short_block, halo)
            scores = dot_nt(key[lo : hi + halo], query[lo + halo : hi + halo])
            scores = jnp.where(visible, scores, NEGATIVE)
            top = jnp.max(scores, axis=0, keepdims=True)
            scores = jnp.exp(scores - top)
            total = jnp.sum(scores, axis=0, keepdims=True)
            out = dot_nn(value_t[:, lo : hi + halo], scores.astype(BF)) / total
            short_wide[:, lo:hi] = out
            short_low[:, lo:hi] = out.astype(BF)
            short_total[0, :, lo:hi] = top + jnp.log(total)

    @pl.when(step == heads)
    def _():
        @pl.loop(0, blocks)
        def _(slot):
            rows = pl.ds(pl.multiple_of(slot * block, block), block)
            project(rows_buf[slot], rows, [z], long_store)

    @pl.when(step >= heads)
    def _():
        head = step - heads
        query, key, value = (long_store[kind, head] for kind in range(3))
        for kind, part in enumerate((query, key, value)):
            long_qkv[kind, 0] = part
        query = scaled(query)
        value_t = value.T
        visible = causal(block, block, 0)
        for i in range(blocks):
            lo, hi = i * block, (i + 1) * block
            own = query[lo:hi]
            near = jnp.where(visible, dot_nt(key[lo:hi], own), NEGATIVE)
            top = jnp.max(near, axis=0, keepdims=True)
            if i:
                far = dot_nt(key[:lo], own)
                top = jnp.maximum(top, jnp.max(far, axis=0, keepdims=True))
            near = jnp.exp(near - top)
            total = jnp.sum(near, axis=0, keepdims=True)
            out = dot_nn(value_t[:, lo:hi], near.astype(BF))
            if i:
                far = jnp.exp(far - top)
                total = total + jnp.sum(far, axis=0, keepdims=True)
                out = out + dot_nn(value_t[:, :lo], far.astype(BF))
            out = out / total
            long_wide[:, lo:hi] = out
            low_stage[i, head] = out.astype(BF)
            long_total[0, :, lo:hi] = top + jnp.log(total)
        low_local(head).start()
        for d in range(1, blocks):
            low_copy(head, d).start()

    @pl.when(step == heads + share - 1)
    def _():
        for head in range(share):
            low_local(head).wait()
            for d in range(1, blocks):
                low_copy(head, d).wait()
        own_cot.wait()
        for d in range(1, experts):
            cot_copy(d).wait()
        for copy in sent + handed:
            copy.wait_send()

        @pl.when(to_right)
        def _():
            own_row(0, right).wait_send()
            edge.wait_send()

        @pl.when(to_left)
        def _():
            own_row(1, left).wait_send()

        for k in range(1, blocks):

            @pl.when((z - k >= 0) & to_right)
            def _(k=k):
                row(jnp.maximum(z - k, 0), 2 * k, right).wait_send()

            @pl.when((z + k < blocks) & to_left)
            def _(k=k):
                row(jnp.minimum(z + k, blocks - 1), 2 * k + 1, left).wait_send()


def run_front(
    qkv_shard, out_shard, row, short_row, cot, routes, vectors, shifts, key_ids, query_ids, experts, blocks
):
    span, width = row.shape
    size = width // HEADS
    halo = key_ids.shape[0] - span
    part = qkv_shard.shape[2]
    share = part // size // 3
    length = blocks * span
    sorted_shape = (experts, 2 * cot.shape[0] // experts, width)
    gathers = qkv_shard.shape[1] % 16 == 0
    if not gathers:
        qkv_shard = lax.all_gather(qkv_shard, "expert", axis=1, tiled=True)
        full_out = lax.all_gather(out_shard, "expert", axis=0, tiled=True)
    any_spec = pl.BlockSpec(memory_space=pl.ANY)
    dma = pltpu.SemaphoreType.DMA

    def whole(shape):
        return pl.BlockSpec(shape, lambda f: (0,) * len(shape), pipeline_mode=pl.Buffered(1))

    def short_head(*shape):
        return pl.BlockSpec(
            shape, lambda f: (0,) * (len(shape) - 3) + (jnp.minimum(f, HEADS - 1), 0, 0)
        )

    def long_head(*shape):
        return pl.BlockSpec(
            shape, lambda f: (0,) * (len(shape) - 3) + (jnp.maximum(f - HEADS, 0), 0, 0)
        )

    def flat_short(*shape):
        return pl.BlockSpec(shape, lambda f: (jnp.minimum(f, HEADS - 1), 0))

    gathered_shapes = (
        jax.ShapeDtypeStruct((blocks, width, part), BF),
        jax.ShapeDtypeStruct((experts,) + out_shard.shape, BF),
    )
    results = pl.pallas_call(
        functools.partial(
            front_kernel, experts, blocks, HEADS, gathers, span, min(SHORT, span)
        ),
        grid=(HEADS + share,),
        in_specs=[any_spec] * 4
        + [
            whole(cot.shape),
            whole(routes.shape),
            whole(vectors.shape),
            whole((blocks, 1, part)),
            whole((halo + span, 1)),
            whole((1, span)),
        ],
        out_specs=((any_spec,) * 2 if gathers else ())
        + (
            any_spec,
            whole(routes.shape),
            any_spec,
            long_head(3, 1, length, size),
            pl.BlockSpec((size, length), lambda f: (jnp.maximum(f - HEADS, 0), 0)),
            long_head(1, 1, length),
            short_head(3, 1, halo + span, size),
            flat_short(size, span),
            flat_short(size, span),
            short_head(1, 1, span),
        ),
        out_shape=(gathered_shapes if gathers else ())
        + (
            jax.ShapeDtypeStruct(sorted_shape, BF),
            jax.ShapeDtypeStruct(routes.shape, jnp.int32),
            jax.ShapeDtypeStruct((blocks, share, size, span), BF),
            jax.ShapeDtypeStruct((3, share, length, size), BF),
            jax.ShapeDtypeStruct((share * size, length), F32),
            jax.ShapeDtypeStruct((share, 1, length), F32),
            jax.ShapeDtypeStruct((3, HEADS, halo + span, size), BF),
            jax.ShapeDtypeStruct((width, span), F32),
            jax.ShapeDtypeStruct((width, span), BF),
            jax.ShapeDtypeStruct((HEADS, 1, span), F32),
        ),
        scratch_shapes=[
            pltpu.VMEM((blocks, width, part), BF),
            pltpu.VMEM((blocks, span, width), BF),
            pltpu.VMEM((halo + span, width), BF),
            pltpu.VMEM((3, share, length, size), BF),
            pltpu.VMEM((3, HEADS, halo + span, size), BF),
            pltpu.VMEM((blocks, share, size, span), BF),
            pltpu.VMEM(sorted_shape, BF),
            dma((2, experts)),
            dma((2, experts)),
            dma((2 * blocks,)),
            dma((blocks,)),
            dma((2,)),
            dma((6,)),
            dma((experts,)),
            dma((experts,)),
            dma((share, blocks)),
            dma((share, blocks)),
        ],
        compiler_params=pltpu.CompilerParams(
            collective_id=0, has_side_effects=True, vmem_limit_bytes=56 << 20
        ),
    )(qkv_shard, out_shard, row, short_row, cot, routes, vectors, shifts, key_ids, query_ids)
    if gathers:
        return results[0], results[1].reshape(-1, out_shard.shape[1]), results[2:]
    return qkv_shard, full_out, results


def line_sums(z, blocks, up_held, down_held, part_send, part_recv, put):
    rounds = len(up_held) - 1

    def part_copies(r, p):
        bit = 1 << r
        mine = lax.rem(z // bit, 2)
        partner = z + bit - 2 * bit * mine
        copies = []
        for k in range((blocks >> r) // 2):
            for n, held in enumerate((up_held, down_held)):
                copies.append(
                    remote(
                        held[r].at[p, 2 * k + 1 - mine],
                        held[r + 1].at[p, k],
                        part_send.at[r, n, p, k],
                        part_recv.at[r, n, p, k],
                        {"blk": partner},
                    )
                )
        return copies

    def add_parts(r, p):
        mine = lax.rem(z // (1 << r), 2)
        for copy in part_copies(r, p):
            copy.wait_recv()
        for k in range((blocks >> r) // 2):
            up = up_held[r][p, 2 * k + mine].astype(F32) + up_held[r + 1][p, k].astype(F32)
            down = down_held[r][p, 2 * k + mine].astype(F32) + down_held[r + 1][p, k].astype(F32)
            if r + 1 < rounds:
                up_held[r + 1][p, k] = up.astype(BF)
                down_held[r + 1][p, k] = down.astype(BF)
            else:
                put(p, up, down.T)
        if r + 1 < rounds:
            for copy in part_copies(r + 1, p):
                copy.start()

    return part_copies, add_parts


def sum_scratch(parts, blocks, depth, width, first):
    rounds = (blocks - 1).bit_length()
    lanes = 128
    dma = pltpu.SemaphoreType.DMA
    return (
        [
            pltpu.VMEM((parts, blocks >> r, depth, blocks * lanes), BF)
            for r in range(first, rounds + 1)
        ]
        + [pltpu.VMEM((parts, blocks >> r, width, lanes), BF) for r in range(first, rounds + 1)]
        + [dma((rounds, 2, parts, blocks // 2)), dma((rounds, 2, parts, blocks // 2))]
    )


def gelu_parts(hidden):
    cdf = 0.5 * (1.0 + lax.erf(hidden * 0.7071067811865476))
    density = jnp.exp(-0.5 * hidden * hidden) * 0.3989422804014327
    return hidden * cdf, cdf + hidden * density


def expert_kernel(
    experts,
    blocks,
    steps,
    rest,
    chunk,
    x_hbm,
    cot_hbm,
    *refs,
):
    ups, refs = refs[:blocks], refs[blocks:]
    downs, refs = refs[:blocks], refs[blocks:]
    up_shifts, refs = refs[:blocks], refs[blocks:]
    (
        down_shift_ref,
        centroid_ref,
        back_grad,
        produced,
        up_sum,
        down_sum,
        up_rest,
        down_rest,
        up_shift_out,
        down_shift_out,
        x_buf,
        low_buf,
        xt_ref,
        gt_ref,
        out_acc,
        grad_acc,
        gate_ref,
        up_acc,
        down_acc,
        shift_acc,
        x_send,
        x_recv,
        back_send,
        back_recv,
        local_sem,
        *refs,
    ) = refs
    rounds = (blocks - 1).bit_length()
    up_held, down_held = refs[: rounds + 1], refs[rounds + 1 : 2 * rounds + 2]
    part_send, part_recv = refs[2 * rounds + 2 :]
    step = pl.program_id(0)
    me, z = lax.axis_index("expert"), lax.axis_index("blk")
    capacity, width = x_buf.shape[1:]
    rows = experts * capacity
    lanes = 128
    sources, chunks = chunk // capacity, rows // chunk

    def x_copy(d):
        target = across(me, jnp.int32(d), experts)
        return remote(
            x_hbm.at[target], x_buf.at[me], x_send.at[d], x_recv.at[d], {"expert": target}
        )

    def back_copy(d):
        target = across(me, jnp.int32(d), experts)
        return remote(
            low_buf.at[target],
            back_grad.at[me],
            back_send.at[d],
            back_recv.at[d],
            {"expert": target},
        )

    back_local = pltpu.make_async_copy(low_buf.at[me], back_grad.at[me], local_sem.at[0])
    out_copy = pltpu.make_async_copy(x_buf, produced, local_sem.at[1])


    def put(p, up, down):
        for j in range(blocks):
            first = (j * steps + p) * lanes
            up_sum[:, first : first + lanes] = up[:, j * lanes : (j + 1) * lanes]
        down_sum[p * lanes : (p + 1) * lanes] = down

    part_copies, add_parts = line_sums(
        z, blocks, up_held, down_held, part_send, part_recv, put
    )
    cot_copy = pltpu.make_async_copy(cot_hbm, low_buf, local_sem.at[2])
    own_copy = pltpu.make_async_copy(x_hbm.at[me], x_buf.at[me], local_sem.at[3])
    x_flat, low_flat = x_buf.reshape(rows, width), low_buf.reshape(rows, width)

    @pl.when(step == 0)
    def _():
        barrier = pltpu.get_barrier_semaphore()
        for d in range(1, experts):
            pl.semaphore_signal(
                barrier, inc=1, device_id={"expert": lax.rem(me + d, experts)}, device_id_type=MESH
            )
        for r in range(rounds):
            bit = 1 << r
            partner = z + bit - 2 * bit * lax.rem(z // bit, 2)
            pl.semaphore_signal(barrier, inc=1, device_id={"blk": partner}, device_id_type=MESH)
        cot_copy.start()
        own_copy.start()
        pl.semaphore_wait(barrier, experts - 1 + rounds)
        for d in range(1, experts):
            x_copy(d).start()
        up_sum[...] = jnp.zeros_like(up_sum)
        down_sum[...] = jnp.zeros_like(down_sum)
        out_acc[...] = jnp.zeros_like(out_acc)
        grad_acc[...] = jnp.zeros_like(grad_acc)
        cot_copy.wait()
        own_copy.wait()
        down_shift_out[...] = jnp.zeros_like(down_shift_out)

    def prepare(at, near):
        for n in range(sources):
            d = near * sources + n

            @pl.when(d != 0)
            def _(d=d):
                x_copy(d).wait_recv()

        x = x_flat[at]
        logit = jnp.sum(x.astype(F32) * centroid_ref[...], axis=1, keepdims=True)
        gate = 1.0 / (1.0 + jnp.exp(-logit))
        gate_ref[at] = gate
        low = (low_flat[at].astype(F32) * gate).astype(BF)
        low_flat[at] = low
        xt_ref[:, at] = x.T
        gt_ref[:, at] = low.T
        down_shift_out[...] += jnp.sum(low.astype(F32), axis=0, keepdims=True)

    def answer(at, near):
        gate = gate_ref[at]
        out = (out_acc[at] + down_shift_ref[...]).astype(BF)
        inner = jnp.sum(low_flat[at].astype(F32) * out.astype(F32), axis=1, keepdims=True)
        x_flat[at] = out
        low_flat[at] = (grad_acc[at] + inner * (1.0 - gate) * centroid_ref[...]).astype(BF)
        for n in range(sources):
            d = near * sources + n

            @pl.when(d != 0)
            def _(d=d):
                back_copy(d).start()

    up = jnp.concatenate([ref[...] for ref in ups], axis=1)
    down = jnp.concatenate([ref[...] for ref in downs], axis=0)
    up_shift = jnp.concatenate([ref[...] for ref in up_shifts], axis=1)
    up_acc[...] = jnp.zeros_like(up_acc)
    down_acc[...] = jnp.zeros_like(down_acc)
    shift_acc[...] = jnp.zeros_like(shift_acc)

    @pl.loop(0, chunks)
    def _(turn):
        near = jnp.where(step == steps - 1, chunks - 1 - turn, turn)
        at = pl.ds(pl.multiple_of(across(me // sources, near, chunks) * chunk, chunk), chunk)

        @pl.when(step == 0)
        def _():
            prepare(at, near)

        x = x_flat[at]
        low = low_flat[at]
        hidden = dot_nn(x, up) + up_shift
        active, slope = gelu_parts(hidden)
        active = active.astype(BF)
        grad_low = (dot_nt(low, down) * slope).astype(BF)
        out_acc[at] += dot_nn(active, down)
        grad_acc[at] += dot_nt(grad_low, up)
        up_acc[...] += dot_nn(xt_ref[:, at], grad_low)
        down_acc[...] += dot_nn(gt_ref[:, at], active)
        shift_acc[...] += jnp.sum(grad_low.astype(F32), axis=0, keepdims=True)

        @pl.when(step == steps - 1)
        def _():
            answer(at, near)

    depth = width // blocks
    keep = steps - rest
    for j in range(blocks):
        up_shift_out[j] = shift_acc[:, j * lanes : (j + 1) * lanes]

    def store(up_target, down_target):
        for j in range(blocks):
            up_target[j] = up_acc[j * depth : (j + 1) * depth].astype(BF)
            down_target[j] = down_acc[:, j * lanes : (j + 1) * lanes].astype(BF)

    @pl.when(step < keep)
    def _():
        store(up_held[0].at[step], down_held[0].at[step])
        for copy in part_copies(0, step):
            copy.start()

    @pl.when(step >= keep)
    def _():
        store(up_rest.at[0], down_rest.at[0])

    tasks = sorted(
        ((r, p) for p in range(keep) for r in range(rounds)), key=lambda task: (sum(task), task[0])
    )
    early = [[] for _ in range(steps)]
    for turn, task in enumerate(tasks):
        at = 2 * (task[1] + 1) + 2 * task[0]
        if at < steps - 1:
            early[at].append(task)
    for at in range(steps):
        if early[at]:

            @pl.when(step == at)
            def _(at=at):
                for r, p in early[at]:
                    add_parts(r, p)

    @pl.when(step == steps - 1)
    def _():
        for d in range(1, experts):
            x_copy(d).wait_send()
        back_local.start()
        out_copy.start()
        for r, p in tasks:
            if all((r, p) not in done for done in early):
                add_parts(r, p)
        back_local.wait()
        out_copy.wait()
        for d in range(1, experts):
            back_copy(d).wait()
        for p in range(keep):
            for r in range(rounds):
                for copy in part_copies(r, p):
                    copy.wait_send()


def run_expert(x, cot, up_weight, down_weight, up_shift, down_shift, centroid, blocks):
    experts, capacity, width = x.shape
    rows = experts * capacity
    hidden = up_weight.shape[1]
    lanes = 128
    steps = hidden // blocks // lanes
    rounds = (blocks - 1).bit_length()
    chunk = min(512, rows)
    depth = width // blocks
    rest = steps // 3
    keep = steps - rest
    any_spec = pl.BlockSpec(memory_space=pl.ANY)

    def once(shape):
        return pl.BlockSpec(shape, lambda f: (0,) * len(shape), pipeline_mode=pl.Buffered(1))

    return pl.pallas_call(
        functools.partial(expert_kernel, experts, blocks, steps, rest, chunk),
        grid=(steps,),
        in_specs=[any_spec] * 2
        + [pl.BlockSpec((width, lanes), lambda f, j=j: (0, j * steps + f)) for j in range(blocks)]
        + [pl.BlockSpec((lanes, width), lambda f, j=j: (j * steps + f, 0)) for j in range(blocks)]
        + [pl.BlockSpec((1, lanes), lambda f, j=j: (0, j * steps + f)) for j in range(blocks)]
        + [once((1, width))] * 2,
        out_specs=(
            any_spec,
            any_spec,
            once((depth, hidden)),
            once((hidden // blocks, width)),
            pl.BlockSpec(
                (1, blocks, depth, blocks * lanes), lambda f: (jnp.maximum(f - keep, 0), 0, 0, 0)
            ),
            pl.BlockSpec(
                (1, blocks, width, lanes), lambda f: (jnp.maximum(f - keep, 0), 0, 0, 0)
            ),
            pl.BlockSpec((blocks, 1, lanes), lambda f: (0, 0, f)),
            once((1, width)),
        ),
        out_shape=(
            jax.ShapeDtypeStruct(x.shape, BF),
            jax.ShapeDtypeStruct(x.shape, BF),
            jax.ShapeDtypeStruct((depth, hidden), F32),
            jax.ShapeDtypeStruct((hidden // blocks, width), F32),
            jax.ShapeDtypeStruct((rest, blocks, depth, blocks * lanes), BF),
            jax.ShapeDtypeStruct((rest, blocks, width, lanes), BF),
            jax.ShapeDtypeStruct((blocks, 1, hidden // blocks), F32),
            jax.ShapeDtypeStruct((1, width), F32),
        ),
        scratch_shapes=[
            pltpu.VMEM(x.shape, BF),
            pltpu.VMEM(x.shape, BF),
            pltpu.VMEM((width, rows), BF),
            pltpu.VMEM((width, rows), BF),
            pltpu.VMEM((rows, width), F32),
            pltpu.VMEM((rows, width), F32),
            pltpu.VMEM((rows, 1), F32),
            pltpu.VMEM((width, blocks * lanes), F32),
            pltpu.VMEM((width, blocks * lanes), F32),
            pltpu.VMEM((1, blocks * lanes), F32),
            pltpu.SemaphoreType.DMA((experts,)),
            pltpu.SemaphoreType.DMA((experts,)),
            pltpu.SemaphoreType.DMA((experts,)),
            pltpu.SemaphoreType.DMA((experts,)),
            pltpu.SemaphoreType.DMA((4,)),
        ]
        + sum_scratch(keep, blocks, depth, width, 0),
        compiler_params=pltpu.CompilerParams(
            collective_id=1, has_side_effects=True, vmem_limit_bytes=62 << 20
        ),
        cost_estimate=pl.CostEstimate(
            flops=12 * rows * width * hidden, bytes_accessed=40 << 20, transcendentals=0
        ),
    )(
        x,
        cot,
        *([up_weight] * blocks),
        *([down_weight] * blocks),
        *([up_shift] * blocks),
        down_shift,
        centroid,
    )


def long_back_head(query, key, value, grad_ref, wide_ref, total_ref, out_ref, head, key_acc, value_acc):
    scale = query.shape[1] ** (-0.5)
    query = scaled(query)
    key_t = key.T
    count, _, _, block = grad_ref.shape
    visible = causal(block, block, 0)
    key_acc[...] = jnp.zeros_like(key_acc)
    value_acc[...] = jnp.zeros_like(value_acc)
    for i in range(count):
        lo, hi = i * block, (i + 1) * block
        own = query[lo:hi]
        grad_t = grad_ref[i, head]
        grad = grad_t.T
        delta = jnp.sum(grad_t.astype(F32) * wide_ref[:, lo:hi], axis=0, keepdims=True)
        total = total_ref[0, :, lo:hi]
        query_grad = None
        for start, stop in ((lo, hi), (0, lo)):
            if start == stop:
                continue
            weights = jnp.exp(dot_nt(key[start:stop], own) - total)
            if start == lo:
                weights = jnp.where(visible, weights, 0.0)
            scores = weights * (dot_nt(value[start:stop], grad) - delta)
            scores_low = scores.astype(BF)
            value_acc[start:stop] += dot_nn(weights.astype(BF), grad)
            key_acc[start:stop] += dot_nn(scores_low, own)
            part = dot_nn(key_t[:, start:stop], scores_low)
            query_grad = part if query_grad is None else query_grad + part
        out_ref[i, 0, head] = (query_grad * scale).astype(BF)
    key_grad = key_acc[...].T.astype(BF)
    value_grad = value_acc[...].T.astype(BF)
    for i in range(count):
        out_ref[i, 1, head] = key_grad[:, i * block : (i + 1) * block]
        out_ref[i, 2, head] = value_grad[:, i * block : (i + 1) * block]


def short_back_head(
    query, key, value, grad_t, wide_ref, total_ref, key_ids, query_ids, key_acc, value_acc, block
):
    scale = query.shape[1] ** (-0.5)
    query = scaled(query)
    key_t = key.T
    extent, span = query.shape[0], query_ids.shape[1]
    halo = extent - span
    key_acc[0:extent] = jnp.zeros((extent, key_acc.shape[1]), F32)
    value_acc[0:extent] = jnp.zeros((extent, key_acc.shape[1]), F32)
    query_grads = []
    for i in range(span // block):
        lo, hi = i * block, (i + 1) * block
        visible = short_visible(key_ids[...], query_ids[...], i, block, halo)
        own = query[lo + halo : hi + halo]
        part_t = grad_t[:, lo:hi]
        grad = part_t.T
        delta = jnp.sum(part_t.astype(F32) * wide_ref[:, lo:hi], axis=0, keepdims=True)
        scores = dot_nt(key[lo : hi + halo], own)
        weights = jnp.exp(jnp.where(visible, scores, NEGATIVE) - total_ref[0, :, lo:hi])
        scores = weights * (dot_nt(value[lo : hi + halo], grad) - delta)
        scores_low = scores.astype(BF)
        value_acc[lo : hi + halo] += dot_nn(weights.astype(BF), grad)
        key_acc[lo : hi + halo] += dot_nn(scores_low, own)
        part = dot_nn(key_t[:, lo : hi + halo], scores_low)
        query_grads.append(part * scale)
    query_grad = jnp.concatenate(query_grads, axis=1)
    return query_grad, key_acc[0:extent].T, value_acc[0:extent].T


def tail_kernel(
    experts,
    blocks,
    heads,
    lead,
    rest,
    back_grad,
    slot_ref,
    route_ref,
    middle_ref,
    cot_ref,
    vectors,
    centroid_ref,
    long_attended,
    short_attended,
    out_weight,
    long_qkv,
    long_wide,
    long_total,
    short_qkv,
    short_wide,
    short_total,
    key_ids,
    query_ids,
    produced,
    up_rest,
    down_rest,
    up_first,
    down_first,
    shift_ref,
    long_back,
    short_back,
    grad_middle,
    result_ref,
    out_term,
    sums_ref,
    centroid_out,
    up_sum,
    down_sum,
    shift_sum,
    grad_low,
    long_stage,
    short_grad,
    long_grad,
    back_stage,
    halo_stage,
    halo_in,
    own_edge,
    back_out,
    up_last,
    down_last,
    shift_in,
    key_acc,
    value_acc,
    out_send,
    out_recv,
    grad_send,
    grad_recv,
    back_send,
    back_recv,
    halo_send,
    halo_recv,
    shift_send,
    shift_recv,
    local_sem,
    put_sem,
    *refs,
):
    rounds = (blocks - 1).bit_length()
    up_held = (up_rest,) + refs[:rounds]
    down_held = (down_rest,) + refs[rounds : 2 * rounds]
    part_send, part_recv = refs[2 * rounds :]
    step = pl.program_id(0)
    me, z = lax.axis_index("expert"), lax.axis_index("blk")
    share, size, span = long_stage.shape[1:]
    width = out_weight.shape[0]
    count = slot_ref.shape[0]
    halo = halo_stage.shape[3]
    chunk = min(256, span)
    lanes = 128
    steps = up_sum.shape[1] // blocks // lanes
    keep = steps - rest

    def put_copies(p):
        copies = []
        for j in range(blocks):
            first = (j * steps + keep + p) * lanes
            copies.append(
                pltpu.make_async_copy(
                    up_last.at[p, j], up_sum.at[:, pl.ds(first, lanes)], put_sem.at[p, j]
                )
            )
        copies.append(
            pltpu.make_async_copy(
                down_last.at[p], down_sum.at[pl.ds((keep + p) * lanes, lanes)], put_sem.at[p, blocks]
            )
        )
        return copies

    def put(p, up, down):
        for j in range(blocks):
            up_last[p, j] = up[:, j * lanes : (j + 1) * lanes]
        down_last[p] = down
        for copy in put_copies(p):
            copy.start()

    part_copies, add_parts = line_sums(
        z, blocks, up_held, down_held, part_send, part_recv, put
    )
    line = [lax.rem(z + d, blocks) for d in range(blocks)]

    def out_copy(d):
        target = lax.rem(me + d, experts)
        return remote(
            produced.at[target], back_out.at[me], out_send.at[d], out_recv.at[d], {"expert": target}
        )

    def grad_copy(d):
        return remote(
            long_stage.at[line[d]], long_grad.at[z], grad_send.at[d], grad_recv.at[d], {"blk": line[d]}
        )

    def back_copy(head, d):
        return remote(
            back_stage.at[line[d], :, head],
            long_back.at[z, :, head],
            back_send.at[head, d],
            back_recv.at[head, d],
            {"blk": line[d]},
        )

    def back_local(head):
        return pltpu.make_async_copy(
            back_stage.at[z, :, head], long_back.at[z, :, head], back_send.at[head, 0]
        )

    def shift_copy(d):
        return remote(
            shift_ref.at[line[d]], shift_in.at[d], shift_send.at[d], shift_recv.at[d], {"blk": line[d]}
        )

    def halo_copy(n):
        part = pl.ds(0, lead) if n == 0 else pl.ds(lead, heads - lead)
        left = lax.rem(z + blocks - 1, blocks)
        return remote(
            halo_stage.at[:, part], halo_in.at[:, part], halo_send.at[n], halo_recv.at[n], {"blk": left}
        )

    own_out_copy = pltpu.make_async_copy(produced.at[me], back_out.at[me], local_sem.at[0])

    def send_halo(n):
        @pl.when(z > 0)
        def _():
            halo_copy(n).start()

    @pl.when(step == 0)
    def _():
        greet(experts, blocks)
        for copy in part_copies(0, 0):
            copy.start()
        for d in range(1, blocks):
            shift_copy(d).start()
        own_out_copy.start()
        for d in range(1, experts):
            out_copy(d).start()
        spare = blocks * share - heads
        flat_stage = long_stage.reshape(blocks * share, size, span)
        if spare:
            flat_stage[heads:] = jnp.zeros((spare, size, span), BF)
            short_back[...] = jnp.zeros_like(short_back)
        slot_line = lax.broadcasted_iota(jnp.int32, (chunk, back_grad.shape[0]), 1)
        sums_ref[...] = jnp.zeros_like(sums_ref)

        def back_rows(turn, first, store):
            at = pl.multiple_of(turn * chunk, chunk)
            rows = pl.ds(pl.multiple_of(first + at, chunk), chunk)
            chosen = (slot_ref[rows] == slot_line).astype(F32).astype(BF)
            upstream = dot_nn(chosen, back_grad[...])
            normal, scale = norm_parts(middle_ref[rows])
            inner, gain_part, bias_part = norm_back(upstream, normal, scale, vectors[2:3])
            middle = cot_ref[rows].astype(F32) + inner
            grad_middle[rows] = middle
            low = middle.astype(BF)
            grad_low[rows] = low
            for n, part in enumerate((gain_part, bias_part, jnp.sum(middle, axis=0))):
                sums_ref[n] += part
            grad_t = dot_nt(out_weight[...], low).astype(BF).reshape(heads, size, chunk)
            store[:heads, :, pl.ds(at, chunk)] = grad_t

        pl.loop(0, span // chunk)(lambda turn: back_rows(turn, 0, flat_stage))
        for d in range(1, blocks):
            grad_copy(d).start()
        pl.loop(0, span // chunk)(lambda turn: back_rows(turn, span, short_grad))
        out_term[...] = (
            dot_nn(long_attended[...], grad_low[:span]) + dot_nn(short_attended[...], grad_low[span:])
        ).astype(BF)

    first_long = lead + 1
    is_long = (step >= first_long) & (step < first_long + share)

    @pl.when((step > 0) & jnp.logical_not(is_long))
    def _():
        head = step - 1 - jnp.where(step >= first_long, share, 0)
        query, key, value = (short_qkv[kind, 0] for kind in range(3))
        grads = short_back_head(
            query,
            key,
            value,
            short_grad[head],
            short_wide,
            short_total,
            key_ids,
            query_ids,
            key_acc,
            value_acc,
            min(SHORT, span),
        )
        group = head // share
        place = head - group * share
        for n, grad in enumerate(grads):
            short_back[group, n, place] = grad[:, grad.shape[1] - span :].astype(BF)
            if n:
                halo_stage[n - 1, head] = grad[:, :halo].astype(BF)
                own_edge[n - 1, head] = grad[:, span:]

    @pl.when(step == lead)
    def _():
        send_halo(0)

    @pl.when(step == first_long)
    def _():
        for d in range(1, blocks):
            grad_copy(d).wait_recv()
        long_grad[z] = long_stage[z]
        add_parts(0, 0)
        for p in range(1, rest):
            for copy in part_copies(0, p):
                copy.start()

    @pl.when(is_long)
    def _():
        head = step - first_long
        query, key, value = (long_qkv[kind, 0] for kind in range(3))
        long_back_head(
            query, key, value, long_grad, long_wide, long_total, back_stage, head, key_acc, value_acc
        )
        back_local(head).start()
        for d in range(1, blocks):
            back_copy(head, d).start()

    tasks = sorted(
        ((r, p) for p in range(rest) for r in range(rounds)), key=lambda task: (sum(task), task[0])
    )[1:]

    @pl.when(step == first_long + share)
    def _():
        for r, p in tasks[:-1]:
            add_parts(r, p)

    @pl.when(step == heads + share)
    def _():
        send_halo(1)
        own_out_copy.wait()
        for d in range(1, experts):
            out_copy(d).wait_recv()
        answers = back_out.reshape(back_grad.shape)
        slot_line = lax.broadcasted_iota(jnp.int32, (chunk, back_grad.shape[0]), 1)
        expert_line = lax.broadcasted_iota(jnp.int32, (chunk, 128), 1)
        centroid_rows = jnp.concatenate(
            [centroid_ref[...], jnp.zeros((128 - experts, width), F32)], axis=0
        ).astype(BF)
        centroid_out[...] = jnp.zeros_like(centroid_out)

        @pl.loop(0, count // chunk)
        def _(turn):
            rows = pl.ds(pl.multiple_of(turn * chunk, chunk), chunk)
            chosen = (slot_ref[rows] == slot_line).astype(F32).astype(BF)
            answer = dot_nn(chosen, answers[...])
            middle = middle_ref[rows]
            normed = norm_parts(middle)[0] * vectors[2:3] + vectors[3:4]
            named = (route_ref[rows] == expert_line).astype(F32)
            logit = jnp.sum(
                normed * dot_nn(named.astype(BF), centroid_rows), axis=1, keepdims=True
            )
            gate = 1.0 / (1.0 + jnp.exp(-logit))
            result_ref[rows] = middle + gate * answer
            inner = jnp.sum(cot_ref[rows].astype(F32) * answer, axis=1, keepdims=True)
            part = lax.dot_general(
                named,
                inner * gate * (1.0 - gate) * normed,
                (((0,), (0,)), ((), ())),
                preferred_element_type=F32,
            )
            centroid_out[...] += part[:experts]

        if tasks:
            add_parts(*tasks[-1])
        for p in range(rest):
            for copy in put_copies(p):
                copy.wait()
        for d in range(1, blocks):
            shift_copy(d).wait()
        total = shift_ref[z]
        for d in range(1, blocks):
            total = total + shift_in[d]
        shift_sum[...] = total
        for d in range(1, experts):
            out_copy(d).wait_send()
        for d in range(1, blocks):
            grad_copy(d).wait_send()
        for head in range(share):
            back_local(head).wait()
            for d in range(1, blocks):
                back_copy(head, d).wait()
        for p in range(rest):
            for r in range(rounds):
                for copy in part_copies(r, p):
                    copy.wait_send()
        for n in range(2):

            @pl.when(z > 0)
            def _(n=n):
                halo_copy(n).wait_send()

            @pl.when(z < blocks - 1)
            def _(n=n):
                halo_copy(n).wait_recv()

        @pl.when(z < blocks - 1)
        def _():
            for head in range(heads):
                for n in range(2):
                    edge = own_edge[n, head] + halo_in[n, head].astype(F32)
                    short_back[head // share, 1 + n, head % share, :, span - halo :] = edge.astype(BF)


def run_tail(
    back_grad,
    slot_of,
    route_of,
    middle,
    cot,
    vectors,
    centroids,
    long_attended,
    short_attended,
    out_weight,
    long_parts,
    short_parts,
    key_ids,
    query_ids,
    produced,
    up_rest,
    down_rest,
    up_first,
    down_first,
    shifts,
    blocks,
):
    experts = produced.shape[0]
    slots, width = back_grad.shape
    count = slot_of.shape[0]
    long_qkv, long_wide, long_total = long_parts
    short_qkv, short_wide, short_total = short_parts
    _, share, length, size = long_qkv.shape
    extent, span = short_qkv.shape[2], query_ids.shape[1]
    halo = extent - span
    heads = HEADS
    lead = heads // 2
    rest, _, depth, _ = up_rest.shape
    hidden = up_first.shape[1]
    any_spec = pl.BlockSpec(memory_space=pl.ANY)
    dma = pltpu.SemaphoreType.DMA

    def whole(shape):
        return pl.BlockSpec(shape, lambda f: (0,) * len(shape), pipeline_mode=pl.Buffered(1))

    def short_at(f):
        return jnp.where(f <= lead, jnp.maximum(f - 1, 0), jnp.maximum(f - 1 - share, lead - 1))

    def long_at(f):
        return jnp.clip(f - 1 - lead, 0, share - 1)

    return pl.pallas_call(
        functools.partial(tail_kernel, experts, blocks, heads, lead, rest),
        grid=(1 + heads + share,),
        in_specs=[
            whole(back_grad.shape),
            whole(slot_of.shape),
            whole(route_of.shape),
            whole(middle.shape),
            whole(cot.shape),
            whole(vectors.shape),
            whole(centroids.shape),
            whole(long_attended.shape),
            whole(short_attended.shape),
            whole(out_weight.shape),
            pl.BlockSpec((3, 1, length, size), lambda f: (0, long_at(f), 0, 0)),
            pl.BlockSpec((size, length), lambda f: (long_at(f), 0)),
            pl.BlockSpec((1, 1, length), lambda f: (long_at(f), 0, 0)),
            pl.BlockSpec((3, 1, extent, size), lambda f: (0, short_at(f), 0, 0)),
            pl.BlockSpec((size, span), lambda f: (short_at(f), 0)),
            pl.BlockSpec((1, 1, span), lambda f: (short_at(f), 0, 0)),
            whole(key_ids.shape),
            whole(query_ids.shape),
            any_spec,
            whole(up_rest.shape),
            whole(down_rest.shape),
            any_spec,
            any_spec,
            whole(shifts.shape),
        ],
        out_specs=(
            any_spec,
            whole((blocks, 3, share, size, span)),
            whole((count, width)),
            whole((count, width)),
            whole((width, width)),
            whole((8, width)),
            whole((experts, width)),
            any_spec,
            any_spec,
            whole(shifts.shape[1:]),
        ),
        out_shape=(
            jax.ShapeDtypeStruct((blocks, 3, share, size, span), BF),
            jax.ShapeDtypeStruct((blocks, 3, share, size, span), BF),
            jax.ShapeDtypeStruct((count, width), F32),
            jax.ShapeDtypeStruct((count, width), F32),
            jax.ShapeDtypeStruct((width, width), BF),
            jax.ShapeDtypeStruct((8, width), F32),
            jax.ShapeDtypeStruct((experts, width), F32),
            jax.ShapeDtypeStruct((depth, hidden), F32),
            jax.ShapeDtypeStruct((hidden // blocks, width), F32),
            jax.ShapeDtypeStruct(shifts.shape[1:], F32),
        ),
        scratch_shapes=[
            pltpu.VMEM((count, width), BF),
            pltpu.VMEM((blocks, share, size, span), BF),
            pltpu.VMEM((heads, size, span), BF),
            pltpu.VMEM((blocks, share, size, span), BF),
            pltpu.VMEM((blocks, 3, share, size, span), BF),
            pltpu.VMEM((2, heads, size, halo), BF),
            pltpu.VMEM((2, heads, size, halo), BF),
            pltpu.VMEM((2, heads, size, halo), F32),
            pltpu.VMEM(produced.shape, BF),
            pltpu.VMEM((rest, blocks, depth, 128), F32),
            pltpu.VMEM((rest, 128, width), F32),
            pltpu.VMEM(shifts.shape, F32),
            pltpu.VMEM((length, size), F32),
            pltpu.VMEM((length, size), F32),
            dma((experts,)),
            dma((experts,)),
            dma((blocks,)),
            dma((blocks,)),
            dma((share, blocks)),
            dma((share, blocks)),
            dma((2,)),
            dma((2,)),
            dma((blocks,)),
            dma((blocks,)),
            dma((1,)),
            dma((rest, blocks + 1)),
        ]
        + sum_scratch(rest, blocks, depth, width, 1),
        input_output_aliases={21: 7, 22: 8},
        compiler_params=pltpu.CompilerParams(
            collective_id=3, has_side_effects=True, vmem_limit_bytes=60 << 20
        ),
    )(
        back_grad,
        slot_of,
        route_of,
        middle,
        cot,
        vectors,
        centroids,
        long_attended,
        short_attended,
        out_weight,
        *long_parts,
        *short_parts,
        key_ids,
        query_ids,
        produced,
        up_rest,
        down_rest,
        up_first,
        down_first,
        shifts,
    )


def close_kernel(
    experts,
    blocks,
    out_ref,
    long_back,
    short_back,
    long_tokens,
    short_tokens,
    vectors,
    weights,
    grad_middle,
    sums_ref,
    centroid_ref,
    token_grad,
    *refs,
):
    number = 2 + blocks // 2
    outs, refs = refs[:number], refs[number:]
    made, refs = (out_ref,) + refs[: number - 1], refs[number - 1 :]
    from_mate, refs = refs[:number], refs[number:]
    pair_sum, refs = refs[:number], refs[number:]
    from_chips, refs = refs[:number], refs[number:]
    group_sum, refs = refs[:number], refs[number:]
    from_line, refs = refs[:number], refs[number:]
    whole, refs = refs[:number], refs[number:]
    (
        normed_t,
        rows_ref,
        tokens_buf,
        back_buf,
        load_sem,
        mate_send,
        mate_recv,
        chip_send,
        chip_recv,
        line_send,
        line_recv,
        back_send,
        back_recv,
    ) = refs
    rounds = (blocks - 1).bit_length()
    chips = experts // 2
    me, z = lax.axis_index("expert"), lax.axis_index("blk")
    core = lax.rem(me, 2)
    chip = me // 2
    mate = me + 1 - 2 * core
    span, width = long_tokens.shape
    part = weights.shape[2]
    chunk = min(256, span)

    def line_partner(r):
        bit = 1 << r
        return z + bit - 2 * bit * lax.rem(z // bit, 2)

    loads = [
        pltpu.make_async_copy(source, target, load_sem.at[n])
        for n, (source, target) in enumerate(
            (
                (long_tokens, tokens_buf.at[0]),
                (short_tokens, tokens_buf.at[1]),
                (long_back, back_buf.at[0]),
                (short_back, back_buf.at[1]),
            )
        )
    ]
    for copy in loads:
        copy.start()
    barrier = pltpu.get_barrier_semaphore()
    pl.semaphore_signal(barrier, inc=1, device_id={"expert": mate}, device_id_type=MESH)
    for d in range(1, chips):
        peer = lax.rem(me + 2 * d, experts)
        pl.semaphore_signal(barrier, inc=1, device_id={"expert": peer}, device_id_type=MESH)
    for r in range(rounds):
        pl.semaphore_signal(
            barrier, inc=1, device_id={"blk": line_partner(r)}, device_id_type=MESH
        )
    pl.semaphore_wait(barrier, chips + rounds)

    def mate_copy(p):
        return remote(
            made[p].at[:, 1 - core], from_mate[p], mate_send.at[p], mate_recv.at[p], {"expert": mate}
        )

    def chip_copies(p):
        copies = []
        for d in range(1, chips):
            there = lax.rem(chip + d, chips)
            copies.append(
                remote(
                    pair_sum[p].at[there],
                    from_chips[p].at[d - 1],
                    chip_send.at[p, d],
                    chip_recv.at[p, d],
                    {"expert": 2 * there + core},
                )
            )
        return copies

    def segment(p, r):
        groups = whole[p].shape[0]
        start = 0
        for n in range(r):
            start = start + lax.rem(z // (1 << n), 2) * (groups >> (n + 1))
        return start, groups >> r

    def line_copy(p, r):
        start, groups = segment(p, r)
        half = groups // 2
        mine = lax.rem(z // (1 << r), 2)
        return remote(
            group_sum[p].at[pl.ds(start + (1 - mine) * half, half)],
            from_line[p].at[r, pl.ds(0, half)],
            line_send.at[p, r],
            line_recv.at[p, r],
            {"blk": line_partner(r)},
        )

    def back_copy(p, r, arrives):
        start, groups = segment(p, r + 1)
        if arrives:
            start, _ = segment(p, r)
            start = start + (1 - lax.rem(z // (1 << r), 2)) * groups
        return remote(
            whole[p].at[pl.ds(start, groups)],
            whole[p].at[pl.ds(start, groups)],
            back_send.at[p, r],
            back_recv.at[p, r],
            {"blk": line_partner(r)},
        )

    def add_line(p, r):
        line_copy(p, r).wait_recv()
        start, groups = segment(p, r + 1)
        held = group_sum[p][pl.ds(start, groups)].astype(F32)
        group_sum[p][pl.ds(start, groups)] = (
            held + from_line[p][r, pl.ds(0, groups)].astype(F32)
        ).astype(BF)

    def run(p, stage):
        if stage == 0:
            mate_copy(p).start()
        elif stage == 1:
            mate_copy(p).wait_recv()
            for k in range(chips):
                own = made[p][k, core].astype(F32)
                pair_sum[p][k] = (own + from_mate[p][k].astype(F32)).astype(BF)
            for copy in chip_copies(p):
                copy.start()
        elif stage == 2:
            for copy in chip_copies(p):
                copy.wait_recv()
            total = pair_sum[p][chip].astype(F32)
            for d in range(1, chips):
                total = total + from_chips[p][d - 1].astype(F32)
            low = total.astype(BF)
            used = low.shape[1] // 128
            for g in range(group_sum[p].shape[0]):
                if g < used:
                    group_sum[p][g] = low[:, g * 128 : (g + 1) * 128]
                else:
                    group_sum[p][g] = jnp.zeros(group_sum[p].shape[1:], BF)
            line_copy(p, 0).start()
        elif stage < 2 + rounds:
            add_line(p, stage - 3)
            line_copy(p, stage - 2).start()
        elif stage == 2 + rounds:
            r = rounds - 1
            add_line(p, r)
            start, groups = segment(p, rounds)
            whole[p][pl.ds(start, groups)] = group_sum[p][pl.ds(start, groups)]
            back_copy(p, r, False).start()
        else:
            r = rounds - 1 - (stage - 3 - rounds)
            back_copy(p, r, True).wait_recv()
            if r:
                back_copy(p, r - 1, False).start()
            else:
                for c in range(0, outs[p].shape[1], 128):
                    outs[p][:, c : c + 128] = whole[p][c // 128].astype(F32)

    turns = span // chunk

    def rows_of(turn):
        at = pl.multiple_of(lax.rem(turn, turns) * chunk, chunk)
        return turn // turns, pl.ds(at, chunk), pl.ds(pl.multiple_of(turn * chunk, chunk), chunk)

    def norm_rows():
        for copy in loads:
            copy.wait()

        @pl.loop(0, 2 * turns)
        def _(turn):
            half, inner, outer = rows_of(turn)
            low = norm_low(tokens_buf[half, inner], vectors[0:1], vectors[1:2])
            normed_t[:, outer] = low.T

    def weight_part(q):
        target = made[1 + q]
        rows = target.shape[2]

        def term(lead):
            total = None
            for half in range(2):
                back = back_buf[half, 2 * q : 2 * q + 2].reshape(2 * part, span)
                product = dot_nt(normed_t[lead, half * span : (half + 1) * span], back)
                total = product if total is None else total + product
            return total

        if rows % 16 == 0:
            flat = target.reshape(width, 2 * part)

            @pl.loop(0, width // 256)
            def _(turn):
                lead = pl.ds(pl.multiple_of(turn * 256, 256), 256)
                flat[lead] = term(lead).astype(BF)
        else:
            target[...] = term(slice(None)).reshape(target.shape).astype(BF)

    def finish_rows():
        rows_ref[...] = jnp.zeros_like(rows_ref)
        ones = jnp.ones((span, 128), BF)
        shift_total = None
        for half in range(2):
            shift_part = dot_nn(back_buf[half].reshape(blocks * part, span), ones)
            shift_total = shift_part if shift_total is None else shift_total + shift_part

        @pl.loop(0, 2 * turns)
        def _(turn):
            half, inner, outer = rows_of(turn)
            grad_t = None
            for n in range(blocks):
                product = dot_nn(weights[n], back_buf[half, n, :, :, :, inner].reshape(part, chunk))
                grad_t = product if grad_t is None else grad_t + product
            normal, scale = norm_parts(tokens_buf[half, inner].astype(F32))
            moved, gain_part, bias_part = norm_back(grad_t.T, normal, scale, vectors[0:1])
            token_grad[outer] = grad_middle[outer] + moved
            rows_ref[8 + experts] += gain_part
            rows_ref[9 + experts] += bias_part

        rows_ref[0:8] = sums_ref[...]
        rows_ref[8 : 8 + experts] = centroid_ref[...]
        small = rows_ref[...].T
        lane = lax.broadcasted_iota(jnp.int32, small.shape, 1)
        shift_total = shift_total.reshape(blocks, 3, part // 3, 128)
        for n, kind in enumerate((0, 2)):
            column = shift_total[:, kind].reshape(-1, 128)[:width]
            small = jnp.where(lane == 126 + n, column, small)
        made[number - 1][...] = small.reshape(made[number - 1].shape).astype(BF)

    stages = 3 + 2 * rounds
    for turn in range(number + stages - 1):
        for p in range(number):
            if 0 < turn - p < stages:
                run(p, turn - p)
        if turn < number:
            if turn == 1:
                norm_rows()
            if 0 < turn < number - 1:
                weight_part(turn - 1)
            if turn == number - 1:
                finish_rows()
            run(turn, 0)
    for p in range(number):
        for copy in [mate_copy(p)] + chip_copies(p):
            copy.wait_send()
        for r in range(rounds):
            line_copy(p, r).wait_send()
            back_copy(p, r, False).wait_send()


def run_close(
    out_term,
    long_back,
    short_back,
    long_tokens,
    short_tokens,
    vectors,
    weights,
    grad_middle,
    sums,
    centroid_term,
    experts,
    blocks,
):
    width = out_term.shape[0]
    rows = width // experts
    chips = experts // 2
    rounds = (blocks - 1).bit_length()
    part = weights.shape[2]
    count = grad_middle.shape[0]
    widths = [width] + [2 * part] * (blocks // 2) + [128]
    number = len(widths)
    groups = [-(-w // 128 // blocks) * blocks for w in widths]
    dma = pltpu.SemaphoreType.DMA
    vmem = pl.BlockSpec(memory_space=pltpu.VMEM)
    return pl.pallas_call(
        functools.partial(close_kernel, experts, blocks),
        in_specs=[vmem] + [pl.BlockSpec(memory_space=pl.ANY)] * 4 + [vmem] * 5,
        out_specs=(vmem,) * (1 + number),
        out_shape=(jax.ShapeDtypeStruct((count, width), F32),)
        + tuple(jax.ShapeDtypeStruct((rows, w), F32) for w in widths),
        scratch_shapes=[pltpu.VMEM((chips, 2, rows, w), BF) for w in widths[1:]]
        + [pltpu.VMEM((chips, rows, w), BF) for w in widths]
        + [pltpu.VMEM((chips, rows, w), BF) for w in widths]
        + [pltpu.VMEM((chips - 1, rows, w), BF) for w in widths]
        + [pltpu.VMEM((g, rows, 128), BF) for g in groups]
        + [pltpu.VMEM((rounds, g // 2, rows, 128), BF) for g in groups]
        + [pltpu.VMEM((g, rows, 128), BF) for g in groups]
        + [
            pltpu.VMEM((width, count), BF),
            pltpu.VMEM((128, width), F32),
            pltpu.VMEM((2,) + long_tokens.shape, BF),
            pltpu.VMEM((2,) + long_back.shape, BF),
            dma((4,)),
        ]
        + [dma((number,)), dma((number,)), dma((number, chips)), dma((number, chips))]
        + [dma((number, rounds))] * 4,
        compiler_params=pltpu.CompilerParams(
            collective_id=2, has_side_effects=True, vmem_limit_bytes=60 << 20
        ),
    )(
        out_term.reshape(chips, 2, rows, width),
        long_back,
        short_back,
        long_tokens,
        short_tokens,
        vectors,
        weights,
        grad_middle,
        sums,
        centroid_term,
    )


def on_device(
    tokens,
    doc_ids,
    routes,
    ln1_gain,
    ln1_bias,
    qkv_weight,
    qv_bias,
    out_weight,
    out_bias,
    ln2_gain,
    ln2_bias,
    centroids,
    up_weight,
    up_bias,
    down_weight,
    down_bias,
    cotangent,
):
    rows, span, width = tokens.shape
    heads = HEADS
    size = width // heads
    blocks = lax.axis_size("blk")
    own = lax.axis_index("blk")
    count = rows * span
    length = blocks * span
    halo = min(SHORT, span)
    share = -(-heads // blocks)
    pad_heads = share * blocks - heads

    expert_count = centroids.shape[0]

    long_at = (doc_ids[0, -1] != 0).astype(jnp.int32)

    def ordered(pair):
        first = lax.dynamic_index_in_dim(pair, long_at, 0, keepdims=False)
        second = lax.dynamic_index_in_dim(pair, 1 - long_at, 0, keepdims=False)
        return jnp.stack([first, second])

    long_tokens = lax.dynamic_index_in_dim(tokens, long_at, 0, keepdims=False)
    short_tokens = lax.dynamic_index_in_dim(tokens, 1 - long_at, 0, keepdims=False)
    token_rows = jnp.concatenate([long_tokens, short_tokens]).astype(F32)

    capacity = 2 * count // expert_count
    slots = expert_count * capacity
    slot_line = jnp.arange(slots, dtype=jnp.int32)
    vectors = jnp.concatenate(
        [
            ln1_gain[None],
            ln1_bias[None],
            ln2_gain[None],
            ln2_bias[None],
            jnp.zeros((4, width), F32),
        ]
    )

    def grouped(matrix):
        lead = matrix.shape[0]
        split = matrix.reshape(lead, 3, heads, size)
        split = jnp.pad(split, ((0, 0), (0, 0), (0, pad_heads), (0, 0)))
        split = split.reshape(lead, 3, blocks, share, size).transpose(2, 0, 1, 3, 4)
        return split.reshape(blocks, lead, 3 * share * size)

    def ungrouped(matrix):
        lead = matrix.shape[0]
        split = matrix.reshape(lead, blocks, 3, share, size).transpose(0, 2, 1, 3, 4)
        return split.reshape(lead, 3, blocks * share, size)[:, :, :heads].reshape(lead, 3, width)

    short_ids = jnp.concatenate(
        [
            jnp.full((halo,), -1, jnp.int32),
            lax.dynamic_index_in_dim(doc_ids, 1 - long_at, 0, keepdims=False),
        ]
    )
    short_ids = lax.dynamic_slice_in_dim(short_ids, own * span, halo + span, 0)
    key_ids = short_ids[:, None]
    query_ids = short_ids[None, halo:]
    shifts = jnp.concatenate([qv_bias[0], jnp.zeros((width,), F32), qv_bias[1]])
    full_qkv, full_out, rest = run_front(
        grouped(qkv_weight),
        out_weight,
        long_tokens,
        short_tokens,
        cotangent.reshape(count, width),
        routes.reshape(1, count),
        vectors,
        grouped(shifts[None]),
        key_ids,
        query_ids,
        expert_count,
        blocks,
    )
    (
        received_cot,
        slot_of,
        long_attended,
        long_qkv,
        long_wide,
        long_total,
        short_qkv,
        short_wide,
        short_low,
        short_total,
    ) = rest
    long_attended = long_attended.reshape(-1, span)[:width]
    attended_t = jnp.concatenate([long_attended, short_low], axis=1)
    slot_of = ordered(slot_of.reshape(rows, span)).reshape(count)
    route_flat = ordered(routes.reshape(rows, span)).reshape(count)
    grad_low = ordered(cotangent).reshape(count, width)

    middle = (
        token_rows
        + lax.dot_general(
            attended_t, full_out, (((0,), (0,)), ((), ())), preferred_element_type=F32
        )
        + out_bias
    )
    to_slots = (slot_line[:, None] == slot_of[None, :]).astype(BF)
    expert_in = layer_norm(middle, ln2_gain, ln2_bias).astype(BF)
    outgoing = dot_nn(to_slots, expert_in).astype(BF).reshape(expert_count, capacity, width)

    own_centroid = lax.dynamic_index_in_dim(
        centroids.astype(F32), lax.axis_index("expert"), 0, keepdims=True
    )
    back_grad, produced, up_first, down_first, up_rest, down_rest, up_shift, down_shift = run_expert(
        outgoing,
        received_cot,
        up_weight[0],
        down_weight[0],
        up_bias,
        down_bias,
        own_centroid,
        blocks,
    )
    shift_parts = jnp.concatenate([up_shift, down_shift.reshape(blocks, 1, -1)], axis=2)
    shift_parts = jnp.pad(shift_parts, ((0, 0), (0, 0), (0, -shift_parts.shape[2] % 128)))
    (
        long_back,
        short_back,
        grad_middle,
        result,
        out_term,
        tail_sums,
        centroid_term,
        up_sum,
        down_sum,
        shift_sum,
    ) = run_tail(
        back_grad.reshape(slots, width),
        slot_of[:, None],
        route_flat[:, None],
        middle,
        grad_low,
        vectors,
        centroids.astype(F32),
        long_attended,
        short_low,
        full_out,
        (long_qkv, long_wide, long_total),
        (short_qkv, short_wide, short_total),
        key_ids,
        query_ids,
        produced,
        up_rest,
        down_rest,
        up_first,
        down_first,
        shift_parts,
        blocks,
    )
    grad_tokens, out_sum, *qkv_sums, small_sum = run_close(
        out_term,
        long_back,
        short_back,
        long_tokens,
        short_tokens,
        vectors,
        full_qkv,
        grad_middle,
        tail_sums,
        centroid_term,
        expert_count,
        blocks,
    )
    qkv_sum = jnp.concatenate(qkv_sums, axis=1)
    norm_at = 8 + expert_count
    shift_cut = up_bias.shape[1] // blocks
    up_shift_sum = shift_sum[:, :shift_cut]
    down_shift_sum = shift_sum[:, shift_cut : shift_cut + width // blocks]
    return (
        ordered(result.reshape(rows, span, width)),
        ordered(grad_tokens.reshape(rows, span, width)),
        small_sum[:, norm_at],
        small_sum[:, norm_at + 1],
        ungrouped(qkv_sum).reshape(-1, 3 * width),
        small_sum[:, 126:].T,
        out_sum,
        small_sum[:, 2],
        small_sum[:, 0],
        small_sum[:, 1],
        small_sum[:, 8:norm_at].T,
        up_sum[None],
        up_shift_sum,
        down_sum[None],
        down_shift_sum,
    )


def solution(mesh):
    return jax.shard_map(
        on_device,
        mesh=mesh,
        in_specs=(
            P("expert", "blk", None),
            P("expert", None),
            P("blk", "expert", None, None),
            P(),
            P(),
            P("expert", None),
            P(),
            P("expert", None),
            P(),
            P(),
            P(),
            P(),
            P("expert", None, None),
            P("expert", None),
            P("expert", None, None),
            P("expert", None),
            P("expert", "blk", None),
        ),
        out_specs=(
            P("expert", "blk", None),
            P("expert", "blk", None),
            P("expert"),
            P("expert"),
            P("expert", None),
            P(None, "expert"),
            P("expert", None),
            P("expert"),
            P("expert"),
            P("expert"),
            P(None, "expert"),
            P("expert", "blk", None),
            P("expert", "blk"),
            P("expert", "blk", None),
            P("expert", "blk"),
        ),
        check_vma=False,
    )
```

```python
import functools

import jax
import jax.numpy as jnp
from jax import lax
from jax.experimental import pallas as pl
from jax.experimental.pallas import tpu as pltpu
from jax.sharding import PartitionSpec as P

HEADS = 12
SHORT = 256
NEGATIVE = -1e30
EPSILON = 1e-05
BF = jnp.bfloat16
F32 = jnp.float32


def dot_nn(a, b):
    return lax.dot_general(a, b, (((1,), (0,)), ((), ())), preferred_element_type=F32)


def dot_nt(a, b):
    return lax.dot_general(a, b, (((1,), (1,)), ((), ())), preferred_element_type=F32)


def norm_parts(values):
    average = jnp.mean(values, axis=-1, keepdims=True)
    centred = values - average
    variance = jnp.mean(centred * centred, axis=-1, keepdims=True)
    scale = lax.rsqrt(variance + EPSILON)
    return centred * scale, scale


def layer_norm(values, gain, bias):
    return norm_parts(values)[0] * gain + bias


def norm_back(upstream, normal, scale, gain):
    t = upstream * gain
    inner = (
        t
        - jnp.mean(t, axis=-1, keepdims=True)
        - normal * jnp.mean(t * normal, axis=-1, keepdims=True)
    )
    return inner * scale, jnp.sum(upstream * normal, axis=0), jnp.sum(upstream, axis=0)


def causal(rows, columns, shift):
    row = lax.broadcasted_iota(jnp.int32, (rows, columns), 0)
    column = lax.broadcasted_iota(jnp.int32, (rows, columns), 1)
    return row <= column + shift


def norm_low(values, gain, bias):
    return layer_norm(values.astype(F32), gain, bias).astype(BF)


def scaled(query):
    return (query.astype(F32) * query.shape[-1] ** (-0.5)).astype(BF)


def short_visible(key_ids, query_ids, i, block, halo):
    lo = i * block
    same = key_ids[lo : lo + halo + block] == query_ids[:, lo : lo + block]
    return same & causal(halo + block, block, halo)


MESH = pl.DeviceIdType.MESH


def remote(source, target, send_sem, recv_sem, device):
    return pltpu.make_async_remote_copy(
        src_ref=source,
        dst_ref=target,
        send_sem=send_sem,
        recv_sem=recv_sem,
        device_id=device,
        device_id_type=MESH,
    )


def across(place, mask, count):
    bit = 1
    while bit < count:
        place_bit, mask_bit = lax.rem(place // bit, 2), lax.rem(mask // bit, 2)
        place = place + bit * mask_bit * (1 - 2 * place_bit)
        bit *= 2
    return place


def greet(experts, blocks):
    me, z = lax.axis_index("expert"), lax.axis_index("blk")
    barrier = pltpu.get_barrier_semaphore()
    for d in range(1, experts):
        pl.semaphore_signal(
            barrier, inc=1, device_id={"expert": lax.rem(me + d, experts)}, device_id_type=MESH
        )
    for d in range(1, blocks):
        pl.semaphore_signal(
            barrier, inc=1, device_id={"blk": lax.rem(z + d, blocks)}, device_id_type=MESH
        )
    pl.semaphore_wait(barrier, experts + blocks - 2)


def front_kernel(
    experts,
    blocks,
    heads,
    gathers,
    block,
    short_block,
    qkv_ref,
    out_ref,
    row_ref,
    short_ref,
    cot_ref,
    route_ref,
    vectors,
    shift_ref,
    key_ids,
    query_ids,
    *refs,
):
    if gathers:
        (full_qkv, full_out), refs = refs[:2], refs[2:]
    else:
        full_qkv = qkv_ref
    (
        received_cot,
        slot_out,
        attended,
        long_qkv,
        long_wide,
        long_total,
        short_qkv,
        short_wide,
        short_low,
        short_total,
        weights,
        rows_buf,
        short_buf,
        long_store,
        short_store,
        low_stage,
        cot_stage,
        shard_send,
        shard_recv,
        row_send,
        row_recv,
        edge_sem,
        local_sem,
        cot_send,
        cot_recv,
        low_send,
        low_recv,
    ) = refs
    me, z = lax.axis_index("expert"), lax.axis_index("blk")
    step = pl.program_id(0)
    mate = me + 1 - 2 * lax.rem(me, 2)
    peers = [lax.rem(me + 2 * d, experts) for d in range(1, experts // 2)]
    share, size = long_store.shape[1], long_store.shape[3]
    length = blocks * block
    span = block
    halo = short_buf.shape[0] - span
    shard_rows = qkv_ref.shape[1]

    def qkv_part(slot):
        return full_qkv.at[:, pl.ds(pl.multiple_of(slot * shard_rows, shard_rows), shard_rows)]

    def shard(n, own, slot, turn, target):
        part = (qkv_part(slot), full_out.at[slot])[n]
        source = (qkv_ref, out_ref)[n] if own else part
        return remote(
            source, part, shard_send.at[n, turn], shard_recv.at[n, slot], {"expert": target}
        )

    def row(slot, turn, target):
        return remote(
            rows_buf.at[slot],
            rows_buf.at[slot],
            row_send.at[turn],
            row_recv.at[slot],
            {"blk": target},
        )

    def own_row(turn, target):
        return remote(
            row_ref, rows_buf.at[z], row_send.at[turn], row_recv.at[z], {"blk": target}
        )

    to_right, to_left = z + 1 < blocks, z > 0
    right, left = lax.rem(z + 1, blocks), lax.rem(z + blocks - 1, blocks)
    last_rows = short_ref.at[pl.ds(span - halo, halo)]
    halo_rows = short_buf.at[pl.ds(0, halo)]
    edge = remote(last_rows, halo_rows, edge_sem.at[0], edge_sem.at[1], {"blk": right})
    no_edge = pltpu.make_async_copy(last_rows, halo_rows, edge_sem.at[1])
    local = [
        pltpu.make_async_copy(row_ref, rows_buf.at[z], local_sem.at[0]),
        pltpu.make_async_copy(short_ref, short_buf.at[pl.ds(halo, span)], local_sem.at[1]),
    ]
    own_cot = pltpu.make_async_copy(cot_stage.at[me], received_cot.at[me], local_sem.at[2])
    load_weights = pltpu.make_async_copy(full_qkv, weights, local_sem.at[3])
    own_shards = []
    sent = []
    handed = []
    if gathers:
        own_shards = [
            pltpu.make_async_copy(qkv_ref, qkv_part(me), local_sem.at[4]),
            pltpu.make_async_copy(out_ref, full_out.at[me], local_sem.at[5]),
        ]
        for n in range(2):
            for turn, peer in enumerate(peers):
                sent.append(shard(n, True, me, turn, peer))
            sent.append(shard(n, True, me, len(peers), mate))
            for turn, peer in enumerate(peers):
                handed.append(shard(n, False, peer, len(peers) + 1 + turn, mate))

    def cot_copy(d):
        target = lax.rem(me + d, experts)
        return remote(
            cot_stage.at[target],
            received_cot.at[me],
            cot_send.at[d],
            cot_recv.at[d],
            {"expert": target},
        )

    def low_copy(head, d):
        target = lax.rem(z + d, blocks)
        return remote(
            low_stage.at[target, head],
            attended.at[z, head],
            low_send.at[head, d],
            low_recv.at[head, d],
            {"blk": target},
        )

    def low_local(head):
        return pltpu.make_async_copy(
            low_stage.at[z, head], attended.at[z, head], low_send.at[head, 0]
        )

    def hand_on(k):
        @pl.when(z - k >= 0)
        def _():
            slot = jnp.maximum(z - k, 0)
            row(slot, 2 * k, right).wait_recv()

            @pl.when(to_right)
            def _():
                row(slot, 2 * k, right).start()

        @pl.when(z + k < blocks)
        def _():
            slot = jnp.minimum(z + k, blocks - 1)
            row(slot, 2 * k + 1, left).wait_recv()

            @pl.when(to_left)
            def _():
                row(slot, 2 * k + 1, left).start()

    def project(source, rows, groups, store):
        low = norm_low(source, vectors[0:1], vectors[1:2])
        for n, group in enumerate(groups):
            part = (dot_nn(low, weights[group]) + shift_ref[group]).astype(BF)
            for kind in range(3):
                for head in range(share):
                    at = (kind * share + head) * size
                    if n * share + head < store.shape[1]:
                        store[kind, n * share + head, rows] = part[:, at : at + size]

    def sort_cot():
        capacity, width = cot_stage.shape[1:]
        count = cot_ref.shape[0]
        lines = -(-experts // 8) * 8
        expert_line = lax.broadcasted_iota(jnp.int32, (lines, count), 0)
        named = (route_ref[...] == expert_line).astype(F32)
        upto = lax.broadcasted_iota(jnp.int32, (count, count), 0) <= lax.broadcasted_iota(
            jnp.int32, (count, count), 1
        )
        ranks = dot_nn(named.astype(BF), upto.astype(F32).astype(BF))
        slots = named * (ranks - 1.0 + (expert_line * capacity).astype(F32))
        slots = jnp.sum(slots, axis=0, keepdims=True).astype(jnp.int32)
        slot_out[...] = slots
        flat = cot_stage.reshape(experts * capacity, width)
        block_rows = min(512, experts * capacity)

        @pl.loop(0, experts * capacity // block_rows)
        def _(turn):
            first = pl.multiple_of(turn * block_rows, block_rows)
            line = lax.broadcasted_iota(jnp.int32, (block_rows, count), 0) + first
            chosen = (line == slots).astype(F32).astype(BF)
            flat[pl.ds(first, block_rows)] = dot_nn(chosen, cot_ref[...]).astype(BF)

    @pl.when(step == 0)
    def _():
        for copy in local + own_shards:
            copy.start()
        greet(experts, blocks)

        @pl.when(to_right)
        def _():
            own_row(0, right).start()
            edge.start()

        @pl.when(to_left)
        def _():
            own_row(1, left).start()

        @pl.when(jnp.logical_not(to_left))
        def _():
            no_edge.start()

        for copy in sent:
            copy.start()
        sort_cot()
        hand_on(1)
        for copy in handed:
            copy.wait_recv()
            copy.start()
        if gathers:
            for turn in range(experts // 2):
                for n in range(2):
                    shard(n, False, lax.rem(mate + 2 * turn, experts), 0, mate).wait_recv()
        for copy in own_shards:
            copy.wait()
        load_weights.start()
        own_cot.start()
        for d in range(1, experts):
            cot_copy(d).start()

        @pl.when(to_left)
        def _():
            edge.wait_recv()

        @pl.when(jnp.logical_not(to_left))
        def _():
            no_edge.wait()

        for copy in local:
            copy.wait()
        load_weights.wait()

        @pl.loop(0, (halo + span) // short_block)
        def _(turn):
            rows = pl.ds(pl.multiple_of(turn * short_block, short_block), short_block)
            project(short_buf[rows], rows, range(blocks), short_store)

    for k in range(2, blocks):

        @pl.when(step == (k - 1) * heads // (blocks - 1))
        def _(k=k):
            hand_on(k)

    @pl.when(step < heads)
    def _():
        query, key, value = (short_store[kind, step] for kind in range(3))
        for kind, part in enumerate((query, key, value)):
            short_qkv[kind, 0] = part
        query = scaled(query)
        value_t = value.T
        for i in range(span // short_block):
            lo, hi = i * short_block, (i + 1) * short_block
            visible = short_visible(key_ids[...], query_ids[...], i, short_block, halo)
            scores = dot_nt(key[lo : hi + halo], query[lo + halo : hi + halo])
            scores = jnp.where(visible, scores, NEGATIVE)
            top = jnp.max(scores, axis=0, keepdims=True)
            scores = jnp.exp(scores - top)
            total = jnp.sum(scores, axis=0, keepdims=True)
            out = dot_nn(value_t[:, lo : hi + halo], scores.astype(BF)) / total
            short_wide[:, lo:hi] = out
            short_low[:, lo:hi] = out.astype(BF)
            short_total[0, :, lo:hi] = top + jnp.log(total)

    @pl.when(step == heads)
    def _():
        @pl.loop(0, blocks)
        def _(slot):
            rows = pl.ds(pl.multiple_of(slot * block, block), block)
            project(rows_buf[slot], rows, [z], long_store)

    @pl.when(step >= heads)
    def _():
        head = step - heads
        query, key, value = (long_store[kind, head] for kind in range(3))
        for kind, part in enumerate((query, key, value)):
            long_qkv[kind, 0] = part
        query = scaled(query)
        value_t = value.T
        visible = causal(block, block, 0)
        for i in range(blocks):
            lo, hi = i * block, (i + 1) * block
            own = query[lo:hi]
            near = jnp.where(visible, dot_nt(key[lo:hi], own), NEGATIVE)
            top = jnp.max(near, axis=0, keepdims=True)
            if i:
                far = dot_nt(key[:lo], own)
                top = jnp.maximum(top, jnp.max(far, axis=0, keepdims=True))
            near = jnp.exp(near - top)
            total = jnp.sum(near, axis=0, keepdims=True)
            out = dot_nn(value_t[:, lo:hi], near.astype(BF))
            if i:
                far = jnp.exp(far - top)
                total = total + jnp.sum(far, axis=0, keepdims=True)
                out = out + dot_nn(value_t[:, :lo], far.astype(BF))
            out = out / total
            long_wide[:, lo:hi] = out
            low_stage[i, head] = out.astype(BF)
            long_total[0, :, lo:hi] = top + jnp.log(total)
        low_local(head).start()
        for d in range(1, blocks):
            low_copy(head, d).start()

    @pl.when(step == heads + share - 1)
    def _():
        for head in range(share):
            low_local(head).wait()
            for d in range(1, blocks):
                low_copy(head, d).wait()
        own_cot.wait()
        for d in range(1, experts):
            cot_copy(d).wait()
        for copy in sent + handed:
            copy.wait_send()

        @pl.when(to_right)
        def _():
            own_row(0, right).wait_send()
            edge.wait_send()

        @pl.when(to_left)
        def _():
            own_row(1, left).wait_send()

        for k in range(1, blocks):

            @pl.when((z - k >= 0) & to_right)
            def _(k=k):
                row(jnp.maximum(z - k, 0), 2 * k, right).wait_send()

            @pl.when((z + k < blocks) & to_left)
            def _(k=k):
                row(jnp.minimum(z + k, blocks - 1), 2 * k + 1, left).wait_send()


def run_front(
    qkv_shard, out_shard, row, short_row, cot, routes, vectors, shifts, key_ids, query_ids, experts, blocks
):
    span, width = row.shape
    size = width // HEADS
    halo = key_ids.shape[0] - span
    part = qkv_shard.shape[2]
    share = part // size // 3
    length = blocks * span
    sorted_shape = (experts, 2 * cot.shape[0] // experts, width)
    gathers = qkv_shard.shape[1] % 16 == 0
    if not gathers:
        qkv_shard = lax.all_gather(qkv_shard, "expert", axis=1, tiled=True)
        full_out = lax.all_gather(out_shard, "expert", axis=0, tiled=True)
    any_spec = pl.BlockSpec(memory_space=pl.ANY)
    dma = pltpu.SemaphoreType.DMA

    def whole(shape):
        return pl.BlockSpec(shape, lambda f: (0,) * len(shape), pipeline_mode=pl.Buffered(1))

    def short_head(*shape):
        return pl.BlockSpec(
            shape, lambda f: (0,) * (len(shape) - 3) + (jnp.minimum(f, HEADS - 1), 0, 0)
        )

    def long_head(*shape):
        return pl.BlockSpec(
            shape, lambda f: (0,) * (len(shape) - 3) + (jnp.maximum(f - HEADS, 0), 0, 0)
        )

    def flat_short(*shape):
        return pl.BlockSpec(shape, lambda f: (jnp.minimum(f, HEADS - 1), 0))

    gathered_shapes = (
        jax.ShapeDtypeStruct((blocks, width, part), BF),
        jax.ShapeDtypeStruct((experts,) + out_shard.shape, BF),
    )
    results = pl.pallas_call(
        functools.partial(
            front_kernel, experts, blocks, HEADS, gathers, span, min(SHORT, span)
        ),
        grid=(HEADS + share,),
        in_specs=[any_spec] * 4
        + [
            whole(cot.shape),
            whole(routes.shape),
            whole(vectors.shape),
            whole((blocks, 1, part)),
            whole((halo + span, 1)),
            whole((1, span)),
        ],
        out_specs=((any_spec,) * 2 if gathers else ())
        + (
            any_spec,
            whole(routes.shape),
            any_spec,
            long_head(3, 1, length, size),
            pl.BlockSpec((size, length), lambda f: (jnp.maximum(f - HEADS, 0), 0)),
            long_head(1, 1, length),
            short_head(3, 1, halo + span, size),
            flat_short(size, span),
            flat_short(size, span),
            short_head(1, 1, span),
        ),
        out_shape=(gathered_shapes if gathers else ())
        + (
            jax.ShapeDtypeStruct(sorted_shape, BF),
            jax.ShapeDtypeStruct(routes.shape, jnp.int32),
            jax.ShapeDtypeStruct((blocks, share, size, span), BF),
            jax.ShapeDtypeStruct((3, share, length, size), BF),
            jax.ShapeDtypeStruct((share * size, length), F32),
            jax.ShapeDtypeStruct((share, 1, length), F32),
            jax.ShapeDtypeStruct((3, HEADS, halo + span, size), BF),
            jax.ShapeDtypeStruct((width, span), F32),
            jax.ShapeDtypeStruct((width, span), BF),
            jax.ShapeDtypeStruct((HEADS, 1, span), F32),
        ),
        scratch_shapes=[
            pltpu.VMEM((blocks, width, part), BF),
            pltpu.VMEM((blocks, span, width), BF),
            pltpu.VMEM((halo + span, width), BF),
            pltpu.VMEM((3, share, length, size), BF),
            pltpu.VMEM((3, HEADS, halo + span, size), BF),
            pltpu.VMEM((blocks, share, size, span), BF),
            pltpu.VMEM(sorted_shape, BF),
            dma((2, experts)),
            dma((2, experts)),
            dma((2 * blocks,)),
            dma((blocks,)),
            dma((2,)),
            dma((6,)),
            dma((experts,)),
            dma((experts,)),
            dma((share, blocks)),
            dma((share, blocks)),
        ],
        compiler_params=pltpu.CompilerParams(
            collective_id=0, has_side_effects=True, vmem_limit_bytes=56 << 20
        ),
    )(qkv_shard, out_shard, row, short_row, cot, routes, vectors, shifts, key_ids, query_ids)
    if gathers:
        return results[0], results[1].reshape(-1, out_shard.shape[1]), results[2:]
    return qkv_shard, full_out, results


def line_sums(z, blocks, up_held, down_held, part_send, part_recv, put):
    rounds = len(up_held) - 1

    def part_copies(r, p):
        bit = 1 << r
        mine = lax.rem(z // bit, 2)
        partner = z + bit - 2 * bit * mine
        copies = []
        for k in range((blocks >> r) // 2):
            for n, held in enumerate((up_held, down_held)):
                copies.append(
                    remote(
                        held[r].at[p, 2 * k + 1 - mine],
                        held[r + 1].at[p, k],
                        part_send.at[r, n, p, k],
                        part_recv.at[r, n, p, k],
                        {"blk": partner},
                    )
                )
        return copies

    def add_parts(r, p):
        mine = lax.rem(z // (1 << r), 2)
        for copy in part_copies(r, p):
            copy.wait_recv()
        for k in range((blocks >> r) // 2):
            up = up_held[r][p, 2 * k + mine].astype(F32) + up_held[r + 1][p, k].astype(F32)
            down = down_held[r][p, 2 * k + mine].astype(F32) + down_held[r + 1][p, k].astype(F32)
            if r + 1 < rounds:
                up_held[r + 1][p, k] = up.astype(BF)
                down_held[r + 1][p, k] = down.astype(BF)
            else:
                put(p, up, down.T)
        if r + 1 < rounds:
            for copy in part_copies(r + 1, p):
                copy.start()

    return part_copies, add_parts


def late_sums(up_last, down_last, up_sum, down_sum, put_sem, first_part, steps):
    lanes = down_last.shape[1]
    blocks = up_last.shape[1]

    def put_copies(p):
        copies = []
        for j in range(blocks):
            first = (j * steps + first_part + p) * lanes
            copies.append(
                pltpu.make_async_copy(
                    up_last.at[p, j], up_sum.at[:, pl.ds(first, lanes)], put_sem.at[p, j]
                )
            )
        copies.append(
            pltpu.make_async_copy(
                down_last.at[p],
                down_sum.at[pl.ds((first_part + p) * lanes, lanes)],
                put_sem.at[p, blocks],
            )
        )
        return copies

    def put(p, up, down):
        for j in range(blocks):
            up_last[p, j] = up[:, j * lanes : (j + 1) * lanes]
        down_last[p] = down
        for copy in put_copies(p):
            copy.start()

    return put, put_copies


def sum_scratch(parts, blocks, depth, width, first):
    rounds = (blocks - 1).bit_length()
    lanes = 128
    dma = pltpu.SemaphoreType.DMA
    return (
        [
            pltpu.VMEM((parts, blocks >> r, depth, blocks * lanes), BF)
            for r in range(first, rounds + 1)
        ]
        + [pltpu.VMEM((parts, blocks >> r, width, lanes), BF) for r in range(first, rounds + 1)]
        + [dma((rounds, 2, parts, blocks // 2)), dma((rounds, 2, parts, blocks // 2))]
    )


def gelu_parts(hidden):
    cdf = 0.5 * (1.0 + lax.erf(hidden * 0.7071067811865476))
    density = jnp.exp(-0.5 * hidden * hidden) * 0.3989422804014327
    return hidden * cdf, cdf + hidden * density


def expert_kernel(
    experts,
    blocks,
    steps,
    rest,
    chunk,
    x_hbm,
    cot_hbm,
    *refs,
):
    ups, refs = refs[:blocks], refs[blocks:]
    downs, refs = refs[:blocks], refs[blocks:]
    up_shifts, refs = refs[:blocks], refs[blocks:]
    (
        down_shift_ref,
        centroid_ref,
        back_grad,
        produced,
        up_sum,
        down_sum,
        up_rest,
        down_rest,
        up_shift_out,
        down_shift_out,
        x_buf,
        low_buf,
        xt_ref,
        gt_ref,
        out_acc,
        grad_acc,
        gate_ref,
        up_acc,
        down_acc,
        shift_acc,
        x_send,
        x_recv,
        back_send,
        back_recv,
        local_sem,
        *refs,
    ) = refs
    rounds = (blocks - 1).bit_length()
    up_held, down_held = refs[: rounds + 1], refs[rounds + 1 : 2 * rounds + 2]
    part_send, part_recv = refs[2 * rounds + 2 :]
    step = pl.program_id(0)
    me, z = lax.axis_index("expert"), lax.axis_index("blk")
    capacity, width = x_buf.shape[1:]
    rows = experts * capacity
    lanes = 128
    sources, chunks = chunk // capacity, rows // chunk

    def x_copy(d):
        target = across(me, jnp.int32(d), experts)
        return remote(
            x_hbm.at[target], x_buf.at[me], x_send.at[d], x_recv.at[d], {"expert": target}
        )

    def back_copy(d):
        target = across(me, jnp.int32(d), experts)
        return remote(
            low_buf.at[target],
            back_grad.at[me],
            back_send.at[d],
            back_recv.at[d],
            {"expert": target},
        )

    back_local = pltpu.make_async_copy(low_buf.at[me], back_grad.at[me], local_sem.at[0])
    out_copy = pltpu.make_async_copy(x_buf, produced, local_sem.at[1])


    def put(p, up, down):
        for j in range(blocks):
            first = (j * steps + p) * lanes
            up_sum[:, first : first + lanes] = up[:, j * lanes : (j + 1) * lanes]
        down_sum[p * lanes : (p + 1) * lanes] = down

    part_copies, add_parts = line_sums(
        z, blocks, up_held, down_held, part_send, part_recv, put
    )
    cot_copy = pltpu.make_async_copy(cot_hbm, low_buf, local_sem.at[2])
    own_copy = pltpu.make_async_copy(x_hbm.at[me], x_buf.at[me], local_sem.at[3])
    x_flat, low_flat = x_buf.reshape(rows, width), low_buf.reshape(rows, width)

    @pl.when(step == 0)
    def _():
        barrier = pltpu.get_barrier_semaphore()
        for d in range(1, experts):
            pl.semaphore_signal(
                barrier, inc=1, device_id={"expert": lax.rem(me + d, experts)}, device_id_type=MESH
            )
        for r in range(rounds):
            bit = 1 << r
            partner = z + bit - 2 * bit * lax.rem(z // bit, 2)
            pl.semaphore_signal(barrier, inc=1, device_id={"blk": partner}, device_id_type=MESH)
        cot_copy.start()
        own_copy.start()
        pl.semaphore_wait(barrier, experts - 1 + rounds)
        for d in range(1, experts):
            x_copy(d).start()
        up_sum[...] = jnp.zeros_like(up_sum)
        down_sum[...] = jnp.zeros_like(down_sum)
        out_acc[...] = jnp.zeros_like(out_acc)
        grad_acc[...] = jnp.zeros_like(grad_acc)
        cot_copy.wait()
        own_copy.wait()
        down_shift_out[...] = jnp.zeros_like(down_shift_out)

    def prepare(at, near):
        for n in range(sources):
            d = near * sources + n

            @pl.when(d != 0)
            def _(d=d):
                x_copy(d).wait_recv()

        x = x_flat[at]
        logit = jnp.sum(x.astype(F32) * centroid_ref[...], axis=1, keepdims=True)
        gate = 1.0 / (1.0 + jnp.exp(-logit))
        gate_ref[at] = gate
        low = (low_flat[at].astype(F32) * gate).astype(BF)
        low_flat[at] = low
        xt_ref[:, at] = x.T
        gt_ref[:, at] = low.T
        down_shift_out[...] += jnp.sum(low.astype(F32), axis=0, keepdims=True)

    def answer(at, near):
        gate = gate_ref[at]
        out = (out_acc[at] + down_shift_ref[...]).astype(BF)
        inner = jnp.sum(low_flat[at].astype(F32) * out.astype(F32), axis=1, keepdims=True)
        x_flat[at] = out
        low_flat[at] = (grad_acc[at] + inner * (1.0 - gate) * centroid_ref[...]).astype(BF)
        for n in range(sources):
            d = near * sources + n

            @pl.when(d != 0)
            def _(d=d):
                back_copy(d).start()

    up = jnp.concatenate([ref[...] for ref in ups], axis=1)
    down = jnp.concatenate([ref[...] for ref in downs], axis=0)
    up_shift = jnp.concatenate([ref[...] for ref in up_shifts], axis=1)
    up_acc[...] = jnp.zeros_like(up_acc)
    down_acc[...] = jnp.zeros_like(down_acc)
    shift_acc[...] = jnp.zeros_like(shift_acc)

    @pl.loop(0, chunks)
    def _(turn):
        near = jnp.where(step == steps - 1, chunks - 1 - turn, turn)
        at = pl.ds(pl.multiple_of(across(me // sources, near, chunks) * chunk, chunk), chunk)

        @pl.when(step == 0)
        def _():
            prepare(at, near)

        x = x_flat[at]
        low = low_flat[at]
        hidden = dot_nn(x, up) + up_shift
        active, slope = gelu_parts(hidden)
        active = active.astype(BF)
        grad_low = (dot_nt(low, down) * slope).astype(BF)
        out_acc[at] += dot_nn(active, down)
        grad_acc[at] += dot_nt(grad_low, up)
        up_acc[...] += dot_nn(xt_ref[:, at], grad_low)
        down_acc[...] += dot_nn(gt_ref[:, at], active)
        shift_acc[...] += jnp.sum(grad_low.astype(F32), axis=0, keepdims=True)

        @pl.when(step == steps - 1)
        def _():
            answer(at, near)

    depth = width // blocks
    keep = steps - rest
    for j in range(blocks):
        up_shift_out[j] = shift_acc[:, j * lanes : (j + 1) * lanes]

    def store(up_target, down_target):
        for j in range(blocks):
            up_target[j] = up_acc[j * depth : (j + 1) * depth].astype(BF)
            down_target[j] = down_acc[:, j * lanes : (j + 1) * lanes].astype(BF)

    @pl.when(step < keep)
    def _():
        store(up_held[0].at[step], down_held[0].at[step])
        for copy in part_copies(0, step):
            copy.start()

    @pl.when(step >= keep)
    def _():
        store(up_rest.at[0], down_rest.at[0])

    tasks = sorted(
        ((r, p) for p in range(keep) for r in range(rounds)), key=lambda task: (sum(task), task[0])
    )
    early = [[] for _ in range(steps)]
    for turn, task in enumerate(tasks):
        at = 2 * (task[1] + 1) + 2 * task[0]
        if at < steps - 1:
            early[at].append(task)
    for at in range(steps):
        if early[at]:

            @pl.when(step == at)
            def _(at=at):
                for r, p in early[at]:
                    add_parts(r, p)

    @pl.when(step == steps - 1)
    def _():
        for d in range(1, experts):
            x_copy(d).wait_send()
        back_local.start()
        out_copy.start()
        for r, p in tasks:
            if all((r, p) not in done for done in early):
                add_parts(r, p)
        back_local.wait()
        out_copy.wait()
        for d in range(1, experts):
            back_copy(d).wait()
        for p in range(keep):
            for r in range(rounds):
                for copy in part_copies(r, p):
                    copy.wait_send()


def run_expert(x, cot, up_weight, down_weight, up_shift, down_shift, centroid, blocks):
    experts, capacity, width = x.shape
    rows = experts * capacity
    hidden = up_weight.shape[1]
    lanes = 128
    steps = hidden // blocks // lanes
    rounds = (blocks - 1).bit_length()
    chunk = min(512, rows)
    depth = width // blocks
    rest = steps // 3
    keep = steps - rest
    any_spec = pl.BlockSpec(memory_space=pl.ANY)

    def once(shape):
        return pl.BlockSpec(shape, lambda f: (0,) * len(shape), pipeline_mode=pl.Buffered(1))

    return pl.pallas_call(
        functools.partial(expert_kernel, experts, blocks, steps, rest, chunk),
        grid=(steps,),
        in_specs=[any_spec] * 2
        + [pl.BlockSpec((width, lanes), lambda f, j=j: (0, j * steps + f)) for j in range(blocks)]
        + [pl.BlockSpec((lanes, width), lambda f, j=j: (j * steps + f, 0)) for j in range(blocks)]
        + [pl.BlockSpec((1, lanes), lambda f, j=j: (0, j * steps + f)) for j in range(blocks)]
        + [once((1, width))] * 2,
        out_specs=(
            any_spec,
            any_spec,
            once((depth, hidden)),
            once((hidden // blocks, width)),
            pl.BlockSpec(
                (1, blocks, depth, blocks * lanes), lambda f: (jnp.maximum(f - keep, 0), 0, 0, 0)
            ),
            pl.BlockSpec(
                (1, blocks, width, lanes), lambda f: (jnp.maximum(f - keep, 0), 0, 0, 0)
            ),
            pl.BlockSpec((blocks, 1, lanes), lambda f: (0, 0, f)),
            once((1, width)),
        ),
        out_shape=(
            jax.ShapeDtypeStruct(x.shape, BF),
            jax.ShapeDtypeStruct(x.shape, BF),
            jax.ShapeDtypeStruct((depth, hidden), F32),
            jax.ShapeDtypeStruct((hidden // blocks, width), F32),
            jax.ShapeDtypeStruct((rest, blocks, depth, blocks * lanes), BF),
            jax.ShapeDtypeStruct((rest, blocks, width, lanes), BF),
            jax.ShapeDtypeStruct((blocks, 1, hidden // blocks), F32),
            jax.ShapeDtypeStruct((1, width), F32),
        ),
        scratch_shapes=[
            pltpu.VMEM(x.shape, BF),
            pltpu.VMEM(x.shape, BF),
            pltpu.VMEM((width, rows), BF),
            pltpu.VMEM((width, rows), BF),
            pltpu.VMEM((rows, width), F32),
            pltpu.VMEM((rows, width), F32),
            pltpu.VMEM((rows, 1), F32),
            pltpu.VMEM((width, blocks * lanes), F32),
            pltpu.VMEM((width, blocks * lanes), F32),
            pltpu.VMEM((1, blocks * lanes), F32),
            pltpu.SemaphoreType.DMA((experts,)),
            pltpu.SemaphoreType.DMA((experts,)),
            pltpu.SemaphoreType.DMA((experts,)),
            pltpu.SemaphoreType.DMA((experts,)),
            pltpu.SemaphoreType.DMA((4,)),
        ]
        + sum_scratch(keep, blocks, depth, width, 0),
        compiler_params=pltpu.CompilerParams(
            collective_id=1, has_side_effects=True, vmem_limit_bytes=62 << 20
        ),
        cost_estimate=pl.CostEstimate(
            flops=12 * rows * width * hidden, bytes_accessed=40 << 20, transcendentals=0
        ),
    )(
        x,
        cot,
        *([up_weight] * blocks),
        *([down_weight] * blocks),
        *([up_shift] * blocks),
        down_shift,
        centroid,
    )


def long_back_head(query, key, value, grad_ref, wide_ref, total_ref, out_ref, head, key_acc, value_acc):
    scale = query.shape[1] ** (-0.5)
    query = scaled(query)
    key_t = key.T
    count, _, _, block = grad_ref.shape
    visible = causal(block, block, 0)
    key_acc[...] = jnp.zeros_like(key_acc)
    value_acc[...] = jnp.zeros_like(value_acc)
    for i in range(count):
        lo, hi = i * block, (i + 1) * block
        own = query[lo:hi]
        grad_t = grad_ref[i, head]
        grad = grad_t.T
        delta = jnp.sum(grad_t.astype(F32) * wide_ref[:, lo:hi], axis=0, keepdims=True)
        total = total_ref[0, :, lo:hi]
        query_grad = None
        for start, stop in ((lo, hi), (0, lo)):
            if start == stop:
                continue
            weights = jnp.exp(dot_nt(key[start:stop], own) - total)
            if start == lo:
                weights = jnp.where(visible, weights, 0.0)
            scores = weights * (dot_nt(value[start:stop], grad) - delta)
            scores_low = scores.astype(BF)
            value_acc[start:stop] += dot_nn(weights.astype(BF), grad)
            key_acc[start:stop] += dot_nn(scores_low, own)
            part = dot_nn(key_t[:, start:stop], scores_low)
            query_grad = part if query_grad is None else query_grad + part
        out_ref[i, 0, head] = (query_grad * scale).astype(BF)
    key_grad = key_acc[...].T.astype(BF)
    value_grad = value_acc[...].T.astype(BF)
    for i in range(count):
        out_ref[i, 1, head] = key_grad[:, i * block : (i + 1) * block]
        out_ref[i, 2, head] = value_grad[:, i * block : (i + 1) * block]


def short_back_head(
    query, key, value, grad_t, wide_ref, total_ref, key_ids, query_ids, key_acc, value_acc, block
):
    scale = query.shape[1] ** (-0.5)
    query = scaled(query)
    key_t = key.T
    extent, span = query.shape[0], query_ids.shape[1]
    halo = extent - span
    key_acc[0:extent] = jnp.zeros((extent, key_acc.shape[1]), F32)
    value_acc[0:extent] = jnp.zeros((extent, key_acc.shape[1]), F32)
    query_grads = []
    for i in range(span // block):
        lo, hi = i * block, (i + 1) * block
        visible = short_visible(key_ids[...], query_ids[...], i, block, halo)
        own = query[lo + halo : hi + halo]
        part_t = grad_t[:, lo:hi]
        grad = part_t.T
        delta = jnp.sum(part_t.astype(F32) * wide_ref[:, lo:hi], axis=0, keepdims=True)
        scores = dot_nt(key[lo : hi + halo], own)
        weights = jnp.exp(jnp.where(visible, scores, NEGATIVE) - total_ref[0, :, lo:hi])
        scores = weights * (dot_nt(value[lo : hi + halo], grad) - delta)
        scores_low = scores.astype(BF)
        value_acc[lo : hi + halo] += dot_nn(weights.astype(BF), grad)
        key_acc[lo : hi + halo] += dot_nn(scores_low, own)
        part = dot_nn(key_t[:, lo : hi + halo], scores_low)
        query_grads.append(part * scale)
    query_grad = jnp.concatenate(query_grads, axis=1)
    return query_grad, key_acc[0:extent].T, value_acc[0:extent].T


def tail_kernel(
    experts,
    blocks,
    heads,
    lead,
    rest,
    back_grad,
    slot_ref,
    route_ref,
    middle_ref,
    cot_ref,
    vectors,
    centroid_ref,
    long_attended,
    short_attended,
    out_weight,
    long_qkv,
    long_wide,
    long_total,
    short_qkv,
    short_wide,
    short_total,
    key_ids,
    query_ids,
    produced,
    up_rest,
    down_rest,
    up_first,
    down_first,
    shift_ref,
    long_back,
    short_back,
    grad_middle,
    result_ref,
    out_term,
    sums_ref,
    centroid_out,
    up_sum,
    down_sum,
    shift_sum,
    grad_low,
    long_stage,
    short_grad,
    long_grad,
    back_stage,
    halo_stage,
    halo_in,
    own_edge,
    back_out,
    up_last,
    down_last,
    shift_in,
    key_acc,
    value_acc,
    out_send,
    out_recv,
    grad_send,
    grad_recv,
    back_send,
    back_recv,
    halo_send,
    halo_recv,
    shift_send,
    shift_recv,
    local_sem,
    put_sem,
    *refs,
):
    rounds = (blocks - 1).bit_length()
    up_held = (up_rest,) + refs[:rounds]
    down_held = (down_rest,) + refs[rounds : 2 * rounds]
    part_send, part_recv = refs[2 * rounds :]
    step = pl.program_id(0)
    me, z = lax.axis_index("expert"), lax.axis_index("blk")
    share, size, span = long_stage.shape[1:]
    width = out_weight.shape[0]
    count = slot_ref.shape[0]
    halo = halo_stage.shape[3]
    chunk = min(256, span)
    steps = up_sum.shape[1] // blocks // 128
    keep = steps - up_rest.shape[0]
    put, put_copies = late_sums(up_last, down_last, up_sum, down_sum, put_sem, keep, steps)
    part_copies, add_parts = line_sums(
        z, blocks, up_held, down_held, part_send, part_recv, put
    )
    line = [lax.rem(z + d, blocks) for d in range(blocks)]

    def out_copy(d):
        target = lax.rem(me + d, experts)
        return remote(
            produced.at[target], back_out.at[me], out_send.at[d], out_recv.at[d], {"expert": target}
        )

    def grad_copy(d):
        return remote(
            long_stage.at[line[d]], long_grad.at[z], grad_send.at[d], grad_recv.at[d], {"blk": line[d]}
        )

    def back_copy(head, d):
        return remote(
            back_stage.at[line[d], :, head],
            long_back.at[z, :, head],
            back_send.at[head, d],
            back_recv.at[head, d],
            {"blk": line[d]},
        )

    def back_local(head):
        return pltpu.make_async_copy(
            back_stage.at[z, :, head], long_back.at[z, :, head], back_send.at[head, 0]
        )

    def shift_copy(d):
        return remote(
            shift_ref.at[line[d]], shift_in.at[d], shift_send.at[d], shift_recv.at[d], {"blk": line[d]}
        )

    halo_parts = [part for part in ((0, lead), (lead, heads - lead)) if part[1]]

    def halo_copy(n):
        part = pl.ds(*halo_parts[n])
        left = lax.rem(z + blocks - 1, blocks)
        return remote(
            halo_stage.at[:, part], halo_in.at[:, part], halo_send.at[n], halo_recv.at[n], {"blk": left}
        )

    own_out_copy = pltpu.make_async_copy(produced.at[me], back_out.at[me], local_sem.at[0])

    def send_halo(n):
        @pl.when(z > 0)
        def _():
            halo_copy(n).start()

    @pl.when(step == 0)
    def _():
        greet(experts, blocks)
        for copy in part_copies(0, 0):
            copy.start()
        for d in range(1, blocks):
            shift_copy(d).start()
        own_out_copy.start()
        for d in range(1, experts):
            out_copy(d).start()
        spare = blocks * share - heads
        flat_stage = long_stage.reshape(blocks * share, size, span)
        if spare:
            flat_stage[heads:] = jnp.zeros((spare, size, span), BF)
            short_back[...] = jnp.zeros_like(short_back)
        slot_line = lax.broadcasted_iota(jnp.int32, (chunk, back_grad.shape[0]), 1)
        sums_ref[...] = jnp.zeros_like(sums_ref)

        def back_rows(turn, first, store):
            at = pl.multiple_of(turn * chunk, chunk)
            rows = pl.ds(pl.multiple_of(first + at, chunk), chunk)
            chosen = (slot_ref[rows] == slot_line).astype(F32).astype(BF)
            upstream = dot_nn(chosen, back_grad[...])
            normal, scale = norm_parts(middle_ref[rows])
            inner, gain_part, bias_part = norm_back(upstream, normal, scale, vectors[2:3])
            middle = cot_ref[rows].astype(F32) + inner
            grad_middle[rows] = middle
            low = middle.astype(BF)
            grad_low[rows] = low
            for n, part in enumerate((gain_part, bias_part, jnp.sum(middle, axis=0))):
                sums_ref[n] += part
            grad_t = dot_nt(out_weight[...], low).astype(BF).reshape(heads, size, chunk)
            store[:heads, :, pl.ds(at, chunk)] = grad_t

        pl.loop(0, span // chunk)(lambda turn: back_rows(turn, 0, flat_stage))
        for d in range(1, blocks):
            grad_copy(d).start()
        pl.loop(0, span // chunk)(lambda turn: back_rows(turn, span, short_grad))
        out_term[...] = (
            dot_nn(long_attended[...], grad_low[:span]) + dot_nn(short_attended[...], grad_low[span:])
        ).astype(BF)

    first_long = lead + 1
    is_long = (step >= first_long) & (step < first_long + share)

    @pl.when((step > 0) & jnp.logical_not(is_long))
    def _():
        head = step - 1 - jnp.where(step >= first_long, share, 0)
        query, key, value = (short_qkv[kind, 0] for kind in range(3))
        grads = short_back_head(
            query,
            key,
            value,
            short_grad[head],
            short_wide,
            short_total,
            key_ids,
            query_ids,
            key_acc,
            value_acc,
            min(SHORT, span),
        )
        group = head // share
        place = head - group * share
        for n, grad in enumerate(grads):
            short_back[group, n, place] = grad[:, grad.shape[1] - span :].astype(BF)
            if n:
                halo_stage[n - 1, head] = grad[:, :halo].astype(BF)
                own_edge[n - 1, head] = grad[:, span:]

    @pl.when(step == lead)
    def _():
        send_halo(0)

    @pl.when(step == first_long)
    def _():
        for d in range(1, blocks):
            grad_copy(d).wait_recv()
        long_grad[z] = long_stage[z]
        add_parts(0, 0)
        for p in range(1, rest):
            for copy in part_copies(0, p):
                copy.start()

    @pl.when(is_long)
    def _():
        head = step - first_long
        query, key, value = (long_qkv[kind, 0] for kind in range(3))
        long_back_head(
            query, key, value, long_grad, long_wide, long_total, back_stage, head, key_acc, value_acc
        )
        back_local(head).start()
        for d in range(1, blocks):
            back_copy(head, d).start()

    tasks = sorted(
        ((r, p) for p in range(rest) for r in range(rounds)), key=lambda task: (sum(task), task[0])
    )[1:]

    @pl.when(step == first_long + share)
    def _():
        for r, p in tasks[:-1]:
            add_parts(r, p)

    @pl.when(step == heads + share)
    def _():
        if len(halo_parts) > 1:
            send_halo(1)
        own_out_copy.wait()
        for d in range(1, experts):
            out_copy(d).wait_recv()
        answers = back_out.reshape(back_grad.shape)
        slot_line = lax.broadcasted_iota(jnp.int32, (chunk, back_grad.shape[0]), 1)
        expert_line = lax.broadcasted_iota(jnp.int32, (chunk, 128), 1)
        centroid_rows = jnp.concatenate(
            [centroid_ref[...], jnp.zeros((128 - experts, width), F32)], axis=0
        ).astype(BF)
        centroid_out[...] = jnp.zeros_like(centroid_out)

        @pl.loop(0, count // chunk)
        def _(turn):
            rows = pl.ds(pl.multiple_of(turn * chunk, chunk), chunk)
            chosen = (slot_ref[rows] == slot_line).astype(F32).astype(BF)
            answer = dot_nn(chosen, answers[...])
            middle = middle_ref[rows]
            normed = norm_parts(middle)[0] * vectors[2:3] + vectors[3:4]
            named = (route_ref[rows] == expert_line).astype(F32)
            logit = jnp.sum(
                normed * dot_nn(named.astype(BF), centroid_rows), axis=1, keepdims=True
            )
            gate = 1.0 / (1.0 + jnp.exp(-logit))
            result_ref[rows] = middle + gate * answer
            inner = jnp.sum(cot_ref[rows].astype(F32) * answer, axis=1, keepdims=True)
            part = lax.dot_general(
                named,
                inner * gate * (1.0 - gate) * normed,
                (((0,), (0,)), ((), ())),
                preferred_element_type=F32,
            )
            centroid_out[...] += part[:experts]

        if tasks:
            add_parts(*tasks[-1])
        for p in range(rest):
            for copy in put_copies(p):
                copy.wait()
        for d in range(1, blocks):
            shift_copy(d).wait()
        total = shift_ref[z]
        for d in range(1, blocks):
            total = total + shift_in[d]
        shift_sum[...] = total
        for d in range(1, experts):
            out_copy(d).wait_send()
        for d in range(1, blocks):
            grad_copy(d).wait_send()
        for head in range(share):
            back_local(head).wait()
            for d in range(1, blocks):
                back_copy(head, d).wait()
        for p in range(rest):
            for r in range(rounds):
                for copy in part_copies(r, p):
                    copy.wait_send()
        for n in range(len(halo_parts)):

            @pl.when(z > 0)
            def _(n=n):
                halo_copy(n).wait_send()

            @pl.when(z < blocks - 1)
            def _(n=n):
                halo_copy(n).wait_recv()

        @pl.when(z < blocks - 1)
        def _():
            for head in range(heads):
                for n in range(2):
                    edge = own_edge[n, head] + halo_in[n, head].astype(F32)
                    short_back[head // share, 1 + n, head % share, :, span - halo :] = edge.astype(BF)


def tail_share(rest):
    return (rest + 1) // 2


def run_tail(
    back_grad,
    slot_of,
    route_of,
    middle,
    cot,
    vectors,
    centroids,
    long_attended,
    short_attended,
    out_weight,
    long_parts,
    short_parts,
    key_ids,
    query_ids,
    produced,
    up_rest,
    down_rest,
    up_first,
    down_first,
    shifts,
    blocks,
):
    experts = produced.shape[0]
    slots, width = back_grad.shape
    count = slot_of.shape[0]
    long_qkv, long_wide, long_total = long_parts
    short_qkv, short_wide, short_total = short_parts
    _, share, length, size = long_qkv.shape
    extent, span = short_qkv.shape[2], query_ids.shape[1]
    halo = extent - span
    heads = HEADS
    lead = heads // 2
    depth = up_rest.shape[2]
    rest = tail_share(up_rest.shape[0])
    hidden = up_first.shape[1]
    any_spec = pl.BlockSpec(memory_space=pl.ANY)
    dma = pltpu.SemaphoreType.DMA

    def whole(shape):
        return pl.BlockSpec(shape, lambda f: (0,) * len(shape), pipeline_mode=pl.Buffered(1))

    def short_at(f):
        return jnp.where(f <= lead, jnp.maximum(f - 1, 0), jnp.maximum(f - 1 - share, lead - 1))

    def long_at(f):
        return jnp.clip(f - 1 - lead, 0, share - 1)

    return pl.pallas_call(
        functools.partial(tail_kernel, experts, blocks, heads, lead, rest),
        grid=(1 + heads + share,),
        in_specs=[
            whole(back_grad.shape),
            whole(slot_of.shape),
            whole(route_of.shape),
            whole(middle.shape),
            whole(cot.shape),
            whole(vectors.shape),
            whole(centroids.shape),
            whole(long_attended.shape),
            whole(short_attended.shape),
            whole(out_weight.shape),
            pl.BlockSpec((3, 1, length, size), lambda f: (0, long_at(f), 0, 0)),
            pl.BlockSpec((size, length), lambda f: (long_at(f), 0)),
            pl.BlockSpec((1, 1, length), lambda f: (long_at(f), 0, 0)),
            pl.BlockSpec((3, 1, extent, size), lambda f: (0, short_at(f), 0, 0)),
            pl.BlockSpec((size, span), lambda f: (short_at(f), 0)),
            pl.BlockSpec((1, 1, span), lambda f: (short_at(f), 0, 0)),
            whole(key_ids.shape),
            whole(query_ids.shape),
            any_spec,
            whole(up_rest.shape),
            whole(down_rest.shape),
            any_spec,
            any_spec,
            whole(shifts.shape),
        ],
        out_specs=(
            any_spec,
            whole((blocks, 3, share, size, span)),
            whole((count, width)),
            whole((count, width)),
            whole((width, width)),
            whole((8, width)),
            whole((experts, width)),
            any_spec,
            any_spec,
            whole(shifts.shape[1:]),
        ),
        out_shape=(
            jax.ShapeDtypeStruct((blocks, 3, share, size, span), BF),
            jax.ShapeDtypeStruct((blocks, 3, share, size, span), BF),
            jax.ShapeDtypeStruct((count, width), F32),
            jax.ShapeDtypeStruct((count, width), F32),
            jax.ShapeDtypeStruct((width, width), BF),
            jax.ShapeDtypeStruct((8, width), F32),
            jax.ShapeDtypeStruct((experts, width), F32),
            jax.ShapeDtypeStruct((depth, hidden), F32),
            jax.ShapeDtypeStruct((hidden // blocks, width), F32),
            jax.ShapeDtypeStruct(shifts.shape[1:], F32),
        ),
        scratch_shapes=[
            pltpu.VMEM((count, width), BF),
            pltpu.VMEM((blocks, share, size, span), BF),
            pltpu.VMEM((heads, size, span), BF),
            pltpu.VMEM((blocks, share, size, span), BF),
            pltpu.VMEM((blocks, 3, share, size, span), BF),
            pltpu.VMEM((2, heads, size, halo), BF),
            pltpu.VMEM((2, heads, size, halo), BF),
            pltpu.VMEM((2, heads, size, halo), F32),
            pltpu.VMEM(produced.shape, BF),
            pltpu.VMEM((rest, blocks, depth, 128), F32),
            pltpu.VMEM((rest, 128, width), F32),
            pltpu.VMEM(shifts.shape, F32),
            pltpu.VMEM((length, size), F32),
            pltpu.VMEM((length, size), F32),
            dma((experts,)),
            dma((experts,)),
            dma((blocks,)),
            dma((blocks,)),
            dma((share, blocks)),
            dma((share, blocks)),
            dma((2,)),
            dma((2,)),
            dma((blocks,)),
            dma((blocks,)),
            dma((1,)),
            dma((rest, blocks + 1)),
        ]
        + sum_scratch(rest, blocks, depth, width, 1),
        input_output_aliases={21: 7, 22: 8},
        compiler_params=pltpu.CompilerParams(
            collective_id=3, has_side_effects=True, vmem_limit_bytes=60 << 20
        ),
    )(
        back_grad,
        slot_of,
        route_of,
        middle,
        cot,
        vectors,
        centroids,
        long_attended,
        short_attended,
        out_weight,
        *long_parts,
        *short_parts,
        key_ids,
        query_ids,
        produced,
        up_rest,
        down_rest,
        up_first,
        down_first,
        shifts,
    )


def close_kernel(
    experts,
    blocks,
    out_ref,
    long_back,
    short_back,
    long_tokens,
    short_tokens,
    vectors,
    weights,
    grad_middle,
    sums_ref,
    centroid_ref,
    up_rest,
    down_rest,
    up_first,
    down_first,
    token_grad,
    up_sum,
    down_sum,
    *refs,
):
    number = 2 + blocks // 2
    outs, refs = refs[:number], refs[number:]
    made, refs = (out_ref,) + refs[: number - 1], refs[number - 1 :]
    from_mate, refs = refs[:number], refs[number:]
    pair_sum, refs = refs[:number], refs[number:]
    from_chips, refs = refs[:number], refs[number:]
    group_sum, refs = refs[:number], refs[number:]
    from_line, refs = refs[:number], refs[number:]
    whole, refs = refs[:number], refs[number:]
    (
        normed_t,
        rows_ref,
        tokens_buf,
        back_buf,
        load_sem,
        mate_send,
        mate_recv,
        chip_send,
        chip_recv,
        line_send,
        line_recv,
        back_send,
        back_recv,
        *refs,
    ) = refs
    rounds = (blocks - 1).bit_length()
    done = tail_share(up_rest.shape[0])
    late = up_rest.shape[0] - done
    if late:
        (up_last, down_last, put_sem), refs = refs[:3], refs[3:]
        steps = up_sum.shape[1] // blocks // 128
        put, put_copies = late_sums(
            up_last, down_last, up_sum, down_sum, put_sem, steps - late, steps
        )
        part_copies, add_parts = line_sums(
            lax.axis_index("blk"),
            blocks,
            (up_rest.at[pl.ds(done, late)],) + tuple(refs[:rounds]),
            (down_rest.at[pl.ds(done, late)],) + tuple(refs[rounds : 2 * rounds]),
            refs[2 * rounds],
            refs[2 * rounds + 1],
            put,
        )
    chips = experts // 2
    me, z = lax.axis_index("expert"), lax.axis_index("blk")
    core = lax.rem(me, 2)
    chip = me // 2
    mate = me + 1 - 2 * core
    span, width = long_tokens.shape
    part = weights.shape[2]
    chunk = min(256, span)

    def line_partner(r):
        bit = 1 << r
        return z + bit - 2 * bit * lax.rem(z // bit, 2)

    loads = [
        pltpu.make_async_copy(source, target, load_sem.at[n])
        for n, (source, target) in enumerate(
            (
                (long_tokens, tokens_buf.at[0]),
                (short_tokens, tokens_buf.at[1]),
                (long_back, back_buf.at[0]),
                (short_back, back_buf.at[1]),
            )
        )
    ]
    for copy in loads:
        copy.start()
    barrier = pltpu.get_barrier_semaphore()
    pl.semaphore_signal(barrier, inc=1, device_id={"expert": mate}, device_id_type=MESH)
    for d in range(1, chips):
        peer = lax.rem(me + 2 * d, experts)
        pl.semaphore_signal(barrier, inc=1, device_id={"expert": peer}, device_id_type=MESH)
    for r in range(rounds):
        pl.semaphore_signal(
            barrier, inc=1, device_id={"blk": line_partner(r)}, device_id_type=MESH
        )
    pl.semaphore_wait(barrier, chips + rounds)

    def mate_copy(p):
        return remote(
            made[p].at[:, 1 - core], from_mate[p], mate_send.at[p], mate_recv.at[p], {"expert": mate}
        )

    def chip_copies(p):
        copies = []
        for d in range(1, chips):
            there = lax.rem(chip + d, chips)
            copies.append(
                remote(
                    pair_sum[p].at[there],
                    from_chips[p].at[d - 1],
                    chip_send.at[p, d],
                    chip_recv.at[p, d],
                    {"expert": 2 * there + core},
                )
            )
        return copies

    def segment(p, r):
        groups = whole[p].shape[0]
        start = 0
        for n in range(r):
            start = start + lax.rem(z // (1 << n), 2) * (groups >> (n + 1))
        return start, groups >> r

    def line_copy(p, r):
        start, groups = segment(p, r)
        half = groups // 2
        mine = lax.rem(z // (1 << r), 2)
        return remote(
            group_sum[p].at[pl.ds(start + (1 - mine) * half, half)],
            from_line[p].at[r, pl.ds(0, half)],
            line_send.at[p, r],
            line_recv.at[p, r],
            {"blk": line_partner(r)},
        )

    def back_copy(p, r, arrives):
        start, groups = segment(p, r + 1)
        if arrives:
            start, _ = segment(p, r)
            start = start + (1 - lax.rem(z // (1 << r), 2)) * groups
        return remote(
            whole[p].at[pl.ds(start, groups)],
            whole[p].at[pl.ds(start, groups)],
            back_send.at[p, r],
            back_recv.at[p, r],
            {"blk": line_partner(r)},
        )

    def add_line(p, r):
        line_copy(p, r).wait_recv()
        start, groups = segment(p, r + 1)
        held = group_sum[p][pl.ds(start, groups)].astype(F32)
        group_sum[p][pl.ds(start, groups)] = (
            held + from_line[p][r, pl.ds(0, groups)].astype(F32)
        ).astype(BF)

    def run(p, stage):
        if stage == 0:
            mate_copy(p).start()
        elif stage == 1:
            mate_copy(p).wait_recv()
            for k in range(chips):
                own = made[p][k, core].astype(F32)
                pair_sum[p][k] = (own + from_mate[p][k].astype(F32)).astype(BF)
            for copy in chip_copies(p):
                copy.start()
        elif stage == 2:
            for copy in chip_copies(p):
                copy.wait_recv()
            total = pair_sum[p][chip].astype(F32)
            for d in range(1, chips):
                total = total + from_chips[p][d - 1].astype(F32)
            low = total.astype(BF)
            used = low.shape[1] // 128
            for g in range(group_sum[p].shape[0]):
                if g < used:
                    group_sum[p][g] = low[:, g * 128 : (g + 1) * 128]
                else:
                    group_sum[p][g] = jnp.zeros(group_sum[p].shape[1:], BF)
            line_copy(p, 0).start()
        elif stage < 2 + rounds:
            add_line(p, stage - 3)
            line_copy(p, stage - 2).start()
        elif stage == 2 + rounds:
            r = rounds - 1
            add_line(p, r)
            start, groups = segment(p, rounds)
            whole[p][pl.ds(start, groups)] = group_sum[p][pl.ds(start, groups)]
            back_copy(p, r, False).start()
        else:
            r = rounds - 1 - (stage - 3 - rounds)
            back_copy(p, r, True).wait_recv()
            if r:
                back_copy(p, r - 1, False).start()
            else:
                for c in range(0, outs[p].shape[1], 128):
                    outs[p][:, c : c + 128] = whole[p][c // 128].astype(F32)

    turns = span // chunk

    def rows_of(turn):
        at = pl.multiple_of(lax.rem(turn, turns) * chunk, chunk)
        return turn // turns, pl.ds(at, chunk), pl.ds(pl.multiple_of(turn * chunk, chunk), chunk)

    def norm_rows():
        for copy in loads:
            copy.wait()

        @pl.loop(0, 2 * turns)
        def _(turn):
            half, inner, outer = rows_of(turn)
            low = norm_low(tokens_buf[half, inner], vectors[0:1], vectors[1:2])
            normed_t[:, outer] = low.T

    def weight_part(q):
        target = made[1 + q]
        rows = target.shape[2]

        def term(lead):
            total = None
            for half in range(2):
                back = back_buf[half, 2 * q : 2 * q + 2].reshape(2 * part, span)
                product = dot_nt(normed_t[lead, half * span : (half + 1) * span], back)
                total = product if total is None else total + product
            return total

        if rows % 16 == 0:
            flat = target.reshape(width, 2 * part)

            @pl.loop(0, width // 256)
            def _(turn):
                lead = pl.ds(pl.multiple_of(turn * 256, 256), 256)
                flat[lead] = term(lead).astype(BF)
        else:
            target[...] = term(slice(None)).reshape(target.shape).astype(BF)

    def finish_rows():
        rows_ref[...] = jnp.zeros_like(rows_ref)
        ones = jnp.ones((span, 128), BF)
        shift_total = None
        for half in range(2):
            shift_part = dot_nn(back_buf[half].reshape(blocks * part, span), ones)
            shift_total = shift_part if shift_total is None else shift_total + shift_part

        @pl.loop(0, 2 * turns)
        def _(turn):
            half, inner, outer = rows_of(turn)
            grad_t = None
            for n in range(blocks):
                product = dot_nn(weights[n], back_buf[half, n, :, :, :, inner].reshape(part, chunk))
                grad_t = product if grad_t is None else grad_t + product
            normal, scale = norm_parts(tokens_buf[half, inner].astype(F32))
            moved, gain_part, bias_part = norm_back(grad_t.T, normal, scale, vectors[0:1])
            token_grad[outer] = grad_middle[outer] + moved
            rows_ref[8 + experts] += gain_part
            rows_ref[9 + experts] += bias_part

        rows_ref[0:8] = sums_ref[...]
        rows_ref[8 : 8 + experts] = centroid_ref[...]
        small = rows_ref[...].T
        lane = lax.broadcasted_iota(jnp.int32, small.shape, 1)
        shift_total = shift_total.reshape(blocks, 3, part // 3, 128)
        for n, kind in enumerate((0, 2)):
            column = shift_total[:, kind].reshape(-1, 128)[:width]
            small = jnp.where(lane == 126 + n, column, small)
        made[number - 1][...] = small.reshape(made[number - 1].shape).astype(BF)

    for p in range(late):
        for copy in part_copies(0, p):
            copy.start()
    stages = 3 + 2 * rounds
    for turn in range(number + stages - 1):
        for p in range(number):
            if 0 < turn - p < stages:
                run(p, turn - p)
        if turn < number:
            if turn == 1:
                norm_rows()
            if 0 < turn < number - 1:
                weight_part(turn - 1)
            if turn == number - 1:
                finish_rows()
            run(turn, 0)
        for r in range(rounds):
            if turn == 2 + 2 * r:
                for p in range(late):
                    add_parts(r, p)
    for p in range(number):
        for copy in [mate_copy(p)] + chip_copies(p):
            copy.wait_send()
        for r in range(rounds):
            line_copy(p, r).wait_send()
            back_copy(p, r, False).wait_send()
    for p in range(late):
        for copy in put_copies(p):
            copy.wait()
        for r in range(rounds):
            for copy in part_copies(r, p):
                copy.wait_send()


def run_close(
    out_term,
    long_back,
    short_back,
    long_tokens,
    short_tokens,
    vectors,
    weights,
    grad_middle,
    sums,
    centroid_term,
    up_rest,
    down_rest,
    up_first,
    down_first,
    experts,
    blocks,
):
    width = out_term.shape[0]
    rows = width // experts
    chips = experts // 2
    rounds = (blocks - 1).bit_length()
    part = weights.shape[2]
    count = grad_middle.shape[0]
    widths = [width] + [2 * part] * (blocks // 2) + [128]
    number = len(widths)
    groups = [-(-w // 128 // blocks) * blocks for w in widths]
    dma = pltpu.SemaphoreType.DMA
    vmem = pl.BlockSpec(memory_space=pltpu.VMEM)
    any_spec = pl.BlockSpec(memory_space=pl.ANY)
    late = up_rest.shape[0] - tail_share(up_rest.shape[0])
    depth = up_rest.shape[2]
    late_scratch = []
    if late:
        late_scratch = [
            pltpu.VMEM((late, blocks, depth, 128), F32),
            pltpu.VMEM((late, 128, width), F32),
            dma((late, blocks + 1)),
        ] + sum_scratch(late, blocks, depth, width, 1)
    return pl.pallas_call(
        functools.partial(close_kernel, experts, blocks),
        in_specs=[vmem] + [any_spec] * 4 + [vmem] * 7 + [any_spec] * 2,
        out_specs=(vmem, any_spec, any_spec) + (vmem,) * number,
        out_shape=(
            jax.ShapeDtypeStruct((count, width), F32),
            jax.ShapeDtypeStruct(up_first.shape, F32),
            jax.ShapeDtypeStruct(down_first.shape, F32),
        )
        + tuple(jax.ShapeDtypeStruct((rows, w), F32) for w in widths),
        scratch_shapes=[pltpu.VMEM((chips, 2, rows, w), BF) for w in widths[1:]]
        + [pltpu.VMEM((chips, rows, w), BF) for w in widths]
        + [pltpu.VMEM((chips, rows, w), BF) for w in widths]
        + [pltpu.VMEM((chips - 1, rows, w), BF) for w in widths]
        + [pltpu.VMEM((g, rows, 128), BF) for g in groups]
        + [pltpu.VMEM((rounds, g // 2, rows, 128), BF) for g in groups]
        + [pltpu.VMEM((g, rows, 128), BF) for g in groups]
        + [
            pltpu.VMEM((width, count), BF),
            pltpu.VMEM((128, width), F32),
            pltpu.VMEM((2,) + long_tokens.shape, BF),
            pltpu.VMEM((2,) + long_back.shape, BF),
            dma((4,)),
        ]
        + [dma((number,)), dma((number,)), dma((number, chips)), dma((number, chips))]
        + [dma((number, rounds))] * 4
        + late_scratch,
        input_output_aliases={12: 1, 13: 2},
        compiler_params=pltpu.CompilerParams(
            collective_id=2, has_side_effects=True, vmem_limit_bytes=60 << 20
        ),
    )(
        out_term.reshape(chips, 2, rows, width),
        long_back,
        short_back,
        long_tokens,
        short_tokens,
        vectors,
        weights,
        grad_middle,
        sums,
        centroid_term,
        up_rest,
        down_rest,
        up_first,
        down_first,
    )


def on_device(
    tokens,
    doc_ids,
    routes,
    ln1_gain,
    ln1_bias,
    qkv_weight,
    qv_bias,
    out_weight,
    out_bias,
    ln2_gain,
    ln2_bias,
    centroids,
    up_weight,
    up_bias,
    down_weight,
    down_bias,
    cotangent,
):
    rows, span, width = tokens.shape
    heads = HEADS
    size = width // heads
    blocks = lax.axis_size("blk")
    own = lax.axis_index("blk")
    count = rows * span
    length = blocks * span
    halo = min(SHORT, span)
    share = -(-heads // blocks)
    pad_heads = share * blocks - heads

    expert_count = centroids.shape[0]

    long_at = (doc_ids[0, -1] != 0).astype(jnp.int32)

    def ordered(pair):
        first = lax.dynamic_index_in_dim(pair, long_at, 0, keepdims=False)
        second = lax.dynamic_index_in_dim(pair, 1 - long_at, 0, keepdims=False)
        return jnp.stack([first, second])

    long_tokens = lax.dynamic_index_in_dim(tokens, long_at, 0, keepdims=False)
    short_tokens = lax.dynamic_index_in_dim(tokens, 1 - long_at, 0, keepdims=False)
    token_rows = jnp.concatenate([long_tokens, short_tokens]).astype(F32)

    capacity = 2 * count // expert_count
    slots = expert_count * capacity
    slot_line = jnp.arange(slots, dtype=jnp.int32)
    vectors = jnp.concatenate(
        [
            ln1_gain[None],
            ln1_bias[None],
            ln2_gain[None],
            ln2_bias[None],
            jnp.zeros((4, width), F32),
        ]
    )

    def grouped(matrix):
        lead = matrix.shape[0]
        split = matrix.reshape(lead, 3, heads, size)
        split = jnp.pad(split, ((0, 0), (0, 0), (0, pad_heads), (0, 0)))
        split = split.reshape(lead, 3, blocks, share, size).transpose(2, 0, 1, 3, 4)
        return split.reshape(blocks, lead, 3 * share * size)

    def ungrouped(matrix):
        lead = matrix.shape[0]
        split = matrix.reshape(lead, blocks, 3, share, size).transpose(0, 2, 1, 3, 4)
        return split.reshape(lead, 3, blocks * share, size)[:, :, :heads].reshape(lead, 3, width)

    short_ids = jnp.concatenate(
        [
            jnp.full((halo,), -1, jnp.int32),
            lax.dynamic_index_in_dim(doc_ids, 1 - long_at, 0, keepdims=False),
        ]
    )
    short_ids = lax.dynamic_slice_in_dim(short_ids, own * span, halo + span, 0)
    key_ids = short_ids[:, None]
    query_ids = short_ids[None, halo:]
    shifts = jnp.concatenate([qv_bias[0], jnp.zeros((width,), F32), qv_bias[1]])
    full_qkv, full_out, rest = run_front(
        grouped(qkv_weight),
        out_weight,
        long_tokens,
        short_tokens,
        cotangent.reshape(count, width),
        routes.reshape(1, count),
        vectors,
        grouped(shifts[None]),
        key_ids,
        query_ids,
        expert_count,
        blocks,
    )
    (
        received_cot,
        slot_of,
        long_attended,
        long_qkv,
        long_wide,
        long_total,
        short_qkv,
        short_wide,
        short_low,
        short_total,
    ) = rest
    long_attended = long_attended.reshape(-1, span)[:width]
    attended_t = jnp.concatenate([long_attended, short_low], axis=1)
    slot_of = ordered(slot_of.reshape(rows, span)).reshape(count)
    route_flat = ordered(routes.reshape(rows, span)).reshape(count)
    grad_low = ordered(cotangent).reshape(count, width)

    middle = (
        token_rows
        + lax.dot_general(
            attended_t, full_out, (((0,), (0,)), ((), ())), preferred_element_type=F32
        )
        + out_bias
    )
    to_slots = (slot_line[:, None] == slot_of[None, :]).astype(BF)
    expert_in = layer_norm(middle, ln2_gain, ln2_bias).astype(BF)
    outgoing = dot_nn(to_slots, expert_in).astype(BF).reshape(expert_count, capacity, width)

    own_centroid = lax.dynamic_index_in_dim(
        centroids.astype(F32), lax.axis_index("expert"), 0, keepdims=True
    )
    back_grad, produced, up_first, down_first, up_rest, down_rest, up_shift, down_shift = run_expert(
        outgoing,
        received_cot,
        up_weight[0],
        down_weight[0],
        up_bias,
        down_bias,
        own_centroid,
        blocks,
    )
    shift_parts = jnp.concatenate([up_shift, down_shift.reshape(blocks, 1, -1)], axis=2)
    shift_parts = jnp.pad(shift_parts, ((0, 0), (0, 0), (0, -shift_parts.shape[2] % 128)))
    (
        long_back,
        short_back,
        grad_middle,
        result,
        out_term,
        tail_sums,
        centroid_term,
        up_sum,
        down_sum,
        shift_sum,
    ) = run_tail(
        back_grad.reshape(slots, width),
        slot_of[:, None],
        route_flat[:, None],
        middle,
        grad_low,
        vectors,
        centroids.astype(F32),
        long_attended,
        short_low,
        full_out,
        (long_qkv, long_wide, long_total),
        (short_qkv, short_wide, short_total),
        key_ids,
        query_ids,
        produced,
        up_rest,
        down_rest,
        up_first,
        down_first,
        shift_parts,
        blocks,
    )
    grad_tokens, up_sum, down_sum, out_sum, *qkv_sums, small_sum = run_close(
        out_term,
        long_back,
        short_back,
        long_tokens,
        short_tokens,
        vectors,
        full_qkv,
        grad_middle,
        tail_sums,
        centroid_term,
        up_rest,
        down_rest,
        up_sum,
        down_sum,
        expert_count,
        blocks,
    )
    qkv_sum = jnp.concatenate(qkv_sums, axis=1)
    norm_at = 8 + expert_count
    shift_cut = up_bias.shape[1] // blocks
    up_shift_sum = shift_sum[:, :shift_cut]
    down_shift_sum = shift_sum[:, shift_cut : shift_cut + width // blocks]
    return (
        ordered(result.reshape(rows, span, width)),
        ordered(grad_tokens.reshape(rows, span, width)),
        small_sum[:, norm_at],
        small_sum[:, norm_at + 1],
        ungrouped(qkv_sum).reshape(-1, 3 * width),
        small_sum[:, 126:].T,
        out_sum,
        small_sum[:, 2],
        small_sum[:, 0],
        small_sum[:, 1],
        small_sum[:, 8:norm_at].T,
        up_sum[None],
        up_shift_sum,
        down_sum[None],
        down_shift_sum,
    )


def solution(mesh):
    return jax.shard_map(
        on_device,
        mesh=mesh,
        in_specs=(
            P("expert", "blk", None),
            P("expert", None),
            P("blk", "expert", None, None),
            P(),
            P(),
            P("expert", None),
            P(),
            P("expert", None),
            P(),
            P(),
            P(),
            P(),
            P("expert", None, None),
            P("expert", None),
            P("expert", None, None),
            P("expert", None),
            P("expert", "blk", None),
        ),
        out_specs=(
            P("expert", "blk", None),
            P("expert", "blk", None),
            P("expert"),
            P("expert"),
            P("expert", None),
            P(None, "expert"),
            P("expert", None),
            P("expert"),
            P("expert"),
            P("expert"),
            P(None, "expert"),
            P("expert", "blk", None),
            P("expert", "blk"),
            P("expert", "blk", None),
            P("expert", "blk"),
        ),
        check_vma=False,
    )
```

```python
import functools

import jax
import jax.numpy as jnp
from jax import lax
from jax.experimental import pallas as pl
from jax.experimental.pallas import tpu as pltpu
from jax.sharding import PartitionSpec as P

HEADS = 12
SHORT = 256
NEGATIVE = -1e30
EPSILON = 1e-05
BF = jnp.bfloat16
F32 = jnp.float32


def dot_nn(a, b):
    return lax.dot_general(a, b, (((1,), (0,)), ((), ())), preferred_element_type=F32)


def dot_nt(a, b):
    return lax.dot_general(a, b, (((1,), (1,)), ((), ())), preferred_element_type=F32)


def norm_parts(values):
    average = jnp.mean(values, axis=-1, keepdims=True)
    centred = values - average
    variance = jnp.mean(centred * centred, axis=-1, keepdims=True)
    scale = lax.rsqrt(variance + EPSILON)
    return centred * scale, scale


def layer_norm(values, gain, bias):
    return norm_parts(values)[0] * gain + bias


def norm_back(upstream, normal, scale, gain):
    t = upstream * gain
    inner = (
        t
        - jnp.mean(t, axis=-1, keepdims=True)
        - normal * jnp.mean(t * normal, axis=-1, keepdims=True)
    )
    return inner * scale, jnp.sum(upstream * normal, axis=0), jnp.sum(upstream, axis=0)


def causal(rows, columns, shift):
    row = lax.broadcasted_iota(jnp.int32, (rows, columns), 0)
    column = lax.broadcasted_iota(jnp.int32, (rows, columns), 1)
    return row <= column + shift


def norm_low(values, gain, bias):
    return layer_norm(values.astype(F32), gain, bias).astype(BF)


def scaled(query):
    return (query.astype(F32) * query.shape[-1] ** (-0.5)).astype(BF)


def short_visible(key_ids, query_ids, i, block, halo):
    lo = i * block
    same = key_ids[lo : lo + halo + block] == query_ids[:, lo : lo + block]
    return same & causal(halo + block, block, halo)


MESH = pl.DeviceIdType.MESH


def remote(source, target, send_sem, recv_sem, device):
    return pltpu.make_async_remote_copy(
        src_ref=source,
        dst_ref=target,
        send_sem=send_sem,
        recv_sem=recv_sem,
        device_id=device,
        device_id_type=MESH,
    )


def across(place, mask, count):
    bit = 1
    while bit < count:
        place_bit, mask_bit = lax.rem(place // bit, 2), lax.rem(mask // bit, 2)
        place = place + bit * mask_bit * (1 - 2 * place_bit)
        bit *= 2
    return place


def greet(experts, blocks):
    me, z = lax.axis_index("expert"), lax.axis_index("blk")
    barrier = pltpu.get_barrier_semaphore()
    for d in range(1, experts):
        pl.semaphore_signal(
            barrier, inc=1, device_id={"expert": lax.rem(me + d, experts)}, device_id_type=MESH
        )
    for d in range(1, blocks):
        pl.semaphore_signal(
            barrier, inc=1, device_id={"blk": lax.rem(z + d, blocks)}, device_id_type=MESH
        )
    pl.semaphore_wait(barrier, experts + blocks - 2)


def front_kernel(
    experts,
    blocks,
    heads,
    gathers,
    block,
    short_block,
    qkv_ref,
    out_ref,
    row_ref,
    short_ref,
    cot_ref,
    route_ref,
    vectors,
    shift_ref,
    key_ids,
    query_ids,
    *refs,
):
    if gathers:
        (full_qkv, full_out), refs = refs[:2], refs[2:]
    else:
        full_qkv = qkv_ref
    (
        received_cot,
        slot_out,
        attended,
        long_qkv,
        long_wide,
        long_total,
        short_qkv,
        short_wide,
        short_low,
        short_total,
        weights,
        rows_buf,
        short_buf,
        long_store,
        short_store,
        low_stage,
        cot_stage,
        shard_send,
        shard_recv,
        row_send,
        row_recv,
        edge_sem,
        local_sem,
        cot_send,
        cot_recv,
        low_send,
        low_recv,
    ) = refs
    me, z = lax.axis_index("expert"), lax.axis_index("blk")
    step = pl.program_id(0)
    mate = me + 1 - 2 * lax.rem(me, 2)
    peers = [lax.rem(me + 2 * d, experts) for d in range(1, experts // 2)]
    share, size = long_store.shape[1], long_store.shape[3]
    length = blocks * block
    span = block
    halo = short_buf.shape[0] - span
    shard_rows = qkv_ref.shape[1]

    def qkv_part(slot):
        return full_qkv.at[:, pl.ds(pl.multiple_of(slot * shard_rows, shard_rows), shard_rows)]

    def shard(n, own, slot, turn, target):
        part = (qkv_part(slot), full_out.at[slot])[n]
        source = (qkv_ref, out_ref)[n] if own else part
        return remote(
            source, part, shard_send.at[n, turn], shard_recv.at[n, slot], {"expert": target}
        )

    def row(slot, turn, target):
        return remote(
            rows_buf.at[slot],
            rows_buf.at[slot],
            row_send.at[turn],
            row_recv.at[slot],
            {"blk": target},
        )

    def own_row(turn, target):
        return remote(
            row_ref, rows_buf.at[z], row_send.at[turn], row_recv.at[z], {"blk": target}
        )

    to_right, to_left = z + 1 < blocks, z > 0
    right, left = lax.rem(z + 1, blocks), lax.rem(z + blocks - 1, blocks)
    last_rows = short_ref.at[pl.ds(span - halo, halo)]
    halo_rows = short_buf.at[pl.ds(0, halo)]
    edge = remote(last_rows, halo_rows, edge_sem.at[0], edge_sem.at[1], {"blk": right})
    no_edge = pltpu.make_async_copy(last_rows, halo_rows, edge_sem.at[1])
    local = [
        pltpu.make_async_copy(row_ref, rows_buf.at[z], local_sem.at[0]),
        pltpu.make_async_copy(short_ref, short_buf.at[pl.ds(halo, span)], local_sem.at[1]),
    ]
    own_cot = pltpu.make_async_copy(cot_stage.at[me], received_cot.at[me], local_sem.at[2])
    load_weights = pltpu.make_async_copy(full_qkv, weights, local_sem.at[3])
    own_shards = []
    sent = []
    handed = []
    if gathers:
        own_shards = [
            pltpu.make_async_copy(qkv_ref, qkv_part(me), local_sem.at[4]),
            pltpu.make_async_copy(out_ref, full_out.at[me], local_sem.at[5]),
        ]
        for n in range(2):
            for turn, peer in enumerate(peers):
                sent.append(shard(n, True, me, turn, peer))
            sent.append(shard(n, True, me, len(peers), mate))
            for turn, peer in enumerate(peers):
                handed.append(shard(n, False, peer, len(peers) + 1 + turn, mate))

    def cot_copy(d):
        target = lax.rem(me + d, experts)
        return remote(
            cot_stage.at[target],
            received_cot.at[me],
            cot_send.at[d],
            cot_recv.at[d],
            {"expert": target},
        )

    def low_copy(head, d):
        target = lax.rem(z + d, blocks)
        return remote(
            low_stage.at[target, head],
            attended.at[z, head],
            low_send.at[head, d],
            low_recv.at[head, d],
            {"blk": target},
        )

    def low_local(head):
        return pltpu.make_async_copy(
            low_stage.at[z, head], attended.at[z, head], low_send.at[head, 0]
        )

    def hand_on(k):
        @pl.when(z - k >= 0)
        def _():
            slot = jnp.maximum(z - k, 0)
            row(slot, 2 * k, right).wait_recv()

            @pl.when(to_right)
            def _():
                row(slot, 2 * k, right).start()

        @pl.when(z + k < blocks)
        def _():
            slot = jnp.minimum(z + k, blocks - 1)
            row(slot, 2 * k + 1, left).wait_recv()

            @pl.when(to_left)
            def _():
                row(slot, 2 * k + 1, left).start()

    def project(source, rows, groups, store):
        low = norm_low(source, vectors[0:1], vectors[1:2])
        for n, group in enumerate(groups):
            part = (dot_nn(low, weights[group]) + shift_ref[group]).astype(BF)
            for kind in range(3):
                for head in range(share):
                    at = (kind * share + head) * size
                    if n * share + head < store.shape[1]:
                        store[kind, n * share + head, rows] = part[:, at : at + size]

    def sort_cot():
        capacity, width = cot_stage.shape[1:]
        count = cot_ref.shape[0]
        lines = -(-experts // 8) * 8
        expert_line = lax.broadcasted_iota(jnp.int32, (lines, count), 0)
        named = (route_ref[...] == expert_line).astype(F32)
        upto = lax.broadcasted_iota(jnp.int32, (count, count), 0) <= lax.broadcasted_iota(
            jnp.int32, (count, count), 1
        )
        ranks = dot_nn(named.astype(BF), upto.astype(F32).astype(BF))
        slots = named * (ranks - 1.0 + (expert_line * capacity).astype(F32))
        slots = jnp.sum(slots, axis=0, keepdims=True).astype(jnp.int32)
        slot_out[...] = slots
        flat = cot_stage.reshape(experts * capacity, width)
        block_rows = min(512, experts * capacity)

        @pl.loop(0, experts * capacity // block_rows)
        def _(turn):
            first = pl.multiple_of(turn * block_rows, block_rows)
            line = lax.broadcasted_iota(jnp.int32, (block_rows, count), 0) + first
            chosen = (line == slots).astype(F32).astype(BF)
            flat[pl.ds(first, block_rows)] = dot_nn(chosen, cot_ref[...]).astype(BF)

    @pl.when(step == 0)
    def _():
        for copy in local + own_shards:
            copy.start()
        greet(experts, blocks)

        @pl.when(to_right)
        def _():
            own_row(0, right).start()
            edge.start()

        @pl.when(to_left)
        def _():
            own_row(1, left).start()

        @pl.when(jnp.logical_not(to_left))
        def _():
            no_edge.start()

        for copy in sent:
            copy.start()
        sort_cot()
        hand_on(1)
        for copy in handed:
            copy.wait_recv()
            copy.start()
        if gathers:
            for turn in range(experts // 2):
                for n in range(2):
                    shard(n, False, lax.rem(mate + 2 * turn, experts), 0, mate).wait_recv()
        for copy in own_shards:
            copy.wait()
        load_weights.start()
        own_cot.start()
        for d in range(1, experts):
            cot_copy(d).start()

        @pl.when(to_left)
        def _():
            edge.wait_recv()

        @pl.when(jnp.logical_not(to_left))
        def _():
            no_edge.wait()

        for copy in local:
            copy.wait()
        load_weights.wait()

        @pl.loop(0, (halo + span) // short_block)
        def _(turn):
            rows = pl.ds(pl.multiple_of(turn * short_block, short_block), short_block)
            project(short_buf[rows], rows, range(blocks), short_store)

    for k in range(2, blocks):

        @pl.when(step == (k - 1) * heads // (blocks - 1))
        def _(k=k):
            hand_on(k)

    @pl.when(step < heads)
    def _():
        query, key, value = (short_store[kind, step] for kind in range(3))
        for kind, part in enumerate((query, key, value)):
            short_qkv[kind, 0] = part
        query = scaled(query)
        value_t = value.T
        for i in range(span // short_block):
            lo, hi = i * short_block, (i + 1) * short_block
            visible = short_visible(key_ids[...], query_ids[...], i, short_block, halo)
            scores = dot_nt(key[lo : hi + halo], query[lo + halo : hi + halo])
            scores = jnp.where(visible, scores, NEGATIVE)
            top = jnp.max(scores, axis=0, keepdims=True)
            scores = jnp.exp(scores - top)
            total = jnp.sum(scores, axis=0, keepdims=True)
            out = dot_nn(value_t[:, lo : hi + halo], scores.astype(BF)) / total
            short_wide[:, lo:hi] = out
            short_low[:, lo:hi] = out.astype(BF)
            short_total[0, :, lo:hi] = top + jnp.log(total)

    @pl.when(step == heads)
    def _():
        @pl.loop(0, blocks)
        def _(slot):
            rows = pl.ds(pl.multiple_of(slot * block, block), block)
            project(rows_buf[slot], rows, [z], long_store)

    @pl.when(step >= heads)
    def _():
        head = step - heads
        query, key, value = (long_store[kind, head] for kind in range(3))
        for kind, part in enumerate((query, key, value)):
            long_qkv[kind, 0] = part
        query = scaled(query)
        value_t = value.T
        visible = causal(block, block, 0)
        for i in range(blocks):
            lo, hi = i * block, (i + 1) * block
            own = query[lo:hi]
            near = jnp.where(visible, dot_nt(key[lo:hi], own), NEGATIVE)
            top = jnp.max(near, axis=0, keepdims=True)
            if i:
                far = dot_nt(key[:lo], own)
                top = jnp.maximum(top, jnp.max(far, axis=0, keepdims=True))
            near = jnp.exp(near - top)
            total = jnp.sum(near, axis=0, keepdims=True)
            out = dot_nn(value_t[:, lo:hi], near.astype(BF))
            if i:
                far = jnp.exp(far - top)
                total = total + jnp.sum(far, axis=0, keepdims=True)
                out = out + dot_nn(value_t[:, :lo], far.astype(BF))
            out = out / total
            long_wide[:, lo:hi] = out
            low_stage[i, head] = out.astype(BF)
            long_total[0, :, lo:hi] = top + jnp.log(total)
        low_local(head).start()
        for d in range(1, blocks):
            low_copy(head, d).start()

    @pl.when(step == heads + share - 1)
    def _():
        for head in range(share):
            low_local(head).wait()
            for d in range(1, blocks):
                low_copy(head, d).wait()
        own_cot.wait()
        for d in range(1, experts):
            cot_copy(d).wait()
        for copy in sent + handed:
            copy.wait_send()

        @pl.when(to_right)
        def _():
            own_row(0, right).wait_send()
            edge.wait_send()

        @pl.when(to_left)
        def _():
            own_row(1, left).wait_send()

        for k in range(1, blocks):

            @pl.when((z - k >= 0) & to_right)
            def _(k=k):
                row(jnp.maximum(z - k, 0), 2 * k, right).wait_send()

            @pl.when((z + k < blocks) & to_left)
            def _(k=k):
                row(jnp.minimum(z + k, blocks - 1), 2 * k + 1, left).wait_send()


def run_front(
    qkv_shard, out_shard, row, short_row, cot, routes, vectors, shifts, key_ids, query_ids, experts, blocks
):
    span, width = row.shape
    size = width // HEADS
    halo = key_ids.shape[0] - span
    part = qkv_shard.shape[2]
    share = part // size // 3
    length = blocks * span
    sorted_shape = (experts, 2 * cot.shape[0] // experts, width)
    gathers = qkv_shard.shape[1] % 16 == 0
    if not gathers:
        qkv_shard = lax.all_gather(qkv_shard, "expert", axis=1, tiled=True)
        full_out = lax.all_gather(out_shard, "expert", axis=0, tiled=True)
    any_spec = pl.BlockSpec(memory_space=pl.ANY)
    dma = pltpu.SemaphoreType.DMA

    def whole(shape):
        return pl.BlockSpec(shape, lambda f: (0,) * len(shape), pipeline_mode=pl.Buffered(1))

    def short_head(*shape):
        return pl.BlockSpec(
            shape, lambda f: (0,) * (len(shape) - 3) + (jnp.minimum(f, HEADS - 1), 0, 0)
        )

    def long_head(*shape):
        return pl.BlockSpec(
            shape, lambda f: (0,) * (len(shape) - 3) + (jnp.maximum(f - HEADS, 0), 0, 0)
        )

    def flat_short(*shape):
        return pl.BlockSpec(shape, lambda f: (jnp.minimum(f, HEADS - 1), 0))

    gathered_shapes = (
        jax.ShapeDtypeStruct((blocks, width, part), BF),
        jax.ShapeDtypeStruct((experts,) + out_shard.shape, BF),
    )
    results = pl.pallas_call(
        functools.partial(
            front_kernel, experts, blocks, HEADS, gathers, span, min(SHORT, span)
        ),
        grid=(HEADS + share,),
        in_specs=[any_spec] * 4
        + [
            whole(cot.shape),
            whole(routes.shape),
            whole(vectors.shape),
            whole((blocks, 1, part)),
            whole((halo + span, 1)),
            whole((1, span)),
        ],
        out_specs=((any_spec,) * 2 if gathers else ())
        + (
            any_spec,
            whole(routes.shape),
            any_spec,
            long_head(3, 1, length, size),
            pl.BlockSpec((size, length), lambda f: (jnp.maximum(f - HEADS, 0), 0)),
            long_head(1, 1, length),
            short_head(3, 1, halo + span, size),
            flat_short(size, span),
            flat_short(size, span),
            short_head(1, 1, span),
        ),
        out_shape=(gathered_shapes if gathers else ())
        + (
            jax.ShapeDtypeStruct(sorted_shape, BF),
            jax.ShapeDtypeStruct(routes.shape, jnp.int32),
            jax.ShapeDtypeStruct((blocks, share, size, span), BF),
            jax.ShapeDtypeStruct((3, share, length, size), BF),
            jax.ShapeDtypeStruct((share * size, length), F32),
            jax.ShapeDtypeStruct((share, 1, length), F32),
            jax.ShapeDtypeStruct((3, HEADS, halo + span, size), BF),
            jax.ShapeDtypeStruct((width, span), F32),
            jax.ShapeDtypeStruct((width, span), BF),
            jax.ShapeDtypeStruct((HEADS, 1, span), F32),
        ),
        scratch_shapes=[
            pltpu.VMEM((blocks, width, part), BF),
            pltpu.VMEM((blocks, span, width), BF),
            pltpu.VMEM((halo + span, width), BF),
            pltpu.VMEM((3, share, length, size), BF),
            pltpu.VMEM((3, HEADS, halo + span, size), BF),
            pltpu.VMEM((blocks, share, size, span), BF),
            pltpu.VMEM(sorted_shape, BF),
            dma((2, experts)),
            dma((2, experts)),
            dma((2 * blocks,)),
            dma((blocks,)),
            dma((2,)),
            dma((6,)),
            dma((experts,)),
            dma((experts,)),
            dma((share, blocks)),
            dma((share, blocks)),
        ],
        compiler_params=pltpu.CompilerParams(
            collective_id=0, has_side_effects=True, vmem_limit_bytes=56 << 20
        ),
    )(qkv_shard, out_shard, row, short_row, cot, routes, vectors, shifts, key_ids, query_ids)
    if gathers:
        return results[0], results[1].reshape(-1, out_shard.shape[1]), results[2:]
    return qkv_shard, full_out, results


def line_sums(z, blocks, up_held, down_held, part_send, part_recv, put):
    rounds = len(up_held) - 1

    def part_copies(r, p):
        bit = 1 << r
        mine = lax.rem(z // bit, 2)
        partner = z + bit - 2 * bit * mine
        copies = []
        for k in range((blocks >> r) // 2):
            for n, held in enumerate((up_held, down_held)):
                copies.append(
                    remote(
                        held[r].at[p, 2 * k + 1 - mine],
                        held[r + 1].at[p, k],
                        part_send.at[r, n, p, k],
                        part_recv.at[r, n, p, k],
                        {"blk": partner},
                    )
                )
        return copies

    def add_parts(r, p):
        mine = lax.rem(z // (1 << r), 2)
        for copy in part_copies(r, p):
            copy.wait_recv()
        for k in range((blocks >> r) // 2):
            up = up_held[r][p, 2 * k + mine].astype(F32) + up_held[r + 1][p, k].astype(F32)
            down = down_held[r][p, 2 * k + mine].astype(F32) + down_held[r + 1][p, k].astype(F32)
            if r + 1 < rounds:
                up_held[r + 1][p, k] = up.astype(BF)
                down_held[r + 1][p, k] = down.astype(BF)
            else:
                put(p, up, down.T)
        if r + 1 < rounds:
            for copy in part_copies(r + 1, p):
                copy.start()

    return part_copies, add_parts


def late_sums(up_last, down_last, up_sum, down_sum, put_sem, first_part, steps):
    lanes = down_last.shape[1]
    blocks = up_last.shape[1]

    def put_copies(p):
        copies = []
        for j in range(blocks):
            first = (j * steps + first_part + p) * lanes
            copies.append(
                pltpu.make_async_copy(
                    up_last.at[p, j], up_sum.at[:, pl.ds(first, lanes)], put_sem.at[p, j]
                )
            )
        copies.append(
            pltpu.make_async_copy(
                down_last.at[p],
                down_sum.at[pl.ds((first_part + p) * lanes, lanes)],
                put_sem.at[p, blocks],
            )
        )
        return copies

    def put(p, up, down):
        for j in range(blocks):
            up_last[p, j] = up[:, j * lanes : (j + 1) * lanes]
        down_last[p] = down
        for copy in put_copies(p):
            copy.start()

    return put, put_copies


def sum_scratch(parts, blocks, depth, width, first):
    rounds = (blocks - 1).bit_length()
    lanes = 128
    dma = pltpu.SemaphoreType.DMA
    return (
        [
            pltpu.VMEM((parts, blocks >> r, depth, blocks * lanes), BF)
            for r in range(first, rounds + 1)
        ]
        + [pltpu.VMEM((parts, blocks >> r, width, lanes), BF) for r in range(first, rounds + 1)]
        + [dma((rounds, 2, parts, blocks // 2)), dma((rounds, 2, parts, blocks // 2))]
    )


def gelu_parts(hidden):
    cdf = 0.5 * (1.0 + lax.erf(hidden * 0.7071067811865476))
    density = jnp.exp(-0.5 * hidden * hidden) * 0.3989422804014327
    return hidden * cdf, cdf + hidden * density


def expert_kernel(
    experts,
    blocks,
    steps,
    rest,
    chunk,
    x_hbm,
    cot_hbm,
    *refs,
):
    ups, refs = refs[:blocks], refs[blocks:]
    downs, refs = refs[:blocks], refs[blocks:]
    up_shifts, refs = refs[:blocks], refs[blocks:]
    (
        down_shift_ref,
        centroid_ref,
        back_grad,
        produced,
        up_sum,
        down_sum,
        up_rest,
        down_rest,
        up_shift_out,
        down_shift_out,
        x_buf,
        low_buf,
        xt_ref,
        gt_ref,
        out_acc,
        grad_acc,
        gate_ref,
        up_acc,
        down_acc,
        shift_acc,
        x_send,
        x_recv,
        back_send,
        back_recv,
        local_sem,
        *refs,
    ) = refs
    rounds = (blocks - 1).bit_length()
    up_held, down_held = refs[: rounds + 1], refs[rounds + 1 : 2 * rounds + 2]
    part_send, part_recv = refs[2 * rounds + 2 :]
    step = pl.program_id(0)
    me, z = lax.axis_index("expert"), lax.axis_index("blk")
    capacity, width = x_buf.shape[1:]
    rows = experts * capacity
    lanes = 128
    sources, chunks = chunk // capacity, rows // chunk

    def x_copy(d):
        target = across(me, jnp.int32(d), experts)
        return remote(
            x_hbm.at[target], x_buf.at[me], x_send.at[d], x_recv.at[d], {"expert": target}
        )

    def back_copy(d):
        target = across(me, jnp.int32(d), experts)
        return remote(
            low_buf.at[target],
            back_grad.at[me],
            back_send.at[d],
            back_recv.at[d],
            {"expert": target},
        )

    back_local = pltpu.make_async_copy(low_buf.at[me], back_grad.at[me], local_sem.at[0])
    out_copy = pltpu.make_async_copy(x_buf, produced, local_sem.at[1])


    def put(p, up, down):
        for j in range(blocks):
            first = (j * steps + p) * lanes
            up_sum[:, first : first + lanes] = up[:, j * lanes : (j + 1) * lanes]
        down_sum[p * lanes : (p + 1) * lanes] = down

    part_copies, add_parts = line_sums(
        z, blocks, up_held, down_held, part_send, part_recv, put
    )
    cot_copy = pltpu.make_async_copy(cot_hbm, low_buf, local_sem.at[2])
    own_copy = pltpu.make_async_copy(x_hbm.at[me], x_buf.at[me], local_sem.at[3])
    x_flat, low_flat = x_buf.reshape(rows, width), low_buf.reshape(rows, width)

    @pl.when(step == 0)
    def _():
        barrier = pltpu.get_barrier_semaphore()
        for d in range(1, experts):
            pl.semaphore_signal(
                barrier, inc=1, device_id={"expert": lax.rem(me + d, experts)}, device_id_type=MESH
            )
        for r in range(rounds):
            bit = 1 << r
            partner = z + bit - 2 * bit * lax.rem(z // bit, 2)
            pl.semaphore_signal(barrier, inc=1, device_id={"blk": partner}, device_id_type=MESH)
        cot_copy.start()
        own_copy.start()
        pl.semaphore_wait(barrier, experts - 1 + rounds)
        for d in range(1, experts):
            x_copy(d).start()
        up_sum[...] = jnp.zeros_like(up_sum)
        down_sum[...] = jnp.zeros_like(down_sum)
        out_acc[...] = jnp.zeros_like(out_acc)
        grad_acc[...] = jnp.zeros_like(grad_acc)
        cot_copy.wait()
        own_copy.wait()
        down_shift_out[...] = jnp.zeros_like(down_shift_out)

    def prepare(at, near):
        for n in range(sources):
            d = near * sources + n

            @pl.when(d != 0)
            def _(d=d):
                x_copy(d).wait_recv()

        x = x_flat[at]
        logit = jnp.sum(x.astype(F32) * centroid_ref[...], axis=1, keepdims=True)
        gate = 1.0 / (1.0 + jnp.exp(-logit))
        gate_ref[at] = gate
        low = (low_flat[at].astype(F32) * gate).astype(BF)
        low_flat[at] = low
        xt_ref[:, at] = x.T
        gt_ref[:, at] = low.T
        down_shift_out[...] += jnp.sum(low.astype(F32), axis=0, keepdims=True)

    def answer(at, near):
        gate = gate_ref[at]
        out = (out_acc[at] + down_shift_ref[...]).astype(BF)
        inner = jnp.sum(low_flat[at].astype(F32) * out.astype(F32), axis=1, keepdims=True)
        x_flat[at] = out
        low_flat[at] = (grad_acc[at] + inner * (1.0 - gate) * centroid_ref[...]).astype(BF)
        for n in range(sources):
            d = near * sources + n

            @pl.when(d != 0)
            def _(d=d):
                back_copy(d).start()

    up = jnp.concatenate([ref[...] for ref in ups], axis=1)
    down = jnp.concatenate([ref[...] for ref in downs], axis=0)
    up_shift = jnp.concatenate([ref[...] for ref in up_shifts], axis=1)
    up_acc[...] = jnp.zeros_like(up_acc)
    down_acc[...] = jnp.zeros_like(down_acc)
    shift_acc[...] = jnp.zeros_like(shift_acc)

    @pl.loop(0, chunks)
    def _(turn):
        near = jnp.where(step == steps - 1, chunks - 1 - turn, turn)
        at = pl.ds(pl.multiple_of(across(me // sources, near, chunks) * chunk, chunk), chunk)

        @pl.when(step == 0)
        def _():
            prepare(at, near)

        x = x_flat[at]
        low = low_flat[at]
        hidden = dot_nn(x, up) + up_shift
        active, slope = gelu_parts(hidden)
        active = active.astype(BF)
        grad_low = (dot_nt(low, down) * slope).astype(BF)
        out_acc[at] += dot_nn(active, down)
        grad_acc[at] += dot_nt(grad_low, up)
        up_acc[...] += dot_nn(xt_ref[:, at], grad_low)
        down_acc[...] += dot_nn(gt_ref[:, at], active)
        shift_acc[...] += jnp.sum(grad_low.astype(F32), axis=0, keepdims=True)

        @pl.when(step == steps - 1)
        def _():
            answer(at, near)

    depth = width // blocks
    keep = steps - rest
    for j in range(blocks):
        up_shift_out[j] = shift_acc[:, j * lanes : (j + 1) * lanes]

    def store(up_target, down_target):
        for j in range(blocks):
            up_target[j] = up_acc[j * depth : (j + 1) * depth].astype(BF)
            down_target[j] = down_acc[:, j * lanes : (j + 1) * lanes].astype(BF)

    @pl.when(step < keep)
    def _():
        store(up_held[0].at[step], down_held[0].at[step])
        for copy in part_copies(0, step):
            copy.start()

    @pl.when(step >= keep)
    def _():
        store(up_rest.at[0], down_rest.at[0])

    tasks = sorted(
        ((r, p) for p in range(keep) for r in range(rounds)), key=lambda task: (sum(task), task[0])
    )
    early = [[] for _ in range(steps)]
    for turn, task in enumerate(tasks):
        at = 2 * (task[1] + 1) + 2 * task[0]
        if at < steps - 1:
            early[at].append(task)
    for at in range(steps):
        if early[at]:

            @pl.when(step == at)
            def _(at=at):
                for r, p in early[at]:
                    add_parts(r, p)

    @pl.when(step == steps - 1)
    def _():
        for d in range(1, experts):
            x_copy(d).wait_send()
        back_local.start()
        out_copy.start()
        for r, p in tasks:
            if all((r, p) not in done for done in early):
                add_parts(r, p)
        back_local.wait()
        out_copy.wait()
        for d in range(1, experts):
            back_copy(d).wait()
        for p in range(keep):
            for r in range(rounds):
                for copy in part_copies(r, p):
                    copy.wait_send()


def run_expert(x, cot, up_weight, down_weight, up_shift, down_shift, centroid, blocks):
    experts, capacity, width = x.shape
    rows = experts * capacity
    hidden = up_weight.shape[1]
    lanes = 128
    steps = hidden // blocks // lanes
    rounds = (blocks - 1).bit_length()
    chunk = min(512, rows)
    depth = width // blocks
    rest = steps // 3
    keep = steps - rest
    any_spec = pl.BlockSpec(memory_space=pl.ANY)

    def once(shape):
        return pl.BlockSpec(shape, lambda f: (0,) * len(shape), pipeline_mode=pl.Buffered(1))

    return pl.pallas_call(
        functools.partial(expert_kernel, experts, blocks, steps, rest, chunk),
        grid=(steps,),
        in_specs=[any_spec] * 2
        + [pl.BlockSpec((width, lanes), lambda f, j=j: (0, j * steps + f)) for j in range(blocks)]
        + [pl.BlockSpec((lanes, width), lambda f, j=j: (j * steps + f, 0)) for j in range(blocks)]
        + [pl.BlockSpec((1, lanes), lambda f, j=j: (0, j * steps + f)) for j in range(blocks)]
        + [once((1, width))] * 2,
        out_specs=(
            any_spec,
            any_spec,
            once((depth, hidden)),
            once((hidden // blocks, width)),
            pl.BlockSpec(
                (1, blocks, depth, blocks * lanes), lambda f: (jnp.maximum(f - keep, 0), 0, 0, 0)
            ),
            pl.BlockSpec(
                (1, blocks, width, lanes), lambda f: (jnp.maximum(f - keep, 0), 0, 0, 0)
            ),
            pl.BlockSpec((blocks, 1, lanes), lambda f: (0, 0, f)),
            once((1, width)),
        ),
        out_shape=(
            jax.ShapeDtypeStruct(x.shape, BF),
            jax.ShapeDtypeStruct(x.shape, BF),
            jax.ShapeDtypeStruct((depth, hidden), F32),
            jax.ShapeDtypeStruct((hidden // blocks, width), F32),
            jax.ShapeDtypeStruct((rest, blocks, depth, blocks * lanes), BF),
            jax.ShapeDtypeStruct((rest, blocks, width, lanes), BF),
            jax.ShapeDtypeStruct((blocks, 1, hidden // blocks), F32),
            jax.ShapeDtypeStruct((1, width), F32),
        ),
        scratch_shapes=[
            pltpu.VMEM(x.shape, BF),
            pltpu.VMEM(x.shape, BF),
            pltpu.VMEM((width, rows), BF),
            pltpu.VMEM((width, rows), BF),
            pltpu.VMEM((rows, width), F32),
            pltpu.VMEM((rows, width), F32),
            pltpu.VMEM((rows, 1), F32),
            pltpu.VMEM((width, blocks * lanes), F32),
            pltpu.VMEM((width, blocks * lanes), F32),
            pltpu.VMEM((1, blocks * lanes), F32),
            pltpu.SemaphoreType.DMA((experts,)),
            pltpu.SemaphoreType.DMA((experts,)),
            pltpu.SemaphoreType.DMA((experts,)),
            pltpu.SemaphoreType.DMA((experts,)),
            pltpu.SemaphoreType.DMA((4,)),
        ]
        + sum_scratch(keep, blocks, depth, width, 0),
        compiler_params=pltpu.CompilerParams(
            collective_id=1, has_side_effects=True, vmem_limit_bytes=62 << 20
        ),
        cost_estimate=pl.CostEstimate(
            flops=12 * rows * width * hidden, bytes_accessed=40 << 20, transcendentals=0
        ),
    )(
        x,
        cot,
        *([up_weight] * blocks),
        *([down_weight] * blocks),
        *([up_shift] * blocks),
        down_shift,
        centroid,
    )


def long_back_head(query, key, value, grad_ref, wide_ref, total_ref, out_ref, head, key_acc, value_acc):
    scale = query.shape[1] ** (-0.5)
    query = scaled(query)
    key_t = key.T
    count, _, _, block = grad_ref.shape
    visible = causal(block, block, 0)
    key_acc[...] = jnp.zeros_like(key_acc)
    value_acc[...] = jnp.zeros_like(value_acc)
    for i in range(count):
        lo, hi = i * block, (i + 1) * block
        own = query[lo:hi]
        grad_t = grad_ref[i, head]
        grad = grad_t.T
        delta = jnp.sum(grad_t.astype(F32) * wide_ref[:, lo:hi], axis=0, keepdims=True)
        total = total_ref[0, :, lo:hi]
        query_grad = None
        for start, stop in ((lo, hi), (0, lo)):
            if start == stop:
                continue
            weights = jnp.exp(dot_nt(key[start:stop], own) - total)
            if start == lo:
                weights = jnp.where(visible, weights, 0.0)
            scores = weights * (dot_nt(value[start:stop], grad) - delta)
            scores_low = scores.astype(BF)
            value_acc[start:stop] += dot_nn(weights.astype(BF), grad)
            key_acc[start:stop] += dot_nn(scores_low, own)
            part = dot_nn(key_t[:, start:stop], scores_low)
            query_grad = part if query_grad is None else query_grad + part
        out_ref[i, 0, head] = (query_grad * scale).astype(BF)
    key_grad = key_acc[...].T.astype(BF)
    value_grad = value_acc[...].T.astype(BF)
    for i in range(count):
        out_ref[i, 1, head] = key_grad[:, i * block : (i + 1) * block]
        out_ref[i, 2, head] = value_grad[:, i * block : (i + 1) * block]


def short_back_head(
    query, key, value, grad_t, wide_ref, total_ref, key_ids, query_ids, key_acc, value_acc, block
):
    scale = query.shape[1] ** (-0.5)
    query = scaled(query)
    key_t = key.T
    extent, span = query.shape[0], query_ids.shape[1]
    halo = extent - span
    key_acc[0:extent] = jnp.zeros((extent, key_acc.shape[1]), F32)
    value_acc[0:extent] = jnp.zeros((extent, key_acc.shape[1]), F32)
    query_grads = []
    for i in range(span // block):
        lo, hi = i * block, (i + 1) * block
        visible = short_visible(key_ids[...], query_ids[...], i, block, halo)
        own = query[lo + halo : hi + halo]
        part_t = grad_t[:, lo:hi]
        grad = part_t.T
        delta = jnp.sum(part_t.astype(F32) * wide_ref[:, lo:hi], axis=0, keepdims=True)
        scores = dot_nt(key[lo : hi + halo], own)
        weights = jnp.exp(jnp.where(visible, scores, NEGATIVE) - total_ref[0, :, lo:hi])
        scores = weights * (dot_nt(value[lo : hi + halo], grad) - delta)
        scores_low = scores.astype(BF)
        value_acc[lo : hi + halo] += dot_nn(weights.astype(BF), grad)
        key_acc[lo : hi + halo] += dot_nn(scores_low, own)
        part = dot_nn(key_t[:, lo : hi + halo], scores_low)
        query_grads.append(part * scale)
    query_grad = jnp.concatenate(query_grads, axis=1)
    return query_grad, key_acc[0:extent].T, value_acc[0:extent].T


def tail_kernel(
    experts,
    blocks,
    heads,
    lead,
    rest,
    back_grad,
    slot_ref,
    route_ref,
    middle_ref,
    cot_ref,
    vectors,
    centroid_ref,
    long_attended,
    short_attended,
    out_weight,
    long_qkv,
    long_wide,
    long_total,
    short_qkv,
    short_wide,
    short_total,
    key_ids,
    query_ids,
    produced,
    up_rest,
    down_rest,
    up_first,
    down_first,
    shift_ref,
    long_back,
    short_back,
    grad_middle,
    result_ref,
    out_term,
    sums_ref,
    centroid_out,
    up_sum,
    down_sum,
    shift_sum,
    grad_low,
    long_stage,
    short_grad,
    long_grad,
    back_stage,
    halo_stage,
    halo_in,
    own_edge,
    back_out,
    up_last,
    down_last,
    shift_in,
    key_acc,
    value_acc,
    out_send,
    out_recv,
    grad_send,
    grad_recv,
    back_send,
    back_recv,
    halo_send,
    halo_recv,
    shift_send,
    shift_recv,
    local_sem,
    put_sem,
    *refs,
):
    rounds = (blocks - 1).bit_length()
    up_held = (up_rest,) + refs[:rounds]
    down_held = (down_rest,) + refs[rounds : 2 * rounds]
    part_send, part_recv = refs[2 * rounds :]
    step = pl.program_id(0)
    me, z = lax.axis_index("expert"), lax.axis_index("blk")
    share, size, span = long_stage.shape[1:]
    width = out_weight.shape[0]
    count = slot_ref.shape[0]
    halo = halo_stage.shape[3]
    chunk = min(256, span)
    steps = up_sum.shape[1] // blocks // 128
    keep = steps - up_rest.shape[0]
    put, put_copies = late_sums(up_last, down_last, up_sum, down_sum, put_sem, keep, steps)
    part_copies, add_parts = line_sums(
        z, blocks, up_held, down_held, part_send, part_recv, put
    )
    line = [lax.rem(z + d, blocks) for d in range(blocks)]

    def out_copy(d):
        target = lax.rem(me + d, experts)
        return remote(
            produced.at[target], back_out.at[me], out_send.at[d], out_recv.at[d], {"expert": target}
        )

    def grad_copy(d):
        return remote(
            long_stage.at[line[d]], long_grad.at[z], grad_send.at[d], grad_recv.at[d], {"blk": line[d]}
        )

    def back_copy(head, d):
        return remote(
            back_stage.at[line[d], :, head],
            long_back.at[z, :, head],
            back_send.at[head, d],
            back_recv.at[head, d],
            {"blk": line[d]},
        )

    def back_local(head):
        return pltpu.make_async_copy(
            back_stage.at[z, :, head], long_back.at[z, :, head], back_send.at[head, 0]
        )

    def shift_copy(d):
        return remote(
            shift_ref.at[line[d]], shift_in.at[d], shift_send.at[d], shift_recv.at[d], {"blk": line[d]}
        )

    halo_parts = [part for part in ((0, lead), (lead, heads - lead)) if part[1]]

    def halo_copy(n):
        part = pl.ds(*halo_parts[n])
        left = lax.rem(z + blocks - 1, blocks)
        return remote(
            halo_stage.at[:, part], halo_in.at[:, part], halo_send.at[n], halo_recv.at[n], {"blk": left}
        )

    own_out_copy = pltpu.make_async_copy(produced.at[me], back_out.at[me], local_sem.at[0])

    def send_halo(n):
        @pl.when(z > 0)
        def _():
            halo_copy(n).start()

    @pl.when(step == 0)
    def _():
        greet(experts, blocks)
        for copy in part_copies(0, 0):
            copy.start()
        for d in range(1, blocks):
            shift_copy(d).start()
        own_out_copy.start()
        for d in range(1, experts):
            out_copy(d).start()
        spare = blocks * share - heads
        flat_stage = long_stage.reshape(blocks * share, size, span)
        if spare:
            flat_stage[heads:] = jnp.zeros((spare, size, span), BF)
            short_back[...] = jnp.zeros_like(short_back)
        slot_line = lax.broadcasted_iota(jnp.int32, (chunk, back_grad.shape[0]), 1)
        sums_ref[...] = jnp.zeros_like(sums_ref)

        def back_rows(turn, first, store):
            at = pl.multiple_of(turn * chunk, chunk)
            rows = pl.ds(pl.multiple_of(first + at, chunk), chunk)
            chosen = (slot_ref[rows] == slot_line).astype(F32).astype(BF)
            upstream = dot_nn(chosen, back_grad[...])
            normal, scale = norm_parts(middle_ref[rows])
            inner, gain_part, bias_part = norm_back(upstream, normal, scale, vectors[2:3])
            middle = cot_ref[rows].astype(F32) + inner
            grad_middle[rows] = middle
            low = middle.astype(BF)
            grad_low[rows] = low
            for n, part in enumerate((gain_part, bias_part, jnp.sum(middle, axis=0))):
                sums_ref[n] += part
            grad_t = dot_nt(out_weight[...], low).astype(BF).reshape(heads, size, chunk)
            store[:heads, :, pl.ds(at, chunk)] = grad_t

        pl.loop(0, span // chunk)(lambda turn: back_rows(turn, 0, flat_stage))
        for d in range(1, blocks):
            grad_copy(d).start()
        pl.loop(0, span // chunk)(lambda turn: back_rows(turn, span, short_grad))
        out_term[...] = (
            dot_nn(long_attended[...], grad_low[:span]) + dot_nn(short_attended[...], grad_low[span:])
        ).astype(BF)

    first_long = lead + 1
    is_long = (step >= first_long) & (step < first_long + share)

    @pl.when((step > 0) & jnp.logical_not(is_long))
    def _():
        head = step - 1 - jnp.where(step >= first_long, share, 0)
        query, key, value = (short_qkv[kind, 0] for kind in range(3))
        grads = short_back_head(
            query,
            key,
            value,
            short_grad[head],
            short_wide,
            short_total,
            key_ids,
            query_ids,
            key_acc,
            value_acc,
            min(SHORT, span),
        )
        group = head // share
        place = head - group * share
        for n, grad in enumerate(grads):
            short_back[group, n, place] = grad[:, grad.shape[1] - span :].astype(BF)
            if n:
                halo_stage[n - 1, head] = grad[:, :halo].astype(BF)
                own_edge[n - 1, head] = grad[:, span:]

    @pl.when(step == lead)
    def _():
        send_halo(0)

    @pl.when(step == first_long)
    def _():
        for d in range(1, blocks):
            grad_copy(d).wait_recv()
        long_grad[z] = long_stage[z]
        add_parts(0, 0)
        for p in range(1, rest):
            for copy in part_copies(0, p):
                copy.start()

    @pl.when(is_long)
    def _():
        head = step - first_long
        query, key, value = (long_qkv[kind, 0] for kind in range(3))
        long_back_head(
            query, key, value, long_grad, long_wide, long_total, back_stage, head, key_acc, value_acc
        )
        back_local(head).start()
        for d in range(1, blocks):
            back_copy(head, d).start()

    tasks = sorted(
        ((r, p) for p in range(rest) for r in range(rounds)), key=lambda task: (sum(task), task[0])
    )[1:]

    @pl.when(step == first_long + share)
    def _():
        for r, p in tasks[:-1]:
            add_parts(r, p)

    @pl.when(step == heads + share)
    def _():
        if len(halo_parts) > 1:
            send_halo(1)
        own_out_copy.wait()
        for d in range(1, experts):
            out_copy(d).wait_recv()
        answers = back_out.reshape(back_grad.shape)
        slot_line = lax.broadcasted_iota(jnp.int32, (chunk, back_grad.shape[0]), 1)
        expert_line = lax.broadcasted_iota(jnp.int32, (chunk, 128), 1)
        centroid_rows = jnp.concatenate(
            [centroid_ref[...], jnp.zeros((128 - experts, width), F32)], axis=0
        ).astype(BF)
        centroid_out[...] = jnp.zeros_like(centroid_out)

        @pl.loop(0, count // chunk)
        def _(turn):
            rows = pl.ds(pl.multiple_of(turn * chunk, chunk), chunk)
            chosen = (slot_ref[rows] == slot_line).astype(F32).astype(BF)
            answer = dot_nn(chosen, answers[...])
            middle = middle_ref[rows]
            normed = norm_parts(middle)[0] * vectors[2:3] + vectors[3:4]
            named = (route_ref[rows] == expert_line).astype(F32)
            logit = jnp.sum(
                normed * dot_nn(named.astype(BF), centroid_rows), axis=1, keepdims=True
            )
            gate = 1.0 / (1.0 + jnp.exp(-logit))
            result_ref[rows] = middle + gate * answer
            inner = jnp.sum(cot_ref[rows].astype(F32) * answer, axis=1, keepdims=True)
            part = lax.dot_general(
                named,
                inner * gate * (1.0 - gate) * normed,
                (((0,), (0,)), ((), ())),
                preferred_element_type=F32,
            )
            centroid_out[...] += part[:experts]

        if tasks:
            add_parts(*tasks[-1])
        for p in range(rest):
            for copy in put_copies(p):
                copy.wait()
        for d in range(1, blocks):
            shift_copy(d).wait()
        total = shift_ref[z]
        for d in range(1, blocks):
            total = total + shift_in[d]
        shift_sum[...] = total
        for d in range(1, experts):
            out_copy(d).wait_send()
        for d in range(1, blocks):
            grad_copy(d).wait_send()
        for head in range(share):
            back_local(head).wait()
            for d in range(1, blocks):
                back_copy(head, d).wait()
        for p in range(rest):
            for r in range(rounds):
                for copy in part_copies(r, p):
                    copy.wait_send()
        for n in range(len(halo_parts)):

            @pl.when(z > 0)
            def _(n=n):
                halo_copy(n).wait_send()

            @pl.when(z < blocks - 1)
            def _(n=n):
                halo_copy(n).wait_recv()

        @pl.when(z < blocks - 1)
        def _():
            for head in range(heads):
                for n in range(2):
                    edge = own_edge[n, head] + halo_in[n, head].astype(F32)
                    short_back[head // share, 1 + n, head % share, :, span - halo :] = edge.astype(BF)


def tail_share(rest):
    return (rest + 1) // 2


def run_tail(
    back_grad,
    slot_of,
    route_of,
    middle,
    cot,
    vectors,
    centroids,
    long_attended,
    short_attended,
    out_weight,
    long_parts,
    short_parts,
    key_ids,
    query_ids,
    produced,
    up_rest,
    down_rest,
    up_first,
    down_first,
    shifts,
    blocks,
):
    experts = produced.shape[0]
    slots, width = back_grad.shape
    count = slot_of.shape[0]
    long_qkv, long_wide, long_total = long_parts
    short_qkv, short_wide, short_total = short_parts
    _, share, length, size = long_qkv.shape
    extent, span = short_qkv.shape[2], query_ids.shape[1]
    halo = extent - span
    heads = HEADS
    lead = heads // 2
    depth = up_rest.shape[2]
    rest = tail_share(up_rest.shape[0])
    hidden = up_first.shape[1]
    any_spec = pl.BlockSpec(memory_space=pl.ANY)
    dma = pltpu.SemaphoreType.DMA

    def whole(shape):
        return pl.BlockSpec(shape, lambda f: (0,) * len(shape), pipeline_mode=pl.Buffered(1))

    def short_at(f):
        return jnp.where(f <= lead, jnp.maximum(f - 1, 0), jnp.maximum(f - 1 - share, lead - 1))

    def long_at(f):
        return jnp.clip(f - 1 - lead, 0, share - 1)

    return pl.pallas_call(
        functools.partial(tail_kernel, experts, blocks, heads, lead, rest),
        grid=(1 + heads + share,),
        in_specs=[
            whole(back_grad.shape),
            whole(slot_of.shape),
            whole(route_of.shape),
            whole(middle.shape),
            whole(cot.shape),
            whole(vectors.shape),
            whole(centroids.shape),
            whole(long_attended.shape),
            whole(short_attended.shape),
            whole(out_weight.shape),
            pl.BlockSpec((3, 1, length, size), lambda f: (0, long_at(f), 0, 0)),
            pl.BlockSpec((size, length), lambda f: (long_at(f), 0)),
            pl.BlockSpec((1, 1, length), lambda f: (long_at(f), 0, 0)),
            pl.BlockSpec((3, 1, extent, size), lambda f: (0, short_at(f), 0, 0)),
            pl.BlockSpec((size, span), lambda f: (short_at(f), 0)),
            pl.BlockSpec((1, 1, span), lambda f: (short_at(f), 0, 0)),
            whole(key_ids.shape),
            whole(query_ids.shape),
            any_spec,
            whole(up_rest.shape),
            whole(down_rest.shape),
            any_spec,
            any_spec,
            whole(shifts.shape),
        ],
        out_specs=(
            any_spec,
            whole((blocks, 3, share, size, span)),
            whole((count, width)),
            whole((count, width)),
            whole((width, width)),
            whole((8, width)),
            whole((experts, width)),
            any_spec,
            any_spec,
            whole(shifts.shape[1:]),
        ),
        out_shape=(
            jax.ShapeDtypeStruct((blocks, 3, share, size, span), BF),
            jax.ShapeDtypeStruct((blocks, 3, share, size, span), BF),
            jax.ShapeDtypeStruct((count, width), F32),
            jax.ShapeDtypeStruct((count, width), F32),
            jax.ShapeDtypeStruct((width, width), BF),
            jax.ShapeDtypeStruct((8, width), F32),
            jax.ShapeDtypeStruct((experts, width), F32),
            jax.ShapeDtypeStruct((depth, hidden), F32),
            jax.ShapeDtypeStruct((hidden // blocks, width), F32),
            jax.ShapeDtypeStruct(shifts.shape[1:], F32),
        ),
        scratch_shapes=[
            pltpu.VMEM((count, width), BF),
            pltpu.VMEM((blocks, share, size, span), BF),
            pltpu.VMEM((heads, size, span), BF),
            pltpu.VMEM((blocks, share, size, span), BF),
            pltpu.VMEM((blocks, 3, share, size, span), BF),
            pltpu.VMEM((2, heads, size, halo), BF),
            pltpu.VMEM((2, heads, size, halo), BF),
            pltpu.VMEM((2, heads, size, halo), F32),
            pltpu.VMEM(produced.shape, BF),
            pltpu.VMEM((rest, blocks, depth, 128), F32),
            pltpu.VMEM((rest, 128, width), F32),
            pltpu.VMEM(shifts.shape, F32),
            pltpu.VMEM((length, size), F32),
            pltpu.VMEM((length, size), F32),
            dma((experts,)),
            dma((experts,)),
            dma((blocks,)),
            dma((blocks,)),
            dma((share, blocks)),
            dma((share, blocks)),
            dma((2,)),
            dma((2,)),
            dma((blocks,)),
            dma((blocks,)),
            dma((1,)),
            dma((rest, blocks + 1)),
        ]
        + sum_scratch(rest, blocks, depth, width, 1),
        input_output_aliases={21: 7, 22: 8},
        compiler_params=pltpu.CompilerParams(
            collective_id=3, has_side_effects=True, vmem_limit_bytes=60 << 20
        ),
    )(
        back_grad,
        slot_of,
        route_of,
        middle,
        cot,
        vectors,
        centroids,
        long_attended,
        short_attended,
        out_weight,
        *long_parts,
        *short_parts,
        key_ids,
        query_ids,
        produced,
        up_rest,
        down_rest,
        up_first,
        down_first,
        shifts,
    )


def close_kernel(
    experts,
    blocks,
    out_ref,
    long_back,
    short_back,
    long_tokens,
    short_tokens,
    vectors,
    weights,
    grad_middle,
    sums_ref,
    centroid_ref,
    up_rest,
    down_rest,
    up_first,
    down_first,
    token_grad,
    up_sum,
    down_sum,
    *refs,
):
    number = 2 + blocks // 2
    outs, refs = refs[:number], refs[number:]
    made, refs = (out_ref,) + refs[: number - 1], refs[number - 1 :]
    from_mate, refs = refs[:number], refs[number:]
    pair_sum, refs = refs[:number], refs[number:]
    from_chips, refs = refs[:number], refs[number:]
    group_sum, refs = refs[:number], refs[number:]
    from_line, refs = refs[:number], refs[number:]
    whole, refs = refs[:number], refs[number:]
    (
        normed_t,
        rows_ref,
        tokens_buf,
        back_buf,
        load_sem,
        mate_send,
        mate_recv,
        chip_send,
        chip_recv,
        line_send,
        line_recv,
        back_send,
        back_recv,
        *refs,
    ) = refs
    rounds = (blocks - 1).bit_length()
    done = tail_share(up_rest.shape[0])
    late = up_rest.shape[0] - done
    if late:
        (up_last, down_last, put_sem), refs = refs[:3], refs[3:]
        steps = up_sum.shape[1] // blocks // 128
        put, put_copies = late_sums(
            up_last, down_last, up_sum, down_sum, put_sem, steps - late, steps
        )
        part_copies, add_parts = line_sums(
            lax.axis_index("blk"),
            blocks,
            (up_rest.at[pl.ds(done, late)],) + tuple(refs[:rounds]),
            (down_rest.at[pl.ds(done, late)],) + tuple(refs[rounds : 2 * rounds]),
            refs[2 * rounds],
            refs[2 * rounds + 1],
            put,
        )
    chips = experts // 2
    me, z = lax.axis_index("expert"), lax.axis_index("blk")
    core = lax.rem(me, 2)
    chip = me // 2
    mate = me + 1 - 2 * core
    span, width = long_tokens.shape
    part = weights.shape[2]
    chunk = min(256, span)

    def line_partner(r):
        bit = 1 << r
        return z + bit - 2 * bit * lax.rem(z // bit, 2)

    loads = [
        pltpu.make_async_copy(source, target, load_sem.at[n])
        for n, (source, target) in enumerate(
            (
                (long_tokens, tokens_buf.at[0]),
                (short_tokens, tokens_buf.at[1]),
                (long_back, back_buf.at[0]),
                (short_back, back_buf.at[1]),
            )
        )
    ]
    for copy in loads:
        copy.start()
    barrier = pltpu.get_barrier_semaphore()
    pl.semaphore_signal(barrier, inc=1, device_id={"expert": mate}, device_id_type=MESH)
    for d in range(1, chips):
        peer = lax.rem(me + 2 * d, experts)
        pl.semaphore_signal(barrier, inc=1, device_id={"expert": peer}, device_id_type=MESH)
    for r in range(rounds):
        pl.semaphore_signal(
            barrier, inc=1, device_id={"blk": line_partner(r)}, device_id_type=MESH
        )
    pl.semaphore_wait(barrier, chips + rounds)

    def mate_copy(p):
        return remote(
            made[p].at[:, 1 - core], from_mate[p], mate_send.at[p], mate_recv.at[p], {"expert": mate}
        )

    def chip_copies(p):
        copies = []
        for d in range(1, chips):
            there = lax.rem(chip + d, chips)
            copies.append(
                remote(
                    pair_sum[p].at[there],
                    from_chips[p].at[d - 1],
                    chip_send.at[p, d],
                    chip_recv.at[p, d],
                    {"expert": 2 * there + core},
                )
            )
        return copies

    def segment(p, r):
        groups = whole[p].shape[0]
        start = 0
        for n in range(r):
            start = start + lax.rem(z // (1 << n), 2) * (groups >> (n + 1))
        return start, groups >> r

    def line_copy(p, r):
        start, groups = segment(p, r)
        half = groups // 2
        mine = lax.rem(z // (1 << r), 2)
        return remote(
            group_sum[p].at[pl.ds(start + (1 - mine) * half, half)],
            from_line[p].at[r, pl.ds(0, half)],
            line_send.at[p, r],
            line_recv.at[p, r],
            {"blk": line_partner(r)},
        )

    def back_copy(p, r, arrives):
        start, groups = segment(p, r + 1)
        if arrives:
            start, _ = segment(p, r)
            start = start + (1 - lax.rem(z // (1 << r), 2)) * groups
        return remote(
            whole[p].at[pl.ds(start, groups)],
            whole[p].at[pl.ds(start, groups)],
            back_send.at[p, r],
            back_recv.at[p, r],
            {"blk": line_partner(r)},
        )

    def add_line(p, r):
        line_copy(p, r).wait_recv()
        start, groups = segment(p, r + 1)
        held = group_sum[p][pl.ds(start, groups)].astype(F32)
        group_sum[p][pl.ds(start, groups)] = (
            held + from_line[p][r, pl.ds(0, groups)].astype(F32)
        ).astype(BF)

    def run(p, stage):
        if stage == 0:
            mate_copy(p).start()
        elif stage == 1:
            mate_copy(p).wait_recv()
            for k in range(chips):
                own = made[p][k, core].astype(F32)
                pair_sum[p][k] = (own + from_mate[p][k].astype(F32)).astype(BF)
            for copy in chip_copies(p):
                copy.start()
        elif stage == 2:
            for copy in chip_copies(p):
                copy.wait_recv()
            total = pair_sum[p][chip].astype(F32)
            for d in range(1, chips):
                total = total + from_chips[p][d - 1].astype(F32)
            low = total.astype(BF)
            used = low.shape[1] // 128
            for g in range(group_sum[p].shape[0]):
                if g < used:
                    group_sum[p][g] = low[:, g * 128 : (g + 1) * 128]
                else:
                    group_sum[p][g] = jnp.zeros(group_sum[p].shape[1:], BF)
            line_copy(p, 0).start()
        elif stage < 2 + rounds:
            add_line(p, stage - 3)
            line_copy(p, stage - 2).start()
        elif stage == 2 + rounds:
            r = rounds - 1
            add_line(p, r)
            start, groups = segment(p, rounds)
            whole[p][pl.ds(start, groups)] = group_sum[p][pl.ds(start, groups)]
            back_copy(p, r, False).start()
        else:
            r = rounds - 1 - (stage - 3 - rounds)
            back_copy(p, r, True).wait_recv()
            if r:
                back_copy(p, r - 1, False).start()
            else:
                for c in range(0, outs[p].shape[1], 128):
                    outs[p][:, c : c + 128] = whole[p][c // 128].astype(F32)

    turns = span // chunk

    def rows_of(turn):
        at = pl.multiple_of(lax.rem(turn, turns) * chunk, chunk)
        return turn // turns, pl.ds(at, chunk), pl.ds(pl.multiple_of(turn * chunk, chunk), chunk)

    def norm_rows():
        for copy in loads:
            copy.wait()

        @pl.loop(0, 2 * turns)
        def _(turn):
            half, inner, outer = rows_of(turn)
            low = norm_low(tokens_buf[half, inner], vectors[0:1], vectors[1:2])
            normed_t[:, outer] = low.T

    def weight_part(q):
        target = made[1 + q]
        rows = target.shape[2]

        def term(lead):
            total = None
            for half in range(2):
                back = back_buf[half, 2 * q : 2 * q + 2].reshape(2 * part, span)
                product = dot_nt(normed_t[lead, half * span : (half + 1) * span], back)
                total = product if total is None else total + product
            return total

        if rows % 16 == 0:
            flat = target.reshape(width, 2 * part)

            @pl.loop(0, width // 256)
            def _(turn):
                lead = pl.ds(pl.multiple_of(turn * 256, 256), 256)
                flat[lead] = term(lead).astype(BF)
        else:
            target[...] = term(slice(None)).reshape(target.shape).astype(BF)

    def finish_rows():
        rows_ref[...] = jnp.zeros_like(rows_ref)
        ones = jnp.ones((span, 128), BF)
        shift_total = None
        for half in range(2):
            shift_part = dot_nn(back_buf[half].reshape(blocks * part, span), ones)
            shift_total = shift_part if shift_total is None else shift_total + shift_part

        @pl.loop(0, 2 * turns)
        def _(turn):
            half, inner, outer = rows_of(turn)
            grad_t = None
            for n in range(blocks):
                product = dot_nn(weights[n], back_buf[half, n, :, :, :, inner].reshape(part, chunk))
                grad_t = product if grad_t is None else grad_t + product
            normal, scale = norm_parts(tokens_buf[half, inner].astype(F32))
            moved, gain_part, bias_part = norm_back(grad_t.T, normal, scale, vectors[0:1])
            token_grad[outer] = grad_middle[outer] + moved
            rows_ref[8 + experts] += gain_part
            rows_ref[9 + experts] += bias_part

        rows_ref[0:8] = sums_ref[...]
        rows_ref[8 : 8 + experts] = centroid_ref[...]
        small = rows_ref[...].T
        lane = lax.broadcasted_iota(jnp.int32, small.shape, 1)
        shift_total = shift_total.reshape(blocks, 3, part // 3, 128)
        for n, kind in enumerate((0, 2)):
            column = shift_total[:, kind].reshape(-1, 128)[:width]
            small = jnp.where(lane == 126 + n, column, small)
        made[number - 1][...] = small.reshape(made[number - 1].shape).astype(BF)

    for p in range(late):
        for copy in part_copies(0, p):
            copy.start()
    stages = 3 + 2 * rounds
    for turn in range(number + stages - 1):
        for p in range(number):
            if 0 < turn - p < stages:
                run(p, turn - p)
        if turn < number:
            if turn == 1:
                norm_rows()
            if 0 < turn < number - 1:
                weight_part(turn - 1)
            if turn == number - 1:
                finish_rows()
            run(turn, 0)
        for r in range(rounds):
            if turn == 2 + 2 * r:
                for p in range(late):
                    add_parts(r, p)
    for p in range(number):
        for copy in [mate_copy(p)] + chip_copies(p):
            copy.wait_send()
        for r in range(rounds):
            line_copy(p, r).wait_send()
            back_copy(p, r, False).wait_send()
    for p in range(late):
        for copy in put_copies(p):
            copy.wait()
        for r in range(rounds):
            for copy in part_copies(r, p):
                copy.wait_send()


def run_close(
    out_term,
    long_back,
    short_back,
    long_tokens,
    short_tokens,
    vectors,
    weights,
    grad_middle,
    sums,
    centroid_term,
    up_rest,
    down_rest,
    up_first,
    down_first,
    experts,
    blocks,
):
    width = out_term.shape[0]
    rows = width // experts
    chips = experts // 2
    rounds = (blocks - 1).bit_length()
    part = weights.shape[2]
    count = grad_middle.shape[0]
    widths = [width] + [2 * part] * (blocks // 2) + [128]
    number = len(widths)
    groups = [-(-w // 128 // blocks) * blocks for w in widths]
    dma = pltpu.SemaphoreType.DMA
    vmem = pl.BlockSpec(memory_space=pltpu.VMEM)
    any_spec = pl.BlockSpec(memory_space=pl.ANY)
    late = up_rest.shape[0] - tail_share(up_rest.shape[0])
    depth = up_rest.shape[2]
    late_scratch = []
    if late:
        late_scratch = [
            pltpu.VMEM((late, blocks, depth, 128), F32),
            pltpu.VMEM((late, 128, width), F32),
            dma((late, blocks + 1)),
        ] + sum_scratch(late, blocks, depth, width, 1)
    return pl.pallas_call(
        functools.partial(close_kernel, experts, blocks),
        in_specs=[vmem] + [any_spec] * 4 + [vmem] * 7 + [any_spec] * 2,
        out_specs=(vmem, any_spec, any_spec) + (vmem,) * number,
        out_shape=(
            jax.ShapeDtypeStruct((count, width), F32),
            jax.ShapeDtypeStruct(up_first.shape, F32),
            jax.ShapeDtypeStruct(down_first.shape, F32),
        )
        + tuple(jax.ShapeDtypeStruct((rows, w), F32) for w in widths),
        scratch_shapes=[pltpu.VMEM((chips, 2, rows, w), BF) for w in widths[1:]]
        + [pltpu.VMEM((chips, rows, w), BF) for w in widths]
        + [pltpu.VMEM((chips, rows, w), BF) for w in widths]
        + [pltpu.VMEM((chips - 1, rows, w), BF) for w in widths]
        + [pltpu.VMEM((g, rows, 128), BF) for g in groups]
        + [pltpu.VMEM((rounds, g // 2, rows, 128), BF) for g in groups]
        + [pltpu.VMEM((g, rows, 128), BF) for g in groups]
        + [
            pltpu.VMEM((width, count), BF),
            pltpu.VMEM((128, width), F32),
            pltpu.VMEM((2,) + long_tokens.shape, BF),
            pltpu.VMEM((2,) + long_back.shape, BF),
            dma((4,)),
        ]
        + [dma((number,)), dma((number,)), dma((number, chips)), dma((number, chips))]
        + [dma((number, rounds))] * 4
        + late_scratch,
        input_output_aliases={12: 1, 13: 2},
        compiler_params=pltpu.CompilerParams(
            collective_id=2, has_side_effects=True, vmem_limit_bytes=60 << 20
        ),
    )(
        out_term.reshape(chips, 2, rows, width),
        long_back,
        short_back,
        long_tokens,
        short_tokens,
        vectors,
        weights,
        grad_middle,
        sums,
        centroid_term,
        up_rest,
        down_rest,
        up_first,
        down_first,
    )


def on_device(
    tokens,
    doc_ids,
    routes,
    ln1_gain,
    ln1_bias,
    qkv_weight,
    qv_bias,
    out_weight,
    out_bias,
    ln2_gain,
    ln2_bias,
    centroids,
    up_weight,
    up_bias,
    down_weight,
    down_bias,
    cotangent,
):
    rows, span, width = tokens.shape
    heads = HEADS
    size = width // heads
    blocks = lax.axis_size("blk")
    own = lax.axis_index("blk")
    count = rows * span
    length = blocks * span
    halo = min(SHORT, span)
    share = -(-heads // blocks)
    pad_heads = share * blocks - heads

    expert_count = centroids.shape[0]

    long_at = (doc_ids[0, -1] != 0).astype(jnp.int32)

    def ordered(pair):
        first = lax.dynamic_index_in_dim(pair, long_at, 0, keepdims=False)
        second = lax.dynamic_index_in_dim(pair, 1 - long_at, 0, keepdims=False)
        return jnp.stack([first, second])

    long_tokens = lax.dynamic_index_in_dim(tokens, long_at, 0, keepdims=False)
    short_tokens = lax.dynamic_index_in_dim(tokens, 1 - long_at, 0, keepdims=False)
    token_rows = jnp.concatenate([long_tokens, short_tokens]).astype(F32)

    capacity = 2 * count // expert_count
    slots = expert_count * capacity
    slot_line = jnp.arange(slots, dtype=jnp.int32)
    vectors = jnp.concatenate(
        [
            ln1_gain[None],
            ln1_bias[None],
            ln2_gain[None],
            ln2_bias[None],
            jnp.zeros((4, width), F32),
        ]
    )

    def grouped(matrix):
        lead = matrix.shape[0]
        split = matrix.reshape(lead, 3, heads, size)
        split = jnp.pad(split, ((0, 0), (0, 0), (0, pad_heads), (0, 0)))
        split = split.reshape(lead, 3, blocks, share, size).transpose(2, 0, 1, 3, 4)
        return split.reshape(blocks, lead, 3 * share * size)

    short_ids = jnp.concatenate(
        [
            jnp.full((halo,), -1, jnp.int32),
            lax.dynamic_index_in_dim(doc_ids, 1 - long_at, 0, keepdims=False),
        ]
    )
    short_ids = lax.dynamic_slice_in_dim(short_ids, own * span, halo + span, 0)
    key_ids = short_ids[:, None]
    query_ids = short_ids[None, halo:]
    shifts = jnp.concatenate([qv_bias[0], jnp.zeros((width,), F32), qv_bias[1]])
    full_qkv, full_out, rest = run_front(
        grouped(qkv_weight),
        out_weight,
        long_tokens,
        short_tokens,
        cotangent.reshape(count, width),
        routes.reshape(1, count),
        vectors,
        grouped(shifts[None]),
        key_ids,
        query_ids,
        expert_count,
        blocks,
    )
    (
        received_cot,
        slot_of,
        long_attended,
        long_qkv,
        long_wide,
        long_total,
        short_qkv,
        short_wide,
        short_low,
        short_total,
    ) = rest
    long_attended = long_attended.reshape(-1, span)[:width]
    attended_t = jnp.concatenate([long_attended, short_low], axis=1)
    slot_of = ordered(slot_of.reshape(rows, span)).reshape(count)
    route_flat = ordered(routes.reshape(rows, span)).reshape(count)
    grad_low = ordered(cotangent).reshape(count, width)

    middle = (
        token_rows
        + lax.dot_general(
            attended_t, full_out, (((0,), (0,)), ((), ())), preferred_element_type=F32
        )
        + out_bias
    )
    to_slots = (slot_line[:, None] == slot_of[None, :]).astype(BF)
    expert_in = layer_norm(middle, ln2_gain, ln2_bias).astype(BF)
    outgoing = dot_nn(to_slots, expert_in).astype(BF).reshape(expert_count, capacity, width)

    own_centroid = lax.dynamic_index_in_dim(
        centroids.astype(F32), lax.axis_index("expert"), 0, keepdims=True
    )
    back_grad, produced, up_first, down_first, up_rest, down_rest, up_shift, down_shift = run_expert(
        outgoing,
        received_cot,
        up_weight[0],
        down_weight[0],
        up_bias,
        down_bias,
        own_centroid,
        blocks,
    )
    shift_parts = jnp.concatenate([up_shift, down_shift.reshape(blocks, 1, -1)], axis=2)
    shift_parts = jnp.pad(shift_parts, ((0, 0), (0, 0), (0, -shift_parts.shape[2] % 128)))
    (
        long_back,
        short_back,
        grad_middle,
        result,
        out_term,
        tail_sums,
        centroid_term,
        up_sum,
        down_sum,
        shift_sum,
    ) = run_tail(
        back_grad.reshape(slots, width),
        slot_of[:, None],
        route_flat[:, None],
        middle,
        grad_low,
        vectors,
        centroids.astype(F32),
        long_attended,
        short_low,
        full_out,
        (long_qkv, long_wide, long_total),
        (short_qkv, short_wide, short_total),
        key_ids,
        query_ids,
        produced,
        up_rest,
        down_rest,
        up_first,
        down_first,
        shift_parts,
        blocks,
    )
    grad_tokens, up_sum, down_sum, out_sum, *qkv_sums, small_sum = run_close(
        out_term,
        long_back,
        short_back,
        long_tokens,
        short_tokens,
        vectors,
        full_qkv,
        grad_middle,
        tail_sums,
        centroid_term,
        up_rest,
        down_rest,
        up_sum,
        down_sum,
        expert_count,
        blocks,
    )
    group_columns = share * size
    pieces = []
    for kind in range(3):
        for n in range(blocks):
            kept = min(group_columns, width - n * group_columns)
            if kept > 0:
                first = (n % 2 * 3 + kind) * group_columns
                pieces.append(qkv_sums[n // 2][:, first : first + kept])
    qkv_sum = jnp.concatenate(pieces, axis=1)
    norm_at = 8 + expert_count
    shift_cut = up_bias.shape[1] // blocks
    up_shift_sum = shift_sum[:, :shift_cut]
    down_shift_sum = shift_sum[:, shift_cut : shift_cut + width // blocks]
    return (
        ordered(result.reshape(rows, span, width)),
        ordered(grad_tokens.reshape(rows, span, width)),
        small_sum[:, norm_at],
        small_sum[:, norm_at + 1],
        qkv_sum,
        small_sum[:, 126:].T,
        out_sum,
        small_sum[:, 2],
        small_sum[:, 0],
        small_sum[:, 1],
        small_sum[:, 8:norm_at].T,
        up_sum[None],
        up_shift_sum,
        down_sum[None],
        down_shift_sum,
    )


def solution(mesh):
    return jax.shard_map(
        on_device,
        mesh=mesh,
        in_specs=(
            P("expert", "blk", None),
            P("expert", None),
            P("blk", "expert", None, None),
            P(),
            P(),
            P("expert", None),
            P(),
            P("expert", None),
            P(),
            P(),
            P(),
            P(),
            P("expert", None, None),
            P("expert", None),
            P("expert", None, None),
            P("expert", None),
            P("expert", "blk", None),
        ),
        out_specs=(
            P("expert", "blk", None),
            P("expert", "blk", None),
            P("expert"),
            P("expert"),
            P("expert", None),
            P(None, "expert"),
            P("expert", None),
            P("expert"),
            P("expert"),
            P("expert"),
            P(None, "expert"),
            P("expert", "blk", None),
            P("expert", "blk"),
            P("expert", "blk", None),
            P("expert", "blk"),
        ),
        check_vma=False,
    )
```
